32 devices in a mesh: fsdp: 2 (over x), ctx: 4 (over y, core), tp: 4 (over z).
Axes of the slice: x: 2, y: 2, z: 4, core: 2. Of those that a mesh axis runs over, the one named last changes fastest.
Arguments:
- inputs: bfloat16 [6, 1024, 2048], P('fsdp', 'ctx'), may hold values from -6 to 6
- cotangent: bfloat16 [6, 1024, 2048], P('fsdp', 'ctx'), may hold values from -6 to 6
- master_qkv: float32 [2048, 3, 2048], P(('fsdp', 'ctx'), None, 'tp'), may hold values from -0.125 to 0.125
- qkv_moment1: float32 [2048, 3, 2048], P(('fsdp', 'ctx'), None, 'tp'), may hold values from -448 to 448
- qkv_moment2: float32 [2048, 3, 2048], P(('fsdp', 'ctx'), None, 'tp'), may hold values from 6144 to 24576
- master_out: float32 [2048, 2048], P(('fsdp', 'ctx'), 'tp'), may hold values from -0.375 to 0.375
- out_moment1: float32 [2048, 2048], P(('fsdp', 'ctx'), 'tp'), may hold values from -192 to 192
- out_moment2: float32 [2048, 2048], P(('fsdp', 'ctx'), 'tp'), may hold values from 983.04 to 3932.16
- master_up: float32 [2048, 4, 2048], P(('fsdp', 'ctx'), None, 'tp'), may hold values from -0.125 to 0.125
- up_moment1: float32 [2048, 4, 2048], P(('fsdp', 'ctx'), None, 'tp'), may hold values from -160 to 160
- up_moment2: float32 [2048, 4, 2048], P(('fsdp', 'ctx'), None, 'tp'), may hold values from 675.84 to 2703.36
- master_down: float32 [2048, 4, 2048], P(('fsdp', 'ctx'), None, 'tp'), may hold values from -0.0625 to 0.0625
- down_moment1: float32 [2048, 4, 2048], P(('fsdp', 'ctx'), None, 'tp'), may hold values from -320 to 320
- down_moment2: float32 [2048, 4, 2048], P(('fsdp', 'ctx'), None, 'tp'), may hold values from 2580.48 to 10444.8
- norm_gains: float32 [2, 2048], replicated, may hold values from 0.25 to 1.75
- gain_moment1: float32 [2, 2048], replicated, may hold values from -448 to 448
- gain_moment2: float32 [2, 2048], replicated, may hold values from 6144 to 24576
- shared_biases: float32 [4, 2048], replicated, may hold values from -1.75 to 1.75
- shared_moment1: float32 [4, 2048], replicated, may hold values from -448 to 448
- shared_moment2: float32 [4, 2048], replicated, may hold values from 6144 to 24576
- split_biases: float32 [6, 2048], P(None, 'tp'), may hold values from -1.75 to 1.75
- split_moment1: float32 [6, 2048], P(None, 'tp'), may hold values from -448 to 448
- split_moment2: float32 [6, 2048], P(None, 'tp'), may hold values from 6144 to 24576
Outputs:
- output: bfloat16 [6, 1024, 2048], P('fsdp', 'ctx')
- input_grad: float32 [6, 1024, 2048], P('fsdp', 'ctx')
- new_qkv_moment1: float32 [2048, 3, 2048], P(('fsdp', 'ctx'), None, 'tp')
- new_qkv_moment2: float32 [2048, 3, 2048], P(('fsdp', 'ctx'), None, 'tp')
- new_qkv_master: float32 [2048, 3, 2048], P(('fsdp', 'ctx'), None, 'tp')
- new_qkv_copy: bfloat16 [2048, 3, 2048], P(('fsdp', 'ctx'), None, 'tp')
- new_out_moment1: float32 [2048, 2048], P(('fsdp', 'ctx'), 'tp')
- new_out_moment2: float32 [2048, 2048], P(('fsdp', 'ctx'), 'tp')
- new_out_master: float32 [2048, 2048], P(('fsdp', 'ctx'), 'tp')
- new_out_copy: bfloat16 [2048, 2048], P(('fsdp', 'ctx'), 'tp')
- new_up_moment1: float32 [2048, 4, 2048], P(('fsdp', 'ctx'), None, 'tp')
- new_up_moment2: float32 [2048, 4, 2048], P(('fsdp', 'ctx'), None, 'tp')
- new_up_master: float32 [2048, 4, 2048], P(('fsdp', 'ctx'), None, 'tp')
- new_up_copy: bfloat16 [2048, 4, 2048], P(('fsdp', 'ctx'), None, 'tp')
- new_down_moment1: float32 [2048, 4, 2048], P(('fsdp', 'ctx'), None, 'tp')
- new_down_moment2: float32 [2048, 4, 2048], P(('fsdp', 'ctx'), None, 'tp')
- new_down_master: float32 [2048, 4, 2048], P(('fsdp', 'ctx'), None, 'tp')
- new_down_copy: bfloat16 [2048, 4, 2048], P(('fsdp', 'ctx'), None, 'tp')
- new_gain_moment1: float32 [2, 2048], replicated
- new_gain_moment2: float32 [2, 2048], replicated
- new_gains: float32 [2, 2048], replicated
- new_shared_moment1: float32 [4, 2048], replicated
- new_shared_moment2: float32 [4, 2048], replicated
- new_shared_biases: float32 [4, 2048], replicated
- new_split_moment1: float32 [6, 2048], P(None, 'tp')
- new_split_moment2: float32 [6, 2048], P(None, 'tp')
- new_split_biases: float32 [6, 2048], P(None, 'tp')
The draws below stay inside these ranges and needn't reach their ends.
All inputs are finite; a program needn't handle non-finite values.
Results may differ from the reference program's by a relative error of at most 0.022.
Values may be sent and summed in bfloat16 or wider, within the bound.
A program may use at most 256 MiB of HBM per device.

```python
import math
import jax
import jax.numpy as jnp
from jax import lax

D = 2048
HEADS = 16
HD = 128
FF = 8192
FFR = 4
BLOCK = 256
STEP = 10
SEQS = 6
LEN = 1024
TOKENS = 6144


def shard_levels(key, shape, pieces, smallest, largest):
    factor_of, own = 1.0, jax.random.fold_in(key, 6)
    for dim, blocks in pieces:
        heights = jnp.exp(jax.random.uniform(jax.random.fold_in(own, dim), (blocks,), jnp.float32, smallest / len(pieces), largest / len(pieces)))
        factor_of = factor_of * jnp.repeat(heights, shape[dim] // blocks).reshape([-1 if axis == dim else 1 for axis in range(len(shape))])
    return factor_of


def bell_draw(own_key, dims, scale, most, cuts=(), kind=jnp.bfloat16):
    entries = scale * jax.random.normal(own_key, dims, jnp.float32)
    if cuts:
        entries = entries * shard_levels(own_key, dims, cuts, -0.22, 0.18)
    return jnp.clip(entries, -most, most).astype(kind)


def setup_inputs(seed: int = 0) -> dict:
    arg_keys = jax.random.split(jax.random.key(seed), 24)
    return {
        "inputs": bell_draw(arg_keys[0], (SEQS, LEN, D), 1.0, 6.0, ((0, 2), (1, 4))),
        "cotangent": bell_draw(arg_keys[1], (SEQS, LEN, D), 1.0, 6.0, ((0, 2), (1, 4))),
        "master_qkv": bell_draw(arg_keys[2], (D, 3, D), D ** -0.5, 0.125, ((0, 8), (2, 4)), jnp.float32),
        "qkv_moment1": bell_draw(arg_keys[3], (D, 3, D), (TOKENS ** 0.5), 448.0, ((0, 8), (2, 4)), jnp.float32),
        "qkv_moment2": jnp.clip(jnp.exp(math.log(24576.0) - 1.3862944 * jax.random.uniform(arg_keys[4], (D, 3, D), jnp.float32) ** shard_levels(arg_keys[4], (D, 3, D), ((0, 8), (2, 4)), -0.2, 0.2)), 6144.0, 24576.0),
        "master_out": bell_draw(arg_keys[5], (D, D), (D // 8) ** -0.5, 0.375, ((0, 8), (1, 4)), jnp.float32),
        "out_moment1": bell_draw(arg_keys[6], (D, D), (0.4 * TOKENS ** 0.5), 192.0, ((0, 8), (1, 4)), jnp.float32),
        "out_moment2": jnp.clip(jnp.exp(math.log(3932.16) - 1.3862944 * jax.random.uniform(arg_keys[7], (D, D), jnp.float32) ** shard_levels(arg_keys[7], (D, D), ((0, 8), (1, 4)), -0.2, 0.2)), 983.04, 3932.16),
        "master_up": bell_draw(arg_keys[8], (D, FFR, D), D ** -0.5, 0.125, ((0, 8), (2, 4)), jnp.float32),
        "up_moment1": bell_draw(arg_keys[9], (D, FFR, D), (0.33 * TOKENS ** 0.5), 160.0, ((0, 8), (2, 4)), jnp.float32),
        "up_moment2": jnp.clip(jnp.exp(math.log(2703.36) - 1.3862944 * jax.random.uniform(arg_keys[10], (D, FFR, D), jnp.float32) ** shard_levels(arg_keys[10], (D, FFR, D), ((0, 8), (2, 4)), -0.2, 0.2)), 675.84, 2703.36),
        "master_down": bell_draw(arg_keys[11], (D, FFR, D), FF ** -0.5, 0.0625, ((0, 8), (2, 4)), jnp.float32),
        "down_moment1": bell_draw(arg_keys[12], (D, FFR, D), (0.65 * TOKENS ** 0.5), 320.0, ((0, 8), (2, 4)), jnp.float32),
        "down_moment2": jnp.clip(jnp.exp(math.log(10444.8) - 1.39812881 * jax.random.uniform(arg_keys[13], (D, FFR, D), jnp.float32) ** shard_levels(arg_keys[13], (D, FFR, D), ((0, 8), (2, 4)), -0.2, 0.2)), 2580.48, 10444.8),
        "norm_gains": jnp.clip(1.0 + 0.15 * jax.random.normal(arg_keys[14], (2, D), jnp.float32), 0.25, 1.75),
        "gain_moment1": bell_draw(arg_keys[15], (2, D), (TOKENS ** 0.5), 448.0, (), jnp.float32),
        "gain_moment2": jnp.clip(jnp.exp(jax.random.uniform(arg_keys[16], (2, D), jnp.float32, math.log(6144.0), math.log(24576.0))), 6144.0, 24576.0),
        "shared_biases": bell_draw(arg_keys[17], (4, D), 0.3, 1.75, (), jnp.float32),
        "shared_moment1": bell_draw(arg_keys[18], (4, D), (TOKENS ** 0.5), 448.0, (), jnp.float32),
        "shared_moment2": jnp.clip(jnp.exp(jax.random.uniform(arg_keys[19], (4, D), jnp.float32, math.log(6144.0), math.log(24576.0))), 6144.0, 24576.0),
        "split_biases": bell_draw(arg_keys[20], (2 + FFR, D), 0.3, 1.75, ((1, 4),), jnp.float32),
        "split_moment1": bell_draw(arg_keys[21], (2 + FFR, D), (TOKENS ** 0.5), 448.0, ((1, 4),), jnp.float32),
        "split_moment2": jnp.clip(jnp.exp(math.log(24576.0) - 1.3862944 * jax.random.uniform(arg_keys[22], (2 + FFR, D), jnp.float32) ** shard_levels(arg_keys[22], (2 + FFR, D), ((1, 4),), -0.2, 0.2)), 6144.0, 24576.0),
    }


norm_epsilon = 1e-05
matrix_rate = 0.04
vector_rate = 0.4
decay_weight = 0.1
decay_rate = 0.5
adam_epsilon = 1e-08
highest = lax.Precision.HIGHEST

@jax.custom_vjp
def low(v):
    return lax.optimization_barrier(v.astype(jnp.bfloat16)).astype(jnp.float32)

@jax.custom_vjp
def low_back(v):
    return v

def low_keep(v):
    return (low(v), None)

def low_pass(kept, grad):
    return (grad,)

def back_keep(v):
    return (v, None)

def back_low(kept, grad):
    return (low(grad),)
low.defvjp(low_keep, low_pass)
low_back.defvjp(back_keep, back_low)

def normalize(values):
    center = lax.optimization_barrier(jnp.mean(values, axis=-1, keepdims=True))
    shifted = values - center
    variance = lax.optimization_barrier(jnp.mean(shifted * shifted, axis=-1, keepdims=True))
    return shifted * lax.rsqrt(variance + norm_epsilon)

def gelu_tanh(values):
    return 0.5 * values * (1.0 + jnp.tanh(0.7978845608028654 * (values + 0.044715 * values * values * values)))

def adam_update(master, moment_one, moment_two, gradient, rate, decayed):
    first = decay_rate * moment_one + (1.0 - decay_rate) * gradient
    second = decay_rate * moment_two + (1.0 - decay_rate) * gradient * gradient
    correction = 1.0 - decay_rate ** STEP
    update = first / correction / (jnp.sqrt(second / correction) + adam_epsilon)
    if decayed:
        update = update + decay_weight * master
    return (first, second, master - rate * update)

def one_sequence(sequence, w_qkv, w_out, w_up, w_down, gains, shared, split):
    length = sequence.shape[0]
    act_one = low(normalize(sequence) * gains[0] + shared[0])
    projected = jnp.dot(act_one, w_qkv.reshape(D, 3 * D), precision=highest).reshape(length, 3, D)
    queries = low_back(low(projected[:, 0] + split[0])).reshape(length, HEADS, HD)
    key_rows = low_back(low(projected[:, 1])).reshape(length, HEADS, HD)
    value_rows = low_back(low(projected[:, 2] + split[1])).reshape(length, HEADS, HD)
    position = jnp.arange(length)
    allowed = position[None, :] // BLOCK <= position[:, None] // BLOCK
    distance = jnp.abs(position[:, None] - position[None, :]).astype(jnp.float32)
    slopes = jnp.power(2.0, -8.0 * (jnp.arange(HEADS).astype(jnp.float32) + 1.0) / HEADS)
    scores = jnp.einsum('ihd,jhd->hij', queries, key_rows, precision=highest) * HD ** (-0.5) - slopes[:, None, None] * distance[None]
    scores = jnp.where(allowed[None], low_back(scores), -1e+30)
    row_peak = lax.optimization_barrier(jnp.max(scores, axis=-1, keepdims=True))
    exponent = jnp.exp(scores - row_peak)
    probs = exponent / lax.optimization_barrier(jnp.sum(exponent, axis=-1, keepdims=True))
    context = jnp.einsum('hij,jhd->ihd', low(probs), value_rows, precision=highest).reshape(length, D)
    context = low_back(low(context))
    attention = low_back(jnp.dot(context, w_out.T, precision=highest) + shared[2])
    middle = sequence + attention
    act_two = low(normalize(middle) * gains[1] + shared[1])
    up_proj = low_back(jnp.dot(act_two, w_up.reshape(D, FF), precision=highest) + split[2:].reshape(FF))
    gelu_low = low(gelu_tanh(up_proj))
    branch = low_back(jnp.dot(gelu_low, w_down.reshape(D, FF).T, precision=highest) + shared[3])
    return middle + branch

def forward(stream, master_qkv, master_out, master_up, master_down, norm_gains, shared_biases, split_biases):
    w_qkv = low(master_qkv)
    w_out = low(master_out)
    w_up = low(master_up)
    w_down = low(master_down)

    def apply_one(sequence):
        return one_sequence(sequence, w_qkv, w_out, w_up, w_down, norm_gains, shared_biases, split_biases)
    return lax.map(jax.checkpoint(apply_one), stream)

def reference(inputs, cotangent, master_qkv, qkv_moment1, qkv_moment2, master_out, out_moment1, out_moment2, master_up, up_moment1, up_moment2, master_down, down_moment1, down_moment2, norm_gains, gain_moment1, gain_moment2, shared_biases, shared_moment1, shared_moment2, split_biases, split_moment1, split_moment2):
    stream = inputs.astype(jnp.float32)
    result, pullback = jax.vjp(forward, stream, master_qkv, master_out, master_up, master_down, norm_gains, shared_biases, split_biases)
    grads = pullback(cotangent.astype(jnp.float32))
    q_one, q_two, q_new = adam_update(master_qkv, qkv_moment1, qkv_moment2, grads[1], matrix_rate, True)
    o_one, o_two, o_new = adam_update(master_out, out_moment1, out_moment2, grads[2], matrix_rate, True)
    u_one, u_two, u_new = adam_update(master_up, up_moment1, up_moment2, grads[3], matrix_rate, True)
    d_one, d_two, d_new = adam_update(master_down, down_moment1, down_moment2, grads[4], matrix_rate, True)
    g_one, g_two, g_new = adam_update(norm_gains, gain_moment1, gain_moment2, grads[5], vector_rate, False)
    s_one, s_two, s_new = adam_update(shared_biases, shared_moment1, shared_moment2, grads[6], vector_rate, False)
    p_one, p_two, p_new = adam_update(split_biases, split_moment1, split_moment2, grads[7], vector_rate, False)
    return (result.astype(jnp.bfloat16), grads[0], q_one, q_two, q_new, q_new.astype(jnp.bfloat16), o_one, o_two, o_new, o_new.astype(jnp.bfloat16), u_one, u_two, u_new, u_new.astype(jnp.bfloat16), d_one, d_two, d_new, d_new.astype(jnp.bfloat16), g_one, g_two, g_new, s_one, s_two, s_new, p_one, p_two, p_new)
```

```python
import jax
import jax.numpy as jnp
from jax import lax
from jax.sharding import PartitionSpec as P

HD = 128
STEP = 10


norm_epsilon = 1e-05
matrix_rate = 0.04
vector_rate = 0.4
decay_weight = 0.1
decay_rate = 0.5
adam_epsilon = 1e-08
low = jnp.bfloat16


def normalize(values):
    center = jnp.mean(values, axis=-1, keepdims=True)
    shifted = values - center
    variance = jnp.mean(shifted * shifted, axis=-1, keepdims=True)
    inverse = lax.rsqrt(variance + norm_epsilon)
    return (shifted * inverse, inverse)


def norm_back(incoming, normed, inverse, gain):
    scaled = incoming * gain
    return inverse * (
        scaled
        - jnp.mean(scaled, axis=-1, keepdims=True)
        - normed * jnp.mean(scaled * normed, axis=-1, keepdims=True)
    )


def gelu_tanh(values):
    return (
        0.5
        * values
        * (1.0 + jnp.tanh(0.7978845608028654 * (values + 0.044715 * values * values * values)))
    )


def adam_update(master, moment_one, moment_two, gradient, rate, decayed):
    first = decay_rate * moment_one + (1.0 - decay_rate) * gradient
    second = decay_rate * moment_two + (1.0 - decay_rate) * gradient * gradient
    correction = 1.0 - decay_rate**STEP
    update = first / correction / (jnp.sqrt(second / correction) + adam_epsilon)
    if decayed:
        update = update + decay_weight * master
    return (first, second, master - rate * update)


def contract_rows(left, right):
    return lax.dot_general(
        left, right, (((0,), (0,)), ((), ())), preferred_element_type=jnp.float32
    )


def contract_cols(left, right):
    return lax.dot_general(
        left, right, (((1,), (1,)), ((), ())), preferred_element_type=jnp.float32
    )


def tp_scatter(part, seq_count):
    rows, width = part.shape
    blocks = part.astype(low).reshape(seq_count, rows // seq_count, width)
    own = lax.psum_scatter(blocks, "tp", scatter_dimension=1, tiled=True)
    return own.astype(jnp.float32).reshape(-1, width)


def tp_gather(own, seq_count):
    rows, width = own.shape
    blocks = own.astype(low).reshape(seq_count, rows // seq_count, width)
    return lax.all_gather(blocks, "tp", axis=1, tiled=True).reshape(-1, width)


def local(
    inputs,
    cotangent,
    master_qkv,
    qkv_moment1,
    qkv_moment2,
    master_out,
    out_moment1,
    out_moment2,
    master_up,
    up_moment1,
    up_moment2,
    master_down,
    down_moment1,
    down_moment2,
    norm_gains,
    gain_moment1,
    gain_moment2,
    shared_biases,
    shared_moment1,
    shared_moment2,
    split_biases,
    split_moment1,
    split_moment2,
):
    seq_count, block_len, model_width = inputs.shape
    row_count = seq_count * block_len
    width_part = master_qkv.shape[2]
    hidden_rows = master_up.shape[1]
    local_heads = width_part // HD
    score_scale = HD ** (-0.5)
    own_rows = block_len // lax.axis_size("tp")

    def own_part(values):
        blocks = values.reshape(seq_count, block_len, model_width)
        taken = lax.dynamic_slice_in_dim(blocks, lax.axis_index("tp") * own_rows, own_rows, axis=1)
        return taken.astype(jnp.float32).reshape(-1, model_width)

    def gather_rows(master):
        flat = master.astype(low).reshape(master.shape[0], -1)
        return lax.all_gather(flat, ("fsdp", "ctx"), axis=0, tiled=True)

    qkv_flat = gather_rows(master_qkv)
    out_flat = gather_rows(master_out)
    up_flat = gather_rows(master_up)
    down_flat = gather_rows(master_down)
    offset = lax.axis_index("ctx") * block_len
    key_count = block_len * lax.axis_size("ctx")
    query_pos = offset + jnp.arange(block_len)
    key_pos = jnp.arange(key_count)
    allowed = (key_pos[None, :] < offset + block_len)[None]
    distance = jnp.abs(query_pos[:, None] - key_pos[None, :]).astype(jnp.float32)
    head_ids = (lax.axis_index("tp") * local_heads + jnp.arange(local_heads)).astype(jnp.float32)
    slopes = jnp.power(2.0, -8.0 * (head_ids + 1.0) / (local_heads * lax.axis_size("tp")))
    penalty = slopes[:, None, None] * distance[None]

    def score_block(query_seq, key_seq):
        scores = (
            jnp.einsum("ihd,jhd->hij", query_seq, key_seq, preferred_element_type=jnp.float32)
            * score_scale
            - penalty
        )
        return jnp.where(allowed, scores, -1e30)

    def attend_forward(pieces):
        query_seq, key_seq, value_seq = pieces
        scores = score_block(query_seq, key_seq)
        row_peak = jnp.max(scores, axis=-1, keepdims=True)
        exponent = jnp.exp(scores - row_peak)
        row_total = jnp.sum(exponent, axis=-1, keepdims=True)
        probs_low = (exponent / row_total).astype(jnp.bfloat16)
        context = jnp.einsum(
            "hij,jhd->ihd", probs_low, value_seq, preferred_element_type=jnp.float32
        )
        return (context.astype(jnp.bfloat16), row_peak + jnp.log(row_total))

    def attend_backward(pieces):
        query_seq, key_seq, value_seq, grad_seq, log_total = pieces
        probs = jnp.exp(score_block(query_seq, key_seq) - log_total)
        probs_low = probs.astype(jnp.bfloat16)
        grad_probs = jnp.einsum(
            "ihd,jhd->hij", grad_seq, value_seq, preferred_element_type=jnp.float32
        )
        grad_scores = (
            probs * (grad_probs - jnp.sum(probs * grad_probs, axis=-1, keepdims=True))
        ).astype(jnp.bfloat16)
        grad_query = (
            jnp.einsum("hij,jhd->ihd", grad_scores, key_seq, preferred_element_type=jnp.float32)
            * score_scale
        ).astype(jnp.bfloat16)
        grad_key = (
            jnp.einsum("hij,ihd->jhd", grad_scores, query_seq, preferred_element_type=jnp.float32)
            * score_scale
        )
        grad_value = jnp.einsum(
            "hij,ihd->jhd", probs_low, grad_seq, preferred_element_type=jnp.float32
        )
        return (grad_query, grad_key.astype(low), grad_value.astype(low))

    stream = inputs.astype(jnp.float32).reshape(row_count, model_width)
    normed_one, inverse_one = normalize(stream)
    act_one = (normed_one * norm_gains[0] + shared_biases[0]).astype(jnp.bfloat16)
    projected = jnp.dot(act_one, qkv_flat, preferred_element_type=jnp.float32)
    queries = (
        (projected[:, :width_part] + split_biases[0])
        .astype(jnp.bfloat16)
        .reshape(seq_count, block_len, local_heads, HD)
    )
    key_local = projected[:, width_part : 2 * width_part].astype(low)
    value_local = (projected[:, 2 * width_part :] + split_biases[1]).astype(low)
    pairs = jnp.stack([key_local, value_local]).reshape(2 * seq_count, block_len, width_part)
    pairs_all = lax.all_gather(pairs, "ctx", axis=1, tiled=True)
    keys_heads = pairs_all[:seq_count].reshape(seq_count, key_count, local_heads, HD)
    values_heads = pairs_all[seq_count:].reshape(seq_count, key_count, local_heads, HD)
    context, log_total = lax.map(attend_forward, (queries, keys_heads, values_heads))
    context_flat = context.reshape(row_count, width_part)
    middle = (
        own_part(inputs) + tp_scatter(contract_cols(context_flat, out_flat), seq_count)
    ) + shared_biases[2]
    normed_two, inverse_two = normalize(middle)
    act_two = tp_gather(normed_two * norm_gains[1] + shared_biases[1], seq_count)
    up_proj = jnp.dot(act_two, up_flat, preferred_element_type=jnp.float32) + split_biases[
        2:
    ].reshape(-1)
    gelu_low = gelu_tanh(up_proj).astype(jnp.bfloat16)
    branch = tp_scatter(contract_cols(gelu_low, down_flat), seq_count)
    result = middle + branch + shared_biases[3]
    output = tp_gather(result, seq_count).reshape(seq_count, block_len, model_width)
    grad_branch = cotangent.reshape(row_count, model_width)
    grad_gelu = jnp.dot(grad_branch, down_flat, preferred_element_type=jnp.float32)
    gelu_vjp = jax.vjp(gelu_tanh, up_proj)[1]
    grad_up_proj = gelu_vjp(grad_gelu)[0].astype(jnp.bfloat16)
    grad_down = contract_rows(grad_branch, gelu_low)
    grad_up = contract_rows(act_two, grad_up_proj)
    grad_bias_up = jnp.sum(grad_up_proj, axis=0, dtype=jnp.float32)
    grad_act_two = tp_scatter(contract_cols(grad_up_proj, up_flat), seq_count)
    grad_middle = own_part(cotangent) + norm_back(
        grad_act_two, normed_two, inverse_two, norm_gains[1]
    )
    grad_attn = tp_gather(grad_middle, seq_count)
    grad_out = contract_rows(grad_attn, context_flat)
    grad_context = jnp.dot(grad_attn, out_flat, preferred_element_type=jnp.float32).astype(
        jnp.bfloat16
    )
    grad_context = grad_context.reshape(seq_count, block_len, local_heads, HD)
    grad_query, grad_key, grad_value = lax.map(
        attend_backward, (queries, keys_heads, values_heads, grad_context, log_total)
    )
    grad_pairs = jnp.concatenate([grad_key, grad_value]).reshape(
        2 * seq_count, key_count, width_part
    )
    pair_sum = lax.psum_scatter(grad_pairs, "ctx", scatter_dimension=1, tiled=True)
    query_low = grad_query.reshape(row_count, width_part)
    key_low = pair_sum[:seq_count].reshape(row_count, width_part)
    value_low = pair_sum[seq_count:].reshape(row_count, width_part)
    grad_projected = jnp.concatenate([query_low, key_low, value_low], axis=1)
    grad_qkv = contract_rows(act_one, grad_projected)
    grad_act_one = tp_scatter(contract_cols(grad_projected, qkv_flat), seq_count)
    normed_own, inverse_own = normalize(own_part(inputs))
    input_grad = (
        tp_gather(
            grad_middle + norm_back(grad_act_one, normed_own, inverse_own, norm_gains[0]),
            seq_count,
        )
        .astype(jnp.float32)
        .reshape(seq_count, block_len, model_width)
    )

    def scatter_rows(gradient, master):
        own = lax.psum_scatter(
            gradient.astype(low), ("fsdp", "ctx"), scatter_dimension=0, tiled=True
        )
        return own.astype(jnp.float32).reshape(master.shape)

    sum_down = scatter_rows(grad_down, master_down)
    sum_up = scatter_rows(grad_up, master_up)
    sum_out = scatter_rows(grad_out, master_out)
    sum_qkv = scatter_rows(grad_qkv, master_qkv)
    whole_grads = jnp.stack(
        [
            jnp.sum(grad_act_one * normed_own, axis=0),
            jnp.sum(grad_act_two * normed_two, axis=0),
            jnp.sum(grad_act_one, axis=0),
            jnp.sum(grad_act_two, axis=0),
            jnp.sum(grad_middle.astype(low), axis=0, dtype=jnp.float32),
            jnp.sum(own_part(cotangent), axis=0),
        ]
    )
    split_grads = jnp.concatenate(
        [
            jnp.sum(query_low, axis=0, dtype=jnp.float32)[None],
            jnp.sum(value_low, axis=0, dtype=jnp.float32)[None],
            grad_bias_up.reshape(hidden_rows, width_part),
        ],
        axis=0,
    )
    whole_sum = lax.psum(whole_grads, ("fsdp", "ctx", "tp"))
    split_sum = lax.psum(split_grads, ("fsdp", "ctx"))
    q_one, q_two, q_new = adam_update(
        master_qkv, qkv_moment1, qkv_moment2, sum_qkv, matrix_rate, True
    )
    o_one, o_two, o_new = adam_update(
        master_out, out_moment1, out_moment2, sum_out, matrix_rate, True
    )
    u_one, u_two, u_new = adam_update(master_up, up_moment1, up_moment2, sum_up, matrix_rate, True)
    d_one, d_two, d_new = adam_update(
        master_down, down_moment1, down_moment2, sum_down, matrix_rate, True
    )
    g_one, g_two, g_new = adam_update(
        norm_gains, gain_moment1, gain_moment2, whole_sum[:2], vector_rate, False
    )
    s_one, s_two, s_new = adam_update(
        shared_biases, shared_moment1, shared_moment2, whole_sum[2:], vector_rate, False
    )
    p_one, p_two, p_new = adam_update(
        split_biases, split_moment1, split_moment2, split_sum, vector_rate, False
    )
    return (
        output,
        input_grad,
        q_one,
        q_two,
        q_new,
        q_new.astype(jnp.bfloat16),
        o_one,
        o_two,
        o_new,
        o_new.astype(jnp.bfloat16),
        u_one,
        u_two,
        u_new,
        u_new.astype(jnp.bfloat16),
        d_one,
        d_two,
        d_new,
        d_new.astype(jnp.bfloat16),
        g_one,
        g_two,
        g_new,
        s_one,
        s_two,
        s_new,
        p_one,
        p_two,
        p_new,
    )


def solution(mesh):
    return jax.shard_map(
        local,
        mesh=mesh,
        in_specs=(
            P("fsdp", "ctx", None),
            P("fsdp", "ctx", None),
            P(("fsdp", "ctx"), None, "tp"),
            P(("fsdp", "ctx"), None, "tp"),
            P(("fsdp", "ctx"), None, "tp"),
            P(("fsdp", "ctx"), "tp"),
            P(("fsdp", "ctx"), "tp"),
            P(("fsdp", "ctx"), "tp"),
            P(("fsdp", "ctx"), None, "tp"),
            P(("fsdp", "ctx"), None, "tp"),
            P(("fsdp", "ctx"), None, "tp"),
            P(("fsdp", "ctx"), None, "tp"),
            P(("fsdp", "ctx"), None, "tp"),
            P(("fsdp", "ctx"), None, "tp"),
            P(),
            P(),
            P(),
            P(),
            P(),
            P(),
            P(None, "tp"),
            P(None, "tp"),
            P(None, "tp"),
        ),
        out_specs=(
            P("fsdp", "ctx", None),
            P("fsdp", "ctx", None),
            P(("fsdp", "ctx"), None, "tp"),
            P(("fsdp", "ctx"), None, "tp"),
            P(("fsdp", "ctx"), None, "tp"),
            P(("fsdp", "ctx"), None, "tp"),
            P(("fsdp", "ctx"), "tp"),
            P(("fsdp", "ctx"), "tp"),
            P(("fsdp", "ctx"), "tp"),
            P(("fsdp", "ctx"), "tp"),
            P(("fsdp", "ctx"), None, "tp"),
            P(("fsdp", "ctx"), None, "tp"),
            P(("fsdp", "ctx"), None, "tp"),
            P(("fsdp", "ctx"), None, "tp"),
            P(("fsdp", "ctx"), None, "tp"),
            P(("fsdp", "ctx"), None, "tp"),
            P(("fsdp", "ctx"), None, "tp"),
            P(("fsdp", "ctx"), None, "tp"),
            P(),
            P(),
            P(),
            P(),
            P(),
            P(),
            P(None, "tp"),
            P(None, "tp"),
            P(None, "tp"),
        ),
        check_vma=False,
    )
```

```python
import functools

import jax
import jax.numpy as jnp
from jax import lax
from jax.experimental import pallas as pl
from jax.experimental.pallas import tpu as pltpu
from jax.sharding import PartitionSpec as P

HD = 128
STEP = 10


norm_epsilon = 1e-05
matrix_rate = 0.04
vector_rate = 0.4
decay_weight = 0.1
decay_rate = 0.5
adam_epsilon = 1e-08
low = jnp.bfloat16


def normalize(values):
    center = jnp.mean(values, axis=-1, keepdims=True)
    shifted = values - center
    variance = jnp.mean(shifted * shifted, axis=-1, keepdims=True)
    inverse = lax.rsqrt(variance + norm_epsilon)
    return (shifted * inverse, inverse)


def norm_back(incoming, normed, inverse, gain):
    scaled = incoming * gain
    return inverse * (
        scaled
        - jnp.mean(scaled, axis=-1, keepdims=True)
        - normed * jnp.mean(scaled * normed, axis=-1, keepdims=True)
    )


def gelu_tanh(values):
    return (
        0.5
        * values
        * (1.0 + jnp.tanh(0.7978845608028654 * (values + 0.044715 * values * values * values)))
    )


def adam_update(master, moment_one, moment_two, gradient, rate, decayed):
    first = decay_rate * moment_one + (1.0 - decay_rate) * gradient
    second = decay_rate * moment_two + (1.0 - decay_rate) * gradient * gradient
    correction = 1.0 - decay_rate**STEP
    update = first / correction / (jnp.sqrt(second / correction) + adam_epsilon)
    if decayed:
        update = update + decay_weight * master
    return (first, second, master - rate * update)


def contract_rows(left, right):
    return lax.dot_general(
        left, right, (((0,), (0,)), ((), ())), preferred_element_type=jnp.float32
    )


def contract_cols(left, right):
    return lax.dot_general(
        left, right, (((1,), (1,)), ((), ())), preferred_element_type=jnp.float32
    )


MESH = pl.DeviceIdType.MESH
vmem = pltpu.VMEM


def line_stages(n, chunk_rows, part, full, out_buf, in_buf, sems, finish):
    rs_send, rs_recv, ag_send, ag_recv = sems
    z = lax.axis_index("tp")
    own = chunk_rows // n

    def place(c, j):
        return pl.ds(pl.multiple_of(c * chunk_rows + j * own, own), own)

    def flow(d):
        return z if d == 0 else n - 1 - z

    def toward(d, away=False):
        step = 1 if (d == 0) != away else -1
        return {"tp": z + step}

    def sum_copy(d, c, k, away=False):
        return pltpu.make_async_remote_copy(
            src_ref=out_buf.at[d, c, k - 1],
            dst_ref=in_buf.at[d, c, k - 1],
            send_sem=rs_send.at[d, c, k - 1],
            recv_sem=rs_recv.at[d, c, k - 1],
            device_id=toward(d, away),
            device_id_type=MESH,
        )

    def row_copy(d, c, k, away=False):
        back = k if away else k - 1
        j = z - back if d == 0 else z + back
        return pltpu.make_async_remote_copy(
            src_ref=full.at[place(c, j)],
            dst_ref=full.at[place(c, j)],
            send_sem=ag_send.at[d, c, k - 1],
            recv_sem=ag_recv.at[d, c, k - 1],
            device_id=toward(d, away),
            device_id_type=MESH,
        )

    def stage(c, s):
        if s < n:
            for d in range(2):
                q = flow(d)
                j = z + n - s if d == 0 else z - n + s

                @pl.when(q == 0)
                def first():
                    out_buf[d, c, s - 1] = part[place(c, j)].astype(low)
                    sum_copy(d, c, s).start()

                if s > 1:

                    @pl.when((q >= 1) & (q < s))
                    def later():
                        sum_copy(d, c, s - 1, True).wait_recv()
                        out_buf[d, c, s - 1] = (
                            part[place(c, j)] + in_buf[d, c, s - 2].astype(jnp.float32)
                        ).astype(low)
                        sum_copy(d, c, s).start()

        elif s == n:
            for d in range(2):

                @pl.when(flow(d) >= 1)
                def last():
                    sum_copy(d, c, n - 1, True).wait_recv()
                    part[place(c, z)] = part[place(c, z)] + in_buf[d, c, n - 2].astype(jnp.float32)

            full[place(c, z)] = finish(c, part[place(c, z)]).astype(low)
            for d in range(2):

                @pl.when(flow(d) < n - 1)
                def spread():
                    row_copy(d, c, 1).start()

        else:
            k = s - n + 1
            for d in range(2):
                q = flow(d)

                @pl.when(q >= k - 1)
                def arrived():
                    row_copy(d, c, k - 1, True).wait_recv()

                if k < n:

                    @pl.when((q >= k - 1) & (q < n - 1))
                    def onward():
                        row_copy(d, c, k).start()

    def drain(c):
        for d in range(2):
            q = flow(d)
            for k in range(1, n):

                @pl.when(q < k)
                def sum_sent():
                    sum_copy(d, c, k).wait_send()

                @pl.when((q >= k - 1) & (q < n - 1))
                def row_sent():
                    row_copy(d, c, k).wait_send()

    return stage, drain


def line_barrier(n):
    z = lax.axis_index("tp")
    barrier = pltpu.get_barrier_semaphore()

    @pl.when(z > 0)
    def to_lower():
        pl.semaphore_signal(barrier, inc=1, device_id={"tp": z - 1}, device_id_type=MESH)

    @pl.when(z < n - 1)
    def to_upper():
        pl.semaphore_signal(barrier, inc=1, device_id={"tp": z + 1}, device_id_type=MESH)

    @pl.when((z > 0) & (z < n - 1))
    def from_both():
        pl.semaphore_wait(barrier, 2)

    @pl.when((z == 0) | (z == n - 1))
    def from_one():
        pl.semaphore_wait(barrier, 1)


def line_scratch(n, chunks, chunk_rows, width):
    own = chunk_rows // n
    return [
        vmem((chunks * chunk_rows, width), jnp.float32),
        vmem((2, chunks, n - 1, own, width), low),
        vmem((2, chunks, n - 1, own, width), low),
    ] + [pltpu.SemaphoreType.DMA((2, chunks, n - 1))] * 4


def sum_kernel(n, chunks, tile, epilogue, extra_count, *refs):
    left, right = refs[:2]
    extras = refs[2 : 2 + extra_count]
    full = refs[2 + extra_count]
    part, out_buf, in_buf = refs[-7:-4]
    sems = refs[-4:]
    outs = refs[3 + extra_count : -7]
    rows, width = full.shape
    chunk_rows = rows // chunks
    block = max(chunk_rows, min(rows, 256))
    per_block = block // chunk_rows
    line_barrier(n)
    finish = epilogue(chunk_rows // n, extras, outs)
    stage, drain = line_stages(n, chunk_rows, part, full, out_buf, in_buf, sems, finish)

    def multiply(b):
        @pl.loop(0, width // tile)
        def one(i):
            columns = pl.ds(pl.multiple_of(i * tile, tile), tile)
            part[b * block : (b + 1) * block, columns] = contract_cols(
                left[b * block : (b + 1) * block, :], right[columns, :]
            )

    for t in range(n * (chunks - 1) + 2 * n):
        for c in range(chunks):
            s = t - n * c
            if s == 0 and c % per_block == 0 and c == 0:
                multiply(0)
            if 0 < s < 2 * n:
                stage(c, s)
            if s == 1 and (c + 1) % per_block == 0 and c + 1 < chunks:
                multiply((c + 1) // per_block)
    for c in range(chunks):
        drain(c)


def tp_sum(n, chunks, epilogue, collective, left, right, extras, out_shapes):
    rows, width = left.shape[0], right.shape[0]
    depth = left.shape[1]
    outs = [jax.ShapeDtypeStruct((rows, width), low)] + list(out_shapes)
    return pl.pallas_call(
        functools.partial(sum_kernel, n, chunks, 256, epilogue, len(extras)),
        out_shape=outs,
        in_specs=[pl.BlockSpec(memory_space=vmem)] * (2 + len(extras)),
        out_specs=[pl.BlockSpec(memory_space=vmem)] * len(outs),
        scratch_shapes=line_scratch(n, chunks, rows // chunks, width),
        compiler_params=pltpu.CompilerParams(
            collective_id=collective,
            has_side_effects=True,
            vmem_limit_bytes=56 * 1024 * 1024,
        ),
        cost_estimate=pl.CostEstimate(
            flops=2 * rows * width * depth,
            bytes_accessed=200_000_000,
            transcendentals=0,
        ),
    )(left, right, *extras)


def middle_epilogue(own, extras, outs):
    stream, bias, gain, shift = extras
    (middle,) = outs

    def finish(c, total):
        rows = slice(c * own, (c + 1) * own)
        value = stream[rows].astype(jnp.float32) + total + bias[...]
        middle[rows] = value
        return normalize(value)[0] * gain[...] + shift[...]

    return finish


def output_epilogue(own, extras, outs):
    middle, bias = extras

    def finish(c, total):
        return middle[c * own : (c + 1) * own] + total + bias[...]

    return finish


def attn_epilogue(own, extras, outs):
    middle, cotangent, gain = extras
    grad_middle, sums = outs
    sums[...] = jnp.zeros_like(sums)

    def finish(c, total):
        rows = slice(c * own, (c + 1) * own)
        normed, inverse = normalize(middle[rows])
        value = cotangent[rows].astype(jnp.float32) + norm_back(total, normed, inverse, gain[...])
        grad_middle[rows] = value
        sums[0:1] += jnp.sum(total * normed, axis=0, keepdims=True)
        sums[1:2] += jnp.sum(total, axis=0, keepdims=True)
        sums[2:3] += jnp.sum(value.astype(low).astype(jnp.float32), axis=0, keepdims=True)
        return value

    return finish


def input_epilogue(own, extras, outs):
    stream, grad_middle, gain = extras
    (sums,) = outs
    sums[...] = jnp.zeros_like(sums)

    def finish(c, total):
        rows = slice(c * own, (c + 1) * own)
        normed, inverse = normalize(stream[rows].astype(jnp.float32))
        sums[0:1] += jnp.sum(total * normed, axis=0, keepdims=True)
        sums[1:2] += jnp.sum(total, axis=0, keepdims=True)
        return grad_middle[rows] + norm_back(total, normed, inverse, gain[...])

    return finish


def local(
    inputs,
    cotangent,
    master_qkv,
    qkv_moment1,
    qkv_moment2,
    master_out,
    out_moment1,
    out_moment2,
    master_up,
    up_moment1,
    up_moment2,
    master_down,
    down_moment1,
    down_moment2,
    norm_gains,
    gain_moment1,
    gain_moment2,
    shared_biases,
    shared_moment1,
    shared_moment2,
    split_biases,
    split_moment1,
    split_moment2,
):
    seq_count, block_len, model_width = inputs.shape
    row_count = seq_count * block_len
    width_part = master_qkv.shape[2]
    hidden_rows = master_up.shape[1]
    local_heads = width_part // HD
    score_scale = HD ** (-0.5)
    tp_count = lax.axis_size("tp")
    chunks = 2 * seq_count
    own_rows = row_count // chunks // tp_count

    def own_part(values):
        blocks = values.reshape(chunks, tp_count * own_rows, model_width)
        taken = lax.dynamic_slice_in_dim(blocks, lax.axis_index("tp") * own_rows, own_rows, axis=1)
        return taken.reshape(-1, model_width)

    own_shape = jax.ShapeDtypeStruct((row_count // tp_count, model_width), jnp.float32)
    sums_shape = jax.ShapeDtypeStruct((8, model_width), jnp.float32)
    gains = [norm_gains[i : i + 1] for i in range(2)]
    shared = [shared_biases[i : i + 1] for i in range(4)]
    inputs_own = own_part(inputs)
    cotangent_own = own_part(cotangent)

    def gather_rows(master):
        flat = master.astype(low).reshape(master.shape[0], -1)
        return lax.all_gather(flat, ("fsdp", "ctx"), axis=0, tiled=True)

    qkv_flat = gather_rows(master_qkv)
    out_flat = gather_rows(master_out)
    up_flat = gather_rows(master_up)
    down_flat = gather_rows(master_down)
    offset = lax.axis_index("ctx") * block_len
    key_count = block_len * lax.axis_size("ctx")
    query_pos = offset + jnp.arange(block_len)
    key_pos = jnp.arange(key_count)
    allowed = (key_pos[None, :] < offset + block_len)[None]
    distance = jnp.abs(query_pos[:, None] - key_pos[None, :]).astype(jnp.float32)
    head_ids = (lax.axis_index("tp") * local_heads + jnp.arange(local_heads)).astype(jnp.float32)
    slopes = jnp.power(2.0, -8.0 * (head_ids + 1.0) / (local_heads * lax.axis_size("tp")))
    penalty = slopes[:, None, None] * distance[None]

    def score_block(query_seq, key_seq):
        scores = (
            jnp.einsum("ihd,jhd->hij", query_seq, key_seq, preferred_element_type=jnp.float32)
            * score_scale
            - penalty
        )
        return jnp.where(allowed, scores, -1e30)

    def attend_forward(pieces):
        query_seq, key_seq, value_seq = pieces
        scores = score_block(query_seq, key_seq)
        row_peak = jnp.max(scores, axis=-1, keepdims=True)
        exponent = jnp.exp(scores - row_peak)
        row_total = jnp.sum(exponent, axis=-1, keepdims=True)
        probs_low = (exponent / row_total).astype(jnp.bfloat16)
        context = jnp.einsum(
            "hij,jhd->ihd", probs_low, value_seq, preferred_element_type=jnp.float32
        )
        return (context.astype(jnp.bfloat16), row_peak + jnp.log(row_total))

    def attend_backward(pieces):
        query_seq, key_seq, value_seq, grad_seq, log_total = pieces
        probs = jnp.exp(score_block(query_seq, key_seq) - log_total)
        probs_low = probs.astype(jnp.bfloat16)
        grad_probs = jnp.einsum(
            "ihd,jhd->hij", grad_seq, value_seq, preferred_element_type=jnp.float32
        )
        grad_scores = (
            probs * (grad_probs - jnp.sum(probs * grad_probs, axis=-1, keepdims=True))
        ).astype(jnp.bfloat16)
        grad_query = (
            jnp.einsum("hij,jhd->ihd", grad_scores, key_seq, preferred_element_type=jnp.float32)
            * score_scale
        ).astype(jnp.bfloat16)
        grad_key = (
            jnp.einsum("hij,ihd->jhd", grad_scores, query_seq, preferred_element_type=jnp.float32)
            * score_scale
        )
        grad_value = jnp.einsum(
            "hij,ihd->jhd", probs_low, grad_seq, preferred_element_type=jnp.float32
        )
        return (grad_query, grad_key.astype(low), grad_value.astype(low))

    stream = inputs.astype(jnp.float32).reshape(row_count, model_width)
    normed_one, inverse_one = normalize(stream)
    act_one = (normed_one * norm_gains[0] + shared_biases[0]).astype(jnp.bfloat16)
    projected = jnp.dot(act_one, qkv_flat, preferred_element_type=jnp.float32)
    queries = (
        (projected[:, :width_part] + split_biases[0])
        .astype(jnp.bfloat16)
        .reshape(seq_count, block_len, local_heads, HD)
    )
    key_local = projected[:, width_part : 2 * width_part].astype(low)
    value_local = (projected[:, 2 * width_part :] + split_biases[1]).astype(low)
    pairs = jnp.stack([key_local, value_local]).reshape(2 * seq_count, block_len, width_part)
    pairs_all = lax.all_gather(pairs, "ctx", axis=1, tiled=True)
    keys_heads = pairs_all[:seq_count].reshape(seq_count, key_count, local_heads, HD)
    values_heads = pairs_all[seq_count:].reshape(seq_count, key_count, local_heads, HD)
    context, log_total = lax.map(attend_forward, (queries, keys_heads, values_heads))
    context_flat = context.reshape(row_count, width_part)
    act_two, middle = tp_sum(
        tp_count,
        chunks,
        middle_epilogue,
        0,
        context_flat,
        out_flat,
        (inputs_own, shared[2], gains[1], shared[1]),
        [own_shape],
    )
    up_proj = jnp.dot(act_two, up_flat, preferred_element_type=jnp.float32) + split_biases[
        2:
    ].reshape(-1)
    gelu_low = gelu_tanh(up_proj).astype(jnp.bfloat16)
    output = tp_sum(
        tp_count, chunks, output_epilogue, 1, gelu_low, down_flat, (middle, shared[3]), []
    )[0].reshape(seq_count, block_len, model_width)
    grad_branch = cotangent.reshape(row_count, model_width)
    grad_gelu = jnp.dot(grad_branch, down_flat, preferred_element_type=jnp.float32)
    gelu_vjp = jax.vjp(gelu_tanh, up_proj)[1]
    grad_up_proj = gelu_vjp(grad_gelu)[0].astype(jnp.bfloat16)
    grad_down = contract_rows(grad_branch, gelu_low)
    grad_up = contract_rows(act_two, grad_up_proj)
    grad_bias_up = jnp.sum(grad_up_proj, axis=0, dtype=jnp.float32)
    grad_attn, grad_middle, sums_two = tp_sum(
        tp_count,
        chunks,
        attn_epilogue,
        2,
        grad_up_proj,
        up_flat,
        (middle, cotangent_own, gains[1]),
        [own_shape, sums_shape],
    )
    grad_out = contract_rows(grad_attn, context_flat)
    grad_context = jnp.dot(grad_attn, out_flat, preferred_element_type=jnp.float32).astype(
        jnp.bfloat16
    )
    grad_context = grad_context.reshape(seq_count, block_len, local_heads, HD)
    grad_query, grad_key, grad_value = lax.map(
        attend_backward, (queries, keys_heads, values_heads, grad_context, log_total)
    )
    grad_pairs = jnp.concatenate([grad_key, grad_value]).reshape(
        2 * seq_count, key_count, width_part
    )
    pair_sum = lax.psum_scatter(grad_pairs, "ctx", scatter_dimension=1, tiled=True)
    query_low = grad_query.reshape(row_count, width_part)
    key_low = pair_sum[:seq_count].reshape(row_count, width_part)
    value_low = pair_sum[seq_count:].reshape(row_count, width_part)
    grad_projected = jnp.concatenate([query_low, key_low, value_low], axis=1)
    grad_qkv = contract_rows(act_one, grad_projected)
    input_low, sums_one = tp_sum(
        tp_count,
        chunks,
        input_epilogue,
        3,
        grad_projected,
        qkv_flat,
        (inputs_own, grad_middle, gains[0]),
        [sums_shape],
    )
    input_grad = input_low.astype(jnp.float32).reshape(seq_count, block_len, model_width)

    def scatter_rows(gradient, master):
        own = lax.psum_scatter(
            gradient.astype(low), ("fsdp", "ctx"), scatter_dimension=0, tiled=True
        )
        return own.astype(jnp.float32).reshape(master.shape)

    sum_down = scatter_rows(grad_down, master_down)
    sum_up = scatter_rows(grad_up, master_up)
    sum_out = scatter_rows(grad_out, master_out)
    sum_qkv = scatter_rows(grad_qkv, master_qkv)
    whole_grads = jnp.concatenate(
        [
            sums_one[0:1],
            sums_two[0:1],
            sums_one[1:2],
            sums_two[1:3],
            jnp.sum(cotangent_own, axis=0, dtype=jnp.float32)[None],
        ]
    )
    split_grads = jnp.concatenate(
        [
            jnp.sum(query_low, axis=0, dtype=jnp.float32)[None],
            jnp.sum(value_low, axis=0, dtype=jnp.float32)[None],
            grad_bias_up.reshape(hidden_rows, width_part),
        ],
        axis=0,
    )
    whole_sum = lax.psum(whole_grads, ("fsdp", "ctx", "tp"))
    split_sum = lax.psum(split_grads, ("fsdp", "ctx"))
    q_one, q_two, q_new = adam_update(
        master_qkv, qkv_moment1, qkv_moment2, sum_qkv, matrix_rate, True
    )
    o_one, o_two, o_new = adam_update(
        master_out, out_moment1, out_moment2, sum_out, matrix_rate, True
    )
    u_one, u_two, u_new = adam_update(master_up, up_moment1, up_moment2, sum_up, matrix_rate, True)
    d_one, d_two, d_new = adam_update(
        master_down, down_moment1, down_moment2, sum_down, matrix_rate, True
    )
    g_one, g_two, g_new = adam_update(
        norm_gains, gain_moment1, gain_moment2, whole_sum[:2], vector_rate, False
    )
    s_one, s_two, s_new = adam_update(
        shared_biases, shared_moment1, shared_moment2, whole_sum[2:], vector_rate, False
    )
    p_one, p_two, p_new = adam_update(
        split_biases, split_moment1, split_moment2, split_sum, vector_rate, False
    )
    return (
        output,
        input_grad,
        q_one,
        q_two,
        q_new,
        q_new.astype(jnp.bfloat16),
        o_one,
        o_two,
        o_new,
        o_new.astype(jnp.bfloat16),
        u_one,
        u_two,
        u_new,
        u_new.astype(jnp.bfloat16),
        d_one,
        d_two,
        d_new,
        d_new.astype(jnp.bfloat16),
        g_one,
        g_two,
        g_new,
        s_one,
        s_two,
        s_new,
        p_one,
        p_two,
        p_new,
    )


def solution(mesh):
    return jax.shard_map(
        local,
        mesh=mesh,
        in_specs=(
            P("fsdp", "ctx", None),
            P("fsdp", "ctx", None),
            P(("fsdp", "ctx"), None, "tp"),
            P(("fsdp", "ctx"), None, "tp"),
            P(("fsdp", "ctx"), None, "tp"),
            P(("fsdp", "ctx"), "tp"),
            P(("fsdp", "ctx"), "tp"),
            P(("fsdp", "ctx"), "tp"),
            P(("fsdp", "ctx"), None, "tp"),
            P(("fsdp", "ctx"), None, "tp"),
            P(("fsdp", "ctx"), None, "tp"),
            P(("fsdp", "ctx"), None, "tp"),
            P(("fsdp", "ctx"), None, "tp"),
            P(("fsdp", "ctx"), None, "tp"),
            P(),
            P(),
            P(),
            P(),
            P(),
            P(),
            P(None, "tp"),
            P(None, "tp"),
            P(None, "tp"),
        ),
        out_specs=(
            P("fsdp", "ctx", None),
            P("fsdp", "ctx", None),
            P(("fsdp", "ctx"), None, "tp"),
            P(("fsdp", "ctx"), None, "tp"),
            P(("fsdp", "ctx"), None, "tp"),
            P(("fsdp", "ctx"), None, "tp"),
            P(("fsdp", "ctx"), "tp"),
            P(("fsdp", "ctx"), "tp"),
            P(("fsdp", "ctx"), "tp"),
            P(("fsdp", "ctx"), "tp"),
            P(("fsdp", "ctx"), None, "tp"),
            P(("fsdp", "ctx"), None, "tp"),
            P(("fsdp", "ctx"), None, "tp"),
            P(("fsdp", "ctx"), None, "tp"),
            P(("fsdp", "ctx"), None, "tp"),
            P(("fsdp", "ctx"), None, "tp"),
            P(("fsdp", "ctx"), None, "tp"),
            P(("fsdp", "ctx"), None, "tp"),
            P(),
            P(),
            P(),
            P(),
            P(),
            P(),
            P(None, "tp"),
            P(None, "tp"),
            P(None, "tp"),
        ),
        check_vma=False,
    )
```

```python
import functools

import jax
import jax.numpy as jnp
from jax import lax
from jax.experimental import pallas as pl
from jax.experimental.pallas import tpu as pltpu
from jax.sharding import PartitionSpec as P

HD = 128
STEP = 10


norm_epsilon = 1e-05
matrix_rate = 0.04
vector_rate = 0.4
decay_weight = 0.1
decay_rate = 0.5
adam_epsilon = 1e-08
low = jnp.bfloat16


def normalize(values):
    center = jnp.mean(values, axis=-1, keepdims=True)
    shifted = values - center
    variance = jnp.mean(shifted * shifted, axis=-1, keepdims=True)
    inverse = lax.rsqrt(variance + norm_epsilon)
    return (shifted * inverse, inverse)


def norm_back(incoming, normed, inverse, gain):
    scaled = incoming * gain
    return inverse * (
        scaled
        - jnp.mean(scaled, axis=-1, keepdims=True)
        - normed * jnp.mean(scaled * normed, axis=-1, keepdims=True)
    )


def gelu_tanh(values):
    return (
        0.5
        * values
        * (1.0 + jnp.tanh(0.7978845608028654 * (values + 0.044715 * values * values * values)))
    )


def adam_update(master, moment_one, moment_two, gradient, rate, decayed):
    first = decay_rate * moment_one + (1.0 - decay_rate) * gradient
    second = decay_rate * moment_two + (1.0 - decay_rate) * gradient * gradient
    correction = 1.0 - decay_rate**STEP
    update = first / correction / (jnp.sqrt(second / correction) + adam_epsilon)
    if decayed:
        update = update + decay_weight * master
    return (first, second, master - rate * update)


def contract_rows(left, right):
    return lax.dot_general(
        left, right, (((0,), (0,)), ((), ())), preferred_element_type=jnp.float32
    )


def contract_cols(left, right):
    return lax.dot_general(
        left, right, (((1,), (1,)), ((), ())), preferred_element_type=jnp.float32
    )


MESH = pl.DeviceIdType.MESH
vmem = pltpu.VMEM


class Line:
    def __init__(self, n, chunks, part, full, landing, total, sems, finish):
        self.n, self.chunks = n, chunks
        self.part, self.full, self.landing, self.total = part, full, landing, total
        self.sum_send, self.sum_recv, self.row_send, self.row_recv = sems
        self.finish = finish
        self.z = lax.axis_index("tp")
        self.chunk_rows = full.shape[0] // chunks
        self.own = self.chunk_rows // n
        self.last = 2 * n - 1

    def place(self, c, j):
        return pl.ds(pl.multiple_of(c * self.chunk_rows + j * self.own, self.own), self.own)

    def flow(self, d):
        return self.z if d == 0 else self.n - 1 - self.z

    def toward(self, d, away):
        return {"tp": self.z + (1 if (d == 0) != away else -1)}

    def sum_copy(self, d, c, k, source, away=False):
        return pltpu.make_async_remote_copy(
            src_ref=source,
            dst_ref=self.landing.at[d, c, k - 1],
            send_sem=self.sum_send.at[d, c, k - 1],
            recv_sem=self.sum_recv.at[d, c, k - 1],
            device_id=self.toward(d, away),
            device_id_type=MESH,
        )

    def sum_arrive(self, d, c, k):
        self.sum_copy(d, c, k, self.landing.at[d, c, k - 1], True).wait_recv()

    def row_copy(self, d, c, k, away=False):
        back = k if away else k - 1
        rows = self.place(c, self.z - back if d == 0 else self.z + back)
        return pltpu.make_async_remote_copy(
            src_ref=self.full.at[rows],
            dst_ref=self.full.at[rows],
            send_sem=self.row_send.at[d, c, k - 1],
            recv_sem=self.row_recv.at[d, c, k - 1],
            device_id=self.toward(d, away),
            device_id_type=MESH,
        )

    def stage(self, c, s):
        n, z = self.n, self.z
        if s < n:
            for d in range(2):
                q = self.flow(d)
                rows = self.place(c, z + n - s if d == 0 else z - n + s)

                @pl.when(q == 0)
                def first():
                    self.sum_copy(d, c, s, self.part.at[rows]).start()

                if s > 1:

                    @pl.when((q >= 1) & (q < s))
                    def later():
                        self.sum_arrive(d, c, s - 1)
                        held = self.landing.at[d, c, s - 2]
                        held[...] = (
                            self.part[rows].astype(jnp.float32) + held[...].astype(jnp.float32)
                        ).astype(low)
                        self.sum_copy(d, c, s, held).start()

        elif s == n:
            rows = self.place(c, z)
            self.total[...] = self.part[rows].astype(jnp.float32)
            for d in range(2):

                @pl.when(self.flow(d) >= 1)
                def ended():
                    self.sum_arrive(d, c, n - 1)
                    self.total[...] += self.landing[d, c, n - 2].astype(jnp.float32)

            self.full[rows] = self.finish(c, self.total[...]).astype(low)
            for d in range(2):

                @pl.when(self.flow(d) < n - 1)
                def spread():
                    self.row_copy(d, c, 1).start()

        else:
            k = s - n + 1
            for d in range(2):
                q = self.flow(d)

                @pl.when(q >= k - 1)
                def arrived():
                    self.row_copy(d, c, k - 1, True).wait_recv()

                if k < n:

                    @pl.when((q >= k - 1) & (q < n - 1))
                    def onward():
                        self.row_copy(d, c, k).start()

    def drain(self):
        n = self.n
        for c in range(self.chunks):
            for d in range(2):
                q = self.flow(d)
                for k in range(1, n):

                    @pl.when(q < k)
                    def sum_sent():
                        self.sum_copy(d, c, k, self.landing.at[d, c, k - 1]).wait_send()

                    @pl.when((q >= k - 1) & (q < n - 1))
                    def row_sent():
                        self.row_copy(d, c, k).wait_send()


def peers(axes):
    found = []
    for axis in axes:
        bit = 1
        while bit < lax.axis_size(axis):
            me = lax.axis_index(axis)
            found.append({axis: me + bit * (1 - 2 * ((me // bit) % 2))})
            bit *= 2
    return found


def greet(n, others):
    z = lax.axis_index("tp")
    barrier = pltpu.get_barrier_semaphore()

    @pl.when(z > 0)
    def to_lower():
        pl.semaphore_signal(barrier, inc=1, device_id={"tp": z - 1}, device_id_type=MESH)

    @pl.when(z < n - 1)
    def to_upper():
        pl.semaphore_signal(barrier, inc=1, device_id={"tp": z + 1}, device_id_type=MESH)

    for other in others:
        pl.semaphore_signal(barrier, inc=1, device_id=other, device_id_type=MESH)

    @pl.when((z > 0) & (z < n - 1))
    def from_both():
        pl.semaphore_wait(barrier, 2 + len(others))

    @pl.when((z == 0) | (z == n - 1))
    def from_one():
        pl.semaphore_wait(barrier, 1 + len(others))


def line_scratch(n, chunks, rows, width):
    own = rows // chunks // n
    return [
        vmem((rows, width), low),
        vmem((2, chunks, n - 1, own, width), low),
        vmem((own, width), jnp.float32),
    ] + [pltpu.SemaphoreType.DMA((2, chunks, n - 1))] * 4


class Exchange:
    def __init__(self, whole, start, arrived, send_sem, recv_sem):
        self.whole, self.held, self.arrived = whole, start, arrived
        self.send_sem, self.recv_sem = send_sem, recv_sem
        self.inner = len(peers(("ctx", "fsdp")))
        self.peers = peers(("ctx", "fsdp", "tp"))

    def copy(self, i):
        columns = slice(None) if i < self.inner else slice(0, self.whole)
        return pltpu.make_async_remote_copy(
            src_ref=self.held.at[i, :, columns],
            dst_ref=self.arrived.at[i, :, columns],
            send_sem=self.send_sem.at[i],
            recv_sem=self.recv_sem.at[i],
            device_id=self.peers[i],
            device_id_type=MESH,
        )

    def step(self, i):
        if i > 0:
            self.copy(i - 1).wait_recv()
            if i - 1 < self.inner:
                self.held[i] = self.held[i - 1] + self.arrived[i - 1]
            else:
                self.held[i] = self.held[i - 1]
                self.held[i, :, : self.whole] += self.arrived[i - 1, :, : self.whole]
        if i < len(self.peers):
            self.copy(i).start()

    def drain(self):
        for i in range(len(self.peers)):
            self.copy(i).wait_send()


def sum_kernel(n, chunks, tile, epilogue, extra_count, out_count, with_vectors, *refs):
    left, right = refs[:2]
    extras = refs[2 : 2 + extra_count]
    full = refs[2 + extra_count]
    outs = refs[3 + extra_count : 3 + extra_count + out_count]
    scratch = refs[3 + extra_count + out_count :]
    part, landing, total = scratch[:3]
    rows, width = full.shape
    chunk_rows = rows // chunks
    block = max(chunk_rows, min(rows, 256))
    per_block = block // chunk_rows
    greet(n, peers(("ctx", "fsdp", "tp")) if with_vectors else [])
    finish = epilogue(chunk_rows // n, extras, outs)
    line = Line(n, chunks, part, full, landing, total, scratch[3:7], finish)

    def multiply(b):
        @pl.loop(0, width // tile)
        def one(i):
            columns = pl.ds(pl.multiple_of(i * tile, tile), tile)
            part[b * block : (b + 1) * block, columns] = contract_cols(
                left[b * block : (b + 1) * block, :], right[columns, :]
            ).astype(low)

    multiply(0)
    ended = chunks - 1 + n
    vectors = None
    for t in range(1, chunks + 2 * n - 1):
        for c in range(chunks):
            if 0 < t - c < 2 * n:
                line.stage(c, t - c)
        if t % per_block == 0 and t < chunks:
            multiply(t // per_block)
        if with_vectors and t == ended:
            held, arrived, send_sem, recv_sem = scratch[7:]
            vectors = Exchange(width, held, arrived, send_sem, recv_sem)
            held[0] = extras[-1][...]
            held[0, 0:2, :width] = outs[0][0:2]
        if vectors is not None and t - ended <= len(vectors.peers):
            vectors.step(t - ended)
            done = t - ended
    if vectors is not None:
        for i in range(done + 1, len(vectors.peers) + 1):
            vectors.step(i)
        outs[-1][...] = vectors.held[len(vectors.peers)]
        vectors.drain()
    line.drain()


def tp_sum(n, chunks, epilogue, collective, left, right, extras, out_shapes, vectors=None):
    rows, width = left.shape[0], right.shape[0]
    depth = left.shape[1]
    outs = [jax.ShapeDtypeStruct((rows, width), low)] + list(out_shapes)
    scratch = line_scratch(n, chunks, rows, width)
    if vectors is not None:
        extras = (*extras, vectors)
        outs.append(jax.ShapeDtypeStruct(vectors.shape, jnp.float32))
        steps = len(peers(("ctx", "fsdp", "tp")))
        scratch += [
            vmem((steps + 1, *vectors.shape), jnp.float32),
            vmem((steps, *vectors.shape), jnp.float32),
            pltpu.SemaphoreType.DMA((steps,)),
            pltpu.SemaphoreType.DMA((steps,)),
        ]
    return pl.pallas_call(
        functools.partial(
            sum_kernel,
            n,
            chunks,
            256,
            epilogue,
            len(extras),
            len(outs) - 1,
            vectors is not None,
        ),
        out_shape=outs,
        in_specs=[pl.BlockSpec(memory_space=vmem)] * (2 + len(extras)),
        out_specs=[pl.BlockSpec(memory_space=vmem)] * len(outs),
        scratch_shapes=scratch,
        compiler_params=pltpu.CompilerParams(
            collective_id=collective,
            has_side_effects=True,
            vmem_limit_bytes=56 * 1024 * 1024,
        ),
        cost_estimate=pl.CostEstimate(
            flops=2 * rows * width * depth,
            bytes_accessed=200_000_000,
            transcendentals=0,
        ),
    )(left, right, *extras)


def middle_epilogue(own, extras, outs):
    stream, bias, gain, shift = extras
    (middle,) = outs

    def finish(c, total):
        rows = slice(c * own, (c + 1) * own)
        value = stream[rows].astype(jnp.float32) + total + bias[...]
        middle[rows] = value
        return normalize(value)[0] * gain[...] + shift[...]

    return finish


def output_epilogue(own, extras, outs):
    middle, bias = extras

    def finish(c, total):
        return middle[c * own : (c + 1) * own] + total + bias[...]

    return finish


def attn_epilogue(own, extras, outs):
    middle, cotangent, gain = extras
    grad_middle, sums = outs
    sums[...] = jnp.zeros_like(sums)

    def finish(c, total):
        rows = slice(c * own, (c + 1) * own)
        normed, inverse = normalize(middle[rows])
        value = cotangent[rows].astype(jnp.float32) + norm_back(total, normed, inverse, gain[...])
        grad_middle[rows] = value
        sums[0:1] += jnp.sum(total * normed, axis=0, keepdims=True)
        sums[1:2] += jnp.sum(total, axis=0, keepdims=True)
        sums[2:3] += jnp.sum(value.astype(low).astype(jnp.float32), axis=0, keepdims=True)
        return value

    return finish


def input_epilogue(own, extras, outs):
    stream, grad_middle, gain = extras[:3]
    sums = outs[0]
    sums[...] = jnp.zeros_like(sums)

    def finish(c, total):
        rows = slice(c * own, (c + 1) * own)
        normed, inverse = normalize(stream[rows].astype(jnp.float32))
        sums[0:1] += jnp.sum(total * normed, axis=0, keepdims=True)
        sums[1:2] += jnp.sum(total, axis=0, keepdims=True)
        return grad_middle[rows] + norm_back(total, normed, inverse, gain[...])

    return finish


def local(
    inputs,
    cotangent,
    master_qkv,
    qkv_moment1,
    qkv_moment2,
    master_out,
    out_moment1,
    out_moment2,
    master_up,
    up_moment1,
    up_moment2,
    master_down,
    down_moment1,
    down_moment2,
    norm_gains,
    gain_moment1,
    gain_moment2,
    shared_biases,
    shared_moment1,
    shared_moment2,
    split_biases,
    split_moment1,
    split_moment2,
):
    seq_count, block_len, model_width = inputs.shape
    row_count = seq_count * block_len
    width_part = master_qkv.shape[2]
    hidden_rows = master_up.shape[1]
    local_heads = width_part // HD
    score_scale = HD ** (-0.5)
    tp_count = lax.axis_size("tp")
    chunks = 2 * seq_count
    own_rows = row_count // chunks // tp_count

    def own_part(values):
        blocks = values.reshape(chunks, tp_count * own_rows, model_width)
        taken = lax.dynamic_slice_in_dim(blocks, lax.axis_index("tp") * own_rows, own_rows, axis=1)
        return taken.reshape(-1, model_width)

    own_shape = jax.ShapeDtypeStruct((row_count // tp_count, model_width), jnp.float32)
    sums_shape = jax.ShapeDtypeStruct((8, model_width), jnp.float32)
    gains = [norm_gains[i : i + 1] for i in range(2)]
    shared = [shared_biases[i : i + 1] for i in range(4)]
    inputs_own = own_part(inputs)
    cotangent_own = own_part(cotangent)

    def gather_rows(master):
        flat = master.astype(low).reshape(master.shape[0], -1)
        return lax.all_gather(flat, ("fsdp", "ctx"), axis=0, tiled=True)

    qkv_flat = gather_rows(master_qkv)
    out_flat = gather_rows(master_out)
    up_flat = gather_rows(master_up)
    down_flat = gather_rows(master_down)
    offset = lax.axis_index("ctx") * block_len
    key_count = block_len * lax.axis_size("ctx")
    query_pos = offset + jnp.arange(block_len)
    key_pos = jnp.arange(key_count)
    allowed = (key_pos[None, :] < offset + block_len)[None]
    distance = jnp.abs(query_pos[:, None] - key_pos[None, :]).astype(jnp.float32)
    head_ids = (lax.axis_index("tp") * local_heads + jnp.arange(local_heads)).astype(jnp.float32)
    slopes = jnp.power(2.0, -8.0 * (head_ids + 1.0) / (local_heads * lax.axis_size("tp")))
    penalty = slopes[:, None, None] * distance[None]

    def score_block(query_seq, key_seq):
        scores = (
            jnp.einsum("ihd,jhd->hij", query_seq, key_seq, preferred_element_type=jnp.float32)
            * score_scale
            - penalty
        )
        return jnp.where(allowed, scores, -1e30)

    def attend_forward(pieces):
        query_seq, key_seq, value_seq = pieces
        scores = score_block(query_seq, key_seq)
        row_peak = jnp.max(scores, axis=-1, keepdims=True)
        exponent = jnp.exp(scores - row_peak)
        row_total = jnp.sum(exponent, axis=-1, keepdims=True)
        probs_low = (exponent / row_total).astype(jnp.bfloat16)
        context = jnp.einsum(
            "hij,jhd->ihd", probs_low, value_seq, preferred_element_type=jnp.float32
        )
        return (context.astype(jnp.bfloat16), row_peak + jnp.log(row_total))

    def attend_backward(pieces):
        query_seq, key_seq, value_seq, grad_seq, log_total = pieces
        probs = jnp.exp(score_block(query_seq, key_seq) - log_total)
        probs_low = probs.astype(jnp.bfloat16)
        grad_probs = jnp.einsum(
            "ihd,jhd->hij", grad_seq, value_seq, preferred_element_type=jnp.float32
        )
        grad_scores = (
            probs * (grad_probs - jnp.sum(probs * grad_probs, axis=-1, keepdims=True))
        ).astype(jnp.bfloat16)
        grad_query = (
            jnp.einsum("hij,jhd->ihd", grad_scores, key_seq, preferred_element_type=jnp.float32)
            * score_scale
        ).astype(jnp.bfloat16)
        grad_key = (
            jnp.einsum("hij,ihd->jhd", grad_scores, query_seq, preferred_element_type=jnp.float32)
            * score_scale
        )
        grad_value = jnp.einsum(
            "hij,ihd->jhd", probs_low, grad_seq, preferred_element_type=jnp.float32
        )
        return (grad_query, grad_key.astype(low), grad_value.astype(low))

    stream = inputs.astype(jnp.float32).reshape(row_count, model_width)
    normed_one, inverse_one = normalize(stream)
    act_one = (normed_one * norm_gains[0] + shared_biases[0]).astype(jnp.bfloat16)
    projected = jnp.dot(act_one, qkv_flat, preferred_element_type=jnp.float32)
    queries = (
        (projected[:, :width_part] + split_biases[0])
        .astype(jnp.bfloat16)
        .reshape(seq_count, block_len, local_heads, HD)
    )
    key_local = projected[:, width_part : 2 * width_part].astype(low)
    value_local = (projected[:, 2 * width_part :] + split_biases[1]).astype(low)
    pairs = jnp.stack([key_local, value_local]).reshape(2 * seq_count, block_len, width_part)
    pairs_all = lax.all_gather(pairs, "ctx", axis=1, tiled=True)
    keys_heads = pairs_all[:seq_count].reshape(seq_count, key_count, local_heads, HD)
    values_heads = pairs_all[seq_count:].reshape(seq_count, key_count, local_heads, HD)
    context, log_total = lax.map(attend_forward, (queries, keys_heads, values_heads))
    context_flat = context.reshape(row_count, width_part)
    act_two, middle = tp_sum(
        tp_count,
        chunks,
        middle_epilogue,
        0,
        context_flat,
        out_flat,
        (inputs_own, shared[2], gains[1], shared[1]),
        [own_shape],
    )
    up_proj = jnp.dot(act_two, up_flat, preferred_element_type=jnp.float32) + split_biases[
        2:
    ].reshape(-1)
    gelu_low = gelu_tanh(up_proj).astype(jnp.bfloat16)
    output = tp_sum(
        tp_count, chunks, output_epilogue, 1, gelu_low, down_flat, (middle, shared[3]), []
    )[0].reshape(seq_count, block_len, model_width)
    grad_branch = cotangent.reshape(row_count, model_width)
    grad_gelu = jnp.dot(grad_branch, down_flat, preferred_element_type=jnp.float32)
    gelu_vjp = jax.vjp(gelu_tanh, up_proj)[1]
    grad_up_proj = gelu_vjp(grad_gelu)[0].astype(jnp.bfloat16)
    grad_down = contract_rows(grad_branch, gelu_low)
    grad_up = contract_rows(act_two, grad_up_proj)
    grad_bias_up = jnp.sum(grad_up_proj, axis=0, dtype=jnp.float32)
    grad_attn, grad_middle, sums_two = tp_sum(
        tp_count,
        chunks,
        attn_epilogue,
        2,
        grad_up_proj,
        up_flat,
        (middle, cotangent_own, gains[1]),
        [own_shape, sums_shape],
    )
    grad_out = contract_rows(grad_attn, context_flat)
    grad_context = jnp.dot(grad_attn, out_flat, preferred_element_type=jnp.float32).astype(
        jnp.bfloat16
    )
    grad_context = grad_context.reshape(seq_count, block_len, local_heads, HD)
    grad_query, grad_key, grad_value = lax.map(
        attend_backward, (queries, keys_heads, values_heads, grad_context, log_total)
    )
    grad_pairs = jnp.concatenate([grad_key, grad_value]).reshape(
        2 * seq_count, key_count, width_part
    )
    pair_sum = lax.psum_scatter(grad_pairs, "ctx", scatter_dimension=1, tiled=True)
    query_low = grad_query.reshape(row_count, width_part)
    key_low = pair_sum[:seq_count].reshape(row_count, width_part)
    value_low = pair_sum[seq_count:].reshape(row_count, width_part)
    grad_projected = jnp.concatenate([query_low, key_low, value_low], axis=1)
    grad_qkv = contract_rows(act_one, grad_projected)
    split_grads = jnp.concatenate(
        [
            jnp.sum(query_low, axis=0, dtype=jnp.float32)[None],
            jnp.sum(value_low, axis=0, dtype=jnp.float32)[None],
            grad_bias_up.reshape(hidden_rows, width_part),
        ],
        axis=0,
    )
    vectors = jnp.concatenate(
        [
            jnp.zeros((2, model_width), jnp.float32),
            sums_two[0:3],
            jnp.sum(cotangent_own, axis=0, dtype=jnp.float32)[None],
            jnp.zeros((2, model_width), jnp.float32),
        ]
    )
    vectors = jnp.concatenate([vectors, jnp.pad(split_grads, ((0, 2), (0, 0)))], axis=1)
    input_low, _, vector_sum = tp_sum(
        tp_count,
        chunks,
        input_epilogue,
        3,
        grad_projected,
        qkv_flat,
        (inputs_own, grad_middle, gains[0]),
        [sums_shape],
        vectors,
    )
    input_grad = input_low.astype(jnp.float32).reshape(seq_count, block_len, model_width)

    def scatter_rows(gradient, master):
        own = lax.psum_scatter(
            gradient.astype(low), ("fsdp", "ctx"), scatter_dimension=0, tiled=True
        )
        return own.astype(jnp.float32).reshape(master.shape)

    sum_down = scatter_rows(grad_down, master_down)
    sum_up = scatter_rows(grad_up, master_up)
    sum_out = scatter_rows(grad_out, master_out)
    sum_qkv = scatter_rows(grad_qkv, master_qkv)
    gain_sum = jnp.concatenate([vector_sum[0:1, :model_width], vector_sum[2:3, :model_width]])
    shared_sum = jnp.concatenate([vector_sum[1:2, :model_width], vector_sum[3:6, :model_width]])
    split_sum = vector_sum[: 2 + hidden_rows, model_width:]
    q_one, q_two, q_new = adam_update(
        master_qkv, qkv_moment1, qkv_moment2, sum_qkv, matrix_rate, True
    )
    o_one, o_two, o_new = adam_update(
        master_out, out_moment1, out_moment2, sum_out, matrix_rate, True
    )
    u_one, u_two, u_new = adam_update(master_up, up_moment1, up_moment2, sum_up, matrix_rate, True)
    d_one, d_two, d_new = adam_update(
        master_down, down_moment1, down_moment2, sum_down, matrix_rate, True
    )
    g_one, g_two, g_new = adam_update(
        norm_gains, gain_moment1, gain_moment2, gain_sum, vector_rate, False
    )
    s_one, s_two, s_new = adam_update(
        shared_biases, shared_moment1, shared_moment2, shared_sum, vector_rate, False
    )
    p_one, p_two, p_new = adam_update(
        split_biases, split_moment1, split_moment2, split_sum, vector_rate, False
    )
    return (
        output,
        input_grad,
        q_one,
        q_two,
        q_new,
        q_new.astype(jnp.bfloat16),
        o_one,
        o_two,
        o_new,
        o_new.astype(jnp.bfloat16),
        u_one,
        u_two,
        u_new,
        u_new.astype(jnp.bfloat16),
        d_one,
        d_two,
        d_new,
        d_new.astype(jnp.bfloat16),
        g_one,
        g_two,
        g_new,
        s_one,
        s_two,
        s_new,
        p_one,
        p_two,
        p_new,
    )


def solution(mesh):
    return jax.shard_map(
        local,
        mesh=mesh,
        in_specs=(
            P("fsdp", "ctx", None),
            P("fsdp", "ctx", None),
            P(("fsdp", "ctx"), None, "tp"),
            P(("fsdp", "ctx"), None, "tp"),
            P(("fsdp", "ctx"), None, "tp"),
            P(("fsdp", "ctx"), "tp"),
            P(("fsdp", "ctx"), "tp"),
            P(("fsdp", "ctx"), "tp"),
            P(("fsdp", "ctx"), None, "tp"),
            P(("fsdp", "ctx"), None, "tp"),
            P(("fsdp", "ctx"), None, "tp"),
            P(("fsdp", "ctx"), None, "tp"),
            P(("fsdp", "ctx"), None, "tp"),
            P(("fsdp", "ctx"), None, "tp"),
            P(),
            P(),
            P(),
            P(),
            P(),
            P(),
            P(None, "tp"),
            P(None, "tp"),
            P(None, "tp"),
        ),
        out_specs=(
            P("fsdp", "ctx", None),
            P("fsdp", "ctx", None),
            P(("fsdp", "ctx"), None, "tp"),
            P(("fsdp", "ctx"), None, "tp"),
            P(("fsdp", "ctx"), None, "tp"),
            P(("fsdp", "ctx"), None, "tp"),
            P(("fsdp", "ctx"), "tp"),
            P(("fsdp", "ctx"), "tp"),
            P(("fsdp", "ctx"), "tp"),
            P(("fsdp", "ctx"), "tp"),
            P(("fsdp", "ctx"), None, "tp"),
            P(("fsdp", "ctx"), None, "tp"),
            P(("fsdp", "ctx"), None, "tp"),
            P(("fsdp", "ctx"), None, "tp"),
            P(("fsdp", "ctx"), None, "tp"),
            P(("fsdp", "ctx"), None, "tp"),
            P(("fsdp", "ctx"), None, "tp"),
            P(("fsdp", "ctx"), None, "tp"),
            P(),
            P(),
            P(),
            P(),
            P(),
            P(),
            P(None, "tp"),
            P(None, "tp"),
            P(None, "tp"),
        ),
        check_vma=False,
    )
```

```python
import functools

import jax
import jax.numpy as jnp
from jax import lax
from jax.experimental import pallas as pl
from jax.experimental.pallas import tpu as pltpu
from jax.sharding import PartitionSpec as P

HD = 128
STEP = 10


norm_epsilon = 1e-05
matrix_rate = 0.04
vector_rate = 0.4
decay_weight = 0.1
decay_rate = 0.5
adam_epsilon = 1e-08
low = jnp.bfloat16


def normalize(values):
    center = jnp.mean(values, axis=-1, keepdims=True)
    shifted = values - center
    variance = jnp.mean(shifted * shifted, axis=-1, keepdims=True)
    inverse = lax.rsqrt(variance + norm_epsilon)
    return (shifted * inverse, inverse)


def norm_back(incoming, normed, inverse, gain):
    scaled = incoming * gain
    return inverse * (
        scaled
        - jnp.mean(scaled, axis=-1, keepdims=True)
        - normed * jnp.mean(scaled * normed, axis=-1, keepdims=True)
    )


def gelu_tanh(values):
    return (
        0.5
        * values
        * (1.0 + jnp.tanh(0.7978845608028654 * (values + 0.044715 * values * values * values)))
    )


def adam_update(master, moment_one, moment_two, gradient, rate, decayed):
    first = decay_rate * moment_one + (1.0 - decay_rate) * gradient
    second = decay_rate * moment_two + (1.0 - decay_rate) * gradient * gradient
    correction = 1.0 - decay_rate**STEP
    update = first / correction / (jnp.sqrt(second / correction) + adam_epsilon)
    if decayed:
        update = update + decay_weight * master
    return (first, second, master - rate * update)


def contract_rows(left, right):
    return lax.dot_general(
        left, right, (((0,), (0,)), ((), ())), preferred_element_type=jnp.float32
    )


def contract_cols(left, right):
    return lax.dot_general(
        left, right, (((1,), (1,)), ((), ())), preferred_element_type=jnp.float32
    )


MESH = pl.DeviceIdType.MESH
vmem = pltpu.VMEM


class Line:
    def __init__(self, n, chunks, part, full, landing, total, sems, finish):
        self.n, self.chunks = n, chunks
        self.part, self.full, self.landing, self.total = part, full, landing, total
        self.sum_send, self.sum_recv, self.row_send, self.row_recv = sems
        self.finish = finish
        self.z = lax.axis_index("tp")
        self.chunk_rows = full.shape[0] // chunks
        self.own = self.chunk_rows // n
        self.last = 2 * n - 1

    def place(self, c, j):
        return pl.ds(pl.multiple_of(c * self.chunk_rows + j * self.own, self.own), self.own)

    def flow(self, d):
        return self.z if d == 0 else self.n - 1 - self.z

    def toward(self, d, away):
        return {"tp": self.z + (1 if (d == 0) != away else -1)}

    def sum_copy(self, d, c, k, source, away=False):
        return pltpu.make_async_remote_copy(
            src_ref=source,
            dst_ref=self.landing.at[d, c, k - 1],
            send_sem=self.sum_send.at[d, c, k - 1],
            recv_sem=self.sum_recv.at[d, c, k - 1],
            device_id=self.toward(d, away),
            device_id_type=MESH,
        )

    def sum_arrive(self, d, c, k):
        self.sum_copy(d, c, k, self.landing.at[d, c, k - 1], True).wait_recv()

    def row_copy(self, d, c, k, away=False):
        back = k if away else k - 1
        rows = self.place(c, self.z - back if d == 0 else self.z + back)
        return pltpu.make_async_remote_copy(
            src_ref=self.full.at[rows],
            dst_ref=self.full.at[rows],
            send_sem=self.row_send.at[d, c, k - 1],
            recv_sem=self.row_recv.at[d, c, k - 1],
            device_id=self.toward(d, away),
            device_id_type=MESH,
        )

    def stage(self, c, s):
        n, z = self.n, self.z
        if s < n:
            for d in range(2):
                q = self.flow(d)
                rows = self.place(c, z + n - s if d == 0 else z - n + s)

                @pl.when(q == 0)
                def first():
                    self.sum_copy(d, c, s, self.part.at[rows]).start()

                if s > 1:

                    @pl.when((q >= 1) & (q < s))
                    def later():
                        self.sum_arrive(d, c, s - 1)
                        held = self.landing.at[d, c, s - 2]
                        held[...] = (
                            self.part[rows].astype(jnp.float32) + held[...].astype(jnp.float32)
                        ).astype(low)
                        self.sum_copy(d, c, s, held).start()

        elif s == n:
            rows = self.place(c, z)
            self.total[...] = self.part[rows].astype(jnp.float32)
            for d in range(2):

                @pl.when(self.flow(d) >= 1)
                def ended():
                    self.sum_arrive(d, c, n - 1)
                    self.total[...] += self.landing[d, c, n - 2].astype(jnp.float32)

            self.full[rows] = self.finish(c, self.total[...]).astype(low)
            for d in range(2):

                @pl.when(self.flow(d) < n - 1)
                def spread():
                    self.row_copy(d, c, 1).start()

        else:
            k = s - n + 1
            for d in range(2):
                q = self.flow(d)

                @pl.when(q >= k - 1)
                def arrived():
                    self.row_copy(d, c, k - 1, True).wait_recv()

                if k < n:

                    @pl.when((q >= k - 1) & (q < n - 1))
                    def onward():
                        self.row_copy(d, c, k).start()

    def drain(self):
        n = self.n
        for c in range(self.chunks):
            for d in range(2):
                q = self.flow(d)
                for k in range(1, n):

                    @pl.when(q < k)
                    def sum_sent():
                        self.sum_copy(d, c, k, self.landing.at[d, c, k - 1]).wait_send()

                    @pl.when((q >= k - 1) & (q < n - 1))
                    def row_sent():
                        self.row_copy(d, c, k).wait_send()


def peers(axes):
    found = []
    for axis in axes:
        bit = 1
        while bit < lax.axis_size(axis):
            me = lax.axis_index(axis)
            found.append({axis: me + bit * (1 - 2 * ((me // bit) % 2))})
            bit *= 2
    return found


def greet(n, others):
    z = lax.axis_index("tp")
    barrier = pltpu.get_barrier_semaphore()

    @pl.when(z > 0)
    def to_lower():
        pl.semaphore_signal(barrier, inc=1, device_id={"tp": z - 1}, device_id_type=MESH)

    @pl.when(z < n - 1)
    def to_upper():
        pl.semaphore_signal(barrier, inc=1, device_id={"tp": z + 1}, device_id_type=MESH)

    for other in others:
        pl.semaphore_signal(barrier, inc=1, device_id=other, device_id_type=MESH)

    @pl.when((z > 0) & (z < n - 1))
    def from_both():
        pl.semaphore_wait(barrier, 2 + len(others))

    @pl.when((z == 0) | (z == n - 1))
    def from_one():
        pl.semaphore_wait(barrier, 1 + len(others))


def line_scratch(n, chunks, rows, width):
    own = rows // chunks // n
    return [
        vmem((rows, width), low),
        vmem((2, chunks, n - 1, own, width), low),
        vmem((own, width), jnp.float32),
    ] + [pltpu.SemaphoreType.DMA((2, chunks, n - 1))] * 4


class Exchange:
    def __init__(self, whole, start, arrived, send_sem, recv_sem):
        self.whole, self.held, self.arrived = whole, start, arrived
        self.send_sem, self.recv_sem = send_sem, recv_sem
        self.inner = len(peers(("ctx", "fsdp")))
        self.peers = peers(("ctx", "fsdp", "tp"))

    def copy(self, i):
        columns = slice(None) if i < self.inner else slice(0, self.whole)
        return pltpu.make_async_remote_copy(
            src_ref=self.held.at[i, :, columns],
            dst_ref=self.arrived.at[i, :, columns],
            send_sem=self.send_sem.at[i],
            recv_sem=self.recv_sem.at[i],
            device_id=self.peers[i],
            device_id_type=MESH,
        )

    def step(self, i):
        if i > 0:
            self.copy(i - 1).wait_recv()
            if i - 1 < self.inner:
                self.held[i] = self.held[i - 1] + self.arrived[i - 1]
            else:
                self.held[i] = self.held[i - 1]
                self.held[i, :, : self.whole] += self.arrived[i - 1, :, : self.whole]
        if i < len(self.peers):
            self.copy(i).start()

    def drain(self):
        for i in range(len(self.peers)):
            self.copy(i).wait_send()


def sum_kernel(n, chunks, tile, epilogue, extra_count, out_count, with_vectors, *refs):
    left, right = refs[:2]
    extras = refs[2 : 2 + extra_count]
    full = refs[2 + extra_count]
    outs = refs[3 + extra_count : 3 + extra_count + out_count]
    scratch = refs[3 + extra_count + out_count :]
    part, landing, total = scratch[:3]
    rows, width = full.shape
    chunk_rows = rows // chunks
    block = max(chunk_rows, min(rows, 256))
    per_block = block // chunk_rows
    greet(n, peers(("ctx", "fsdp", "tp")) if with_vectors else [])
    finish = epilogue(chunk_rows // n, extras, outs)
    line = Line(n, chunks, part, full, landing, total, scratch[3:7], finish)

    def multiply(b):
        @pl.loop(0, width // tile)
        def one(i):
            columns = pl.ds(pl.multiple_of(i * tile, tile), tile)
            part[b * block : (b + 1) * block, columns] = contract_cols(
                left[b * block : (b + 1) * block, :], right[columns, :]
            ).astype(low)

    multiply(0)
    ended = chunks - 1 + n
    vectors = None
    for t in range(1, chunks + 2 * n - 1):
        for c in range(chunks):
            if 0 < t - c < 2 * n:
                line.stage(c, t - c)
        if t % per_block == 0 and t < chunks:
            multiply(t // per_block)
        if with_vectors and t == ended:
            held, arrived, send_sem, recv_sem = scratch[7:]
            vectors = Exchange(width, held, arrived, send_sem, recv_sem)
            held[0] = extras[-1][...]
            held[0, 0:2, :width] = outs[0][0:2]
        if vectors is not None and t - ended <= len(vectors.peers):
            vectors.step(t - ended)
            done = t - ended
    if vectors is not None:
        for i in range(done + 1, len(vectors.peers) + 1):
            vectors.step(i)
        outs[-1][...] = vectors.held[len(vectors.peers)]
        vectors.drain()
    line.drain()


def tp_sum(n, chunks, epilogue, collective, left, right, extras, out_shapes, vectors=None):
    rows, width = left.shape[0], right.shape[0]
    depth = left.shape[1]
    outs = [jax.ShapeDtypeStruct((rows, width), low)] + list(out_shapes)
    scratch = line_scratch(n, chunks, rows, width)
    if vectors is not None:
        extras = (*extras, vectors)
        outs.append(jax.ShapeDtypeStruct(vectors.shape, jnp.float32))
        steps = len(peers(("ctx", "fsdp", "tp")))
        scratch += [
            vmem((steps + 1, *vectors.shape), jnp.float32),
            vmem((steps, *vectors.shape), jnp.float32),
            pltpu.SemaphoreType.DMA((steps,)),
            pltpu.SemaphoreType.DMA((steps,)),
        ]
    return pl.pallas_call(
        functools.partial(
            sum_kernel,
            n,
            chunks,
            256,
            epilogue,
            len(extras),
            len(outs) - 1,
            vectors is not None,
        ),
        out_shape=outs,
        in_specs=[pl.BlockSpec(memory_space=vmem)] * (2 + len(extras)),
        out_specs=[pl.BlockSpec(memory_space=vmem)] * len(outs),
        scratch_shapes=scratch,
        compiler_params=pltpu.CompilerParams(
            collective_id=collective,
            has_side_effects=True,
            vmem_limit_bytes=56 * 1024 * 1024,
        ),
        cost_estimate=pl.CostEstimate(
            flops=2 * rows * width * depth,
            bytes_accessed=200_000_000,
            transcendentals=0,
        ),
    )(left, right, *extras)


def middle_epilogue(own, extras, outs):
    stream, bias, gain, shift = extras
    (middle,) = outs

    def finish(c, total):
        rows = slice(c * own, (c + 1) * own)
        value = stream[rows].astype(jnp.float32) + total + bias[...]
        middle[rows] = value
        return normalize(value)[0] * gain[...] + shift[...]

    return finish


def output_epilogue(own, extras, outs):
    middle, bias = extras

    def finish(c, total):
        return middle[c * own : (c + 1) * own] + total + bias[...]

    return finish


def attn_epilogue(own, extras, outs):
    middle, cotangent, gain = extras
    grad_middle, sums = outs
    sums[...] = jnp.zeros_like(sums)

    def finish(c, total):
        rows = slice(c * own, (c + 1) * own)
        normed, inverse = normalize(middle[rows])
        value = cotangent[rows].astype(jnp.float32) + norm_back(total, normed, inverse, gain[...])
        grad_middle[rows] = value
        sums[0:1] += jnp.sum(total * normed, axis=0, keepdims=True)
        sums[1:2] += jnp.sum(total, axis=0, keepdims=True)
        sums[2:3] += jnp.sum(value.astype(low).astype(jnp.float32), axis=0, keepdims=True)
        return value

    return finish


def input_epilogue(own, extras, outs):
    stream, grad_middle, gain = extras[:3]
    sums = outs[0]
    sums[...] = jnp.zeros_like(sums)

    def finish(c, total):
        rows = slice(c * own, (c + 1) * own)
        normed, inverse = normalize(stream[rows].astype(jnp.float32))
        sums[0:1] += jnp.sum(total * normed, axis=0, keepdims=True)
        sums[1:2] += jnp.sum(total, axis=0, keepdims=True)
        return grad_middle[rows] + norm_back(total, normed, inverse, gain[...])

    return finish


def ctx_place():
    me = lax.axis_index("ctx")
    half, side = me // 2, me % 2
    return me, half, side, {"ctx": me + 1 - 2 * side}, {"ctx": me + 2 - 4 * half}


def ctx_copy(source, target, send, recv, device):
    return pltpu.make_async_remote_copy(
        src_ref=source,
        dst_ref=target,
        send_sem=send,
        recv_sem=recv,
        device_id=device,
        device_id_type=MESH,
    )


class Spread:
    def __init__(self, block, own, pairs, send, recv):
        self.block, self.own, self.pairs, self.send, self.recv = block, own, pairs, send, recv
        self.me, self.half, self.side, self.beside, self.across = ctx_place()

    def rows(self, s, b):
        start = (s * lax.axis_size("ctx") + b) * self.block
        return pl.ds(pl.multiple_of(start, self.block), self.block)

    def copy(self, kind, s, b, own, device):
        target = self.pairs.at[self.rows(s, b)]
        wide = self.pairs.shape[1]
        source = self.own.at[s * self.block : (s + 1) * self.block, wide // 2 :] if own else target
        return ctx_copy(source, target, self.send.at[kind, s], self.recv.at[kind, s], device)

    def start(self, s):
        rows = slice(s * self.block, (s + 1) * self.block)

        @pl.when(self.half == 0)
        def over():
            self.copy(0, s, self.me, True, self.across).start()

        @pl.when(self.side == 0)
        def aside():
            self.copy(1, s, self.me, True, self.beside).start()

        self.pairs[self.rows(s, self.me)] = self.own[rows, self.pairs.shape[1] // 2 :]

    def forward(self, s):
        @pl.when(self.half == 1)
        def onward():
            self.copy(0, s, self.me - 2, False, self.across).wait_recv()
            self.copy(2, s, self.me - 2, False, self.beside).start()

    def arrive(self, s):
        @pl.when(self.half == 1)
        def second():
            self.copy(2, s, 1 - self.side, False, self.beside).wait_recv()

        @pl.when(self.side == 1)
        def first():
            self.copy(1, s, self.me - 1, False, self.beside).wait_recv()

    def drain(self, s):
        @pl.when(self.half == 0)
        def over():
            self.copy(0, s, self.me, True, self.across).wait_send()

        @pl.when(self.side == 0)
        def aside():
            self.copy(1, s, self.me, True, self.beside).wait_send()

        @pl.when(self.half == 1)
        def onward():
            self.copy(2, s, self.me - 2, False, self.beside).wait_send()


class Collect:
    def __init__(self, block, parts, beside_in, across_in, send, recv):
        self.block, self.parts = block, parts
        self.beside_in, self.across_in, self.send, self.recv = beside_in, across_in, send, recv
        self.me, self.half, self.side, self.beside, self.across = ctx_place()

    def rows(self, s, b):
        start = (s * lax.axis_size("ctx") + b) * self.block
        return pl.ds(pl.multiple_of(start, self.block), self.block)

    def aside(self, s, k, away=False):
        b = 2 * k + (self.side if away else 1 - self.side)
        return ctx_copy(
            self.parts.at[self.rows(s, b)],
            self.beside_in.at[k, s],
            self.send.at[k, s],
            self.recv.at[k, s],
            self.beside,
        )

    def over(self, s):
        return ctx_copy(
            self.parts.at[self.rows(s, self.side)],
            self.across_in.at[s],
            self.send.at[2, s],
            self.recv.at[2, s],
            self.across,
        )

    def start(self, s):
        for k in range(2):

            @pl.when(2 * k + 1 - self.side < self.me)
            def give():
                self.aside(s, k).start()

    def forward(self, s):
        for k in range(2):

            @pl.when(2 * k + self.side < self.me + 1 - 2 * self.side)
            def take():
                self.aside(s, k, True).wait_recv()

        @pl.when(self.half == 1)
        def onward():
            held = self.parts.at[self.rows(s, self.side)]
            held[...] = (
                held[...].astype(jnp.float32) + self.beside_in[0, s].astype(jnp.float32)
            ).astype(low)
            self.over(s).start()

    def finish(self, s, target):
        target[...] = self.parts[self.rows(s, self.me)]
        for k in range(2):

            @pl.when((self.side == 0) & (self.half == k))
            def near():
                target[...] = (
                    target[...].astype(jnp.float32) + self.beside_in[k, s].astype(jnp.float32)
                ).astype(low)

        @pl.when(self.half == 0)
        def far():
            self.over(s).wait_recv()
            target[...] = (
                target[...].astype(jnp.float32) + self.across_in[s].astype(jnp.float32)
            ).astype(low)

    def drain(self, s):
        for k in range(2):

            @pl.when(2 * k + 1 - self.side < self.me)
            def gave():
                self.aside(s, k).wait_send()

        @pl.when(self.half == 1)
        def sent():
            self.over(s).wait_send()


def offsets(base):
    shape = base.shape
    base[...] = (
        lax.broadcasted_iota(jnp.int32, shape, 0) - lax.broadcasted_iota(jnp.int32, shape, 1)
    ).astype(jnp.float32)


def head_scores(query, key, slope, base, j):
    far = base[...] + (j * base.shape[0]).astype(jnp.float32)
    return contract_cols(query, key) * HD ** (-0.5) - slope * jnp.abs(far)


def head_columns(h, shift=0):
    return pl.ds(pl.multiple_of(shift + h * HD, HD), HD)


def forward_heads(s, first, last, block, projected, pairs, slopes, base, context, log_total):
    me = lax.axis_index("ctx")
    count = lax.axis_size("ctx")
    own = slice(s * block, (s + 1) * block)
    wide = pairs.shape[1] // 2

    @pl.loop(first, last)
    def head(h):
        query = projected[own, head_columns(h)]

        def step(j, carry):
            peak, weight, total = carry
            rows = pl.ds(pl.multiple_of((s * count + me - j) * block, block), block)
            scores = head_scores(query, pairs[rows, head_columns(h)], slopes[h, 0:1], base, j)
            higher = jnp.maximum(peak, jnp.max(scores, axis=-1, keepdims=True))
            shrink = jnp.exp(peak - higher)
            exponent = jnp.exp(scores - higher)
            weight = weight * shrink + jnp.sum(exponent, axis=-1, keepdims=True)
            total = total * shrink + jnp.dot(
                exponent.astype(low),
                pairs[rows, head_columns(h, wide)],
                preferred_element_type=jnp.float32,
            )
            return higher, weight, total

        peak, weight, total = lax.fori_loop(
            0,
            me + 1,
            step,
            (
                jnp.full((block, 1), -1e30, jnp.float32),
                jnp.zeros((block, 1), jnp.float32),
                jnp.zeros((block, HD), jnp.float32),
            ),
        )
        context[own, head_columns(h)] = (total / weight).astype(low)
        log_total[own, head_columns(h)] = jnp.broadcast_to(peak + jnp.log(weight), (block, HD))


def backward_heads(
    s, first, last, block, projected, pairs, slopes, base, context, log_total, grad, parts, out
):
    me = lax.axis_index("ctx")
    count = lax.axis_size("ctx")
    own = slice(s * block, (s + 1) * block)
    wide = pairs.shape[1] // 2

    @pl.loop(first, last)
    def head(h):
        query = projected[own, head_columns(h)]
        incoming = grad[own, head_columns(h)]
        level = log_total[own, head_columns(h)][:, 0:1]
        mean = jnp.sum(
            incoming.astype(jnp.float32) * context[own, head_columns(h)].astype(jnp.float32),
            axis=-1,
            keepdims=True,
        )

        def step(j, total):
            rows = pl.ds(pl.multiple_of((s * count + me - j) * block, block), block)
            key = pairs[rows, head_columns(h)]
            probs = jnp.exp(head_scores(query, key, slopes[h, 0:1], base, j) - level)
            grad_probs = contract_cols(incoming, pairs[rows, head_columns(h, wide)])
            grad_scores = (probs * (grad_probs - mean)).astype(low)
            parts[rows, head_columns(h)] = (
                contract_rows(grad_scores, query) * HD ** (-0.5)
            ).astype(low)
            parts[rows, head_columns(h, wide)] = contract_rows(probs.astype(low), incoming).astype(
                low
            )
            return total + jnp.dot(grad_scores, key, preferred_element_type=jnp.float32)

        total = lax.fori_loop(0, me + 1, step, jnp.zeros((block, HD), jnp.float32))
        out[own, head_columns(h)] = (total * HD ** (-0.5)).astype(low)


def attend_kernel(n, chunks, tile, *refs):
    (
        projected,
        slopes,
        out_weight,
        stream,
        bias,
        gain,
        shift,
        full,
        middle,
        context,
        log_total,
        pairs,
        part,
        landing,
        total,
        *rest,
    ) = refs
    sems, (base, send, recv) = rest[:4], rest[4:]
    rows, width = full.shape
    seqs = chunks // 2
    block = rows // seqs
    heads = context.shape[1] // HD
    pace = heads // 2
    _, _, _, beside, across = ctx_place()
    greet(n, [beside, across])
    finish = middle_epilogue(rows // chunks // n, (stream, bias, gain, shift), (middle,))
    line = Line(n, chunks, part, full, landing, total, sems, finish)
    spread = Spread(block, projected, pairs, send, recv)
    for s in range(seqs):
        spread.start(s)
    offsets(base)

    def attend(s, first, last):
        if first == 0:
            spread.forward(s)
            spread.arrive(s)
        forward_heads(
            s, first, last, block, projected, pairs, slopes, base, context, log_total
        )

    def multiply(s):
        own = slice(s * block, (s + 1) * block)

        @pl.loop(0, width // tile)
        def one(i):
            columns = pl.ds(pl.multiple_of(i * tile, tile), tile)
            part[own, columns] = contract_cols(context[own, :], out_weight[columns, :]).astype(low)

    attend(0, 0, heads)
    multiply(0)
    for t in range(1, chunks + 2 * n - 1):
        for c in range(chunks):
            if 0 < t - c < 2 * n:
                line.stage(c, t - c)
        s = (t + 1) // 2
        if s < seqs:
            attend(s, 0 if t % 2 else pace, pace if t % 2 else heads)
            if t % 2 == 0:
                multiply(s)
    for s in range(seqs):
        spread.drain(s)
    line.drain()


def backward_kernel(n, chunks, *refs):
    (
        part,
        middle,
        bias,
        grad_attn,
        out_weight,
        projected,
        pairs,
        context,
        log_total,
        slopes,
        act,
        full,
        grad_projected,
        grad_qkv,
        grad_out,
        landing,
        total,
        *rest,
    ) = refs
    sems, (base, grad_context, parts, beside_in, across_in, send, recv) = rest[:4], rest[4:]
    rows, width = full.shape
    seqs = chunks // 2
    block = rows // seqs
    heads = context.shape[1] // HD
    wide = context.shape[1]
    pace = heads // 2
    _, _, _, beside, across = ctx_place()
    greet(n, [beside, across])
    finish = output_epilogue(rows // chunks // n, (middle, bias), ())
    line = Line(n, chunks, part, full, landing, total, sems, finish)
    collect = Collect(block, parts, beside_in, across_in, send, recv)
    offsets(base)

    def backward(s, first, last):
        own = slice(s * block, (s + 1) * block)
        if first == 0:
            grad_context[own, :] = jnp.dot(
                grad_attn[own, :], out_weight[...], preferred_element_type=jnp.float32
            ).astype(low)
        backward_heads(
            s,
            first,
            last,
            block,
            projected,
            pairs,
            slopes,
            base,
            context,
            log_total,
            grad_context,
            parts,
            grad_projected,
        )
        if last == heads:
            collect.start(s)

    def finished(s):
        collect.finish(s, grad_projected.at[s * block : (s + 1) * block, wide:])

    def features(source, right, out, first, last):
        @pl.loop(first, last)
        def one(i):
            place = pl.ds(pl.multiple_of(i * 256, 256), 256)
            out[place, :] = contract_rows(source[:, place], right[...]).astype(low)

    tiles = width // 256
    tasks = []
    for s in range(seqs):
        tasks.append([functools.partial(backward, s, 0, pace)])
        tasks.append([functools.partial(backward, s, pace, heads)])
    tasks += [[] for _ in range(chunks + 2 * n - 2 - len(tasks))]
    for s in range(seqs):
        tasks[2 * s + 2].append(functools.partial(collect.forward, s))
    after = 2 * seqs + 1
    tasks[after].append(functools.partial(features, grad_attn, context, grad_out, 0, tiles))
    for s in range(seqs):
        tasks[after + s].append(functools.partial(finished, s))
    left = len(tasks) - after - seqs
    for i in range(left):
        tasks[after + seqs + i].append(
            functools.partial(
                features, act, grad_projected, grad_qkv, tiles * i // left, tiles * (i + 1) // left
            )
        )
    for t in range(1, chunks + 2 * n - 1):
        for c in range(chunks):
            if 0 < t - c < 2 * n:
                line.stage(c, t - c)
        for task in tasks[t - 1]:
            task()
    for s in range(seqs):
        collect.drain(s)
    line.drain()


def fused_call(body, collective, operands, outs, scratch, flops):
    whole = pl.BlockSpec(memory_space=vmem)
    return pl.pallas_call(
        body,
        out_shape=outs,
        in_specs=[whole] * len(operands),
        out_specs=[whole] * len(outs),
        scratch_shapes=scratch,
        compiler_params=pltpu.CompilerParams(
            collective_id=collective,
            has_side_effects=True,
            vmem_limit_bytes=60 * 1024 * 1024,
        ),
        cost_estimate=pl.CostEstimate(flops=flops, bytes_accessed=200_000_000, transcendentals=0),
    )(*operands)


def local(
    inputs,
    cotangent,
    master_qkv,
    qkv_moment1,
    qkv_moment2,
    master_out,
    out_moment1,
    out_moment2,
    master_up,
    up_moment1,
    up_moment2,
    master_down,
    down_moment1,
    down_moment2,
    norm_gains,
    gain_moment1,
    gain_moment2,
    shared_biases,
    shared_moment1,
    shared_moment2,
    split_biases,
    split_moment1,
    split_moment2,
):
    seq_count, block_len, model_width = inputs.shape
    row_count = seq_count * block_len
    width_part = master_qkv.shape[2]
    hidden_rows = master_up.shape[1]
    local_heads = width_part // HD
    tp_count = lax.axis_size("tp")
    chunks = 2 * seq_count
    own_rows = row_count // chunks // tp_count

    def own_part(values):
        blocks = values.reshape(chunks, tp_count * own_rows, model_width)
        taken = lax.dynamic_slice_in_dim(blocks, lax.axis_index("tp") * own_rows, own_rows, axis=1)
        return taken.reshape(-1, model_width)

    own_shape = jax.ShapeDtypeStruct((row_count // tp_count, model_width), jnp.float32)
    sums_shape = jax.ShapeDtypeStruct((8, model_width), jnp.float32)
    gains = [norm_gains[i : i + 1] for i in range(2)]
    shared = [shared_biases[i : i + 1] for i in range(4)]
    inputs_own = own_part(inputs)
    cotangent_own = own_part(cotangent)

    def gather_rows(master):
        flat = master.astype(low).reshape(master.shape[0], -1)
        return lax.all_gather(flat, ("fsdp", "ctx"), axis=0, tiled=True)

    qkv_flat = gather_rows(master_qkv)
    out_flat = gather_rows(master_out)
    up_flat = gather_rows(master_up)
    down_flat = gather_rows(master_down)
    head_ids = (lax.axis_index("tp") * local_heads + jnp.arange(local_heads)).astype(jnp.float32)
    slopes = jnp.power(2.0, -8.0 * (head_ids + 1.0) / (local_heads * lax.axis_size("tp")))
    slopes = jnp.broadcast_to(slopes[:, None, None], (local_heads, 8, block_len))
    stream = inputs.astype(jnp.float32).reshape(row_count, model_width)
    normed_one, inverse_one = normalize(stream)
    act_one = (normed_one * norm_gains[0] + shared_biases[0]).astype(jnp.bfloat16)
    projected = jnp.dot(act_one, qkv_flat, preferred_element_type=jnp.float32)
    projected_bias = jnp.concatenate(
        [split_biases[0], jnp.zeros((width_part,), jnp.float32), split_biases[1]]
    )
    projected = (projected + projected_bias).astype(low)
    sems = line_scratch(tp_count, chunks, row_count, model_width)
    pair_rows = row_count * lax.axis_size("ctx")
    square = vmem((block_len, block_len), jnp.float32)
    pair_sems = [pltpu.SemaphoreType.DMA((3, seq_count))] * 2
    act_two, middle, context, log_total, pairs = fused_call(
        functools.partial(attend_kernel, tp_count, chunks, 256),
        0,
        (projected, slopes, out_flat, inputs_own, shared[2], gains[1], shared[1]),
        [
            jax.ShapeDtypeStruct((row_count, model_width), low),
            own_shape,
            jax.ShapeDtypeStruct((row_count, width_part), low),
            jax.ShapeDtypeStruct((row_count, width_part), jnp.float32),
            jax.ShapeDtypeStruct((pair_rows, 2 * width_part), low),
        ],
        sems + [square] + pair_sems,
        4 * row_count * model_width * width_part,
    )
    up_proj = jnp.dot(act_two, up_flat, preferred_element_type=jnp.float32) + split_biases[
        2:
    ].reshape(-1)
    gelu_low = gelu_tanh(up_proj).astype(jnp.bfloat16)
    branch_part = contract_cols(gelu_low, down_flat).astype(low)
    grad_branch = cotangent.reshape(row_count, model_width)
    grad_gelu = jnp.dot(grad_branch, down_flat, preferred_element_type=jnp.float32)
    gelu_vjp = jax.vjp(gelu_tanh, up_proj)[1]
    grad_up_proj = gelu_vjp(grad_gelu)[0].astype(jnp.bfloat16)
    grad_down = contract_rows(grad_branch, gelu_low)
    grad_up = contract_rows(act_two, grad_up_proj)
    grad_bias_up = jnp.sum(grad_up_proj, axis=0, dtype=jnp.float32)
    grad_attn, grad_middle, sums_two = tp_sum(
        tp_count,
        chunks,
        attn_epilogue,
        2,
        grad_up_proj,
        up_flat,
        (middle, cotangent_own, gains[1]),
        [own_shape, sums_shape],
    )
    pair_block = (block_len, 2 * width_part)
    output, grad_projected, grad_qkv, grad_out = fused_call(
        functools.partial(backward_kernel, tp_count, chunks),
        1,
        (
            branch_part,
            middle,
            shared[3],
            grad_attn,
            out_flat,
            projected,
            pairs,
            context,
            log_total,
            slopes,
            act_one,
        ),
        [
            jax.ShapeDtypeStruct((row_count, model_width), low),
            jax.ShapeDtypeStruct((row_count, 3 * width_part), low),
            jax.ShapeDtypeStruct((model_width, 3 * width_part), low),
            jax.ShapeDtypeStruct((model_width, width_part), low),
        ],
        sems[1:]
        + [
            square,
            vmem((row_count, width_part), low),
            vmem((pair_rows, 2 * width_part), low),
            vmem((2, seq_count, *pair_block), low),
            vmem((seq_count, *pair_block), low),
        ]
        + pair_sems,
        12 * row_count * model_width * width_part,
    )
    output = output.reshape(seq_count, block_len, model_width)
    query_low = grad_projected[:, :width_part]
    value_low = grad_projected[:, 2 * width_part :]
    split_grads = jnp.concatenate(
        [
            jnp.sum(query_low, axis=0, dtype=jnp.float32)[None],
            jnp.sum(value_low, axis=0, dtype=jnp.float32)[None],
            grad_bias_up.reshape(hidden_rows, width_part),
        ],
        axis=0,
    )
    vectors = jnp.concatenate(
        [
            jnp.zeros((2, model_width), jnp.float32),
            sums_two[0:3],
            jnp.sum(cotangent_own, axis=0, dtype=jnp.float32)[None],
            jnp.zeros((2, model_width), jnp.float32),
        ]
    )
    vectors = jnp.concatenate([vectors, jnp.pad(split_grads, ((0, 2), (0, 0)))], axis=1)
    input_low, _, vector_sum = tp_sum(
        tp_count,
        chunks,
        input_epilogue,
        3,
        grad_projected,
        qkv_flat,
        (inputs_own, grad_middle, gains[0]),
        [sums_shape],
        vectors,
    )
    input_grad = input_low.astype(jnp.float32).reshape(seq_count, block_len, model_width)

    def scatter_rows(gradient, master):
        own = lax.psum_scatter(
            gradient.astype(low), ("fsdp", "ctx"), scatter_dimension=0, tiled=True
        )
        return own.astype(jnp.float32).reshape(master.shape)

    sum_down = scatter_rows(grad_down, master_down)
    sum_up = scatter_rows(grad_up, master_up)
    sum_out = scatter_rows(grad_out, master_out)
    sum_qkv = scatter_rows(grad_qkv, master_qkv)
    gain_sum = jnp.concatenate([vector_sum[0:1, :model_width], vector_sum[2:3, :model_width]])
    shared_sum = jnp.concatenate([vector_sum[1:2, :model_width], vector_sum[3:6, :model_width]])
    split_sum = vector_sum[: 2 + hidden_rows, model_width:]
    q_one, q_two, q_new = adam_update(
        master_qkv, qkv_moment1, qkv_moment2, sum_qkv, matrix_rate, True
    )
    o_one, o_two, o_new = adam_update(
        master_out, out_moment1, out_moment2, sum_out, matrix_rate, True
    )
    u_one, u_two, u_new = adam_update(master_up, up_moment1, up_moment2, sum_up, matrix_rate, True)
    d_one, d_two, d_new = adam_update(
        master_down, down_moment1, down_moment2, sum_down, matrix_rate, True
    )
    g_one, g_two, g_new = adam_update(
        norm_gains, gain_moment1, gain_moment2, gain_sum, vector_rate, False
    )
    s_one, s_two, s_new = adam_update(
        shared_biases, shared_moment1, shared_moment2, shared_sum, vector_rate, False
    )
    p_one, p_two, p_new = adam_update(
        split_biases, split_moment1, split_moment2, split_sum, vector_rate, False
    )
    return (
        output,
        input_grad,
        q_one,
        q_two,
        q_new,
        q_new.astype(jnp.bfloat16),
        o_one,
        o_two,
        o_new,
        o_new.astype(jnp.bfloat16),
        u_one,
        u_two,
        u_new,
        u_new.astype(jnp.bfloat16),
        d_one,
        d_two,
        d_new,
        d_new.astype(jnp.bfloat16),
        g_one,
        g_two,
        g_new,
        s_one,
        s_two,
        s_new,
        p_one,
        p_two,
        p_new,
    )


def solution(mesh):
    return jax.shard_map(
        local,
        mesh=mesh,
        in_specs=(
            P("fsdp", "ctx", None),
            P("fsdp", "ctx", None),
            P(("fsdp", "ctx"), None, "tp"),
            P(("fsdp", "ctx"), None, "tp"),
            P(("fsdp", "ctx"), None, "tp"),
            P(("fsdp", "ctx"), "tp"),
            P(("fsdp", "ctx"), "tp"),
            P(("fsdp", "ctx"), "tp"),
            P(("fsdp", "ctx"), None, "tp"),
            P(("fsdp", "ctx"), None, "tp"),
            P(("fsdp", "ctx"), None, "tp"),
            P(("fsdp", "ctx"), None, "tp"),
            P(("fsdp", "ctx"), None, "tp"),
            P(("fsdp", "ctx"), None, "tp"),
            P(),
            P(),
            P(),
            P(),
            P(),
            P(),
            P(None, "tp"),
            P(None, "tp"),
            P(None, "tp"),
        ),
        out_specs=(
            P("fsdp", "ctx", None),
            P("fsdp", "ctx", None),
            P(("fsdp", "ctx"), None, "tp"),
            P(("fsdp", "ctx"), None, "tp"),
            P(("fsdp", "ctx"), None, "tp"),
            P(("fsdp", "ctx"), None, "tp"),
            P(("fsdp", "ctx"), "tp"),
            P(("fsdp", "ctx"), "tp"),
            P(("fsdp", "ctx"), "tp"),
            P(("fsdp", "ctx"), "tp"),
            P(("fsdp", "ctx"), None, "tp"),
            P(("fsdp", "ctx"), None, "tp"),
            P(("fsdp", "ctx"), None, "tp"),
            P(("fsdp", "ctx"), None, "tp"),
            P(("fsdp", "ctx"), None, "tp"),
            P(("fsdp", "ctx"), None, "tp"),
            P(("fsdp", "ctx"), None, "tp"),
            P(("fsdp", "ctx"), None, "tp"),
            P(),
            P(),
            P(),
            P(),
            P(),
            P(),
            P(None, "tp"),
            P(None, "tp"),
            P(None, "tp"),
        ),
        check_vma=False,
    )
```

```python
import functools

import jax
import jax.numpy as jnp
from jax import lax
from jax.experimental import pallas as pl
from jax.experimental.pallas import tpu as pltpu
from jax.sharding import PartitionSpec as P

HD = 128
STEP = 10


norm_epsilon = 1e-05
matrix_rate = 0.04
vector_rate = 0.4
decay_weight = 0.1
decay_rate = 0.5
adam_epsilon = 1e-08
low = jnp.bfloat16


def normalize(values):
    center = jnp.mean(values, axis=-1, keepdims=True)
    shifted = values - center
    variance = jnp.mean(shifted * shifted, axis=-1, keepdims=True)
    inverse = lax.rsqrt(variance + norm_epsilon)
    return (shifted * inverse, inverse)


def norm_back(incoming, normed, inverse, gain):
    scaled = incoming * gain
    return inverse * (
        scaled
        - jnp.mean(scaled, axis=-1, keepdims=True)
        - normed * jnp.mean(scaled * normed, axis=-1, keepdims=True)
    )


def gelu_tanh(values):
    return (
        0.5
        * values
        * (1.0 + jnp.tanh(0.7978845608028654 * (values + 0.044715 * values * values * values)))
    )


def adam_update(master, moment_one, moment_two, gradient, rate, decayed):
    first = decay_rate * moment_one + (1.0 - decay_rate) * gradient
    second = decay_rate * moment_two + (1.0 - decay_rate) * gradient * gradient
    correction = 1.0 - decay_rate**STEP
    update = first / correction / (jnp.sqrt(second / correction) + adam_epsilon)
    if decayed:
        update = update + decay_weight * master
    return (first, second, master - rate * update)


def contract_rows(left, right):
    return lax.dot_general(
        left, right, (((0,), (0,)), ((), ())), preferred_element_type=jnp.float32
    )


def contract_cols(left, right):
    return lax.dot_general(
        left, right, (((1,), (1,)), ((), ())), preferred_element_type=jnp.float32
    )


MESH = pl.DeviceIdType.MESH
vmem = pltpu.VMEM


class Line:
    def __init__(self, n, chunks, part, full, landing, total, sems, finish):
        self.n, self.chunks = n, chunks
        self.part, self.full, self.landing, self.total = part, full, landing, total
        self.sum_send, self.sum_recv, self.row_send, self.row_recv = sems
        self.finish = finish
        self.z = lax.axis_index("tp")
        self.chunk_rows = full.shape[0] // chunks
        self.own = self.chunk_rows // n
        self.last = 2 * n - 1

    def place(self, c, j):
        return pl.ds(pl.multiple_of(c * self.chunk_rows + j * self.own, self.own), self.own)

    def flow(self, d):
        return self.z if d == 0 else self.n - 1 - self.z

    def toward(self, d, away):
        return {"tp": self.z + (1 if (d == 0) != away else -1)}

    def sum_copy(self, d, c, k, source, away=False):
        return pltpu.make_async_remote_copy(
            src_ref=source,
            dst_ref=self.landing.at[d, c, k - 1],
            send_sem=self.sum_send.at[d, c, k - 1],
            recv_sem=self.sum_recv.at[d, c, k - 1],
            device_id=self.toward(d, away),
            device_id_type=MESH,
        )

    def sum_arrive(self, d, c, k):
        self.sum_copy(d, c, k, self.landing.at[d, c, k - 1], True).wait_recv()

    def row_copy(self, d, c, k, away=False):
        back = k if away else k - 1
        rows = self.place(c, self.z - back if d == 0 else self.z + back)
        return pltpu.make_async_remote_copy(
            src_ref=self.full.at[rows],
            dst_ref=self.full.at[rows],
            send_sem=self.row_send.at[d, c, k - 1],
            recv_sem=self.row_recv.at[d, c, k - 1],
            device_id=self.toward(d, away),
            device_id_type=MESH,
        )

    def stage(self, c, s):
        n, z = self.n, self.z
        if s < n:
            for d in range(2):
                q = self.flow(d)
                rows = self.place(c, z + n - s if d == 0 else z - n + s)

                @pl.when(q == 0)
                def first():
                    self.sum_copy(d, c, s, self.part.at[rows]).start()

                if s > 1:

                    @pl.when((q >= 1) & (q < s))
                    def later():
                        self.sum_arrive(d, c, s - 1)
                        held = self.landing.at[d, c, s - 2]
                        held[...] = (
                            self.part[rows].astype(jnp.float32) + held[...].astype(jnp.float32)
                        ).astype(low)
                        self.sum_copy(d, c, s, held).start()

        elif s == n:
            rows = self.place(c, z)
            self.total[...] = self.part[rows].astype(jnp.float32)
            for d in range(2):

                @pl.when(self.flow(d) >= 1)
                def ended():
                    self.sum_arrive(d, c, n - 1)
                    self.total[...] += self.landing[d, c, n - 2].astype(jnp.float32)

            self.full[rows] = self.finish(c, self.total[...]).astype(low)
            for d in range(2):

                @pl.when(self.flow(d) < n - 1)
                def spread():
                    self.row_copy(d, c, 1).start()

        else:
            k = s - n + 1
            for d in range(2):
                q = self.flow(d)

                @pl.when(q >= k - 1)
                def arrived():
                    self.row_copy(d, c, k - 1, True).wait_recv()

                if k < n:

                    @pl.when((q >= k - 1) & (q < n - 1))
                    def onward():
                        self.row_copy(d, c, k).start()

    def drain(self):
        n = self.n
        for c in range(self.chunks):
            for d in range(2):
                q = self.flow(d)
                for k in range(1, n):

                    @pl.when(q < k)
                    def sum_sent():
                        self.sum_copy(d, c, k, self.landing.at[d, c, k - 1]).wait_send()

                    @pl.when((q >= k - 1) & (q < n - 1))
                    def row_sent():
                        self.row_copy(d, c, k).wait_send()


def peers(axes):
    found = []
    for axis in axes:
        bit = 1
        while bit < lax.axis_size(axis):
            me = lax.axis_index(axis)
            found.append({axis: me + bit * (1 - 2 * ((me // bit) % 2))})
            bit *= 2
    return found


def greet(n, others):
    z = lax.axis_index("tp")
    barrier = pltpu.get_barrier_semaphore()

    @pl.when(z > 0)
    def to_lower():
        pl.semaphore_signal(barrier, inc=1, device_id={"tp": z - 1}, device_id_type=MESH)

    @pl.when(z < n - 1)
    def to_upper():
        pl.semaphore_signal(barrier, inc=1, device_id={"tp": z + 1}, device_id_type=MESH)

    for other in others:
        pl.semaphore_signal(barrier, inc=1, device_id=other, device_id_type=MESH)

    @pl.when((z > 0) & (z < n - 1))
    def from_both():
        pl.semaphore_wait(barrier, 2 + len(others))

    @pl.when((z == 0) | (z == n - 1))
    def from_one():
        pl.semaphore_wait(barrier, 1 + len(others))


def line_scratch(n, chunks, rows, width):
    own = rows // chunks // n
    return [
        vmem((rows, width), low),
        vmem((2, chunks, n - 1, own, width), low),
        vmem((own, width), jnp.float32),
    ] + [pltpu.SemaphoreType.DMA((2, chunks, n - 1))] * 4


class Exchange:
    def __init__(self, whole, start, arrived, send_sem, recv_sem):
        self.whole, self.held, self.arrived = whole, start, arrived
        self.send_sem, self.recv_sem = send_sem, recv_sem
        self.inner = len(peers(("ctx", "fsdp")))
        self.peers = peers(("ctx", "fsdp", "tp"))

    def copy(self, i):
        columns = slice(None) if i < self.inner else slice(0, self.whole)
        return pltpu.make_async_remote_copy(
            src_ref=self.held.at[i, :, columns],
            dst_ref=self.arrived.at[i, :, columns],
            send_sem=self.send_sem.at[i],
            recv_sem=self.recv_sem.at[i],
            device_id=self.peers[i],
            device_id_type=MESH,
        )

    def step(self, i):
        if i > 0:
            self.copy(i - 1).wait_recv()
            if i - 1 < self.inner:
                self.held[i] = self.held[i - 1] + self.arrived[i - 1]
            else:
                self.held[i] = self.held[i - 1]
                self.held[i, :, : self.whole] += self.arrived[i - 1, :, : self.whole]
        if i < len(self.peers):
            self.copy(i).start()

    def drain(self):
        for i in range(len(self.peers)):
            self.copy(i).wait_send()


def sum_kernel(n, chunks, tile, epilogue, extra_count, out_count, with_vectors, filled, *refs):
    left, right = refs[:2]
    extras = refs[2 : 2 + extra_count]
    full = refs[2 + extra_count]
    outs = refs[3 + extra_count : 3 + extra_count + out_count]
    scratch = refs[3 + extra_count + out_count :]
    part, landing, total = scratch[:3]
    rows, width = full.shape
    chunk_rows = rows // chunks
    block = max(chunk_rows, min(rows, 256))
    per_block = block // chunk_rows
    greet(n, peers(("ctx", "fsdp", "tp")) if with_vectors else [])
    finish = epilogue(chunk_rows // n, extras, outs)
    line = Line(n, chunks, part, full, landing, total, scratch[3:7], finish)

    def multiply(b):
        @pl.loop(0, width // tile)
        def one(i):
            columns = pl.ds(pl.multiple_of(i * tile, tile), tile)
            part[b * block : (b + 1) * block, columns] = contract_cols(
                left[b * block : (b + 1) * block, :], right[columns, :]
            ).astype(low)

    def fill(first, last):
        @pl.loop(first, last)
        def one(i):
            columns = pl.ds(pl.multiple_of(i * tile, tile), tile)
            outs[-1][:, columns] = contract_cols(extras[-2][...], extras[-1][columns, :]).astype(low)

    multiply(0)
    ended = chunks - 1 + n
    slots = chunks + 2 * n - 2
    vectors = None
    for t in range(1, chunks + 2 * n - 1):
        for c in range(chunks):
            if 0 < t - c < 2 * n:
                line.stage(c, t - c)
        if t % per_block == 0 and t < chunks:
            multiply(t // per_block)
        if filled and t > chunks:
            span = slots - chunks
            tiles = width // tile
            fill(tiles * (t - chunks - 1) // span, tiles * (t - chunks) // span)
        if with_vectors and t == ended:
            held, arrived, send_sem, recv_sem = scratch[7:]
            vectors = Exchange(width, held, arrived, send_sem, recv_sem)
            held[0] = extras[-1][...]
            held[0, 0:2, :width] = outs[0][0:2]
        if vectors is not None and t - ended <= len(vectors.peers):
            vectors.step(t - ended)
            done = t - ended
    if vectors is not None:
        for i in range(done + 1, len(vectors.peers) + 1):
            vectors.step(i)
        outs[-1][...] = vectors.held[len(vectors.peers)]
        vectors.drain()
    line.drain()


def tp_sum(
    n, chunks, epilogue, collective, left, right, extras, out_shapes, vectors=None, filler=None
):
    rows, width = left.shape[0], right.shape[0]
    depth = left.shape[1]
    outs = [jax.ShapeDtypeStruct((rows, width), low)] + list(out_shapes)
    scratch = line_scratch(n, chunks, rows, width)
    if filler is not None:
        extras = (*extras, *filler)
        outs.append(jax.ShapeDtypeStruct((rows, width), low))
    if vectors is not None:
        extras = (*extras, vectors)
        outs.append(jax.ShapeDtypeStruct(vectors.shape, jnp.float32))
        steps = len(peers(("ctx", "fsdp", "tp")))
        scratch += [
            vmem((steps + 1, *vectors.shape), jnp.float32),
            vmem((steps, *vectors.shape), jnp.float32),
            pltpu.SemaphoreType.DMA((steps,)),
            pltpu.SemaphoreType.DMA((steps,)),
        ]
    return pl.pallas_call(
        functools.partial(
            sum_kernel,
            n,
            chunks,
            256,
            epilogue,
            len(extras),
            len(outs) - 1,
            vectors is not None,
            filler is not None,
        ),
        out_shape=outs,
        in_specs=[pl.BlockSpec(memory_space=vmem)] * (2 + len(extras)),
        out_specs=[pl.BlockSpec(memory_space=vmem)] * len(outs),
        scratch_shapes=scratch,
        compiler_params=pltpu.CompilerParams(
            collective_id=collective,
            has_side_effects=True,
            vmem_limit_bytes=56 * 1024 * 1024,
        ),
        cost_estimate=pl.CostEstimate(
            flops=2 * rows * width * depth,
            bytes_accessed=200_000_000,
            transcendentals=0,
        ),
    )(left, right, *extras)


def middle_epilogue(own, extras, outs):
    stream, bias, gain, shift = extras
    (middle,) = outs

    def finish(c, total):
        rows = slice(c * own, (c + 1) * own)
        value = stream[rows].astype(jnp.float32) + total + bias[...]
        middle[rows] = value
        return normalize(value)[0] * gain[...] + shift[...]

    return finish


def output_epilogue(own, extras, outs):
    middle, bias = extras

    def finish(c, total):
        return middle[c * own : (c + 1) * own] + total + bias[...]

    return finish


def attn_epilogue(own, extras, outs):
    middle, cotangent, gain = extras[:3]
    grad_middle, sums = outs[:2]
    sums[...] = jnp.zeros_like(sums)

    def finish(c, total):
        rows = slice(c * own, (c + 1) * own)
        normed, inverse = normalize(middle[rows])
        value = cotangent[rows].astype(jnp.float32) + norm_back(total, normed, inverse, gain[...])
        grad_middle[rows] = value
        sums[0:1] += jnp.sum(total * normed, axis=0, keepdims=True)
        sums[1:2] += jnp.sum(total, axis=0, keepdims=True)
        sums[2:3] += jnp.sum(value.astype(low).astype(jnp.float32), axis=0, keepdims=True)
        return value

    return finish


def input_epilogue(own, extras, outs):
    stream, grad_middle, gain = extras[:3]
    sums = outs[0]
    sums[...] = jnp.zeros_like(sums)

    def finish(c, total):
        rows = slice(c * own, (c + 1) * own)
        normed, inverse = normalize(stream[rows].astype(jnp.float32))
        sums[0:1] += jnp.sum(total * normed, axis=0, keepdims=True)
        sums[1:2] += jnp.sum(total, axis=0, keepdims=True)
        return grad_middle[rows] + norm_back(total, normed, inverse, gain[...])

    return finish


def swap(values, axis, bit):
    pairs = [(i, i + bit * (1 - 2 * ((i // bit) % 2))) for i in range(lax.axis_size(axis))]
    return lax.ppermute(values, axis, pairs)


def add_low(left, right):
    return (left.astype(jnp.float32) + right.astype(jnp.float32)).astype(low)


def halving(kept, axis, outer):
    width = kept.shape[1]
    bit = 2 if axis == "ctx" else lax.axis_size(axis) // 2
    while bit:
        mine = (lax.axis_index(axis) // bit) % 2
        cut = kept.reshape(outer, 2, -1, width)
        given = lax.dynamic_index_in_dim(cut, 1 - mine, 1, False).reshape(-1, width)
        own = lax.dynamic_index_in_dim(cut, mine, 1, False).reshape(-1, width)
        kept = add_low(own, swap(given, axis, bit))
        bit = 0 if axis == "ctx" else bit // 2
    return kept


def ctx_place():
    me = lax.axis_index("ctx")
    half, side = me // 2, me % 2
    return me, half, side, {"ctx": me + 1 - 2 * side}, {"ctx": me + 2 - 4 * half}


def ctx_copy(source, target, send, recv, device):
    return pltpu.make_async_remote_copy(
        src_ref=source,
        dst_ref=target,
        send_sem=send,
        recv_sem=recv,
        device_id=device,
        device_id_type=MESH,
    )


class Spread:
    def __init__(self, block, own, pairs, send, recv):
        self.block, self.own, self.pairs, self.send, self.recv = block, own, pairs, send, recv
        self.me, self.half, self.side, self.beside, self.across = ctx_place()

    def rows(self, s, b):
        start = (s * lax.axis_size("ctx") + b) * self.block
        return pl.ds(pl.multiple_of(start, self.block), self.block)

    def copy(self, kind, s, b, own, device):
        target = self.pairs.at[self.rows(s, b)]
        wide = self.pairs.shape[1]
        source = self.own.at[s * self.block : (s + 1) * self.block, wide // 2 :] if own else target
        return ctx_copy(source, target, self.send.at[kind, s], self.recv.at[kind, s], device)

    def start(self, s):
        rows = slice(s * self.block, (s + 1) * self.block)

        @pl.when(self.half == 0)
        def over():
            self.copy(0, s, self.me, True, self.across).start()

        @pl.when(self.side == 0)
        def aside():
            self.copy(1, s, self.me, True, self.beside).start()

        self.pairs[self.rows(s, self.me)] = self.own[rows, self.pairs.shape[1] // 2 :]

    def forward(self, s):
        @pl.when(self.half == 1)
        def onward():
            self.copy(0, s, self.me - 2, False, self.across).wait_recv()
            self.copy(2, s, self.me - 2, False, self.beside).start()

    def arrive(self, s):
        @pl.when(self.half == 1)
        def second():
            self.copy(2, s, 1 - self.side, False, self.beside).wait_recv()

        @pl.when(self.side == 1)
        def first():
            self.copy(1, s, self.me - 1, False, self.beside).wait_recv()

    def drain_own(self, s):
        @pl.when(self.half == 0)
        def over():
            self.copy(0, s, self.me, True, self.across).wait_send()

        @pl.when(self.side == 0)
        def aside():
            self.copy(1, s, self.me, True, self.beside).wait_send()

    def drain(self, s):
        @pl.when(self.half == 1)
        def onward():
            self.copy(2, s, self.me - 2, False, self.beside).wait_send()


class Collect:
    def __init__(self, block, parts, beside_in, across_in, send, recv):
        self.block, self.parts = block, parts
        self.beside_in, self.across_in, self.send, self.recv = beside_in, across_in, send, recv
        self.me, self.half, self.side, self.beside, self.across = ctx_place()

    def rows(self, s, b):
        start = (s * lax.axis_size("ctx") + b) * self.block
        return pl.ds(pl.multiple_of(start, self.block), self.block)

    def aside(self, s, k, away=False):
        b = 2 * k + (self.side if away else 1 - self.side)
        return ctx_copy(
            self.parts.at[self.rows(s, b)],
            self.beside_in.at[k, s],
            self.send.at[k, s],
            self.recv.at[k, s],
            self.beside,
        )

    def over(self, s):
        return ctx_copy(
            self.parts.at[self.rows(s, self.side)],
            self.across_in.at[s],
            self.send.at[2, s],
            self.recv.at[2, s],
            self.across,
        )

    def start(self, s):
        for k in range(2):

            @pl.when(2 * k + 1 - self.side < self.me)
            def give():
                self.aside(s, k).start()

    def forward(self, s):
        for k in range(2):

            @pl.when(2 * k + self.side < self.me + 1 - 2 * self.side)
            def take():
                self.aside(s, k, True).wait_recv()

        @pl.when(self.half == 1)
        def onward():
            held = self.parts.at[self.rows(s, self.side)]
            held[...] = (
                held[...].astype(jnp.float32) + self.beside_in[0, s].astype(jnp.float32)
            ).astype(low)
            self.over(s).start()

    def finish(self, s, target):
        target[...] = self.parts[self.rows(s, self.me)]
        for k in range(2):

            @pl.when((self.side == 0) & (self.half == k))
            def near():
                target[...] = (
                    target[...].astype(jnp.float32) + self.beside_in[k, s].astype(jnp.float32)
                ).astype(low)

        @pl.when(self.half == 0)
        def far():
            self.over(s).wait_recv()
            target[...] = (
                target[...].astype(jnp.float32) + self.across_in[s].astype(jnp.float32)
            ).astype(low)

    def drain(self, s):
        for k in range(2):

            @pl.when(2 * k + 1 - self.side < self.me)
            def gave():
                self.aside(s, k).wait_send()

        @pl.when(self.half == 1)
        def sent():
            self.over(s).wait_send()


def offsets(base):
    shape = base.shape
    base[...] = (
        lax.broadcasted_iota(jnp.int32, shape, 0) - lax.broadcasted_iota(jnp.int32, shape, 1)
    ).astype(jnp.float32)


def head_scores(query, key, slope, base, j):
    far = base[...] + (j * base.shape[0]).astype(jnp.float32)
    return contract_cols(query, key) * HD ** (-0.5) - slope * jnp.abs(far)


def head_columns(h, shift=0):
    return pl.ds(pl.multiple_of(shift + h * HD, HD), HD)


def forward_heads(s, first, last, block, projected, pairs, slopes, base, context, log_total):
    me = lax.axis_index("ctx")
    count = lax.axis_size("ctx")
    own = slice(s * block, (s + 1) * block)
    wide = pairs.shape[1] // 2

    @pl.loop(first, last)
    def head(h):
        query = projected[own, head_columns(h)]

        def step(j, carry):
            peak, weight, total = carry
            rows = pl.ds(pl.multiple_of((s * count + me - j) * block, block), block)
            scores = head_scores(query, pairs[rows, head_columns(h)], slopes[h, 0:1], base, j)
            higher = jnp.maximum(peak, jnp.max(scores, axis=-1, keepdims=True))
            shrink = jnp.exp(peak - higher)
            exponent = jnp.exp(scores - higher)
            weight = weight * shrink + jnp.sum(exponent, axis=-1, keepdims=True)
            total = total * shrink + jnp.dot(
                exponent.astype(low),
                pairs[rows, head_columns(h, wide)],
                preferred_element_type=jnp.float32,
            )
            return higher, weight, total

        peak, weight, total = lax.fori_loop(
            0,
            me + 1,
            step,
            (
                jnp.full((block, 1), -1e30, jnp.float32),
                jnp.zeros((block, 1), jnp.float32),
                jnp.zeros((block, HD), jnp.float32),
            ),
        )
        context[own, head_columns(h)] = (total / weight).astype(low)
        log_total[own, head_columns(h)] = jnp.broadcast_to(peak + jnp.log(weight), (block, HD))


def backward_heads(
    s, first, last, block, projected, pairs, slopes, base, context, log_total, grad, parts, out
):
    me = lax.axis_index("ctx")
    count = lax.axis_size("ctx")
    own = slice(s * block, (s + 1) * block)
    wide = pairs.shape[1] // 2

    @pl.loop(first, last)
    def head(h):
        query = projected[own, head_columns(h)]
        incoming = grad[own, head_columns(h)]
        level = log_total[own, head_columns(h)][:, 0:1]
        mean = jnp.sum(
            incoming.astype(jnp.float32) * context[own, head_columns(h)].astype(jnp.float32),
            axis=-1,
            keepdims=True,
        )

        def step(j, total):
            rows = pl.ds(pl.multiple_of((s * count + me - j) * block, block), block)
            key = pairs[rows, head_columns(h)]
            probs = jnp.exp(head_scores(query, key, slopes[h, 0:1], base, j) - level)
            grad_probs = contract_cols(incoming, pairs[rows, head_columns(h, wide)])
            grad_scores = (probs * (grad_probs - mean)).astype(low)
            parts[rows, head_columns(h)] = (
                contract_rows(grad_scores, query) * HD ** (-0.5)
            ).astype(low)
            parts[rows, head_columns(h, wide)] = contract_rows(probs.astype(low), incoming).astype(
                low
            )
            return total + jnp.dot(grad_scores, key, preferred_element_type=jnp.float32)

        total = lax.fori_loop(0, me + 1, step, jnp.zeros((block, HD), jnp.float32))
        out[own, head_columns(h)] = (total * HD ** (-0.5)).astype(low)


def attend_kernel(n, chunks, tile, *refs):
    (
        projected,
        slopes,
        out_weight,
        stream,
        bias,
        gain,
        shift,
        full,
        middle,
        context,
        log_total,
        pairs,
        part,
        landing,
        total,
        *rest,
    ) = refs
    sems, (base, send, recv) = rest[:4], rest[4:]
    rows, width = full.shape
    seqs = chunks // 2
    block = rows // seqs
    heads = context.shape[1] // HD
    pace = heads // 2
    _, _, _, beside, across = ctx_place()
    greet(n, [beside, across])
    finish = middle_epilogue(rows // chunks // n, (stream, bias, gain, shift), (middle,))
    line = Line(n, chunks, part, full, landing, total, sems, finish)
    spread = Spread(block, projected, pairs, send, recv)
    spread.start(0)
    offsets(base)

    def attend(s, first, last):
        if first == 0:
            spread.forward(s)
            if s + 1 < seqs:
                spread.drain_own(s)
                spread.start(s + 1)
            spread.arrive(s)
        forward_heads(
            s, first, last, block, projected, pairs, slopes, base, context, log_total
        )

    def multiply(s):
        own = slice(s * block, (s + 1) * block)

        @pl.loop(0, width // tile)
        def one(i):
            columns = pl.ds(pl.multiple_of(i * tile, tile), tile)
            part[own, columns] = contract_cols(context[own, :], out_weight[columns, :]).astype(low)

    attend(0, 0, heads)
    multiply(0)
    for t in range(1, chunks + 2 * n - 1):
        for c in range(chunks):
            if 0 < t - c < 2 * n:
                line.stage(c, t - c)
        s = (t + 1) // 2
        if s < seqs:
            attend(s, 0 if t % 2 else pace, pace if t % 2 else heads)
            if t % 2 == 0:
                multiply(s)
    spread.drain_own(seqs - 1)
    for s in range(seqs):
        spread.drain(s)
    line.drain()


def backward_kernel(n, chunks, *refs):
    (
        part,
        middle,
        bias,
        grad_attn,
        out_weight,
        projected,
        pairs,
        context,
        log_total,
        slopes,
        act,
        full,
        grad_projected,
        grad_weights,
        landing,
        total,
        *rest,
    ) = refs
    sems, (base, grad_context, parts, beside_in, across_in, send, recv) = rest[:4], rest[4:]
    rows, width = full.shape
    seqs = chunks // 2
    block = rows // seqs
    heads = context.shape[1] // HD
    wide = context.shape[1]
    pace = heads // 2
    _, _, _, beside, across = ctx_place()
    greet(n, [beside, across])
    finish = output_epilogue(rows // chunks // n, (middle, bias), ())
    line = Line(n, chunks, part, full, landing, total, sems, finish)
    collect = Collect(block, parts, beside_in, across_in, send, recv)
    offsets(base)

    def backward(s, first, last):
        own = slice(s * block, (s + 1) * block)
        if first == 0:
            grad_context[own, :] = jnp.dot(
                grad_attn[own, :], out_weight[...], preferred_element_type=jnp.float32
            ).astype(low)
        backward_heads(
            s,
            first,
            last,
            block,
            projected,
            pairs,
            slopes,
            base,
            context,
            log_total,
            grad_context,
            parts,
            grad_projected,
        )
        if last == heads:
            collect.start(s)

    def finished(s):
        collect.finish(s, grad_projected.at[s * block : (s + 1) * block, wide:])

    def features(source, right, columns, first, last):
        @pl.loop(first, last)
        def one(i):
            place = pl.ds(pl.multiple_of(i * 256, 256), 256)
            grad_weights[place, columns] = contract_rows(source[:, place], right[...]).astype(low)

    attn_columns = slice(0, 3 * wide)
    out_columns = slice(3 * wide, 4 * wide)

    tiles = width // 256
    tasks = []
    for s in range(seqs):
        tasks.append([functools.partial(backward, s, 0, pace)])
        tasks.append([functools.partial(backward, s, pace, heads)])
    tasks += [[] for _ in range(chunks + 2 * n - 2 - len(tasks))]
    for s in range(seqs):
        tasks[2 * s + 2].append(functools.partial(collect.forward, s))
    after = 2 * seqs + 1
    tasks[after].append(functools.partial(features, grad_attn, context, out_columns, 0, tiles))
    for s in range(seqs):
        tasks[after + s].append(functools.partial(finished, s))
    left = len(tasks) - after - seqs
    for i in range(left):
        tasks[after + seqs + i].append(
            functools.partial(
                features,
                act,
                grad_projected,
                attn_columns,
                tiles * i // left,
                tiles * (i + 1) // left,
            )
        )
    for t in range(1, chunks + 2 * n - 1):
        for c in range(chunks):
            if 0 < t - c < 2 * n:
                line.stage(c, t - c)
        for task in tasks[t - 1]:
            task()
    for s in range(seqs):
        collect.drain(s)
    line.drain()


def fused_call(body, collective, operands, outs, scratch, flops):
    whole = pl.BlockSpec(memory_space=vmem)
    return pl.pallas_call(
        body,
        out_shape=outs,
        in_specs=[whole] * len(operands),
        out_specs=[whole] * len(outs),
        scratch_shapes=scratch,
        compiler_params=pltpu.CompilerParams(
            collective_id=collective,
            has_side_effects=True,
            vmem_limit_bytes=60 * 1024 * 1024,
        ),
        cost_estimate=pl.CostEstimate(flops=flops, bytes_accessed=200_000_000, transcendentals=0),
    )(*operands)


def local(
    inputs,
    cotangent,
    master_qkv,
    qkv_moment1,
    qkv_moment2,
    master_out,
    out_moment1,
    out_moment2,
    master_up,
    up_moment1,
    up_moment2,
    master_down,
    down_moment1,
    down_moment2,
    norm_gains,
    gain_moment1,
    gain_moment2,
    shared_biases,
    shared_moment1,
    shared_moment2,
    split_biases,
    split_moment1,
    split_moment2,
):
    seq_count, block_len, model_width = inputs.shape
    row_count = seq_count * block_len
    width_part = master_qkv.shape[2]
    hidden_rows = master_up.shape[1]
    local_heads = width_part // HD
    tp_count = lax.axis_size("tp")
    chunks = 2 * seq_count
    own_rows = row_count // chunks // tp_count

    def own_part(values):
        blocks = values.reshape(chunks, tp_count * own_rows, model_width)
        taken = lax.dynamic_slice_in_dim(blocks, lax.axis_index("tp") * own_rows, own_rows, axis=1)
        return taken.reshape(-1, model_width)

    own_shape = jax.ShapeDtypeStruct((row_count // tp_count, model_width), jnp.float32)
    sums_shape = jax.ShapeDtypeStruct((8, model_width), jnp.float32)
    gains = [norm_gains[i : i + 1] for i in range(2)]
    shared = [shared_biases[i : i + 1] for i in range(4)]
    inputs_own = own_part(inputs)
    cotangent_own = own_part(cotangent)

    def flat(master):
        return master.astype(low).reshape(master.shape[0], -1)

    def gather_rows(rows):
        return lax.all_gather(rows, ("fsdp", "ctx"), axis=0, tiled=True)

    attn_flat = gather_rows(jnp.concatenate([flat(master_qkv), flat(master_out)], axis=1))
    qkv_flat, out_flat = attn_flat[:, : 3 * width_part], attn_flat[:, 3 * width_part :]
    up_flat = gather_rows(flat(master_up))
    down_flat = gather_rows(flat(master_down))
    head_ids = (lax.axis_index("tp") * local_heads + jnp.arange(local_heads)).astype(jnp.float32)
    slopes = jnp.power(2.0, -8.0 * (head_ids + 1.0) / (local_heads * lax.axis_size("tp")))
    slopes = jnp.broadcast_to(slopes[:, None, None], (local_heads, 8, block_len))
    shards = lax.axis_size("fsdp") * lax.axis_size("ctx")
    side = lax.axis_index("ctx") % 2

    def split_side(values, flip):
        cut = values.reshape(shards // 2, 2, -1, values.shape[1])
        place = side + flip * (1 - 2 * side)
        return lax.dynamic_index_in_dim(cut, place, 1, False).reshape(-1, values.shape[1])

    def first_half(kept):
        half = kept.shape[1] // 2
        count = lax.axis_size("fsdp")
        return halving(kept[:, :half], "ctx", count), halving(kept[:, half:], "fsdp", 1)

    def second_half(pieces):
        return jnp.concatenate(
            [halving(pieces[0], "fsdp", 1), halving(pieces[1], "ctx", 1)], axis=1
        )

    def weight_sum(left, right):
        columns = left.reshape(row_count, shards // 2, 2, -1)

        def product(flip):
            place = side + flip * (1 - 2 * side)
            chosen = lax.dynamic_index_in_dim(columns, place, 2, False).reshape(row_count, -1)
            return contract_rows(chosen, right)

        given = swap(product(1).astype(low), "ctx", 1)
        return add_low(product(0), given)

    stream = inputs.astype(jnp.float32).reshape(row_count, model_width)
    normed_one, inverse_one = normalize(stream)
    act_one = (normed_one * norm_gains[0] + shared_biases[0]).astype(jnp.bfloat16)
    projected = jnp.dot(act_one, qkv_flat, preferred_element_type=jnp.float32)
    projected_bias = jnp.concatenate(
        [split_biases[0], jnp.zeros((width_part,), jnp.float32), split_biases[1]]
    )
    projected = (projected + projected_bias).astype(low)
    sems = line_scratch(tp_count, chunks, row_count, model_width)
    pair_rows = row_count * lax.axis_size("ctx")
    square = vmem((block_len, block_len), jnp.float32)
    pair_sems = [pltpu.SemaphoreType.DMA((3, seq_count))] * 2
    act_two, middle, context, log_total, pairs = fused_call(
        functools.partial(attend_kernel, tp_count, chunks, 256),
        0,
        (projected, slopes, out_flat, inputs_own, shared[2], gains[1], shared[1]),
        [
            jax.ShapeDtypeStruct((row_count, model_width), low),
            own_shape,
            jax.ShapeDtypeStruct((row_count, width_part), low),
            jax.ShapeDtypeStruct((row_count, width_part), jnp.float32),
            jax.ShapeDtypeStruct((pair_rows, 2 * width_part), low),
        ],
        sems + [square] + pair_sems,
        4 * row_count * model_width * width_part,
    )
    up_proj = jnp.dot(act_two, up_flat, preferred_element_type=jnp.float32) + split_biases[
        2:
    ].reshape(-1)
    gelu_low = gelu_tanh(up_proj).astype(jnp.bfloat16)
    grad_branch = cotangent.reshape(row_count, model_width)
    grad_gelu = jnp.dot(grad_branch, down_flat, preferred_element_type=jnp.float32)
    gelu_vjp = jax.vjp(gelu_tanh, up_proj)[1]
    grad_up_proj = gelu_vjp(grad_gelu)[0].astype(jnp.bfloat16)
    sum_down = weight_sum(grad_branch, gelu_low)
    sum_up = weight_sum(act_two, grad_up_proj)
    grad_bias_up = jnp.sum(grad_up_proj, axis=0, dtype=jnp.float32)
    grad_attn, grad_middle, sums_two, branch_part = tp_sum(
        tp_count,
        chunks,
        attn_epilogue,
        2,
        grad_up_proj,
        up_flat,
        (middle, cotangent_own, gains[1]),
        [own_shape, sums_shape],
        filler=(gelu_low, down_flat),
    )
    pair_block = (block_len, 2 * width_part)
    sum_up, sum_down, grad_attn = lax.optimization_barrier((sum_up, sum_down, grad_attn))
    sum_up, sum_down = first_half(sum_up), first_half(sum_down)
    output, grad_projected, grad_attn_weights = fused_call(
        functools.partial(backward_kernel, tp_count, chunks),
        1,
        (
            branch_part,
            middle,
            shared[3],
            grad_attn,
            out_flat,
            projected,
            pairs,
            context,
            log_total,
            slopes,
            act_one,
        ),
        [
            jax.ShapeDtypeStruct((row_count, model_width), low),
            jax.ShapeDtypeStruct((row_count, 3 * width_part), low),
            jax.ShapeDtypeStruct((model_width, 4 * width_part), low),
        ],
        sems[1:]
        + [
            square,
            vmem((row_count, width_part), low),
            vmem((pair_rows, 2 * width_part), low),
            vmem((2, seq_count, *pair_block), low),
            vmem((seq_count, *pair_block), low),
        ]
        + pair_sems,
        12 * row_count * model_width * width_part,
    )
    sum_up, sum_down, output, grad_projected, grad_attn_weights = lax.optimization_barrier(
        (sum_up, sum_down, output, grad_projected, grad_attn_weights)
    )
    output = output.reshape(seq_count, block_len, model_width)
    sum_attn = add_low(
        split_side(grad_attn_weights, 0), swap(split_side(grad_attn_weights, 1), "ctx", 1)
    )
    sum_up, sum_down, sum_attn, grad_projected = lax.optimization_barrier(
        (sum_up, sum_down, sum_attn, grad_projected)
    )
    sum_attn = first_half(sum_attn)
    sum_up, sum_down = second_half(sum_up), second_half(sum_down)
    query_low = grad_projected[:, :width_part]
    value_low = grad_projected[:, 2 * width_part :]
    split_grads = jnp.concatenate(
        [
            jnp.sum(query_low, axis=0, dtype=jnp.float32)[None],
            jnp.sum(value_low, axis=0, dtype=jnp.float32)[None],
            grad_bias_up.reshape(hidden_rows, width_part),
        ],
        axis=0,
    )
    vectors = jnp.concatenate(
        [
            jnp.zeros((2, model_width), jnp.float32),
            sums_two[0:3],
            jnp.sum(cotangent_own, axis=0, dtype=jnp.float32)[None],
            jnp.zeros((2, model_width), jnp.float32),
        ]
    )
    vectors = jnp.concatenate([vectors, jnp.pad(split_grads, ((0, 2), (0, 0)))], axis=1)
    input_low, _, vector_sum = tp_sum(
        tp_count,
        chunks,
        input_epilogue,
        3,
        grad_projected,
        qkv_flat,
        (inputs_own, grad_middle, gains[0]),
        [sums_shape],
        vectors,
    )
    sum_up, sum_down, sum_attn, input_low, vector_sum = lax.optimization_barrier(
        (sum_up, sum_down, sum_attn, input_low, vector_sum)
    )
    input_grad = input_low.astype(jnp.float32).reshape(seq_count, block_len, model_width)

    sum_attn = second_half(sum_attn)
    sum_qkv = sum_attn[:, : 3 * width_part].reshape(master_qkv.shape)
    sum_out = sum_attn[:, 3 * width_part :]
    sum_up = sum_up.reshape(master_up.shape)
    sum_down = sum_down.reshape(master_down.shape)
    gain_sum = jnp.concatenate([vector_sum[0:1, :model_width], vector_sum[2:3, :model_width]])
    shared_sum = jnp.concatenate([vector_sum[1:2, :model_width], vector_sum[3:6, :model_width]])
    split_sum = vector_sum[: 2 + hidden_rows, model_width:]
    q_one, q_two, q_new = adam_update(
        master_qkv, qkv_moment1, qkv_moment2, sum_qkv, matrix_rate, True
    )
    o_one, o_two, o_new = adam_update(
        master_out, out_moment1, out_moment2, sum_out, matrix_rate, True
    )
    u_one, u_two, u_new = adam_update(master_up, up_moment1, up_moment2, sum_up, matrix_rate, True)
    d_one, d_two, d_new = adam_update(
        master_down, down_moment1, down_moment2, sum_down, matrix_rate, True
    )
    g_one, g_two, g_new = adam_update(
        norm_gains, gain_moment1, gain_moment2, gain_sum, vector_rate, False
    )
    s_one, s_two, s_new = adam_update(
        shared_biases, shared_moment1, shared_moment2, shared_sum, vector_rate, False
    )
    p_one, p_two, p_new = adam_update(
        split_biases, split_moment1, split_moment2, split_sum, vector_rate, False
    )
    return (
        output,
        input_grad,
        q_one,
        q_two,
        q_new,
        q_new.astype(jnp.bfloat16),
        o_one,
        o_two,
        o_new,
        o_new.astype(jnp.bfloat16),
        u_one,
        u_two,
        u_new,
        u_new.astype(jnp.bfloat16),
        d_one,
        d_two,
        d_new,
        d_new.astype(jnp.bfloat16),
        g_one,
        g_two,
        g_new,
        s_one,
        s_two,
        s_new,
        p_one,
        p_two,
        p_new,
    )


def solution(mesh):
    return jax.shard_map(
        local,
        mesh=mesh,
        in_specs=(
            P("fsdp", "ctx", None),
            P("fsdp", "ctx", None),
            P(("fsdp", "ctx"), None, "tp"),
            P(("fsdp", "ctx"), None, "tp"),
            P(("fsdp", "ctx"), None, "tp"),
            P(("fsdp", "ctx"), "tp"),
            P(("fsdp", "ctx"), "tp"),
            P(("fsdp", "ctx"), "tp"),
            P(("fsdp", "ctx"), None, "tp"),
            P(("fsdp", "ctx"), None, "tp"),
            P(("fsdp", "ctx"), None, "tp"),
            P(("fsdp", "ctx"), None, "tp"),
            P(("fsdp", "ctx"), None, "tp"),
            P(("fsdp", "ctx"), None, "tp"),
            P(),
            P(),
            P(),
            P(),
            P(),
            P(),
            P(None, "tp"),
            P(None, "tp"),
            P(None, "tp"),
        ),
        out_specs=(
            P("fsdp", "ctx", None),
            P("fsdp", "ctx", None),
            P(("fsdp", "ctx"), None, "tp"),
            P(("fsdp", "ctx"), None, "tp"),
            P(("fsdp", "ctx"), None, "tp"),
            P(("fsdp", "ctx"), None, "tp"),
            P(("fsdp", "ctx"), "tp"),
            P(("fsdp", "ctx"), "tp"),
            P(("fsdp", "ctx"), "tp"),
            P(("fsdp", "ctx"), "tp"),
            P(("fsdp", "ctx"), None, "tp"),
            P(("fsdp", "ctx"), None, "tp"),
            P(("fsdp", "ctx"), None, "tp"),
            P(("fsdp", "ctx"), None, "tp"),
            P(("fsdp", "ctx"), None, "tp"),
            P(("fsdp", "ctx"), None, "tp"),
            P(("fsdp", "ctx"), None, "tp"),
            P(("fsdp", "ctx"), None, "tp"),
            P(),
            P(),
            P(),
            P(),
            P(),
            P(),
            P(None, "tp"),
            P(None, "tp"),
            P(None, "tp"),
        ),
        check_vma=False,
    )
```

```python
import functools

import jax
import jax.numpy as jnp
from jax import lax
from jax.experimental import pallas as pl
from jax.experimental.pallas import tpu as pltpu
from jax.sharding import PartitionSpec as P

HD = 128
STEP = 10


norm_epsilon = 1e-05
matrix_rate = 0.04
vector_rate = 0.4
decay_weight = 0.1
decay_rate = 0.5
adam_epsilon = 1e-08
low = jnp.bfloat16


def normalize(values):
    center = jnp.mean(values, axis=-1, keepdims=True)
    shifted = values - center
    variance = jnp.mean(shifted * shifted, axis=-1, keepdims=True)
    inverse = lax.rsqrt(variance + norm_epsilon)
    return (shifted * inverse, inverse)


def norm_back(incoming, normed, inverse, gain):
    scaled = incoming * gain
    return inverse * (
        scaled
        - jnp.mean(scaled, axis=-1, keepdims=True)
        - normed * jnp.mean(scaled * normed, axis=-1, keepdims=True)
    )


def gelu_tanh(values):
    return (
        0.5
        * values
        * (1.0 + jnp.tanh(0.7978845608028654 * (values + 0.044715 * values * values * values)))
    )


def adam_update(master, moment_one, moment_two, gradient, rate, decayed):
    first = decay_rate * moment_one + (1.0 - decay_rate) * gradient
    second = decay_rate * moment_two + (1.0 - decay_rate) * gradient * gradient
    correction = 1.0 - decay_rate**STEP
    update = first / correction / (jnp.sqrt(second / correction) + adam_epsilon)
    if decayed:
        update = update + decay_weight * master
    return (first, second, master - rate * update)


def contract_rows(left, right):
    return lax.dot_general(
        left, right, (((0,), (0,)), ((), ())), preferred_element_type=jnp.float32
    )


def contract_cols(left, right):
    return lax.dot_general(
        left, right, (((1,), (1,)), ((), ())), preferred_element_type=jnp.float32
    )


MESH = pl.DeviceIdType.MESH
vmem = pltpu.VMEM


class Line:
    def __init__(self, n, chunks, part, full, landing, total, sems, finish):
        self.n, self.chunks = n, chunks
        self.part, self.full, self.landing, self.total = part, full, landing, total
        self.sum_send, self.sum_recv, self.row_send, self.row_recv = sems
        self.finish = finish
        self.z = lax.axis_index("tp")
        self.chunk_rows = full.shape[0] // chunks
        self.own = self.chunk_rows // n
        self.last = 2 * n - 1

    def place(self, c, j):
        return pl.ds(pl.multiple_of(c * self.chunk_rows + j * self.own, self.own), self.own)

    def flow(self, d):
        return self.z if d == 0 else self.n - 1 - self.z

    def toward(self, d, away):
        return {"tp": self.z + (1 if (d == 0) != away else -1)}

    def sum_copy(self, d, c, k, source, away=False):
        return pltpu.make_async_remote_copy(
            src_ref=source,
            dst_ref=self.landing.at[d, c, k - 1],
            send_sem=self.sum_send.at[d, c, k - 1],
            recv_sem=self.sum_recv.at[d, c, k - 1],
            device_id=self.toward(d, away),
            device_id_type=MESH,
        )

    def sum_arrive(self, d, c, k):
        self.sum_copy(d, c, k, self.landing.at[d, c, k - 1], True).wait_recv()

    def row_copy(self, d, c, k, away=False):
        back = k if away else k - 1
        rows = self.place(c, self.z - back if d == 0 else self.z + back)
        return pltpu.make_async_remote_copy(
            src_ref=self.full.at[rows],
            dst_ref=self.full.at[rows],
            send_sem=self.row_send.at[d, c, k - 1],
            recv_sem=self.row_recv.at[d, c, k - 1],
            device_id=self.toward(d, away),
            device_id_type=MESH,
        )

    def stage(self, c, s):
        n, z = self.n, self.z
        if s < n:
            for d in range(2):
                q = self.flow(d)
                rows = self.place(c, z + n - s if d == 0 else z - n + s)

                @pl.when(q == 0)
                def first():
                    self.sum_copy(d, c, s, self.part.at[rows]).start()

                if s > 1:

                    @pl.when((q >= 1) & (q < s))
                    def later():
                        self.sum_arrive(d, c, s - 1)
                        held = self.landing.at[d, c, s - 2]
                        held[...] = (
                            self.part[rows].astype(jnp.float32) + held[...].astype(jnp.float32)
                        ).astype(low)
                        self.sum_copy(d, c, s, held).start()

        elif s == n:
            rows = self.place(c, z)
            self.total[...] = self.part[rows].astype(jnp.float32)
            for d in range(2):

                @pl.when(self.flow(d) >= 1)
                def ended():
                    self.sum_arrive(d, c, n - 1)
                    self.total[...] += self.landing[d, c, n - 2].astype(jnp.float32)

            self.full[rows] = self.finish(c, self.total[...]).astype(low)
            for d in range(2):

                @pl.when(self.flow(d) < n - 1)
                def spread():
                    self.row_copy(d, c, 1).start()

        else:
            k = s - n + 1
            for d in range(2):
                q = self.flow(d)

                @pl.when(q >= k - 1)
                def arrived():
                    self.row_copy(d, c, k - 1, True).wait_recv()

                if k < n:

                    @pl.when((q >= k - 1) & (q < n - 1))
                    def onward():
                        self.row_copy(d, c, k).start()

    def drain(self):
        n = self.n
        for c in range(self.chunks):
            for d in range(2):
                q = self.flow(d)
                for k in range(1, n):

                    @pl.when(q < k)
                    def sum_sent():
                        self.sum_copy(d, c, k, self.landing.at[d, c, k - 1]).wait_send()

                    @pl.when((q >= k - 1) & (q < n - 1))
                    def row_sent():
                        self.row_copy(d, c, k).wait_send()


def peers(axes):
    found = []
    for axis in axes:
        bit = 1
        while bit < lax.axis_size(axis):
            me = lax.axis_index(axis)
            found.append({axis: me + bit * (1 - 2 * ((me // bit) % 2))})
            bit *= 2
    return found


def greet(n, others):
    z = lax.axis_index("tp")
    barrier = pltpu.get_barrier_semaphore()

    @pl.when(z > 0)
    def to_lower():
        pl.semaphore_signal(barrier, inc=1, device_id={"tp": z - 1}, device_id_type=MESH)

    @pl.when(z < n - 1)
    def to_upper():
        pl.semaphore_signal(barrier, inc=1, device_id={"tp": z + 1}, device_id_type=MESH)

    for other in others:
        pl.semaphore_signal(barrier, inc=1, device_id=other, device_id_type=MESH)

    @pl.when((z > 0) & (z < n - 1))
    def from_both():
        pl.semaphore_wait(barrier, 2 + len(others))

    @pl.when((z == 0) | (z == n - 1))
    def from_one():
        pl.semaphore_wait(barrier, 1 + len(others))


def line_scratch(n, chunks, rows, width):
    own = rows // chunks // n
    return [
        vmem((rows, width), low),
        vmem((2, chunks, n - 1, own, width), low),
        vmem((own, width), jnp.float32),
    ] + [pltpu.SemaphoreType.DMA((2, chunks, n - 1))] * 4


class Exchange:
    def __init__(self, whole, start, arrived, send_sem, recv_sem):
        self.whole, self.held, self.arrived = whole, start, arrived
        self.send_sem, self.recv_sem = send_sem, recv_sem
        self.inner = len(peers(("ctx", "fsdp")))
        self.peers = peers(("ctx", "fsdp", "tp"))

    def copy(self, i):
        columns = slice(None) if i < self.inner else slice(0, self.whole)
        return pltpu.make_async_remote_copy(
            src_ref=self.held.at[i, :, columns],
            dst_ref=self.arrived.at[i, :, columns],
            send_sem=self.send_sem.at[i],
            recv_sem=self.recv_sem.at[i],
            device_id=self.peers[i],
            device_id_type=MESH,
        )

    def step(self, i):
        if i > 0:
            self.copy(i - 1).wait_recv()
            if i - 1 < self.inner:
                self.held[i] = self.held[i - 1] + self.arrived[i - 1]
            else:
                self.held[i] = self.held[i - 1]
                self.held[i, :, : self.whole] += self.arrived[i - 1, :, : self.whole]
        if i < len(self.peers):
            self.copy(i).start()

    def drain(self):
        for i in range(len(self.peers)):
            self.copy(i).wait_send()


def sum_kernel(n, chunks, epilogue, counts, with_product, with_vectors, plan, *refs):
    refs = list(refs)

    def taken(count):
        out = refs[:count]
        del refs[:count]
        return out

    operands = taken(2 if with_product else 1)
    extras, weights = taken(counts[0]), taken(2 * counts[2])
    (full,) = taken(1)
    outs, sums = taken(counts[1]), taken(counts[2])
    part = taken(1)[0] if with_product else operands[0]
    landing, total = taken(2)
    sems = taken(4)
    moves = [
        Halving(weights[2 * i], weights[2 * i + 1], sums[i], taken(8)) for i in range(counts[2])
    ]
    rows, width = full.shape
    chunk_rows = rows // chunks
    block = max(chunk_rows, min(rows, 256))
    per_block = block // chunk_rows
    greet(n, peers(("ctx", "fsdp", "tp") if with_vectors else ("ctx", "fsdp")))
    finish = epilogue(chunk_rows // n, extras, outs)
    line = Line(n, chunks, part, full, landing, total, sems, finish)

    def multiply(b):
        if not with_product:
            return
        own = slice(b * block, (b + 1) * block)

        @pl.loop(0, width // 256)
        def one(i):
            columns = pl.ds(pl.multiple_of(i * 256, 256), 256)
            part[own, columns] = contract_cols(operands[0][own, :], operands[1][columns, :]).astype(
                low
            )

    for move in moves:
        move.start()
    multiply(0)
    ended = chunks - 1 + n
    vectors = None
    for t in range(1, chunks + 2 * n - 1):
        for c in range(chunks):
            if 0 < t - c < 2 * n:
                line.stage(c, t - c)
        if t % per_block == 0 and t < chunks:
            multiply(t // per_block)
        for i, move in enumerate(moves):
            if t == plan[i][0]:
                move.core_step()
            if t == plan[i][1]:
                move.middle_step()
        if with_vectors and t == ended:
            held, arrived, send_sem, recv_sem = refs
            vectors = Exchange(width, held, arrived, send_sem, recv_sem)
            held[0] = extras[-1][...]
            held[0, 0:2, :width] = outs[0][0:2]
        if vectors is not None and t - ended <= len(vectors.peers):
            vectors.step(t - ended)
            done = t - ended
    if vectors is not None:
        for i in range(done + 1, len(vectors.peers) + 1):
            vectors.step(i)
        outs[-1][...] = vectors.held[len(vectors.peers)]
        vectors.drain()
    for move in moves:
        move.last_step()
    for move in moves:
        move.drain()
    line.drain()


def tp_sum(
    n, chunks, epilogue, collective, operands, extras, out_shapes, weights, plan, vectors=None
):
    rows = operands[0].shape[0]
    with_product = len(operands) == 2
    width = operands[-1].shape[0] if with_product else operands[0].shape[1]
    outs = list(out_shapes)
    scratch = line_scratch(n, chunks, rows, width)
    if not with_product:
        scratch = scratch[1:]
    count = lax.axis_size("fsdp")
    sums = []
    for given, _ in weights:
        own = jax.ShapeDtypeStruct((given.shape[0] // (2 * count), given.shape[1]), low)
        sums.append(own)
        scratch += halving_scratch(count, *own.shape)
    if vectors is not None:
        extras = (*extras, vectors)
        outs.append(jax.ShapeDtypeStruct(vectors.shape, jnp.float32))
        steps = len(peers(("ctx", "fsdp", "tp")))
        scratch += [
            vmem((steps + 1, *vectors.shape), jnp.float32),
            vmem((steps, *vectors.shape), jnp.float32),
            pltpu.SemaphoreType.DMA((steps,)),
            pltpu.SemaphoreType.DMA((steps,)),
        ]
    counts = (len(extras), len(outs), len(weights))
    return fused_call(
        functools.partial(
            sum_kernel, n, chunks, epilogue, counts, with_product, vectors is not None, plan
        ),
        collective,
        (*operands, *extras, *[ref for pair in weights for ref in pair]),
        [jax.ShapeDtypeStruct((rows, width), low)] + outs + sums,
        scratch,
        12 * rows * width * 512,
        2 * len(weights),
    )


def middle_epilogue(own, extras, outs):
    stream, bias, gain, shift = extras
    (middle,) = outs

    def finish(c, total):
        rows = slice(c * own, (c + 1) * own)
        value = stream[rows].astype(jnp.float32) + total + bias[...]
        middle[rows] = value
        return normalize(value)[0] * gain[...] + shift[...]

    return finish


def output_epilogue(own, extras, outs):
    middle, bias = extras

    def finish(c, total):
        return middle[c * own : (c + 1) * own] + total + bias[...]

    return finish


def attn_epilogue(own, extras, outs):
    middle, cotangent, gain = extras[:3]
    grad_middle, sums = outs[:2]
    sums[...] = jnp.zeros_like(sums)

    def finish(c, total):
        rows = slice(c * own, (c + 1) * own)
        normed, inverse = normalize(middle[rows])
        value = cotangent[rows].astype(jnp.float32) + norm_back(total, normed, inverse, gain[...])
        grad_middle[rows] = value
        sums[0:1] += jnp.sum(total * normed, axis=0, keepdims=True)
        sums[1:2] += jnp.sum(total, axis=0, keepdims=True)
        sums[2:3] += jnp.sum(value.astype(low).astype(jnp.float32), axis=0, keepdims=True)
        return value

    return finish


def input_epilogue(own, extras, outs):
    stream, grad_middle, gain = extras[:3]
    sums = outs[0]
    sums[...] = jnp.zeros_like(sums)

    def finish(c, total):
        rows = slice(c * own, (c + 1) * own)
        normed, inverse = normalize(stream[rows].astype(jnp.float32))
        sums[0:1] += jnp.sum(total * normed, axis=0, keepdims=True)
        sums[1:2] += jnp.sum(total, axis=0, keepdims=True)
        return grad_middle[rows] + norm_back(total, normed, inverse, gain[...])

    return finish


def flipped(index, bits):
    out, bit = index, 1
    while bit <= bits:
        if bits & bit:
            out = out + bit * (1 - 2 * ((index // bit) % 2))
        bit *= 2
    return out


class Halving:
    def __init__(self, given, kept, out, refs):
        self.given, self.kept, self.out = given, kept, out
        self.mine, self.held, self.landing = refs[:3]
        self.own_sem, self.core_send, self.core_recv, self.half_send, self.half_recv = refs[3:]
        self.count = lax.axis_size("fsdp")
        self.rows = out.shape[0]
        self.half = out.shape[1] // 2
        _, self.place, _, self.beside, self.across = ctx_place()
        self.turn = lax.axis_index("fsdp")

    def shards(self):
        return [(far, over) for far in range(self.count - 1, -1, -1) for over in (1, 0)]

    def shard(self, far, over):
        p = flipped(self.turn, far) * 2 + flipped(self.place, over)
        return pl.ds(pl.multiple_of(p * self.rows, self.rows), self.rows)

    def core_copy(self, far, over):
        i = 2 * far + over
        return ctx_copy(
            self.given.at[self.shard(far, over)],
            self.held.at[i],
            self.core_send.at[i],
            self.core_recv.at[i],
            self.beside,
        )

    def own_copy(self, far, over):
        i = 2 * far + over
        return pltpu.make_async_copy(
            self.kept.at[self.shard(far, over)], self.mine.at[i], self.own_sem.at[i]
        )

    def half_copy(self, way, bit, far, over):
        n = self.count
        if way == 0:
            i = n + far - 1 if bit else far
        else:
            i = 2 * n - 1 + 2 * (far - 1) + over if bit else 4 * n - 3
        device = {"fsdp": flipped(self.turn, bit)} if bit else self.across
        columns = slice(way * self.half, (way + 1) * self.half)
        copy = ctx_copy(
            self.held.at[2 * far + over, :, columns],
            self.landing.at[i],
            self.half_send.at[i],
            self.half_recv.at[i],
            device,
        )
        return copy, i, columns

    def start(self):
        for far, over in self.shards():
            self.core_copy(far, over).start()
        for far, over in self.shards():
            self.own_copy(far, over).start()

    def send(self, way, bit, far, over):
        self.half_copy(way, bit, far, over)[0].start()

    def take(self, way, bit, far, over):
        copy, i, columns = self.half_copy(way, bit, far, over)
        copy.wait_recv()
        far, over = (far - bit, over) if bit else (far, 0)
        k = 2 * far + over
        self.held[k, :, columns] = add_low(self.held[k, :, columns], self.landing[i])
        return far

    def core_step(self):
        top = self.count // 2
        for far, over in self.shards():
            k = 2 * far + over
            self.own_copy(far, over).wait()
            self.core_copy(far, over).wait_recv()
            self.held[k] = add_low(self.held[k], self.mine[k])
            if over:
                self.send(0, 0, far, over)
            if far >= top:
                self.send(1, top, far, over)

    def middle_step(self):
        top = self.count // 2
        for far in range(self.count - 1, -1, -1):
            self.take(0, 0, far, 1)
            if far >= top:
                self.send(0, top, far, 0)
        bit = top
        while bit > 1:
            for far in range(2 * bit - 1, bit - 1, -1):
                left = self.take(0, bit, far, 0)
                if left >= bit // 2:
                    self.send(0, bit // 2, left, 0)
            bit //= 2
        bit = top
        while bit:
            for far in range(2 * bit - 1, bit - 1, -1):
                for over in (1, 0):
                    left = self.take(1, bit, far, over)
                    if bit > 1 and left >= bit // 2:
                        self.send(1, bit // 2, left, over)
                    if bit == 1 and over:
                        self.send(1, 0, 0, 1)
            bit //= 2

    def last_step(self):
        self.take(0, 1, 1, 0)
        self.take(1, 0, 0, 1)
        self.out[...] = self.held[0]

    def drain(self):
        for far in range(self.count):
            for over in range(2):
                self.core_copy(far, over).wait_send()
            self.half_copy(0, 0, far, 1)[0].wait_send()
            if far:
                bit = 1
                while 2 * bit <= far:
                    bit *= 2
                self.half_copy(0, bit, far, 0)[0].wait_send()
                for over in range(2):
                    self.half_copy(1, bit, far, over)[0].wait_send()
        self.half_copy(1, 0, 0, 1)[0].wait_send()


def add_low(left, right):
    return (left.astype(jnp.float32) + right.astype(jnp.float32)).astype(low)


def halving_scratch(count, rows, width):
    sem = pltpu.SemaphoreType.DMA
    return (
        [vmem((2 * count, rows, width), low)] * 2
        + [vmem((4 * count - 2, rows, width // 2), low)]
        + [sem((2 * count,))] * 3
        + [sem((4 * count - 2,))] * 2
    )


def split_store(value, tile, rows, given, kept, columns):
    side = lax.axis_index("ctx") % 2
    height = value.shape[0]
    step = min(rows, height)
    for k in range(height // step):
        start = tile * height + k * step
        shard = start // rows
        place = shard // 2 * rows + start % rows
        place = pl.ds(place if isinstance(place, int) else pl.multiple_of(place, step), step)
        piece = value[k * step : (k + 1) * step].astype(low)

        @pl.when((shard + side) % 2 == 0)
        def keep():
            kept[place, columns] = piece

        @pl.when((shard + side) % 2 == 1)
        def give():
            given[place, columns] = piece


def hidden_kernel(shard_rows, *refs):
    (
        act,
        grad_branch,
        grad_turned,
        up,
        down,
        bias,
        down_given,
        down_kept,
        up_given,
        up_kept,
        branch_part,
        back_part,
        bias_sum,
        act_turned,
        branch_total,
        back_total,
    ) = refs
    i = pl.program_id(0)
    width = act.shape[1]

    @pl.when(i == 0)
    def begin():
        @pl.loop(0, width // 256)
        def turn(k):
            place = pl.ds(pl.multiple_of(k * 256, 256), 256)
            act_turned[place, :] = act[:, place].T

    hidden = jnp.dot(act[...], up[...], preferred_element_type=jnp.float32) + bias[...]
    squared = hidden * hidden
    bend = jnp.tanh(0.7978845608028654 * (hidden + 0.044715 * squared * hidden))
    gelu_low = (0.5 * hidden * (1.0 + bend)).astype(low)
    slope = 0.5 * (1.0 + bend) + 0.5 * hidden * (1.0 - bend * bend) * 0.7978845608028654 * (
        1.0 + 3.0 * 0.044715 * squared
    )
    incoming = jnp.dot(grad_branch[...], down[...], preferred_element_type=jnp.float32)
    grad_up_proj = (incoming * slope).astype(low)
    bias_sum[...] = jnp.broadcast_to(
        jnp.sum(grad_up_proj.astype(jnp.float32), axis=0, keepdims=True), bias_sum.shape
    )
    for k in range(width // 256):
        place = slice(k * 256, (k + 1) * 256)
        split_store(
            jnp.dot(grad_turned[place, :], gelu_low, preferred_element_type=jnp.float32),
            k,
            shard_rows,
            down_given,
            down_kept,
            slice(None),
        )
        split_store(
            jnp.dot(act_turned[place, :], grad_up_proj, preferred_element_type=jnp.float32),
            k,
            shard_rows,
            up_given,
            up_kept,
            slice(None),
        )
    branch = contract_cols(gelu_low, down[...])
    back = contract_cols(grad_up_proj, up[...])

    @pl.when(i == 0)
    def first():
        branch_total[...] = branch
        back_total[...] = back

    @pl.when(i > 0)
    def later():
        branch_total[...] += branch
        back_total[...] += back

    @pl.when(i == pl.num_programs(0) - 1)
    def end():
        branch_part[...] = branch_total[...].astype(low)
        back_part[...] = back_total[...].astype(low)


def hidden_layer(shard_rows, act, grad_branch, up, down, bias):
    rows, width = act.shape
    hidden = up.shape[1]
    tile = 256

    def whole(shape):
        return pl.BlockSpec(shape, lambda i: (0, 0))

    def tiles(height):
        return pl.BlockSpec((height, tile), lambda i: (0, i))

    return pl.pallas_call(
        functools.partial(hidden_kernel, shard_rows),
        grid=(hidden // tile,),
        out_shape=[jax.ShapeDtypeStruct((width // 2, hidden), low)] * 4
        + [jax.ShapeDtypeStruct((rows, width), low)] * 2
        + [jax.ShapeDtypeStruct((8, hidden), jnp.float32)],
        in_specs=[
            whole((rows, width)),
            whole((rows, width)),
            whole((width, rows)),
            tiles(width),
            tiles(width),
            tiles(1),
        ],
        out_specs=[tiles(width // 2)] * 4 + [whole((rows, width))] * 2 + [tiles(8)],
        scratch_shapes=[
            vmem((width, rows), low),
            vmem((rows, width), jnp.float32),
            vmem((rows, width), jnp.float32),
        ],
        compiler_params=pltpu.CompilerParams(vmem_limit_bytes=60 * 1024 * 1024),
        cost_estimate=pl.CostEstimate(
            flops=12 * rows * width * hidden, bytes_accessed=100_000_000, transcendentals=0
        ),
    )(act, grad_branch, grad_branch.T, up, down, bias)


def ctx_place():
    me = lax.axis_index("ctx")
    half, side = me // 2, me % 2
    return me, half, side, {"ctx": me + 1 - 2 * side}, {"ctx": me + 2 - 4 * half}


def ctx_copy(source, target, send, recv, device):
    return pltpu.make_async_remote_copy(
        src_ref=source,
        dst_ref=target,
        send_sem=send,
        recv_sem=recv,
        device_id=device,
        device_id_type=MESH,
    )


class Spread:
    def __init__(self, block, own, pairs, send, recv):
        self.block, self.own, self.pairs, self.send, self.recv = block, own, pairs, send, recv
        self.me, self.half, self.side, self.beside, self.across = ctx_place()

    def rows(self, s, b):
        start = (s * lax.axis_size("ctx") + b) * self.block
        return pl.ds(pl.multiple_of(start, self.block), self.block)

    def copy(self, kind, s, b, own, device):
        target = self.pairs.at[self.rows(s, b)]
        wide = self.pairs.shape[1]
        source = self.own.at[s * self.block : (s + 1) * self.block, wide // 2 :] if own else target
        return ctx_copy(source, target, self.send.at[kind, s], self.recv.at[kind, s], device)

    def start(self, s):
        rows = slice(s * self.block, (s + 1) * self.block)

        @pl.when(self.half == 0)
        def over():
            self.copy(0, s, self.me, True, self.across).start()

        @pl.when(self.side == 0)
        def aside():
            self.copy(1, s, self.me, True, self.beside).start()

        self.pairs[self.rows(s, self.me)] = self.own[rows, self.pairs.shape[1] // 2 :]

    def forward(self, s):
        @pl.when(self.half == 1)
        def onward():
            self.copy(0, s, self.me - 2, False, self.across).wait_recv()
            self.copy(2, s, self.me - 2, False, self.beside).start()

    def arrive(self, s):
        @pl.when(self.half == 1)
        def second():
            self.copy(2, s, 1 - self.side, False, self.beside).wait_recv()

        @pl.when(self.side == 1)
        def first():
            self.copy(1, s, self.me - 1, False, self.beside).wait_recv()

    def drain_own(self, s):
        @pl.when(self.half == 0)
        def over():
            self.copy(0, s, self.me, True, self.across).wait_send()

        @pl.when(self.side == 0)
        def aside():
            self.copy(1, s, self.me, True, self.beside).wait_send()

    def drain(self, s):
        @pl.when(self.half == 1)
        def onward():
            self.copy(2, s, self.me - 2, False, self.beside).wait_send()


class Collect:
    def __init__(self, block, parts, beside_in, across_in, send, recv):
        self.block, self.parts = block, parts
        self.beside_in, self.across_in, self.send, self.recv = beside_in, across_in, send, recv
        self.me, self.half, self.side, self.beside, self.across = ctx_place()

    def rows(self, s, b):
        start = (s * lax.axis_size("ctx") + b) * self.block
        return pl.ds(pl.multiple_of(start, self.block), self.block)

    def aside(self, s, k, away=False):
        b = 2 * k + (self.side if away else 1 - self.side)
        return ctx_copy(
            self.parts.at[self.rows(s, b)],
            self.beside_in.at[k, s],
            self.send.at[k, s],
            self.recv.at[k, s],
            self.beside,
        )

    def over(self, s):
        return ctx_copy(
            self.parts.at[self.rows(s, self.side)],
            self.across_in.at[s],
            self.send.at[2, s],
            self.recv.at[2, s],
            self.across,
        )

    def start(self, s):
        for k in range(2):

            @pl.when(2 * k + 1 - self.side < self.me)
            def give():
                self.aside(s, k).start()

    def forward(self, s):
        for k in range(2):

            @pl.when(2 * k + self.side < self.me + 1 - 2 * self.side)
            def take():
                self.aside(s, k, True).wait_recv()

        @pl.when(self.half == 1)
        def onward():
            held = self.parts.at[self.rows(s, self.side)]
            held[...] = (
                held[...].astype(jnp.float32) + self.beside_in[0, s].astype(jnp.float32)
            ).astype(low)
            self.over(s).start()

    def finish(self, s, target):
        target[...] = self.parts[self.rows(s, self.me)]
        for k in range(2):

            @pl.when((self.side == 0) & (self.half == k))
            def near():
                target[...] = (
                    target[...].astype(jnp.float32) + self.beside_in[k, s].astype(jnp.float32)
                ).astype(low)

        @pl.when(self.half == 0)
        def far():
            self.over(s).wait_recv()
            target[...] = (
                target[...].astype(jnp.float32) + self.across_in[s].astype(jnp.float32)
            ).astype(low)

    def drain(self, s):
        for k in range(2):

            @pl.when(2 * k + 1 - self.side < self.me)
            def gave():
                self.aside(s, k).wait_send()

        @pl.when(self.half == 1)
        def sent():
            self.over(s).wait_send()


def offsets(base):
    shape = base.shape
    base[...] = (
        lax.broadcasted_iota(jnp.int32, shape, 0) - lax.broadcasted_iota(jnp.int32, shape, 1)
    ).astype(jnp.float32)


def head_scores(query, key, slope, base, j):
    far = base[...] + (j * base.shape[0]).astype(jnp.float32)
    return contract_cols(query, key) * HD ** (-0.5) - slope * jnp.abs(far)


def head_columns(h, shift=0):
    return pl.ds(pl.multiple_of(shift + h * HD, HD), HD)


def forward_heads(s, first, last, block, projected, pairs, slopes, base, context, log_total):
    me = lax.axis_index("ctx")
    count = lax.axis_size("ctx")
    own = slice(s * block, (s + 1) * block)
    wide = pairs.shape[1] // 2

    @pl.loop(first, last)
    def head(h):
        query = projected[own, head_columns(h)]

        def step(j, carry):
            peak, weight, total = carry
            rows = pl.ds(pl.multiple_of((s * count + me - j) * block, block), block)
            scores = head_scores(query, pairs[rows, head_columns(h)], slopes[h, 0:1], base, j)
            higher = jnp.maximum(peak, jnp.max(scores, axis=-1, keepdims=True))
            shrink = jnp.exp(peak - higher)
            exponent = jnp.exp(scores - higher)
            weight = weight * shrink + jnp.sum(exponent, axis=-1, keepdims=True)
            total = total * shrink + jnp.dot(
                exponent.astype(low),
                pairs[rows, head_columns(h, wide)],
                preferred_element_type=jnp.float32,
            )
            return higher, weight, total

        peak, weight, total = lax.fori_loop(
            0,
            me + 1,
            step,
            (
                jnp.full((block, 1), -1e30, jnp.float32),
                jnp.zeros((block, 1), jnp.float32),
                jnp.zeros((block, HD), jnp.float32),
            ),
        )
        context[own, head_columns(h)] = (total / weight).astype(low)
        log_total[own, head_columns(h)] = jnp.broadcast_to(peak + jnp.log(weight), (block, HD))


def backward_heads(
    s, first, last, block, projected, pairs, slopes, base, context, log_total, grad, parts, out
):
    me = lax.axis_index("ctx")
    count = lax.axis_size("ctx")
    own = slice(s * block, (s + 1) * block)
    wide = pairs.shape[1] // 2

    @pl.loop(first, last)
    def head(h):
        query = projected[own, head_columns(h)]
        incoming = grad[own, head_columns(h)]
        level = log_total[own, head_columns(h)][:, 0:1]
        mean = jnp.sum(
            incoming.astype(jnp.float32) * context[own, head_columns(h)].astype(jnp.float32),
            axis=-1,
            keepdims=True,
        )

        def step(j, total):
            rows = pl.ds(pl.multiple_of((s * count + me - j) * block, block), block)
            key = pairs[rows, head_columns(h)]
            probs = jnp.exp(head_scores(query, key, slopes[h, 0:1], base, j) - level)
            grad_probs = contract_cols(incoming, pairs[rows, head_columns(h, wide)])
            grad_scores = (probs * (grad_probs - mean)).astype(low)
            parts[rows, head_columns(h)] = (
                contract_rows(grad_scores, query) * HD ** (-0.5)
            ).astype(low)
            parts[rows, head_columns(h, wide)] = contract_rows(probs.astype(low), incoming).astype(
                low
            )
            return total + jnp.dot(grad_scores, key, preferred_element_type=jnp.float32)

        total = lax.fori_loop(0, me + 1, step, jnp.zeros((block, HD), jnp.float32))
        out[own, head_columns(h)] = (total * HD ** (-0.5)).astype(low)


def attend_kernel(n, chunks, tile, *refs):
    (
        projected,
        slopes,
        out_weight,
        stream,
        bias,
        gain,
        shift,
        full,
        middle,
        context,
        log_total,
        pairs,
        part,
        landing,
        total,
        *rest,
    ) = refs
    sems, (base, send, recv) = rest[:4], rest[4:]
    rows, width = full.shape
    seqs = chunks // 2
    block = rows // seqs
    heads = context.shape[1] // HD
    pace = heads // 2
    _, _, _, beside, across = ctx_place()
    greet(n, [beside, across])
    finish = middle_epilogue(rows // chunks // n, (stream, bias, gain, shift), (middle,))
    line = Line(n, chunks, part, full, landing, total, sems, finish)
    spread = Spread(block, projected, pairs, send, recv)
    spread.start(0)
    offsets(base)

    def attend(s, first, last):
        if first == 0:
            spread.forward(s)
            if s + 1 < seqs:
                spread.drain_own(s)
                spread.start(s + 1)
            spread.arrive(s)
        forward_heads(
            s, first, last, block, projected, pairs, slopes, base, context, log_total
        )

    def multiply(s):
        own = slice(s * block, (s + 1) * block)

        @pl.loop(0, width // tile)
        def one(i):
            columns = pl.ds(pl.multiple_of(i * tile, tile), tile)
            part[own, columns] = contract_cols(context[own, :], out_weight[columns, :]).astype(low)

    attend(0, 0, heads)
    multiply(0)
    for t in range(1, chunks + 2 * n - 1):
        for c in range(chunks):
            if 0 < t - c < 2 * n:
                line.stage(c, t - c)
        s = (t + 1) // 2
        if s < seqs:
            attend(s, 0 if t % 2 else pace, pace if t % 2 else heads)
            if t % 2 == 0:
                multiply(s)
    spread.drain_own(seqs - 1)
    for s in range(seqs):
        spread.drain(s)
    line.drain()


def backward_kernel(n, chunks, shard_rows, *refs):
    (
        part,
        middle,
        bias,
        grad_attn,
        out_weight,
        projected,
        pairs,
        context,
        log_total,
        slopes,
        act,
        full,
        grad_projected,
        given,
        kept,
        landing,
        total,
        *rest,
    ) = refs
    sems, (base, grad_context, parts, beside_in, across_in, send, recv) = rest[:4], rest[4:]
    rows, width = full.shape
    seqs = chunks // 2
    block = rows // seqs
    heads = context.shape[1] // HD
    wide = context.shape[1]
    pace = heads // 2
    _, _, _, beside, across = ctx_place()
    greet(n, [beside, across])
    finish = output_epilogue(rows // chunks // n, (middle, bias), ())
    line = Line(n, chunks, part, full, landing, total, sems, finish)
    collect = Collect(block, parts, beside_in, across_in, send, recv)
    offsets(base)

    def backward(s, first, last):
        own = slice(s * block, (s + 1) * block)
        if first == 0:
            grad_context[own, :] = jnp.dot(
                grad_attn[own, :], out_weight[...], preferred_element_type=jnp.float32
            ).astype(low)
        backward_heads(
            s,
            first,
            last,
            block,
            projected,
            pairs,
            slopes,
            base,
            context,
            log_total,
            grad_context,
            parts,
            grad_projected,
        )
        if last == heads:
            collect.start(s)

    def finished(s):
        collect.finish(s, grad_projected.at[s * block : (s + 1) * block, wide:])

    def features(source, right, columns, first, last):
        @pl.loop(first, last)
        def one(i):
            place = pl.ds(pl.multiple_of(i * 256, 256), 256)
            value = contract_rows(source[:, place], right[...])
            split_store(value, i, shard_rows, given, kept, columns)

    attn_columns = slice(0, 3 * wide)
    out_columns = slice(3 * wide, 4 * wide)

    tiles = width // 256
    tasks = []
    for s in range(seqs):
        tasks.append([functools.partial(backward, s, 0, pace)])
        tasks.append([functools.partial(backward, s, pace, heads)])
    tasks += [[] for _ in range(chunks + 2 * n - 2 - len(tasks))]
    for s in range(seqs):
        tasks[2 * s + 2].append(functools.partial(collect.forward, s))
    after = 2 * seqs + 1
    tasks[after].append(functools.partial(features, grad_attn, context, out_columns, 0, tiles))
    for s in range(seqs):
        tasks[after + s].append(functools.partial(finished, s))
    left = len(tasks) - after - seqs
    for i in range(left):
        tasks[after + seqs + i].append(
            functools.partial(
                features,
                act,
                grad_projected,
                attn_columns,
                tiles * i // left,
                tiles * (i + 1) // left,
            )
        )
    for t in range(1, chunks + 2 * n - 1):
        for c in range(chunks):
            if 0 < t - c < 2 * n:
                line.stage(c, t - c)
        for task in tasks[t - 1]:
            task()
    for s in range(seqs):
        collect.drain(s)
    line.drain()


def fused_call(body, collective, operands, outs, scratch, flops, loose=0):
    whole = pl.BlockSpec(memory_space=vmem)
    specs = [whole] * (len(operands) - loose) + [pl.BlockSpec(memory_space=pl.ANY)] * loose
    return pl.pallas_call(
        body,
        out_shape=outs,
        in_specs=specs,
        out_specs=[whole] * len(outs),
        scratch_shapes=scratch,
        compiler_params=pltpu.CompilerParams(
            collective_id=collective,
            has_side_effects=True,
            vmem_limit_bytes=60 * 1024 * 1024,
        ),
        cost_estimate=pl.CostEstimate(flops=flops, bytes_accessed=200_000_000, transcendentals=0),
    )(*operands)


def local(
    inputs,
    cotangent,
    master_qkv,
    qkv_moment1,
    qkv_moment2,
    master_out,
    out_moment1,
    out_moment2,
    master_up,
    up_moment1,
    up_moment2,
    master_down,
    down_moment1,
    down_moment2,
    norm_gains,
    gain_moment1,
    gain_moment2,
    shared_biases,
    shared_moment1,
    shared_moment2,
    split_biases,
    split_moment1,
    split_moment2,
):
    seq_count, block_len, model_width = inputs.shape
    row_count = seq_count * block_len
    width_part = master_qkv.shape[2]
    hidden_rows = master_up.shape[1]
    local_heads = width_part // HD
    tp_count = lax.axis_size("tp")
    chunks = 2 * seq_count
    own_rows = row_count // chunks // tp_count

    def own_part(values):
        blocks = values.reshape(chunks, tp_count * own_rows, model_width)
        taken = lax.dynamic_slice_in_dim(blocks, lax.axis_index("tp") * own_rows, own_rows, axis=1)
        return taken.reshape(-1, model_width)

    own_shape = jax.ShapeDtypeStruct((row_count // tp_count, model_width), jnp.float32)
    sums_shape = jax.ShapeDtypeStruct((8, model_width), jnp.float32)
    gains = [norm_gains[i : i + 1] for i in range(2)]
    shared = [shared_biases[i : i + 1] for i in range(4)]
    inputs_own = own_part(inputs)
    cotangent_own = own_part(cotangent)

    def flat(master):
        return master.astype(low).reshape(master.shape[0], -1)

    def gather_rows(rows):
        return lax.all_gather(rows, ("fsdp", "ctx"), axis=0, tiled=True)

    attn_flat = gather_rows(jnp.concatenate([flat(master_qkv), flat(master_out)], axis=1))
    qkv_flat, out_flat = attn_flat[:, : 3 * width_part], attn_flat[:, 3 * width_part :]
    up_flat = gather_rows(flat(master_up))
    down_flat = gather_rows(flat(master_down))
    head_ids = (lax.axis_index("tp") * local_heads + jnp.arange(local_heads)).astype(jnp.float32)
    slopes = jnp.power(2.0, -8.0 * (head_ids + 1.0) / (local_heads * lax.axis_size("tp")))
    slopes = jnp.broadcast_to(slopes[:, None, None], (local_heads, 8, block_len))
    stream = inputs.astype(jnp.float32).reshape(row_count, model_width)
    normed_one, inverse_one = normalize(stream)
    act_one = (normed_one * norm_gains[0] + shared_biases[0]).astype(jnp.bfloat16)
    projected = jnp.dot(act_one, qkv_flat, preferred_element_type=jnp.float32)
    projected_bias = jnp.concatenate(
        [split_biases[0], jnp.zeros((width_part,), jnp.float32), split_biases[1]]
    )
    projected = (projected + projected_bias).astype(low)
    sems = line_scratch(tp_count, chunks, row_count, model_width)
    pair_rows = row_count * lax.axis_size("ctx")
    square = vmem((block_len, block_len), jnp.float32)
    pair_sems = [pltpu.SemaphoreType.DMA((3, seq_count))] * 2
    act_two, middle, context, log_total, pairs = fused_call(
        functools.partial(attend_kernel, tp_count, chunks, 256),
        0,
        (projected, slopes, out_flat, inputs_own, shared[2], gains[1], shared[1]),
        [
            jax.ShapeDtypeStruct((row_count, model_width), low),
            own_shape,
            jax.ShapeDtypeStruct((row_count, width_part), low),
            jax.ShapeDtypeStruct((row_count, width_part), jnp.float32),
            jax.ShapeDtypeStruct((pair_rows, 2 * width_part), low),
        ],
        sems + [square] + pair_sems,
        4 * row_count * model_width * width_part,
    )
    down_given, down_kept, up_given, up_kept, branch_part, back_part, bias_sum = hidden_layer(
        master_qkv.shape[0],
        act_two,
        cotangent.reshape(row_count, model_width),
        up_flat,
        down_flat,
        split_biases[2:].reshape(1, -1),
    )
    grad_attn, grad_middle, sums_two, sum_down, sum_up = tp_sum(
        tp_count,
        chunks,
        attn_epilogue,
        2,
        (back_part,),
        (middle, cotangent_own, gains[1]),
        [own_shape, sums_shape],
        [(down_given, down_kept), (up_given, up_kept)],
        ((2, 7), (4, 11)),
    )
    pair_block = (block_len, 2 * width_part)
    output, grad_projected, attn_given, attn_kept = fused_call(
        functools.partial(backward_kernel, tp_count, chunks, master_qkv.shape[0]),
        1,
        (
            branch_part,
            middle,
            shared[3],
            grad_attn,
            out_flat,
            projected,
            pairs,
            context,
            log_total,
            slopes,
            act_one,
        ),
        [
            jax.ShapeDtypeStruct((row_count, model_width), low),
            jax.ShapeDtypeStruct((row_count, 3 * width_part), low),
            jax.ShapeDtypeStruct((model_width // 2, 4 * width_part), low),
            jax.ShapeDtypeStruct((model_width // 2, 4 * width_part), low),
        ],
        sems[1:]
        + [
            square,
            vmem((row_count, width_part), low),
            vmem((pair_rows, 2 * width_part), low),
            vmem((2, seq_count, *pair_block), low),
            vmem((seq_count, *pair_block), low),
        ]
        + pair_sems,
        12 * row_count * model_width * width_part,
    )
    output = output.reshape(seq_count, block_len, model_width)
    query_low = grad_projected[:, :width_part]
    value_low = grad_projected[:, 2 * width_part :]
    split_grads = jnp.concatenate(
        [
            jnp.sum(query_low, axis=0, dtype=jnp.float32)[None],
            jnp.sum(value_low, axis=0, dtype=jnp.float32)[None],
            bias_sum[0].reshape(hidden_rows, width_part),
        ],
        axis=0,
    )
    vectors = jnp.concatenate(
        [
            jnp.zeros((2, model_width), jnp.float32),
            sums_two[0:3],
            jnp.sum(cotangent_own, axis=0, dtype=jnp.float32)[None],
            jnp.zeros((2, model_width), jnp.float32),
        ]
    )
    vectors = jnp.concatenate([vectors, jnp.pad(split_grads, ((0, 2), (0, 0)))], axis=1)
    input_low, _, vector_sum, sum_attn = tp_sum(
        tp_count,
        chunks,
        input_epilogue,
        3,
        (grad_projected, qkv_flat),
        (inputs_own, grad_middle, gains[0]),
        [sums_shape],
        [(attn_given, attn_kept)],
        ((2, 8),),
        vectors,
    )
    input_grad = input_low.astype(jnp.float32).reshape(seq_count, block_len, model_width)

    sum_attn = sum_attn.astype(jnp.float32)
    sum_qkv = sum_attn[:, : 3 * width_part].reshape(master_qkv.shape)
    sum_out = sum_attn[:, 3 * width_part :]
    sum_up = sum_up.astype(jnp.float32).reshape(master_up.shape)
    sum_down = sum_down.astype(jnp.float32).reshape(master_down.shape)
    gain_sum = jnp.concatenate([vector_sum[0:1, :model_width], vector_sum[2:3, :model_width]])
    shared_sum = jnp.concatenate([vector_sum[1:2, :model_width], vector_sum[3:6, :model_width]])
    split_sum = vector_sum[: 2 + hidden_rows, model_width:]
    q_one, q_two, q_new = adam_update(
        master_qkv, qkv_moment1, qkv_moment2, sum_qkv, matrix_rate, True
    )
    o_one, o_two, o_new = adam_update(
        master_out, out_moment1, out_moment2, sum_out, matrix_rate, True
    )
    u_one, u_two, u_new = adam_update(master_up, up_moment1, up_moment2, sum_up, matrix_rate, True)
    d_one, d_two, d_new = adam_update(
        master_down, down_moment1, down_moment2, sum_down, matrix_rate, True
    )
    g_one, g_two, g_new = adam_update(
        norm_gains, gain_moment1, gain_moment2, gain_sum, vector_rate, False
    )
    s_one, s_two, s_new = adam_update(
        shared_biases, shared_moment1, shared_moment2, shared_sum, vector_rate, False
    )
    p_one, p_two, p_new = adam_update(
        split_biases, split_moment1, split_moment2, split_sum, vector_rate, False
    )
    return (
        output,
        input_grad,
        q_one,
        q_two,
        q_new,
        q_new.astype(jnp.bfloat16),
        o_one,
        o_two,
        o_new,
        o_new.astype(jnp.bfloat16),
        u_one,
        u_two,
        u_new,
        u_new.astype(jnp.bfloat16),
        d_one,
        d_two,
        d_new,
        d_new.astype(jnp.bfloat16),
        g_one,
        g_two,
        g_new,
        s_one,
        s_two,
        s_new,
        p_one,
        p_two,
        p_new,
    )


def solution(mesh):
    return jax.shard_map(
        local,
        mesh=mesh,
        in_specs=(
            P("fsdp", "ctx", None),
            P("fsdp", "ctx", None),
            P(("fsdp", "ctx"), None, "tp"),
            P(("fsdp", "ctx"), None, "tp"),
            P(("fsdp", "ctx"), None, "tp"),
            P(("fsdp", "ctx"), "tp"),
            P(("fsdp", "ctx"), "tp"),
            P(("fsdp", "ctx"), "tp"),
            P(("fsdp", "ctx"), None, "tp"),
            P(("fsdp", "ctx"), None, "tp"),
            P(("fsdp", "ctx"), None, "tp"),
            P(("fsdp", "ctx"), None, "tp"),
            P(("fsdp", "ctx"), None, "tp"),
            P(("fsdp", "ctx"), None, "tp"),
            P(),
            P(),
            P(),
            P(),
            P(),
            P(),
            P(None, "tp"),
            P(None, "tp"),
            P(None, "tp"),
        ),
        out_specs=(
            P("fsdp", "ctx", None),
            P("fsdp", "ctx", None),
            P(("fsdp", "ctx"), None, "tp"),
            P(("fsdp", "ctx"), None, "tp"),
            P(("fsdp", "ctx"), None, "tp"),
            P(("fsdp", "ctx"), None, "tp"),
            P(("fsdp", "ctx"), "tp"),
            P(("fsdp", "ctx"), "tp"),
            P(("fsdp", "ctx"), "tp"),
            P(("fsdp", "ctx"), "tp"),
            P(("fsdp", "ctx"), None, "tp"),
            P(("fsdp", "ctx"), None, "tp"),
            P(("fsdp", "ctx"), None, "tp"),
            P(("fsdp", "ctx"), None, "tp"),
            P(("fsdp", "ctx"), None, "tp"),
            P(("fsdp", "ctx"), None, "tp"),
            P(("fsdp", "ctx"), None, "tp"),
            P(("fsdp", "ctx"), None, "tp"),
            P(),
            P(),
            P(),
            P(),
            P(),
            P(),
            P(None, "tp"),
            P(None, "tp"),
            P(None, "tp"),
        ),
        check_vma=False,
    )
```

```python
import functools

import jax
import jax.numpy as jnp
from jax import lax
from jax.experimental import pallas as pl
from jax.experimental.pallas import tpu as pltpu
from jax.sharding import PartitionSpec as P

HD = 128
STEP = 10


norm_epsilon = 1e-05
matrix_rate = 0.04
vector_rate = 0.4
decay_weight = 0.1
decay_rate = 0.5
adam_epsilon = 1e-08
low = jnp.bfloat16


def normalize(values):
    center = jnp.mean(values, axis=-1, keepdims=True)
    shifted = values - center
    variance = jnp.mean(shifted * shifted, axis=-1, keepdims=True)
    inverse = lax.rsqrt(variance + norm_epsilon)
    return (shifted * inverse, inverse)


def norm_back(incoming, normed, inverse, gain):
    scaled = incoming * gain
    return inverse * (
        scaled
        - jnp.mean(scaled, axis=-1, keepdims=True)
        - normed * jnp.mean(scaled * normed, axis=-1, keepdims=True)
    )


def gelu_tanh(values):
    return (
        0.5
        * values
        * (1.0 + jnp.tanh(0.7978845608028654 * (values + 0.044715 * values * values * values)))
    )


def adam_update(master, moment_one, moment_two, gradient, rate, decayed):
    first = decay_rate * moment_one + (1.0 - decay_rate) * gradient
    second = decay_rate * moment_two + (1.0 - decay_rate) * gradient * gradient
    correction = 1.0 - decay_rate**STEP
    update = first / correction / (jnp.sqrt(second / correction) + adam_epsilon)
    if decayed:
        update = update + decay_weight * master
    return (first, second, master - rate * update)


def contract_rows(left, right):
    return lax.dot_general(
        left, right, (((0,), (0,)), ((), ())), preferred_element_type=jnp.float32
    )


def contract_cols(left, right):
    return lax.dot_general(
        left, right, (((1,), (1,)), ((), ())), preferred_element_type=jnp.float32
    )


MESH = pl.DeviceIdType.MESH
vmem = pltpu.VMEM


class Line:
    def __init__(self, n, chunks, part, full, landing, total, sems, finish):
        self.n, self.chunks = n, chunks
        self.part, self.full, self.landing, self.total = part, full, landing, total
        self.sum_send, self.sum_recv, self.row_send, self.row_recv = sems
        self.finish = finish
        self.z = lax.axis_index("tp")
        self.chunk_rows = full.shape[0] // chunks
        self.own = self.chunk_rows // n
        self.last = 2 * n - 1

    def place(self, c, j):
        return pl.ds(pl.multiple_of(c * self.chunk_rows + j * self.own, self.own), self.own)

    def flow(self, d):
        return self.z if d == 0 else self.n - 1 - self.z

    def toward(self, d, away):
        return {"tp": self.z + (1 if (d == 0) != away else -1)}

    def sum_copy(self, d, c, k, source, away=False):
        return pltpu.make_async_remote_copy(
            src_ref=source,
            dst_ref=self.landing.at[d, c, k - 1],
            send_sem=self.sum_send.at[d, c, k - 1],
            recv_sem=self.sum_recv.at[d, c, k - 1],
            device_id=self.toward(d, away),
            device_id_type=MESH,
        )

    def sum_arrive(self, d, c, k):
        self.sum_copy(d, c, k, self.landing.at[d, c, k - 1], True).wait_recv()

    def row_copy(self, d, c, k, away=False):
        back = k if away else k - 1
        rows = self.place(c, self.z - back if d == 0 else self.z + back)
        return pltpu.make_async_remote_copy(
            src_ref=self.full.at[rows],
            dst_ref=self.full.at[rows],
            send_sem=self.row_send.at[d, c, k - 1],
            recv_sem=self.row_recv.at[d, c, k - 1],
            device_id=self.toward(d, away),
            device_id_type=MESH,
        )

    def stage(self, c, s):
        n, z = self.n, self.z
        if s < n:
            for d in range(2):
                q = self.flow(d)
                rows = self.place(c, z + n - s if d == 0 else z - n + s)

                @pl.when(q == 0)
                def first():
                    self.sum_copy(d, c, s, self.part.at[rows]).start()

                if s > 1:

                    @pl.when((q >= 1) & (q < s))
                    def later():
                        self.sum_arrive(d, c, s - 1)
                        held = self.landing.at[d, c, s - 2]
                        held[...] = (
                            self.part[rows].astype(jnp.float32) + held[...].astype(jnp.float32)
                        ).astype(low)
                        self.sum_copy(d, c, s, held).start()

        elif s == n:
            rows = self.place(c, z)
            self.total[...] = self.part[rows].astype(jnp.float32)
            for d in range(2):

                @pl.when(self.flow(d) >= 1)
                def ended():
                    self.sum_arrive(d, c, n - 1)
                    self.total[...] += self.landing[d, c, n - 2].astype(jnp.float32)

            self.full[rows] = self.finish(c, self.total[...]).astype(low)
            for d in range(2):

                @pl.when(self.flow(d) < n - 1)
                def spread():
                    self.row_copy(d, c, 1).start()

        else:
            k = s - n + 1
            for d in range(2):
                q = self.flow(d)

                @pl.when(q >= k - 1)
                def arrived():
                    self.row_copy(d, c, k - 1, True).wait_recv()

                if k < n:

                    @pl.when((q >= k - 1) & (q < n - 1))
                    def onward():
                        self.row_copy(d, c, k).start()

    def drain(self):
        n = self.n
        for c in range(self.chunks):
            for d in range(2):
                q = self.flow(d)
                for k in range(1, n):

                    @pl.when(q < k)
                    def sum_sent():
                        self.sum_copy(d, c, k, self.landing.at[d, c, k - 1]).wait_send()

                    @pl.when((q >= k - 1) & (q < n - 1))
                    def row_sent():
                        self.row_copy(d, c, k).wait_send()


def peers(axes):
    found = []
    for axis in axes:
        bit = 1
        while bit < lax.axis_size(axis):
            me = lax.axis_index(axis)
            found.append({axis: me + bit * (1 - 2 * ((me // bit) % 2))})
            bit *= 2
    return found


def greet(n, others):
    z = lax.axis_index("tp")
    barrier = pltpu.get_barrier_semaphore()

    @pl.when(z > 0)
    def to_lower():
        pl.semaphore_signal(barrier, inc=1, device_id={"tp": z - 1}, device_id_type=MESH)

    @pl.when(z < n - 1)
    def to_upper():
        pl.semaphore_signal(barrier, inc=1, device_id={"tp": z + 1}, device_id_type=MESH)

    for other in others:
        pl.semaphore_signal(barrier, inc=1, device_id=other, device_id_type=MESH)

    @pl.when((z > 0) & (z < n - 1))
    def from_both():
        pl.semaphore_wait(barrier, 2 + len(others))

    @pl.when((z == 0) | (z == n - 1))
    def from_one():
        pl.semaphore_wait(barrier, 1 + len(others))


def line_scratch(n, chunks, rows, width):
    own = rows // chunks // n
    return [
        vmem((rows, width), low),
        vmem((2, chunks, n - 1, own, width), low),
        vmem((own, width), jnp.float32),
    ] + [pltpu.SemaphoreType.DMA((2, chunks, n - 1))] * 4


class Exchange:
    def __init__(self, whole, start, arrived, send_sem, recv_sem):
        self.whole, self.held, self.arrived = whole, start, arrived
        self.send_sem, self.recv_sem = send_sem, recv_sem
        self.inner = len(peers(("ctx", "fsdp")))
        self.peers = peers(("ctx", "fsdp", "tp"))

    def copy(self, i):
        columns = slice(None) if i < self.inner else slice(0, self.whole)
        return pltpu.make_async_remote_copy(
            src_ref=self.held.at[i, :, columns],
            dst_ref=self.arrived.at[i, :, columns],
            send_sem=self.send_sem.at[i],
            recv_sem=self.recv_sem.at[i],
            device_id=self.peers[i],
            device_id_type=MESH,
        )

    def step(self, i):
        if i > 0:
            self.copy(i - 1).wait_recv()
            if i - 1 < self.inner:
                self.held[i] = self.held[i - 1] + self.arrived[i - 1]
            else:
                self.held[i] = self.held[i - 1]
                self.held[i, :, : self.whole] += self.arrived[i - 1, :, : self.whole]
        if i < len(self.peers):
            self.copy(i).start()

    def drain(self):
        for i in range(len(self.peers)):
            self.copy(i).wait_send()


def sum_kernel(n, chunks, epilogue, counts, with_product, with_vectors, plan, *refs):
    refs = list(refs)

    def taken(count):
        out = refs[:count]
        del refs[:count]
        return out

    operands = taken(2 if with_product else 1)
    extras, weights = taken(counts[0]), taken(2 * counts[2])
    (full,) = taken(1)
    outs, sums = taken(counts[1]), taken(counts[2])
    part = taken(1)[0] if with_product else operands[0]
    landing, total = taken(2)
    sems = taken(4)
    moves = [
        Halving(weights[2 * i], weights[2 * i + 1], sums[i], taken(8)) for i in range(counts[2])
    ]
    rows, width = full.shape
    chunk_rows = rows // chunks
    block = max(chunk_rows, min(rows, 256))
    per_block = block // chunk_rows
    greet(n, peers(("ctx", "fsdp", "tp") if with_vectors else ("ctx", "fsdp")))
    finish = epilogue(chunk_rows // n, extras, outs)
    line = Line(n, chunks, part, full, landing, total, sems, finish)

    def multiply(b):
        if not with_product:
            return
        own = slice(b * block, (b + 1) * block)

        @pl.loop(0, width // 256)
        def one(i):
            columns = pl.ds(pl.multiple_of(i * 256, 256), 256)
            part[own, columns] = contract_cols(operands[0][own, :], operands[1][columns, :]).astype(
                low
            )

    for move in moves:
        move.start()
    multiply(0)
    ended = chunks - 1 + n
    vectors = None
    for t in range(1, chunks + 2 * n - 1):
        for c in range(chunks):
            if 0 < t - c < 2 * n:
                line.stage(c, t - c)
        if t % per_block == 0 and t < chunks:
            multiply(t // per_block)
        for i, move in enumerate(moves):
            if t == plan[i][0]:
                move.core_step()
            if t == plan[i][1]:
                move.middle_step()
        if with_vectors and t == ended:
            held, arrived, send_sem, recv_sem = refs
            vectors = Exchange(width, held, arrived, send_sem, recv_sem)
            held[0] = extras[-1][...]
            held[0, 0:2, :width] = outs[0][0:2]
        if vectors is not None and t - ended <= len(vectors.peers):
            vectors.step(t - ended)
            done = t - ended
    if vectors is not None:
        for i in range(done + 1, len(vectors.peers) + 1):
            vectors.step(i)
        outs[-1][...] = vectors.held[len(vectors.peers)]
        vectors.drain()
    for move in moves:
        move.last_step()
    for move in moves:
        move.drain()
    line.drain()


def tp_sum(
    n, chunks, epilogue, collective, operands, extras, out_shapes, weights, plan, vectors=None
):
    rows = operands[0].shape[0]
    with_product = len(operands) == 2
    width = operands[-1].shape[0] if with_product else operands[0].shape[1]
    outs = list(out_shapes)
    scratch = line_scratch(n, chunks, rows, width)
    if not with_product:
        scratch = scratch[1:]
    count = lax.axis_size("fsdp")
    sums = []
    for given, _ in weights:
        own = jax.ShapeDtypeStruct((given.shape[0] // (2 * count), given.shape[1]), low)
        sums.append(own)
        scratch += halving_scratch(count, *own.shape)
    if vectors is not None:
        extras = (*extras, vectors)
        outs.append(jax.ShapeDtypeStruct(vectors.shape, jnp.float32))
        steps = len(peers(("ctx", "fsdp", "tp")))
        scratch += [
            vmem((steps + 1, *vectors.shape), jnp.float32),
            vmem((steps, *vectors.shape), jnp.float32),
            pltpu.SemaphoreType.DMA((steps,)),
            pltpu.SemaphoreType.DMA((steps,)),
        ]
    counts = (len(extras), len(outs), len(weights))
    return fused_call(
        functools.partial(
            sum_kernel, n, chunks, epilogue, counts, with_product, vectors is not None, plan
        ),
        collective,
        (*operands, *extras, *[ref for pair in weights for ref in pair]),
        [jax.ShapeDtypeStruct((rows, width), low)] + outs + sums,
        scratch,
        12 * rows * width * 512,
        2 * len(weights),
    )


def middle_epilogue(own, extras, outs):
    stream, bias, gain, shift = extras
    (middle,) = outs

    def finish(c, total):
        rows = slice(c * own, (c + 1) * own)
        value = stream[rows].astype(jnp.float32) + total + bias[...]
        middle[rows] = value
        return normalize(value)[0] * gain[...] + shift[...]

    return finish


def output_epilogue(own, extras, outs):
    middle, bias = extras

    def finish(c, total):
        return middle[c * own : (c + 1) * own] + total + bias[...]

    return finish


def attn_epilogue(own, extras, outs):
    middle, cotangent, gain = extras[:3]
    grad_middle, sums = outs[:2]
    sums[...] = jnp.zeros_like(sums)

    def finish(c, total):
        rows = slice(c * own, (c + 1) * own)
        normed, inverse = normalize(middle[rows])
        value = cotangent[rows].astype(jnp.float32) + norm_back(total, normed, inverse, gain[...])
        grad_middle[rows] = value
        sums[0:1] += jnp.sum(total * normed, axis=0, keepdims=True)
        sums[1:2] += jnp.sum(total, axis=0, keepdims=True)
        sums[2:3] += jnp.sum(value.astype(low).astype(jnp.float32), axis=0, keepdims=True)
        return value

    return finish


def input_epilogue(own, extras, outs):
    stream, grad_middle, gain = extras[:3]
    sums = outs[0]
    sums[...] = jnp.zeros_like(sums)

    def finish(c, total):
        rows = slice(c * own, (c + 1) * own)
        normed, inverse = normalize(stream[rows].astype(jnp.float32))
        sums[0:1] += jnp.sum(total * normed, axis=0, keepdims=True)
        sums[1:2] += jnp.sum(total, axis=0, keepdims=True)
        return grad_middle[rows] + norm_back(total, normed, inverse, gain[...])

    return finish


def flipped(index, bits):
    out, bit = index, 1
    while bit <= bits:
        if bits & bit:
            out = out + bit * (1 - 2 * ((index // bit) % 2))
        bit *= 2
    return out


class Halving:
    def __init__(self, given, kept, out, refs):
        self.given, self.kept, self.out = given, kept, out
        self.mine, self.held, self.landing = refs[:3]
        self.own_sem, self.core_send, self.core_recv, self.half_send, self.half_recv = refs[3:]
        self.count = lax.axis_size("fsdp")
        self.rows = out.shape[0]
        self.half = out.shape[1] // 2
        _, self.place, _, self.beside, self.across = ctx_place()
        self.turn = lax.axis_index("fsdp")

    def shards(self):
        return [(far, over) for far in range(self.count - 1, -1, -1) for over in (1, 0)]

    def shard(self, far, over):
        p = flipped(self.turn, far) * 2 + flipped(self.place, over)
        return pl.ds(pl.multiple_of(p * self.rows, self.rows), self.rows)

    def core_copy(self, far, over):
        i = 2 * far + over
        return ctx_copy(
            self.given.at[self.shard(far, over)],
            self.held.at[i],
            self.core_send.at[i],
            self.core_recv.at[i],
            self.beside,
        )

    def own_copy(self, far, over):
        i = 2 * far + over
        return pltpu.make_async_copy(
            self.kept.at[self.shard(far, over)], self.mine.at[i], self.own_sem.at[i]
        )

    def half_copy(self, way, bit, far, over):
        n = self.count
        if way == 0:
            i = n + far - 1 if bit else far
        else:
            i = 2 * n - 1 + 2 * (far - 1) + over if bit else 4 * n - 3
        device = {"fsdp": flipped(self.turn, bit)} if bit else self.across
        columns = slice(way * self.half, (way + 1) * self.half)
        copy = ctx_copy(
            self.held.at[2 * far + over, :, columns],
            self.landing.at[i],
            self.half_send.at[i],
            self.half_recv.at[i],
            device,
        )
        return copy, i, columns

    def start(self):
        for far, over in self.shards():
            self.core_copy(far, over).start()
        for far, over in self.shards():
            self.own_copy(far, over).start()

    def send(self, way, bit, far, over):
        self.half_copy(way, bit, far, over)[0].start()

    def take(self, way, bit, far, over):
        copy, i, columns = self.half_copy(way, bit, far, over)
        copy.wait_recv()
        far, over = (far - bit, over) if bit else (far, 0)
        k = 2 * far + over
        self.held[k, :, columns] = add_low(self.held[k, :, columns], self.landing[i])
        return far

    def core_step(self):
        top = self.count // 2
        for far, over in self.shards():
            k = 2 * far + over
            self.own_copy(far, over).wait()
            self.core_copy(far, over).wait_recv()
            self.held[k] = add_low(self.held[k], self.mine[k])
            if over:
                self.send(0, 0, far, over)
            if far >= top:
                self.send(1, top, far, over)

    def middle_step(self):
        top = self.count // 2
        for far in range(self.count - 1, -1, -1):
            self.take(0, 0, far, 1)
            if far >= top:
                self.send(0, top, far, 0)
        bit = top
        while bit > 1:
            for far in range(2 * bit - 1, bit - 1, -1):
                left = self.take(0, bit, far, 0)
                if left >= bit // 2:
                    self.send(0, bit // 2, left, 0)
            bit //= 2
        bit = top
        while bit:
            for far in range(2 * bit - 1, bit - 1, -1):
                for over in (1, 0):
                    left = self.take(1, bit, far, over)
                    if bit > 1 and left >= bit // 2:
                        self.send(1, bit // 2, left, over)
                    if bit == 1 and over:
                        self.send(1, 0, 0, 1)
            bit //= 2

    def last_step(self):
        self.take(0, 1, 1, 0)
        self.take(1, 0, 0, 1)
        self.out[...] = self.held[0]

    def drain(self):
        for far in range(self.count):
            for over in range(2):
                self.core_copy(far, over).wait_send()
            self.half_copy(0, 0, far, 1)[0].wait_send()
            if far:
                bit = 1
                while 2 * bit <= far:
                    bit *= 2
                self.half_copy(0, bit, far, 0)[0].wait_send()
                for over in range(2):
                    self.half_copy(1, bit, far, over)[0].wait_send()
        self.half_copy(1, 0, 0, 1)[0].wait_send()


def add_low(left, right):
    return (left.astype(jnp.float32) + right.astype(jnp.float32)).astype(low)


def halving_scratch(count, rows, width):
    sem = pltpu.SemaphoreType.DMA
    return (
        [vmem((2 * count, rows, width), low)] * 2
        + [vmem((4 * count - 2, rows, width // 2), low)]
        + [sem((2 * count,))] * 3
        + [sem((4 * count - 2,))] * 2
    )


def split_store(value, tile, rows, given, kept, columns):
    side = lax.axis_index("ctx") % 2
    height = value.shape[0]
    step = min(rows, height)
    for k in range(height // step):
        start = tile * height + k * step
        shard = start // rows
        place = shard // 2 * rows + start % rows
        place = pl.ds(place if isinstance(place, int) else pl.multiple_of(place, step), step)
        piece = value[k * step : (k + 1) * step].astype(low)

        @pl.when((shard + side) % 2 == 0)
        def keep():
            kept[place, columns] = piece

        @pl.when((shard + side) % 2 == 1)
        def give():
            given[place, columns] = piece


def hidden_kernel(shard_rows, tiles, *refs):
    (
        act,
        grad_branch,
        grad_turned,
        up,
        down,
        bias,
        up_rows,
        down_rows,
        down_given,
        down_kept,
        up_given,
        up_kept,
        branch_part,
        back_part,
        bias_sum,
        act_turned,
        gelu_all,
        grad_all,
    ) = refs
    i = pl.program_id(0)
    width = act.shape[1]
    tile = up.shape[1]

    @pl.when(i == 0)
    def begin():
        @pl.loop(0, width // 256)
        def turn(k):
            place = pl.ds(pl.multiple_of(k * 256, 256), 256)
            act_turned[place, :] = act[:, place].T

    @pl.when(i < tiles)
    def units():
        columns = pl.ds(pl.multiple_of(i * tile, tile), tile)
        hidden = jnp.dot(act[...], up[...], preferred_element_type=jnp.float32) + bias[...]
        squared = hidden * hidden
        bend = jnp.tanh(0.7978845608028654 * (hidden + 0.044715 * squared * hidden))
        gelu_low = (0.5 * hidden * (1.0 + bend)).astype(low)
        slope = 0.5 * (1.0 + bend) + 0.5 * hidden * (1.0 - bend * bend) * 0.7978845608028654 * (
            1.0 + 3.0 * 0.044715 * squared
        )
        incoming = jnp.dot(grad_branch[...], down[...], preferred_element_type=jnp.float32)
        grad_up_proj = (incoming * slope).astype(low)
        gelu_all[:, columns] = gelu_low
        grad_all[:, columns] = grad_up_proj
        bias_sum[...] = jnp.broadcast_to(
            jnp.sum(grad_up_proj.astype(jnp.float32), axis=0, keepdims=True), bias_sum.shape
        )
        for k in range(width // 256):
            place = slice(k * 256, (k + 1) * 256)
            split_store(
                jnp.dot(grad_turned[place, :], gelu_low, preferred_element_type=jnp.float32),
                k,
                shard_rows,
                down_given,
                down_kept,
                slice(None),
            )
            split_store(
                jnp.dot(act_turned[place, :], grad_up_proj, preferred_element_type=jnp.float32),
                k,
                shard_rows,
                up_given,
                up_kept,
                slice(None),
            )

    @pl.when(i >= tiles)
    def products():
        branch_part[...] = contract_cols(gelu_all[...], down_rows[...]).astype(low)
        back_part[...] = contract_cols(grad_all[...], up_rows[...]).astype(low)


def hidden_layer(shard_rows, act, grad_branch, up, down, bias):
    rows, width = act.shape
    hidden = up.shape[1]
    tile = 256
    tiles = hidden // tile

    def whole(shape):
        return pl.BlockSpec(shape, lambda i: (0, 0), pipeline_mode=pl.Buffered(1))

    def columns(height):
        return pl.BlockSpec((height, tile), lambda i: (0, jnp.minimum(i, tiles - 1)))

    later = pl.BlockSpec((tile, hidden), lambda i: (jnp.maximum(i - tiles, 0), 0))
    parts = pl.BlockSpec((rows, tile), lambda i: (0, jnp.maximum(i - tiles, 0)))
    return pl.pallas_call(
        functools.partial(hidden_kernel, shard_rows, tiles),
        grid=(tiles + width // tile,),
        out_shape=[jax.ShapeDtypeStruct((width // 2, hidden), low)] * 4
        + [jax.ShapeDtypeStruct((rows, width), low)] * 2
        + [jax.ShapeDtypeStruct((8, hidden), jnp.float32)],
        in_specs=[
            whole((rows, width)),
            whole((rows, width)),
            whole((width, rows)),
            columns(width),
            columns(width),
            columns(1),
            later,
            later,
        ],
        out_specs=[columns(width // 2)] * 4 + [parts] * 2 + [columns(8)],
        scratch_shapes=[
            vmem((width, rows), low),
            vmem((rows, hidden), low),
            vmem((rows, hidden), low),
        ],
        compiler_params=pltpu.CompilerParams(vmem_limit_bytes=60 * 1024 * 1024),
        cost_estimate=pl.CostEstimate(
            flops=12 * rows * width * hidden, bytes_accessed=100_000_000, transcendentals=0
        ),
    )(act, grad_branch, grad_branch.T, up, down, bias, up, down)


class Gather:
    def __init__(self, rows, whole, refs):
        self.rows, self.whole = rows, whole
        self.half_send, self.half_recv, self.core_send, self.core_recv = refs
        count = lax.axis_size("fsdp")
        self.group = 2 * count
        bits = [2 * b for b in (1, 2, 4, 8, 16, 32) if b < count]
        self.orders = [[1, *bits], [*bits, 1]]
        self.half = whole.shape[1] // 2
        _, self.place, self.side, self.beside, self.across = ctx_place()
        self.turn = lax.axis_index("fsdp")

    def piece(self, way, d, other=False):
        pair = flipped(self.turn, d // 2) * 2 + flipped(self.place, d % 2)
        shard = 2 * pair + (1 - self.side if other else self.side)
        return self.whole.at[
            pl.ds(pl.multiple_of(shard * self.rows, self.rows), self.rows),
            way * self.half : (way + 1) * self.half,
        ]

    def bit_copy(self, way, d, bit):
        device = self.across if bit == 1 else {"fsdp": flipped(self.turn, bit // 2)}
        piece = self.piece(way, d - bit)
        return ctx_copy(
            piece, piece, self.half_send.at[way, d], self.half_recv.at[way, d], device
        )

    def core_copy(self, way, d, other=False):
        piece = self.piece(way, d, other)
        return ctx_copy(
            piece, piece, self.core_send.at[way, d], self.core_recv.at[way, d], self.beside
        )

    def pass_on(self, way, d, after):
        for bit in self.orders[way][after:]:
            self.bit_copy(way, d + bit, bit).start()
        self.core_copy(way, d).start()

    def run(self):
        for way in range(2):
            self.pass_on(way, 0, 0)
        have = [[0], [0]]
        for step in range(len(self.orders[0])):
            fresh = [[d + self.orders[way][step] for d in have[way]] for way in range(2)]
            for i in range(len(fresh[0])):
                for way in range(2):
                    d, bit = fresh[way][i], self.orders[way][step]
                    piece = self.piece(way, d)
                    device = self.across if bit == 1 else {"fsdp": flipped(self.turn, bit // 2)}
                    ctx_copy(
                        piece, piece, self.half_send.at[way, d], self.half_recv.at[way, d], device
                    ).wait_recv()
                    self.pass_on(way, d, step + 1)
            for way in range(2):
                have[way] += fresh[way]

    def finish(self):
        for d in range(self.group):
            for way in range(2):
                self.core_copy(way, d, True).wait_recv()

    def drain(self):
        for way in range(2):
            have = [0]
            for bit in self.orders[way]:
                for d in have:
                    self.bit_copy(way, d + bit, bit).wait_send()
                have += [d + bit for d in have]
            for d in range(self.group):
                self.core_copy(way, d).wait_send()


def meet(others):
    barrier = pltpu.get_barrier_semaphore()
    for other in others:
        pl.semaphore_signal(barrier, inc=1, device_id=other, device_id_type=MESH)
    pl.semaphore_wait(barrier, len(others))


def project_kernel(*refs):
    stream, own, gain, shift, bias, projected, act, qkv_out, out_out, whole, *rest = refs
    sems, out_sem = rest[:4], rest[4]
    meet(peers(("ctx", "fsdp")))
    shard_rows = own.shape[0]
    rows, width = stream.shape
    gather = Gather(shard_rows, whole, sems)
    for way in range(2):
        gather.piece(way, 0)[...] = own[:, way * gather.half : (way + 1) * gather.half]
    gather.run()

    @pl.loop(0, rows // 64)
    def norm(i):
        place = pl.ds(pl.multiple_of(i * 64, 64), 64)
        act[place, :] = (
            normalize(stream[place, :].astype(jnp.float32))[0] * gain[...] + shift[...]
        ).astype(low)

    gather.finish()
    wide = projected.shape[1]
    copies = [
        pltpu.make_async_copy(whole.at[:, :wide], qkv_out, out_sem.at[0]),
        pltpu.make_async_copy(whole.at[:, wide:], out_out, out_sem.at[1]),
    ]
    for copy in copies:
        copy.start()

    @pl.loop(0, wide // 256)
    def product(i):
        columns = pl.ds(pl.multiple_of(i * 256, 256), 256)
        projected[:, columns] = (
            jnp.dot(act[...], whole[:, columns], preferred_element_type=jnp.float32)
            + bias[:, columns]
        ).astype(low)

    for copy in copies:
        copy.wait()
    gather.drain()


def project(stream, own, gain, shift, bias):
    rows, width = stream.shape
    wide = bias.shape[1]
    count = 2 * lax.axis_size("fsdp")
    in_vmem, loose = pl.BlockSpec(memory_space=vmem), pl.BlockSpec(memory_space=pl.ANY)
    depth = own.shape[0] * 2 * count
    return pl.pallas_call(
        project_kernel,
        out_shape=[
            jax.ShapeDtypeStruct((rows, wide), low),
            jax.ShapeDtypeStruct((rows, width), low),
            jax.ShapeDtypeStruct((depth, wide), low),
            jax.ShapeDtypeStruct((depth, own.shape[1] - wide), low),
        ],
        in_specs=[in_vmem] * 5,
        out_specs=[in_vmem] * 2 + [loose] * 2,
        scratch_shapes=[vmem((depth, own.shape[1]), low)]
        + [pltpu.SemaphoreType.DMA((2, count))] * 4
        + [pltpu.SemaphoreType.DMA((2,))],
        compiler_params=pltpu.CompilerParams(
            collective_id=4, has_side_effects=True, vmem_limit_bytes=56 * 1024 * 1024
        ),
        cost_estimate=pl.CostEstimate(
            flops=2 * rows * width * wide, bytes_accessed=150_000_000, transcendentals=0
        ),
    )(stream, own, gain, shift, bias)


def ctx_place():
    me = lax.axis_index("ctx")
    half, side = me // 2, me % 2
    return me, half, side, {"ctx": me + 1 - 2 * side}, {"ctx": me + 2 - 4 * half}


def ctx_copy(source, target, send, recv, device):
    return pltpu.make_async_remote_copy(
        src_ref=source,
        dst_ref=target,
        send_sem=send,
        recv_sem=recv,
        device_id=device,
        device_id_type=MESH,
    )


class Spread:
    def __init__(self, block, own, pairs, send, recv):
        self.block, self.own, self.pairs, self.send, self.recv = block, own, pairs, send, recv
        self.me, self.half, self.side, self.beside, self.across = ctx_place()

    def rows(self, s, b):
        start = (s * lax.axis_size("ctx") + b) * self.block
        return pl.ds(pl.multiple_of(start, self.block), self.block)

    def copy(self, kind, s, b, own, device):
        target = self.pairs.at[self.rows(s, b)]
        wide = self.pairs.shape[1]
        source = self.own.at[s * self.block : (s + 1) * self.block, wide // 2 :] if own else target
        return ctx_copy(source, target, self.send.at[kind, s], self.recv.at[kind, s], device)

    def start(self, s):
        rows = slice(s * self.block, (s + 1) * self.block)

        @pl.when(self.half == 0)
        def over():
            self.copy(0, s, self.me, True, self.across).start()

        @pl.when(self.side == 0)
        def aside():
            self.copy(1, s, self.me, True, self.beside).start()

        self.pairs[self.rows(s, self.me)] = self.own[rows, self.pairs.shape[1] // 2 :]

    def forward(self, s):
        @pl.when(self.half == 1)
        def onward():
            self.copy(0, s, self.me - 2, False, self.across).wait_recv()
            self.copy(2, s, self.me - 2, False, self.beside).start()

    def arrive(self, s):
        @pl.when(self.half == 1)
        def second():
            self.copy(2, s, 1 - self.side, False, self.beside).wait_recv()

        @pl.when(self.side == 1)
        def first():
            self.copy(1, s, self.me - 1, False, self.beside).wait_recv()

    def drain_own(self, s):
        @pl.when(self.half == 0)
        def over():
            self.copy(0, s, self.me, True, self.across).wait_send()

        @pl.when(self.side == 0)
        def aside():
            self.copy(1, s, self.me, True, self.beside).wait_send()

    def drain(self, s):
        @pl.when(self.half == 1)
        def onward():
            self.copy(2, s, self.me - 2, False, self.beside).wait_send()


class Collect:
    def __init__(self, block, parts, beside_in, across_in, send, recv):
        self.block, self.parts = block, parts
        self.beside_in, self.across_in, self.send, self.recv = beside_in, across_in, send, recv
        self.me, self.half, self.side, self.beside, self.across = ctx_place()

    def rows(self, s, b):
        start = (s * lax.axis_size("ctx") + b) * self.block
        return pl.ds(pl.multiple_of(start, self.block), self.block)

    def aside(self, s, k, away=False):
        b = 2 * k + (self.side if away else 1 - self.side)
        return ctx_copy(
            self.parts.at[self.rows(s, b)],
            self.beside_in.at[k, s],
            self.send.at[k, s],
            self.recv.at[k, s],
            self.beside,
        )

    def over(self, s):
        return ctx_copy(
            self.parts.at[self.rows(s, self.side)],
            self.across_in.at[s],
            self.send.at[2, s],
            self.recv.at[2, s],
            self.across,
        )

    def start(self, s):
        for k in range(2):

            @pl.when(2 * k + 1 - self.side < self.me)
            def give():
                self.aside(s, k).start()

    def forward(self, s):
        for k in range(2):

            @pl.when(2 * k + self.side < self.me + 1 - 2 * self.side)
            def take():
                self.aside(s, k, True).wait_recv()

        @pl.when(self.half == 1)
        def onward():
            held = self.parts.at[self.rows(s, self.side)]
            held[...] = (
                held[...].astype(jnp.float32) + self.beside_in[0, s].astype(jnp.float32)
            ).astype(low)
            self.over(s).start()

    def finish(self, s, target):
        target[...] = self.parts[self.rows(s, self.me)]
        for k in range(2):

            @pl.when((self.side == 0) & (self.half == k))
            def near():
                target[...] = (
                    target[...].astype(jnp.float32) + self.beside_in[k, s].astype(jnp.float32)
                ).astype(low)

        @pl.when(self.half == 0)
        def far():
            self.over(s).wait_recv()
            target[...] = (
                target[...].astype(jnp.float32) + self.across_in[s].astype(jnp.float32)
            ).astype(low)

    def drain(self, s):
        for k in range(2):

            @pl.when(2 * k + 1 - self.side < self.me)
            def gave():
                self.aside(s, k).wait_send()

        @pl.when(self.half == 1)
        def sent():
            self.over(s).wait_send()


def offsets(base):
    shape = base.shape
    base[...] = (
        lax.broadcasted_iota(jnp.int32, shape, 0) - lax.broadcasted_iota(jnp.int32, shape, 1)
    ).astype(jnp.float32)


def head_scores(query, key, slope, base, j):
    far = base[...] + (j * base.shape[0]).astype(jnp.float32)
    return contract_cols(query, key) * HD ** (-0.5) - slope * jnp.abs(far)


def head_columns(h, shift=0):
    return pl.ds(pl.multiple_of(shift + h * HD, HD), HD)


def forward_heads(s, first, last, block, projected, pairs, slopes, base, context, log_total):
    me = lax.axis_index("ctx")
    count = lax.axis_size("ctx")
    own = slice(s * block, (s + 1) * block)
    wide = pairs.shape[1] // 2

    @pl.loop(first, last)
    def head(h):
        query = projected[own, head_columns(h)]

        def step(j, carry):
            peak, weight, total = carry
            rows = pl.ds(pl.multiple_of((s * count + me - j) * block, block), block)
            scores = head_scores(query, pairs[rows, head_columns(h)], slopes[h, 0:1], base, j)
            higher = jnp.maximum(peak, jnp.max(scores, axis=-1, keepdims=True))
            shrink = jnp.exp(peak - higher)
            exponent = jnp.exp(scores - higher)
            weight = weight * shrink + jnp.sum(exponent, axis=-1, keepdims=True)
            total = total * shrink + jnp.dot(
                exponent.astype(low),
                pairs[rows, head_columns(h, wide)],
                preferred_element_type=jnp.float32,
            )
            return higher, weight, total

        peak, weight, total = lax.fori_loop(
            0,
            me + 1,
            step,
            (
                jnp.full((block, 1), -1e30, jnp.float32),
                jnp.zeros((block, 1), jnp.float32),
                jnp.zeros((block, HD), jnp.float32),
            ),
        )
        context[own, head_columns(h)] = (total / weight).astype(low)
        log_total[own, head_columns(h)] = jnp.broadcast_to(peak + jnp.log(weight), (block, HD))


def backward_heads(
    s, first, last, block, projected, pairs, slopes, base, context, log_total, grad, parts, out
):
    me = lax.axis_index("ctx")
    count = lax.axis_size("ctx")
    own = slice(s * block, (s + 1) * block)
    wide = pairs.shape[1] // 2

    @pl.loop(first, last)
    def head(h):
        query = projected[own, head_columns(h)]
        incoming = grad[own, head_columns(h)]
        level = log_total[own, head_columns(h)][:, 0:1]
        mean = jnp.sum(
            incoming.astype(jnp.float32) * context[own, head_columns(h)].astype(jnp.float32),
            axis=-1,
            keepdims=True,
        )

        def step(j, total):
            rows = pl.ds(pl.multiple_of((s * count + me - j) * block, block), block)
            key = pairs[rows, head_columns(h)]
            probs = jnp.exp(head_scores(query, key, slopes[h, 0:1], base, j) - level)
            grad_probs = contract_cols(incoming, pairs[rows, head_columns(h, wide)])
            grad_scores = (probs * (grad_probs - mean)).astype(low)
            parts[rows, head_columns(h)] = (
                contract_rows(grad_scores, query) * HD ** (-0.5)
            ).astype(low)
            parts[rows, head_columns(h, wide)] = contract_rows(probs.astype(low), incoming).astype(
                low
            )
            return total + jnp.dot(grad_scores, key, preferred_element_type=jnp.float32)

        total = lax.fori_loop(0, me + 1, step, jnp.zeros((block, HD), jnp.float32))
        out[own, head_columns(h)] = (total * HD ** (-0.5)).astype(low)


def attend_kernel(n, chunks, tile, *refs):
    (
        projected,
        slopes,
        out_weight,
        stream,
        bias,
        gain,
        shift,
        full,
        middle,
        context,
        log_total,
        pairs,
        part,
        landing,
        total,
        *rest,
    ) = refs
    sems, (base, send, recv) = rest[:4], rest[4:]
    rows, width = full.shape
    seqs = chunks // 2
    block = rows // seqs
    heads = context.shape[1] // HD
    pace = heads // 2
    _, _, _, beside, across = ctx_place()
    greet(n, [beside, across])
    finish = middle_epilogue(rows // chunks // n, (stream, bias, gain, shift), (middle,))
    line = Line(n, chunks, part, full, landing, total, sems, finish)
    spread = Spread(block, projected, pairs, send, recv)
    spread.start(0)
    offsets(base)

    def attend(s, first, last):
        if first == 0:
            spread.forward(s)
            if s + 1 < seqs:
                spread.drain_own(s)
                spread.start(s + 1)
            spread.arrive(s)
        forward_heads(
            s, first, last, block, projected, pairs, slopes, base, context, log_total
        )

    def multiply(s):
        own = slice(s * block, (s + 1) * block)

        @pl.loop(0, width // tile)
        def one(i):
            columns = pl.ds(pl.multiple_of(i * tile, tile), tile)
            part[own, columns] = contract_cols(context[own, :], out_weight[columns, :]).astype(low)

    attend(0, 0, heads)
    multiply(0)
    for t in range(1, chunks + 2 * n - 1):
        for c in range(chunks):
            if 0 < t - c < 2 * n:
                line.stage(c, t - c)
        s = (t + 1) // 2
        if s < seqs:
            attend(s, 0 if t % 2 else pace, pace if t % 2 else heads)
            if t % 2 == 0:
                multiply(s)
    spread.drain_own(seqs - 1)
    for s in range(seqs):
        spread.drain(s)
    line.drain()


def backward_kernel(n, chunks, shard_rows, *refs):
    (
        part,
        middle,
        bias,
        grad_attn,
        out_weight,
        projected,
        pairs,
        context,
        log_total,
        slopes,
        act,
        full,
        grad_projected,
        given,
        kept,
        landing,
        total,
        *rest,
    ) = refs
    sems, (base, grad_context, parts, beside_in, across_in, send, recv) = rest[:4], rest[4:]
    rows, width = full.shape
    seqs = chunks // 2
    block = rows // seqs
    heads = context.shape[1] // HD
    wide = context.shape[1]
    pace = heads // 2
    _, _, _, beside, across = ctx_place()
    greet(n, [beside, across])
    finish = output_epilogue(rows // chunks // n, (middle, bias), ())
    line = Line(n, chunks, part, full, landing, total, sems, finish)
    collect = Collect(block, parts, beside_in, across_in, send, recv)
    offsets(base)

    def backward(s, first, last):
        own = slice(s * block, (s + 1) * block)
        if first == 0:
            grad_context[own, :] = jnp.dot(
                grad_attn[own, :], out_weight[...], preferred_element_type=jnp.float32
            ).astype(low)
        backward_heads(
            s,
            first,
            last,
            block,
            projected,
            pairs,
            slopes,
            base,
            context,
            log_total,
            grad_context,
            parts,
            grad_projected,
        )
        if last == heads:
            collect.start(s)

    def finished(s):
        collect.finish(s, grad_projected.at[s * block : (s + 1) * block, wide:])

    def features(source, right, columns, first, last):
        @pl.loop(first, last)
        def one(i):
            place = pl.ds(pl.multiple_of(i * 256, 256), 256)
            value = contract_rows(source[:, place], right[...])
            split_store(value, i, shard_rows, given, kept, columns)

    attn_columns = slice(0, 3 * wide)
    out_columns = slice(3 * wide, 4 * wide)

    tiles = width // 256
    tasks = []
    for s in range(seqs):
        tasks.append([functools.partial(backward, s, 0, pace)])
        tasks.append([functools.partial(backward, s, pace, heads)])
    tasks += [[] for _ in range(chunks + 2 * n - 2 - len(tasks))]
    for s in range(seqs):
        tasks[2 * s + 2].append(functools.partial(collect.forward, s))
    after = 2 * seqs + 1
    tasks[after].append(functools.partial(features, grad_attn, context, out_columns, 0, tiles))
    for s in range(seqs):
        tasks[after + s].append(functools.partial(finished, s))
    left = len(tasks) - after - seqs
    for i in range(left):
        tasks[after + seqs + i].append(
            functools.partial(
                features,
                act,
                grad_projected,
                attn_columns,
                tiles * i // left,
                tiles * (i + 1) // left,
            )
        )
    for t in range(1, chunks + 2 * n - 1):
        for c in range(chunks):
            if 0 < t - c < 2 * n:
                line.stage(c, t - c)
        for task in tasks[t - 1]:
            task()
    for s in range(seqs):
        collect.drain(s)
    line.drain()


def fused_call(body, collective, operands, outs, scratch, flops, loose=0):
    whole = pl.BlockSpec(memory_space=vmem)
    specs = [whole] * (len(operands) - loose) + [pl.BlockSpec(memory_space=pl.ANY)] * loose
    return pl.pallas_call(
        body,
        out_shape=outs,
        in_specs=specs,
        out_specs=[whole] * len(outs),
        scratch_shapes=scratch,
        compiler_params=pltpu.CompilerParams(
            collective_id=collective,
            has_side_effects=True,
            vmem_limit_bytes=60 * 1024 * 1024,
        ),
        cost_estimate=pl.CostEstimate(flops=flops, bytes_accessed=200_000_000, transcendentals=0),
    )(*operands)


def local(
    inputs,
    cotangent,
    master_qkv,
    qkv_moment1,
    qkv_moment2,
    master_out,
    out_moment1,
    out_moment2,
    master_up,
    up_moment1,
    up_moment2,
    master_down,
    down_moment1,
    down_moment2,
    norm_gains,
    gain_moment1,
    gain_moment2,
    shared_biases,
    shared_moment1,
    shared_moment2,
    split_biases,
    split_moment1,
    split_moment2,
):
    seq_count, block_len, model_width = inputs.shape
    row_count = seq_count * block_len
    width_part = master_qkv.shape[2]
    hidden_rows = master_up.shape[1]
    local_heads = width_part // HD
    tp_count = lax.axis_size("tp")
    chunks = 2 * seq_count
    own_rows = row_count // chunks // tp_count

    def own_part(values):
        blocks = values.reshape(chunks, tp_count * own_rows, model_width)
        taken = lax.dynamic_slice_in_dim(blocks, lax.axis_index("tp") * own_rows, own_rows, axis=1)
        return taken.reshape(-1, model_width)

    own_shape = jax.ShapeDtypeStruct((row_count // tp_count, model_width), jnp.float32)
    sums_shape = jax.ShapeDtypeStruct((8, model_width), jnp.float32)
    gains = [norm_gains[i : i + 1] for i in range(2)]
    shared = [shared_biases[i : i + 1] for i in range(4)]
    inputs_own = own_part(inputs)
    cotangent_own = own_part(cotangent)

    def flat(master):
        return master.astype(low).reshape(master.shape[0], -1)

    def gather_rows(rows):
        return lax.all_gather(rows, ("fsdp", "ctx"), axis=0, tiled=True)

    projected_bias = jnp.concatenate(
        [split_biases[0], jnp.zeros((width_part,), jnp.float32), split_biases[1]]
    )
    projected, act_one, qkv_flat, out_flat = project(
        inputs.reshape(row_count, model_width),
        jnp.concatenate([flat(master_qkv), flat(master_out)], axis=1),
        gains[0],
        shared[0],
        projected_bias[None],
    )
    up_flat = gather_rows(flat(master_up))
    down_flat = gather_rows(flat(master_down))
    head_ids = (lax.axis_index("tp") * local_heads + jnp.arange(local_heads)).astype(jnp.float32)
    slopes = jnp.power(2.0, -8.0 * (head_ids + 1.0) / (local_heads * lax.axis_size("tp")))
    slopes = jnp.broadcast_to(slopes[:, None, None], (local_heads, 8, block_len))
    sems = line_scratch(tp_count, chunks, row_count, model_width)
    pair_rows = row_count * lax.axis_size("ctx")
    square = vmem((block_len, block_len), jnp.float32)
    pair_sems = [pltpu.SemaphoreType.DMA((3, seq_count))] * 2
    act_two, middle, context, log_total, pairs = fused_call(
        functools.partial(attend_kernel, tp_count, chunks, 256),
        0,
        (projected, slopes, out_flat, inputs_own, shared[2], gains[1], shared[1]),
        [
            jax.ShapeDtypeStruct((row_count, model_width), low),
            own_shape,
            jax.ShapeDtypeStruct((row_count, width_part), low),
            jax.ShapeDtypeStruct((row_count, width_part), jnp.float32),
            jax.ShapeDtypeStruct((pair_rows, 2 * width_part), low),
        ],
        sems + [square] + pair_sems,
        4 * row_count * model_width * width_part,
    )
    down_given, down_kept, up_given, up_kept, branch_part, back_part, bias_sum = hidden_layer(
        master_qkv.shape[0],
        act_two,
        cotangent.reshape(row_count, model_width),
        up_flat,
        down_flat,
        split_biases[2:].reshape(1, -1),
    )
    grad_attn, grad_middle, sums_two, sum_down, sum_up = tp_sum(
        tp_count,
        chunks,
        attn_epilogue,
        2,
        (back_part,),
        (middle, cotangent_own, gains[1]),
        [own_shape, sums_shape],
        [(down_given, down_kept), (up_given, up_kept)],
        ((2, 7), (4, 11)),
    )
    pair_block = (block_len, 2 * width_part)
    output, grad_projected, attn_given, attn_kept = fused_call(
        functools.partial(backward_kernel, tp_count, chunks, master_qkv.shape[0]),
        1,
        (
            branch_part,
            middle,
            shared[3],
            grad_attn,
            out_flat,
            projected,
            pairs,
            context,
            log_total,
            slopes,
            act_one,
        ),
        [
            jax.ShapeDtypeStruct((row_count, model_width), low),
            jax.ShapeDtypeStruct((row_count, 3 * width_part), low),
            jax.ShapeDtypeStruct((model_width // 2, 4 * width_part), low),
            jax.ShapeDtypeStruct((model_width // 2, 4 * width_part), low),
        ],
        sems[1:]
        + [
            square,
            vmem((row_count, width_part), low),
            vmem((pair_rows, 2 * width_part), low),
            vmem((2, seq_count, *pair_block), low),
            vmem((seq_count, *pair_block), low),
        ]
        + pair_sems,
        12 * row_count * model_width * width_part,
    )
    output = output.reshape(seq_count, block_len, model_width)
    query_low = grad_projected[:, :width_part]
    value_low = grad_projected[:, 2 * width_part :]
    split_grads = jnp.concatenate(
        [
            jnp.sum(query_low, axis=0, dtype=jnp.float32)[None],
            jnp.sum(value_low, axis=0, dtype=jnp.float32)[None],
            bias_sum[0].reshape(hidden_rows, width_part),
        ],
        axis=0,
    )
    vectors = jnp.concatenate(
        [
            jnp.zeros((2, model_width), jnp.float32),
            sums_two[0:3],
            jnp.sum(cotangent_own, axis=0, dtype=jnp.float32)[None],
            jnp.zeros((2, model_width), jnp.float32),
        ]
    )
    vectors = jnp.concatenate([vectors, jnp.pad(split_grads, ((0, 2), (0, 0)))], axis=1)
    input_low, _, vector_sum, sum_attn = tp_sum(
        tp_count,
        chunks,
        input_epilogue,
        3,
        (grad_projected, qkv_flat),
        (inputs_own, grad_middle, gains[0]),
        [sums_shape],
        [(attn_given, attn_kept)],
        ((2, 8),),
        vectors,
    )
    input_grad = input_low.astype(jnp.float32).reshape(seq_count, block_len, model_width)

    sum_attn = sum_attn.astype(jnp.float32)
    sum_qkv = sum_attn[:, : 3 * width_part].reshape(master_qkv.shape)
    sum_out = sum_attn[:, 3 * width_part :]
    sum_up = sum_up.astype(jnp.float32).reshape(master_up.shape)
    sum_down = sum_down.astype(jnp.float32).reshape(master_down.shape)
    gain_sum = jnp.concatenate([vector_sum[0:1, :model_width], vector_sum[2:3, :model_width]])
    shared_sum = jnp.concatenate([vector_sum[1:2, :model_width], vector_sum[3:6, :model_width]])
    split_sum = vector_sum[: 2 + hidden_rows, model_width:]
    q_one, q_two, q_new = adam_update(
        master_qkv, qkv_moment1, qkv_moment2, sum_qkv, matrix_rate, True
    )
    o_one, o_two, o_new = adam_update(
        master_out, out_moment1, out_moment2, sum_out, matrix_rate, True
    )
    u_one, u_two, u_new = adam_update(master_up, up_moment1, up_moment2, sum_up, matrix_rate, True)
    d_one, d_two, d_new = adam_update(
        master_down, down_moment1, down_moment2, sum_down, matrix_rate, True
    )
    g_one, g_two, g_new = adam_update(
        norm_gains, gain_moment1, gain_moment2, gain_sum, vector_rate, False
    )
    s_one, s_two, s_new = adam_update(
        shared_biases, shared_moment1, shared_moment2, shared_sum, vector_rate, False
    )
    p_one, p_two, p_new = adam_update(
        split_biases, split_moment1, split_moment2, split_sum, vector_rate, False
    )
    return (
        output,
        input_grad,
        q_one,
        q_two,
        q_new,
        q_new.astype(jnp.bfloat16),
        o_one,
        o_two,
        o_new,
        o_new.astype(jnp.bfloat16),
        u_one,
        u_two,
        u_new,
        u_new.astype(jnp.bfloat16),
        d_one,
        d_two,
        d_new,
        d_new.astype(jnp.bfloat16),
        g_one,
        g_two,
        g_new,
        s_one,
        s_two,
        s_new,
        p_one,
        p_two,
        p_new,
    )


def solution(mesh):
    return jax.shard_map(
        local,
        mesh=mesh,
        in_specs=(
            P("fsdp", "ctx", None),
            P("fsdp", "ctx", None),
            P(("fsdp", "ctx"), None, "tp"),
            P(("fsdp", "ctx"), None, "tp"),
            P(("fsdp", "ctx"), None, "tp"),
            P(("fsdp", "ctx"), "tp"),
            P(("fsdp", "ctx"), "tp"),
            P(("fsdp", "ctx"), "tp"),
            P(("fsdp", "ctx"), None, "tp"),
            P(("fsdp", "ctx"), None, "tp"),
            P(("fsdp", "ctx"), None, "tp"),
            P(("fsdp", "ctx"), None, "tp"),
            P(("fsdp", "ctx"), None, "tp"),
            P(("fsdp", "ctx"), None, "tp"),
            P(),
            P(),
            P(),
            P(),
            P(),
            P(),
            P(None, "tp"),
            P(None, "tp"),
            P(None, "tp"),
        ),
        out_specs=(
            P("fsdp", "ctx", None),
            P("fsdp", "ctx", None),
            P(("fsdp", "ctx"), None, "tp"),
            P(("fsdp", "ctx"), None, "tp"),
            P(("fsdp", "ctx"), None, "tp"),
            P(("fsdp", "ctx"), None, "tp"),
            P(("fsdp", "ctx"), "tp"),
            P(("fsdp", "ctx"), "tp"),
            P(("fsdp", "ctx"), "tp"),
            P(("fsdp", "ctx"), "tp"),
            P(("fsdp", "ctx"), None, "tp"),
            P(("fsdp", "ctx"), None, "tp"),
            P(("fsdp", "ctx"), None, "tp"),
            P(("fsdp", "ctx"), None, "tp"),
            P(("fsdp", "ctx"), None, "tp"),
            P(("fsdp", "ctx"), None, "tp"),
            P(("fsdp", "ctx"), None, "tp"),
            P(("fsdp", "ctx"), None, "tp"),
            P(),
            P(),
            P(),
            P(),
            P(),
            P(),
            P(None, "tp"),
            P(None, "tp"),
            P(None, "tp"),
        ),
        check_vma=False,
    )
```

```python
import functools

import jax
import jax.numpy as jnp
from jax import lax
from jax.experimental import pallas as pl
from jax.experimental.pallas import tpu as pltpu
from jax.sharding import PartitionSpec as P

HD = 128
STEP = 10


norm_epsilon = 1e-05
matrix_rate = 0.04
vector_rate = 0.4
decay_weight = 0.1
decay_rate = 0.5
adam_epsilon = 1e-08
low = jnp.bfloat16


def normalize(values):
    center = jnp.mean(values, axis=-1, keepdims=True)
    shifted = values - center
    variance = jnp.mean(shifted * shifted, axis=-1, keepdims=True)
    inverse = lax.rsqrt(variance + norm_epsilon)
    return (shifted * inverse, inverse)


def norm_back(incoming, normed, inverse, gain):
    scaled = incoming * gain
    return inverse * (
        scaled
        - jnp.mean(scaled, axis=-1, keepdims=True)
        - normed * jnp.mean(scaled * normed, axis=-1, keepdims=True)
    )


def gelu_tanh(values):
    return (
        0.5
        * values
        * (1.0 + jnp.tanh(0.7978845608028654 * (values + 0.044715 * values * values * values)))
    )


def adam_update(master, moment_one, moment_two, gradient, rate, decayed):
    first = decay_rate * moment_one + (1.0 - decay_rate) * gradient
    second = decay_rate * moment_two + (1.0 - decay_rate) * gradient * gradient
    correction = 1.0 - decay_rate**STEP
    update = first / correction / (jnp.sqrt(second / correction) + adam_epsilon)
    if decayed:
        update = update + decay_weight * master
    return (first, second, master - rate * update)


def contract_rows(left, right):
    return lax.dot_general(
        left, right, (((0,), (0,)), ((), ())), preferred_element_type=jnp.float32
    )


def contract_cols(left, right):
    return lax.dot_general(
        left, right, (((1,), (1,)), ((), ())), preferred_element_type=jnp.float32
    )


MESH = pl.DeviceIdType.MESH
vmem = pltpu.VMEM


class Line:
    def __init__(self, n, chunks, part, full, landing, total, sems, finish):
        self.n, self.chunks = n, chunks
        self.part, self.full, self.landing, self.total = part, full, landing, total
        self.sum_send, self.sum_recv, self.row_send, self.row_recv = sems
        self.finish = finish
        self.z = lax.axis_index("tp")
        self.chunk_rows = full.shape[0] // chunks
        self.own = self.chunk_rows // n
        self.last = 2 * n - 1

    def place(self, c, j):
        return pl.ds(pl.multiple_of(c * self.chunk_rows + j * self.own, self.own), self.own)

    def flow(self, d):
        return self.z if d == 0 else self.n - 1 - self.z

    def toward(self, d, away):
        return {"tp": self.z + (1 if (d == 0) != away else -1)}

    def sum_copy(self, d, c, k, source, away=False):
        return pltpu.make_async_remote_copy(
            src_ref=source,
            dst_ref=self.landing.at[d, c, k - 1],
            send_sem=self.sum_send.at[d, c, k - 1],
            recv_sem=self.sum_recv.at[d, c, k - 1],
            device_id=self.toward(d, away),
            device_id_type=MESH,
        )

    def sum_arrive(self, d, c, k):
        self.sum_copy(d, c, k, self.landing.at[d, c, k - 1], True).wait_recv()

    def row_copy(self, d, c, k, away=False):
        back = k if away else k - 1
        rows = self.place(c, self.z - back if d == 0 else self.z + back)
        return pltpu.make_async_remote_copy(
            src_ref=self.full.at[rows],
            dst_ref=self.full.at[rows],
            send_sem=self.row_send.at[d, c, k - 1],
            recv_sem=self.row_recv.at[d, c, k - 1],
            device_id=self.toward(d, away),
            device_id_type=MESH,
        )

    def stage(self, c, s):
        n, z = self.n, self.z
        if s < n:
            for d in range(2):
                q = self.flow(d)
                rows = self.place(c, z + n - s if d == 0 else z - n + s)

                @pl.when(q == 0)
                def first():
                    self.sum_copy(d, c, s, self.part.at[rows]).start()

                if s > 1:

                    @pl.when((q >= 1) & (q < s))
                    def later():
                        self.sum_arrive(d, c, s - 1)
                        held = self.landing.at[d, c, s - 2]
                        held[...] = (
                            self.part[rows].astype(jnp.float32) + held[...].astype(jnp.float32)
                        ).astype(low)
                        self.sum_copy(d, c, s, held).start()

        elif s == n:
            rows = self.place(c, z)
            self.total[...] = self.part[rows].astype(jnp.float32)
            for d in range(2):

                @pl.when(self.flow(d) >= 1)
                def ended():
                    self.sum_arrive(d, c, n - 1)
                    self.total[...] += self.landing[d, c, n - 2].astype(jnp.float32)

            self.full[rows] = self.finish(c, self.total[...]).astype(low)
            for d in range(2):

                @pl.when(self.flow(d) < n - 1)
                def spread():
                    self.row_copy(d, c, 1).start()

        else:
            k = s - n + 1
            for d in range(2):
                q = self.flow(d)

                @pl.when(q >= k - 1)
                def arrived():
                    self.row_copy(d, c, k - 1, True).wait_recv()

                if k < n:

                    @pl.when((q >= k - 1) & (q < n - 1))
                    def onward():
                        self.row_copy(d, c, k).start()

    def drain(self):
        n = self.n
        for c in range(self.chunks):
            for d in range(2):
                q = self.flow(d)
                for k in range(1, n):

                    @pl.when(q < k)
                    def sum_sent():
                        self.sum_copy(d, c, k, self.landing.at[d, c, k - 1]).wait_send()

                    @pl.when((q >= k - 1) & (q < n - 1))
                    def row_sent():
                        self.row_copy(d, c, k).wait_send()


def peers(axes):
    found = []
    for axis in axes:
        bit = 1
        while bit < lax.axis_size(axis):
            me = lax.axis_index(axis)
            found.append({axis: me + bit * (1 - 2 * ((me // bit) % 2))})
            bit *= 2
    return found


def greet(n, others):
    z = lax.axis_index("tp")
    barrier = pltpu.get_barrier_semaphore()

    @pl.when(z > 0)
    def to_lower():
        pl.semaphore_signal(barrier, inc=1, device_id={"tp": z - 1}, device_id_type=MESH)

    @pl.when(z < n - 1)
    def to_upper():
        pl.semaphore_signal(barrier, inc=1, device_id={"tp": z + 1}, device_id_type=MESH)

    for other in others:
        pl.semaphore_signal(barrier, inc=1, device_id=other, device_id_type=MESH)

    @pl.when((z > 0) & (z < n - 1))
    def from_both():
        pl.semaphore_wait(barrier, 2 + len(others))

    @pl.when((z == 0) | (z == n - 1))
    def from_one():
        pl.semaphore_wait(barrier, 1 + len(others))


def line_scratch(n, chunks, rows, width):
    own = rows // chunks // n
    return [
        vmem((rows, width), low),
        vmem((2, chunks, n - 1, own, width), low),
        vmem((own, width), jnp.float32),
    ] + [pltpu.SemaphoreType.DMA((2, chunks, n - 1))] * 4


class Exchange:
    def __init__(self, whole, start, arrived, send_sem, recv_sem):
        self.whole, self.held, self.arrived = whole, start, arrived
        self.send_sem, self.recv_sem = send_sem, recv_sem
        self.inner = len(peers(("ctx", "fsdp")))
        self.peers = peers(("ctx", "fsdp", "tp"))

    def copy(self, i):
        columns = slice(None) if i < self.inner else slice(0, self.whole)
        return pltpu.make_async_remote_copy(
            src_ref=self.held.at[i, :, columns],
            dst_ref=self.arrived.at[i, :, columns],
            send_sem=self.send_sem.at[i],
            recv_sem=self.recv_sem.at[i],
            device_id=self.peers[i],
            device_id_type=MESH,
        )

    def step(self, i):
        if i > 0:
            self.copy(i - 1).wait_recv()
            if i - 1 < self.inner:
                self.held[i] = self.held[i - 1] + self.arrived[i - 1]
            else:
                self.held[i] = self.held[i - 1]
                self.held[i, :, : self.whole] += self.arrived[i - 1, :, : self.whole]
        if i < len(self.peers):
            self.copy(i).start()

    def drain(self):
        for i in range(len(self.peers)):
            self.copy(i).wait_send()


def sum_kernel(n, chunks, epilogue, counts, with_product, with_vectors, plan, *refs):
    refs = list(refs)

    def taken(count):
        out = refs[:count]
        del refs[:count]
        return out

    operands = taken(2 if with_product else 1)
    extras, weights = taken(counts[0]), taken(2 * counts[2])
    (full,) = taken(1)
    outs, sums = taken(counts[1]), taken(counts[2])
    part = taken(1)[0] if with_product else operands[0]
    landing, total = taken(2)
    sems = taken(4)
    moves = [
        Halving(weights[2 * i], weights[2 * i + 1], sums[i], taken(8)) for i in range(counts[2])
    ]
    rows, width = full.shape
    chunk_rows = rows // chunks
    block = max(chunk_rows, min(rows, 256))
    per_block = block // chunk_rows
    greet(n, peers(("ctx", "fsdp", "tp") if with_vectors else ("ctx", "fsdp")))
    finish = epilogue(chunk_rows // n, extras, outs)
    line = Line(n, chunks, part, full, landing, total, sems, finish)

    def multiply(b):
        if not with_product:
            return
        own = slice(b * block, (b + 1) * block)

        @pl.loop(0, width // 256)
        def one(i):
            columns = pl.ds(pl.multiple_of(i * 256, 256), 256)
            part[own, columns] = contract_cols(operands[0][own, :], operands[1][columns, :]).astype(
                low
            )

    for move in moves:
        move.start()
    multiply(0)
    ended = chunks - 1 + n
    vectors = None
    for t in range(1, chunks + 2 * n - 1):
        for c in range(chunks):
            if 0 < t - c < 2 * n:
                line.stage(c, t - c)
        if t % per_block == 0 and t < chunks:
            multiply(t // per_block)
        for i, move in enumerate(moves):
            if t == plan[i][0]:
                move.core_step()
            if t == plan[i][1]:
                move.middle_step()
        if with_vectors and t == ended:
            held, arrived, send_sem, recv_sem = refs
            vectors = Exchange(width, held, arrived, send_sem, recv_sem)
            held[0] = extras[-1][...]
            held[0, 0:2, :width] = outs[0][0:2]
        if vectors is not None and t - ended <= len(vectors.peers):
            vectors.step(t - ended)
            done = t - ended
    if vectors is not None:
        for i in range(done + 1, len(vectors.peers) + 1):
            vectors.step(i)
        outs[-1][...] = vectors.held[len(vectors.peers)]
        vectors.drain()
    for move in moves:
        move.last_step()
    for move in moves:
        move.drain()
    line.drain()


def tp_sum(
    n, chunks, epilogue, collective, operands, extras, out_shapes, weights, plan, vectors=None
):
    rows = operands[0].shape[0]
    with_product = len(operands) == 2
    width = operands[-1].shape[0] if with_product else operands[0].shape[1]
    outs = list(out_shapes)
    scratch = line_scratch(n, chunks, rows, width)
    if not with_product:
        scratch = scratch[1:]
    count = lax.axis_size("fsdp")
    sums = []
    for given, _ in weights:
        own = jax.ShapeDtypeStruct((given.shape[0] // (2 * count), given.shape[1]), low)
        sums.append(own)
        scratch += halving_scratch(count, *own.shape)
    if vectors is not None:
        extras = (*extras, vectors)
        outs.append(jax.ShapeDtypeStruct(vectors.shape, jnp.float32))
        steps = len(peers(("ctx", "fsdp", "tp")))
        scratch += [
            vmem((steps + 1, *vectors.shape), jnp.float32),
            vmem((steps, *vectors.shape), jnp.float32),
            pltpu.SemaphoreType.DMA((steps,)),
            pltpu.SemaphoreType.DMA((steps,)),
        ]
    counts = (len(extras), len(outs), len(weights))
    return fused_call(
        functools.partial(
            sum_kernel, n, chunks, epilogue, counts, with_product, vectors is not None, plan
        ),
        collective,
        (*operands, *extras, *[ref for pair in weights for ref in pair]),
        [jax.ShapeDtypeStruct((rows, width), low)] + outs + sums,
        scratch,
        12 * rows * width * 512,
        2 * len(weights),
    )


def middle_epilogue(own, extras, outs):
    stream, bias, gain, shift = extras
    (middle,) = outs

    def finish(c, total):
        rows = slice(c * own, (c + 1) * own)
        value = stream[rows].astype(jnp.float32) + total + bias[...]
        middle[rows] = value
        return normalize(value)[0] * gain[...] + shift[...]

    return finish


def output_epilogue(own, extras, outs):
    middle, bias = extras

    def finish(c, total):
        return middle[c * own : (c + 1) * own] + total + bias[...]

    return finish


def attn_epilogue(own, extras, outs):
    middle, cotangent, gain = extras[:3]
    grad_middle, sums = outs[:2]
    sums[...] = jnp.zeros_like(sums)

    def finish(c, total):
        rows = slice(c * own, (c + 1) * own)
        normed, inverse = normalize(middle[rows])
        value = cotangent[rows].astype(jnp.float32) + norm_back(total, normed, inverse, gain[...])
        grad_middle[rows] = value
        sums[0:1] += jnp.sum(total * normed, axis=0, keepdims=True)
        sums[1:2] += jnp.sum(total, axis=0, keepdims=True)
        sums[2:3] += jnp.sum(value.astype(low).astype(jnp.float32), axis=0, keepdims=True)
        return value

    return finish


def input_epilogue(own, extras, outs):
    stream, grad_middle, gain = extras[:3]
    sums = outs[0]
    sums[...] = jnp.zeros_like(sums)

    def finish(c, total):
        rows = slice(c * own, (c + 1) * own)
        normed, inverse = normalize(stream[rows].astype(jnp.float32))
        sums[0:1] += jnp.sum(total * normed, axis=0, keepdims=True)
        sums[1:2] += jnp.sum(total, axis=0, keepdims=True)
        return grad_middle[rows] + norm_back(total, normed, inverse, gain[...])

    return finish


def flipped(index, bits):
    out, bit = index, 1
    while bit <= bits:
        if bits & bit:
            out = out + bit * (1 - 2 * ((index // bit) % 2))
        bit *= 2
    return out


class Halving:
    def __init__(self, given, kept, out, refs):
        self.given, self.kept, self.out = given, kept, out
        self.mine, self.held, self.landing = refs[:3]
        self.own_sem, self.core_send, self.core_recv, self.half_send, self.half_recv = refs[3:]
        self.count = lax.axis_size("fsdp")
        self.rows = out.shape[0]
        self.half = out.shape[1] // 2
        _, self.place, _, self.beside, self.across = ctx_place()
        self.turn = lax.axis_index("fsdp")

    def shards(self):
        return [(far, over) for far in range(self.count - 1, -1, -1) for over in (1, 0)]

    def shard(self, far, over):
        p = flipped(self.turn, far) * 2 + flipped(self.place, over)
        return pl.ds(pl.multiple_of(p * self.rows, self.rows), self.rows)

    def core_copy(self, far, over):
        i = 2 * far + over
        return ctx_copy(
            self.given.at[self.shard(far, over)],
            self.held.at[i],
            self.core_send.at[i],
            self.core_recv.at[i],
            self.beside,
        )

    def own_copy(self, far, over):
        i = 2 * far + over
        return pltpu.make_async_copy(
            self.kept.at[self.shard(far, over)], self.mine.at[i], self.own_sem.at[i]
        )

    def half_copy(self, way, bit, far, over):
        n = self.count
        if way == 0:
            i = n + far - 1 if bit else far
        else:
            i = 2 * n - 1 + 2 * (far - 1) + over if bit else 4 * n - 3
        device = {"fsdp": flipped(self.turn, bit)} if bit else self.across
        columns = slice(way * self.half, (way + 1) * self.half)
        copy = ctx_copy(
            self.held.at[2 * far + over, :, columns],
            self.landing.at[i],
            self.half_send.at[i],
            self.half_recv.at[i],
            device,
        )
        return copy, i, columns

    def start(self):
        for far, over in self.shards():
            self.core_copy(far, over).start()
        for far, over in self.shards():
            self.own_copy(far, over).start()

    def send(self, way, bit, far, over):
        self.half_copy(way, bit, far, over)[0].start()

    def take(self, way, bit, far, over):
        copy, i, columns = self.half_copy(way, bit, far, over)
        copy.wait_recv()
        far, over = (far - bit, over) if bit else (far, 0)
        k = 2 * far + over
        self.held[k, :, columns] = add_low(self.held[k, :, columns], self.landing[i])
        return far

    def core_step(self):
        top = self.count // 2
        for far, over in self.shards():
            k = 2 * far + over
            self.own_copy(far, over).wait()
            self.core_copy(far, over).wait_recv()
            self.held[k] = add_low(self.held[k], self.mine[k])
            if over:
                self.send(0, 0, far, over)
            if far >= top:
                self.send(1, top, far, over)

    def middle_step(self):
        top = self.count // 2
        for far in range(self.count - 1, -1, -1):
            self.take(0, 0, far, 1)
            if far >= top:
                self.send(0, top, far, 0)
        bit = top
        while bit > 1:
            for far in range(2 * bit - 1, bit - 1, -1):
                left = self.take(0, bit, far, 0)
                if left >= bit // 2:
                    self.send(0, bit // 2, left, 0)
            bit //= 2
        bit = top
        while bit:
            for far in range(2 * bit - 1, bit - 1, -1):
                for over in (1, 0):
                    left = self.take(1, bit, far, over)
                    if bit > 1 and left >= bit // 2:
                        self.send(1, bit // 2, left, over)
                    if bit == 1 and over:
                        self.send(1, 0, 0, 1)
            bit //= 2

    def last_step(self):
        self.take(0, 1, 1, 0)
        self.take(1, 0, 0, 1)
        self.out[...] = self.held[0]

    def drain(self):
        for far in range(self.count):
            for over in range(2):
                self.core_copy(far, over).wait_send()
            self.half_copy(0, 0, far, 1)[0].wait_send()
            if far:
                bit = 1
                while 2 * bit <= far:
                    bit *= 2
                self.half_copy(0, bit, far, 0)[0].wait_send()
                for over in range(2):
                    self.half_copy(1, bit, far, over)[0].wait_send()
        self.half_copy(1, 0, 0, 1)[0].wait_send()


def add_low(left, right):
    return (left.astype(jnp.float32) + right.astype(jnp.float32)).astype(low)


def halving_scratch(count, rows, width):
    sem = pltpu.SemaphoreType.DMA
    return (
        [vmem((2 * count, rows, width), low)] * 2
        + [vmem((4 * count - 2, rows, width // 2), low)]
        + [sem((2 * count,))] * 3
        + [sem((4 * count - 2,))] * 2
    )


def split_store(value, tile, rows, given, kept, columns):
    side = lax.axis_index("ctx") % 2
    height = value.shape[0]
    step = min(rows, height)
    for k in range(height // step):
        start = tile * height + k * step
        shard = start // rows
        place = shard // 2 * rows + start % rows
        place = pl.ds(place if isinstance(place, int) else pl.multiple_of(place, step), step)
        piece = value[k * step : (k + 1) * step].astype(low)

        @pl.when((shard + side) % 2 == 0)
        def keep():
            kept[place, columns] = piece

        @pl.when((shard + side) % 2 == 1)
        def give():
            given[place, columns] = piece


def hidden_kernel(shard_rows, tiles, *refs):
    (
        act,
        grad_branch,
        grad_turned,
        up,
        down,
        bias,
        up_rows,
        down_rows,
        down_given,
        down_kept,
        up_given,
        up_kept,
        branch_part,
        back_part,
        bias_sum,
        act_turned,
        gelu_all,
        grad_all,
    ) = refs
    i = pl.program_id(0)
    width = act.shape[1]
    tile = up.shape[1]

    @pl.when(i == 0)
    def begin():
        @pl.loop(0, width // 256)
        def turn(k):
            place = pl.ds(pl.multiple_of(k * 256, 256), 256)
            act_turned[place, :] = act[:, place].T

    @pl.when(i < tiles)
    def units():
        columns = pl.ds(pl.multiple_of(i * tile, tile), tile)
        hidden = jnp.dot(act[...], up[...], preferred_element_type=jnp.float32) + bias[...]
        squared = hidden * hidden
        bend = jnp.tanh(0.7978845608028654 * (hidden + 0.044715 * squared * hidden))
        gelu_low = (0.5 * hidden * (1.0 + bend)).astype(low)
        slope = 0.5 * (1.0 + bend) + 0.5 * hidden * (1.0 - bend * bend) * 0.7978845608028654 * (
            1.0 + 3.0 * 0.044715 * squared
        )
        incoming = jnp.dot(grad_branch[...], down[...], preferred_element_type=jnp.float32)
        grad_up_proj = (incoming * slope).astype(low)
        gelu_all[:, columns] = gelu_low
        grad_all[:, columns] = grad_up_proj
        bias_sum[...] = jnp.broadcast_to(
            jnp.sum(grad_up_proj.astype(jnp.float32), axis=0, keepdims=True), bias_sum.shape
        )
        for k in range(width // 512):
            place = slice(k * 512, (k + 1) * 512)
            split_store(
                jnp.dot(grad_turned[place, :], gelu_low, preferred_element_type=jnp.float32),
                k,
                shard_rows,
                down_given,
                down_kept,
                slice(None),
            )
            split_store(
                jnp.dot(act_turned[place, :], grad_up_proj, preferred_element_type=jnp.float32),
                k,
                shard_rows,
                up_given,
                up_kept,
                slice(None),
            )

    @pl.when(i >= tiles)
    def products():
        branch_part[...] = contract_cols(gelu_all[...], down_rows[...]).astype(low)
        back_part[...] = contract_cols(grad_all[...], up_rows[...]).astype(low)


def hidden_layer(shard_rows, act, grad_branch, up, down, bias):
    rows, width = act.shape
    hidden = up.shape[1]
    tile = 512
    tiles = hidden // tile

    def whole(shape):
        return pl.BlockSpec(shape, lambda i: (0, 0), pipeline_mode=pl.Buffered(1))

    def columns(height):
        return pl.BlockSpec((height, tile), lambda i: (0, jnp.minimum(i, tiles - 1)))

    later = pl.BlockSpec((tile, hidden), lambda i: (jnp.maximum(i - tiles, 0), 0))
    parts = pl.BlockSpec((rows, tile), lambda i: (0, jnp.maximum(i - tiles, 0)))
    return pl.pallas_call(
        functools.partial(hidden_kernel, shard_rows, tiles),
        grid=(tiles + width // tile,),
        out_shape=[jax.ShapeDtypeStruct((width // 2, hidden), low)] * 4
        + [jax.ShapeDtypeStruct((rows, width), low)] * 2
        + [jax.ShapeDtypeStruct((8, hidden), jnp.float32)],
        in_specs=[
            whole((rows, width)),
            whole((rows, width)),
            whole((width, rows)),
            columns(width),
            columns(width),
            columns(1),
            later,
            later,
        ],
        out_specs=[columns(width // 2)] * 4 + [parts] * 2 + [columns(8)],
        scratch_shapes=[
            vmem((width, rows), low),
            vmem((rows, hidden), low),
            vmem((rows, hidden), low),
        ],
        compiler_params=pltpu.CompilerParams(vmem_limit_bytes=60 * 1024 * 1024),
        cost_estimate=pl.CostEstimate(
            flops=12 * rows * width * hidden, bytes_accessed=100_000_000, transcendentals=0
        ),
    )(act, grad_branch, grad_branch.T, up, down, bias, up, down)


class Gather:
    def __init__(self, rows, whole, refs):
        self.rows, self.whole = rows, whole
        self.half_send, self.half_recv, self.core_send, self.core_recv = refs
        count = lax.axis_size("fsdp")
        self.group = 2 * count
        bits = [2 * b for b in (1, 2, 4, 8, 16, 32) if b < count]
        self.orders = [[1, *bits], [*bits, 1]]
        self.half = whole.shape[1] // 2
        _, self.place, self.side, self.beside, self.across = ctx_place()
        self.turn = lax.axis_index("fsdp")

    def piece(self, way, d, other=False):
        pair = flipped(self.turn, d // 2) * 2 + flipped(self.place, d % 2)
        shard = 2 * pair + (1 - self.side if other else self.side)
        return self.whole.at[
            pl.ds(pl.multiple_of(shard * self.rows, self.rows), self.rows),
            way * self.half : (way + 1) * self.half,
        ]

    def bit_copy(self, way, d, bit):
        device = self.across if bit == 1 else {"fsdp": flipped(self.turn, bit // 2)}
        piece = self.piece(way, d - bit)
        return ctx_copy(
            piece, piece, self.half_send.at[way, d], self.half_recv.at[way, d], device
        )

    def core_copy(self, way, d, other=False):
        piece = self.piece(way, d, other)
        return ctx_copy(
            piece, piece, self.core_send.at[way, d], self.core_recv.at[way, d], self.beside
        )

    def pass_on(self, way, d, after):
        for bit in self.orders[way][after:]:
            self.bit_copy(way, d + bit, bit).start()
        self.core_copy(way, d).start()

    def begin(self):
        for way in range(2):
            self.pass_on(way, 0, 0)

    def take(self, step):
        for i in range(2**step):
            for way in range(2):
                order = self.orders[way]
                d = order[step] + sum(order[k] for k in range(step) if i & 2**k)
                device = {"fsdp": flipped(self.turn, order[step] // 2)}
                piece = self.piece(way, d)
                ctx_copy(
                    piece,
                    piece,
                    self.half_send.at[way, d],
                    self.half_recv.at[way, d],
                    self.across if order[step] == 1 else device,
                ).wait_recv()
                self.pass_on(way, d, step + 1)

    def finish(self):
        for d in range(self.group):
            for way in range(2):
                self.core_copy(way, d, True).wait_recv()

    def drain(self):
        for way in range(2):
            have = [0]
            for bit in self.orders[way]:
                for d in have:
                    self.bit_copy(way, d + bit, bit).wait_send()
                have += [d + bit for d in have]
            for d in range(self.group):
                self.core_copy(way, d).wait_send()


def meet(others):
    barrier = pltpu.get_barrier_semaphore()
    for other in others:
        pl.semaphore_signal(barrier, inc=1, device_id=other, device_id_type=MESH)
    pl.semaphore_wait(barrier, len(others))


def gather_sems():
    return [pltpu.SemaphoreType.DMA((2, 2 * lax.axis_size("fsdp")))] * 4


def project_kernel(*refs):
    stream, gain, shift, bias, master_qkv, master_out, master_up, master_down = refs[:8]
    projected, act, qkv_out, out_out, up_low, down_low, whole, own, *rest = refs[8:]
    sems, out_sem = rest[:4], rest[4]
    meet(peers(("ctx", "fsdp")))
    shard_rows, groups, piece = master_qkv.shape
    rows, width = stream.shape
    gather = Gather(shard_rows, whole, sems)
    for r in range(groups):
        own[:, r * piece : (r + 1) * piece] = master_qkv[:, r, :].astype(low)
    own[:, groups * piece :] = master_out[...].astype(low)
    for way in range(2):
        gather.piece(way, 0)[...] = own[:, way * gather.half : (way + 1) * gather.half]
    gather.begin()
    for master, flat in ((master_up, up_low), (master_down, down_low)):
        for r in range(master.shape[1]):
            flat[:, r * piece : (r + 1) * piece] = master[:, r, :].astype(low)

    @pl.loop(0, rows // 64)
    def norm(i):
        place = pl.ds(pl.multiple_of(i * 64, 64), 64)
        act[place, :] = (
            normalize(stream[place, :].astype(jnp.float32))[0] * gain[...] + shift[...]
        ).astype(low)

    for step in range(len(gather.orders[0])):
        gather.take(step)
    gather.finish()
    wide = projected.shape[1]
    copies = [
        pltpu.make_async_copy(whole.at[:, :wide], qkv_out, out_sem.at[0]),
        pltpu.make_async_copy(whole.at[:, wide:], out_out, out_sem.at[1]),
    ]
    for copy in copies:
        copy.start()

    @pl.loop(0, wide // 512)
    def product(i):
        columns = pl.ds(pl.multiple_of(i * 512, 512), 512)
        projected[:, columns] = (
            jnp.dot(act[...], whole[:, columns], preferred_element_type=jnp.float32)
            + bias[:, columns]
        ).astype(low)

    for copy in copies:
        copy.wait()
    gather.drain()


def project(stream, gain, shift, bias, masters):
    rows, width = stream.shape
    wide = bias.shape[1]
    shard_rows, _, piece = masters[0].shape
    hidden = masters[2].shape[1] * piece
    in_vmem, loose = pl.BlockSpec(memory_space=vmem), pl.BlockSpec(memory_space=pl.ANY)
    depth = shard_rows * lax.axis_size("ctx") * lax.axis_size("fsdp")
    return pl.pallas_call(
        project_kernel,
        out_shape=[
            jax.ShapeDtypeStruct((rows, wide), low),
            jax.ShapeDtypeStruct((rows, width), low),
            jax.ShapeDtypeStruct((depth, wide), low),
            jax.ShapeDtypeStruct((depth, piece), low),
            jax.ShapeDtypeStruct((shard_rows, hidden), low),
            jax.ShapeDtypeStruct((shard_rows, hidden), low),
        ],
        in_specs=[in_vmem] * 8,
        out_specs=[in_vmem] * 2 + [loose] * 2 + [in_vmem] * 2,
        scratch_shapes=[vmem((depth, wide + piece), low), vmem((shard_rows, wide + piece), low)]
        + gather_sems()
        + [pltpu.SemaphoreType.DMA((2,))],
        compiler_params=pltpu.CompilerParams(
            collective_id=4, has_side_effects=True, vmem_limit_bytes=56 * 1024 * 1024
        ),
        cost_estimate=pl.CostEstimate(
            flops=2 * rows * width * wide, bytes_accessed=150_000_000, transcendentals=0
        ),
    )(stream, gain, shift, bias, *masters)


def ctx_place():
    me = lax.axis_index("ctx")
    half, side = me // 2, me % 2
    return me, half, side, {"ctx": me + 1 - 2 * side}, {"ctx": me + 2 - 4 * half}


def ctx_copy(source, target, send, recv, device):
    return pltpu.make_async_remote_copy(
        src_ref=source,
        dst_ref=target,
        send_sem=send,
        recv_sem=recv,
        device_id=device,
        device_id_type=MESH,
    )


class Spread:
    def __init__(self, block, own, pairs, send, recv):
        self.block, self.own, self.pairs, self.send, self.recv = block, own, pairs, send, recv
        self.me, self.half, self.side, self.beside, self.across = ctx_place()

    def rows(self, s, b):
        start = (s * lax.axis_size("ctx") + b) * self.block
        return pl.ds(pl.multiple_of(start, self.block), self.block)

    def copy(self, kind, s, b, own, device):
        target = self.pairs.at[self.rows(s, b)]
        wide = self.pairs.shape[1]
        source = self.own.at[s * self.block : (s + 1) * self.block, wide // 2 :] if own else target
        return ctx_copy(source, target, self.send.at[kind, s], self.recv.at[kind, s], device)

    def start(self, s):
        rows = slice(s * self.block, (s + 1) * self.block)

        @pl.when(self.half == 0)
        def over():
            self.copy(0, s, self.me, True, self.across).start()

        @pl.when(self.side == 0)
        def aside():
            self.copy(1, s, self.me, True, self.beside).start()

        self.pairs[self.rows(s, self.me)] = self.own[rows, self.pairs.shape[1] // 2 :]

    def forward(self, s):
        @pl.when(self.half == 1)
        def onward():
            self.copy(0, s, self.me - 2, False, self.across).wait_recv()
            self.copy(2, s, self.me - 2, False, self.beside).start()

    def arrive(self, s):
        @pl.when(self.half == 1)
        def second():
            self.copy(2, s, 1 - self.side, False, self.beside).wait_recv()

        @pl.when(self.side == 1)
        def first():
            self.copy(1, s, self.me - 1, False, self.beside).wait_recv()

    def drain_own(self, s):
        @pl.when(self.half == 0)
        def over():
            self.copy(0, s, self.me, True, self.across).wait_send()

        @pl.when(self.side == 0)
        def aside():
            self.copy(1, s, self.me, True, self.beside).wait_send()

    def drain(self, s):
        @pl.when(self.half == 1)
        def onward():
            self.copy(2, s, self.me - 2, False, self.beside).wait_send()


class Collect:
    def __init__(self, block, parts, beside_in, across_in, send, recv):
        self.block, self.parts = block, parts
        self.beside_in, self.across_in, self.send, self.recv = beside_in, across_in, send, recv
        self.me, self.half, self.side, self.beside, self.across = ctx_place()

    def rows(self, s, b):
        start = (s * lax.axis_size("ctx") + b) * self.block
        return pl.ds(pl.multiple_of(start, self.block), self.block)

    def aside(self, s, k, away=False):
        b = 2 * k + (self.side if away else 1 - self.side)
        return ctx_copy(
            self.parts.at[self.rows(s, b)],
            self.beside_in.at[k, s],
            self.send.at[k, s],
            self.recv.at[k, s],
            self.beside,
        )

    def over(self, s):
        return ctx_copy(
            self.parts.at[self.rows(s, self.side)],
            self.across_in.at[s],
            self.send.at[2, s],
            self.recv.at[2, s],
            self.across,
        )

    def start(self, s):
        for k in range(2):

            @pl.when(2 * k + 1 - self.side < self.me)
            def give():
                self.aside(s, k).start()

    def forward(self, s):
        for k in range(2):

            @pl.when(2 * k + self.side < self.me + 1 - 2 * self.side)
            def take():
                self.aside(s, k, True).wait_recv()

        @pl.when(self.half == 1)
        def onward():
            held = self.parts.at[self.rows(s, self.side)]
            held[...] = (
                held[...].astype(jnp.float32) + self.beside_in[0, s].astype(jnp.float32)
            ).astype(low)
            self.over(s).start()

    def finish(self, s, target):
        target[...] = self.parts[self.rows(s, self.me)]
        for k in range(2):

            @pl.when((self.side == 0) & (self.half == k))
            def near():
                target[...] = (
                    target[...].astype(jnp.float32) + self.beside_in[k, s].astype(jnp.float32)
                ).astype(low)

        @pl.when(self.half == 0)
        def far():
            self.over(s).wait_recv()
            target[...] = (
                target[...].astype(jnp.float32) + self.across_in[s].astype(jnp.float32)
            ).astype(low)

    def drain(self, s):
        for k in range(2):

            @pl.when(2 * k + 1 - self.side < self.me)
            def gave():
                self.aside(s, k).wait_send()

        @pl.when(self.half == 1)
        def sent():
            self.over(s).wait_send()


def offsets(base):
    shape = base.shape
    base[...] = (
        lax.broadcasted_iota(jnp.int32, shape, 0) - lax.broadcasted_iota(jnp.int32, shape, 1)
    ).astype(jnp.float32)


def head_scores(query, key, slope, base, j):
    far = base[...] + (j * base.shape[0]).astype(jnp.float32)
    return contract_cols(query, key) * HD ** (-0.5) - slope * jnp.abs(far)


def head_columns(h, shift=0):
    return pl.ds(pl.multiple_of(shift + h * HD, HD), HD)


def forward_heads(s, first, last, block, projected, pairs, slopes, base, context, log_total):
    me = lax.axis_index("ctx")
    count = lax.axis_size("ctx")
    own = slice(s * block, (s + 1) * block)
    wide = pairs.shape[1] // 2

    @pl.loop(first, last)
    def head(h):
        query = projected[own, head_columns(h)]

        def step(j, carry):
            peak, weight, total = carry
            rows = pl.ds(pl.multiple_of((s * count + me - j) * block, block), block)
            scores = head_scores(query, pairs[rows, head_columns(h)], slopes[h, 0:1], base, j)
            higher = jnp.maximum(peak, jnp.max(scores, axis=-1, keepdims=True))
            shrink = jnp.exp(peak - higher)
            exponent = jnp.exp(scores - higher)
            weight = weight * shrink + jnp.sum(exponent, axis=-1, keepdims=True)
            total = total * shrink + jnp.dot(
                exponent.astype(low),
                pairs[rows, head_columns(h, wide)],
                preferred_element_type=jnp.float32,
            )
            return higher, weight, total

        peak, weight, total = lax.fori_loop(
            0,
            me + 1,
            step,
            (
                jnp.full((block, 1), -1e30, jnp.float32),
                jnp.zeros((block, 1), jnp.float32),
                jnp.zeros((block, HD), jnp.float32),
            ),
        )
        context[own, head_columns(h)] = (total / weight).astype(low)
        log_total[own, head_columns(h)] = jnp.broadcast_to(peak + jnp.log(weight), (block, HD))


def backward_heads(
    s, first, last, block, projected, pairs, slopes, base, context, log_total, grad, parts, out
):
    me = lax.axis_index("ctx")
    count = lax.axis_size("ctx")
    own = slice(s * block, (s + 1) * block)
    wide = pairs.shape[1] // 2

    @pl.loop(first, last)
    def head(h):
        query = projected[own, head_columns(h)]
        incoming = grad[own, head_columns(h)]
        level = log_total[own, head_columns(h)][:, 0:1]
        mean = jnp.sum(
            incoming.astype(jnp.float32) * context[own, head_columns(h)].astype(jnp.float32),
            axis=-1,
            keepdims=True,
        )

        def step(j, total):
            rows = pl.ds(pl.multiple_of((s * count + me - j) * block, block), block)
            key = pairs[rows, head_columns(h)]
            probs = jnp.exp(head_scores(query, key, slopes[h, 0:1], base, j) - level)
            grad_probs = contract_cols(incoming, pairs[rows, head_columns(h, wide)])
            grad_scores = (probs * (grad_probs - mean)).astype(low)
            parts[rows, head_columns(h)] = (
                contract_rows(grad_scores, query) * HD ** (-0.5)
            ).astype(low)
            parts[rows, head_columns(h, wide)] = contract_rows(probs.astype(low), incoming).astype(
                low
            )
            return total + jnp.dot(grad_scores, key, preferred_element_type=jnp.float32)

        total = lax.fori_loop(0, me + 1, step, jnp.zeros((block, HD), jnp.float32))
        out[own, head_columns(h)] = (total * HD ** (-0.5)).astype(low)


def attend_kernel(n, chunks, tile, *refs):
    (
        projected,
        slopes,
        out_weight,
        stream,
        bias,
        gain,
        shift,
        up_own,
        down_own,
        full,
        middle,
        context,
        log_total,
        pairs,
        up_all,
        down_all,
        part,
        landing,
        total,
        *rest,
    ) = refs
    sems, (base, send, recv), own_sem = rest[:4], rest[4:7], rest[15]
    rows, width = full.shape
    seqs = chunks // 2
    block = rows // seqs
    heads = context.shape[1] // HD
    pace = heads // 2
    _, _, _, beside, across = ctx_place()
    greet(n, peers(("ctx", "fsdp")))
    gathers = [
        Gather(up_own.shape[0], up_all, rest[7:11]),
        Gather(down_own.shape[0], down_all, rest[11:15]),
    ]

    def place_own(i, own):
        return [
            pltpu.make_async_copy(
                own.at[:, way * gathers[i].half : (way + 1) * gathers[i].half],
                gathers[i].piece(way, 0),
                own_sem.at[i, way],
            )
            for way in range(2)
        ]

    own_copies = place_own(0, up_own) + place_own(1, down_own)
    for copy in own_copies:
        copy.start()
    finish = middle_epilogue(rows // chunks // n, (stream, bias, gain, shift), (middle,))
    line = Line(n, chunks, part, full, landing, total, sems, finish)
    spread = Spread(block, projected, pairs, send, recv)
    spread.start(0)
    offsets(base)

    def attend(s, first, last):
        if first == 0:
            spread.forward(s)
            if s + 1 < seqs:
                spread.drain_own(s)
                spread.start(s + 1)
            spread.arrive(s)
        forward_heads(
            s, first, last, block, projected, pairs, slopes, base, context, log_total
        )

    def multiply(s):
        own = slice(s * block, (s + 1) * block)

        @pl.loop(0, width // tile)
        def one(i):
            columns = pl.ds(pl.multiple_of(i * tile, tile), tile)
            part[own, columns] = contract_cols(context[own, :], out_weight[columns, :]).astype(low)

    attend(0, 0, heads)
    for copy in own_copies:
        copy.wait()
    gathers[0].begin()
    multiply(0)
    last_step = len(gathers[0].orders[0]) - 1
    for t in range(1, chunks + 2 * n - 1):
        for c in range(chunks):
            if 0 < t - c < 2 * n:
                line.stage(c, t - c)
        s = (t + 1) // 2
        if s < seqs:
            attend(s, 0 if t % 2 else pace, pace if t % 2 else heads)
            if t % 2 == 0:
                multiply(s)
        if t == 2:
            gathers[1].begin()
        for i, (early, late) in enumerate(((5, 7), (8, 11))):
            if t == early:
                for step in range(last_step):
                    gathers[i].take(step)
            if t == late:
                gathers[i].take(last_step)
    spread.drain_own(seqs - 1)
    for s in range(seqs):
        spread.drain(s)
    for gather in gathers:
        gather.finish()
        gather.drain()
    line.drain()


def backward_kernel(n, chunks, shard_rows, *refs):
    (
        part,
        middle,
        bias,
        grad_attn,
        out_weight,
        projected,
        pairs,
        context,
        log_total,
        slopes,
        act,
        full,
        grad_projected,
        given,
        kept,
        landing,
        total,
        *rest,
    ) = refs
    sems, (base, grad_context, parts, beside_in, across_in, send, recv) = rest[:4], rest[4:]
    rows, width = full.shape
    seqs = chunks // 2
    block = rows // seqs
    heads = context.shape[1] // HD
    wide = context.shape[1]
    pace = heads // 2
    _, _, _, beside, across = ctx_place()
    greet(n, [beside, across])
    finish = output_epilogue(rows // chunks // n, (middle, bias), ())
    line = Line(n, chunks, part, full, landing, total, sems, finish)
    collect = Collect(block, parts, beside_in, across_in, send, recv)
    offsets(base)

    def backward(s, first, last):
        own = slice(s * block, (s + 1) * block)
        if first == 0:
            grad_context[own, :] = jnp.dot(
                grad_attn[own, :], out_weight[...], preferred_element_type=jnp.float32
            ).astype(low)
        backward_heads(
            s,
            first,
            last,
            block,
            projected,
            pairs,
            slopes,
            base,
            context,
            log_total,
            grad_context,
            parts,
            grad_projected,
        )
        if last == heads:
            collect.start(s)

    def finished(s):
        collect.finish(s, grad_projected.at[s * block : (s + 1) * block, wide:])

    def features(source, right, columns, first, last):
        @pl.loop(first, last)
        def one(i):
            place = pl.ds(pl.multiple_of(i * 256, 256), 256)
            value = contract_rows(source[:, place], right[...])
            split_store(value, i, shard_rows, given, kept, columns)

    attn_columns = slice(0, 3 * wide)
    out_columns = slice(3 * wide, 4 * wide)

    tiles = width // 256
    tasks = []
    for s in range(seqs):
        tasks.append([functools.partial(backward, s, 0, pace)])
        tasks.append([functools.partial(backward, s, pace, heads)])
    tasks += [[] for _ in range(chunks + 2 * n - 2 - len(tasks))]
    for s in range(seqs):
        tasks[2 * s + 2].append(functools.partial(collect.forward, s))
    after = 2 * seqs + 1
    tasks[after].append(functools.partial(features, grad_attn, context, out_columns, 0, tiles))
    for s in range(seqs):
        tasks[after + s].append(functools.partial(finished, s))
    left = len(tasks) - after - seqs
    for i in range(left):
        tasks[after + seqs + i].append(
            functools.partial(
                features,
                act,
                grad_projected,
                attn_columns,
                tiles * i // left,
                tiles * (i + 1) // left,
            )
        )
    for t in range(1, chunks + 2 * n - 1):
        for c in range(chunks):
            if 0 < t - c < 2 * n:
                line.stage(c, t - c)
        for task in tasks[t - 1]:
            task()
    for s in range(seqs):
        collect.drain(s)
    line.drain()


def fused_call(body, collective, operands, outs, scratch, flops, loose=0, loose_outs=0):
    whole = pl.BlockSpec(memory_space=vmem)
    away = pl.BlockSpec(memory_space=pl.ANY)
    specs = [whole] * (len(operands) - loose) + [away] * loose
    return pl.pallas_call(
        body,
        out_shape=outs,
        in_specs=specs,
        out_specs=[whole] * (len(outs) - loose_outs) + [away] * loose_outs,
        scratch_shapes=scratch,
        compiler_params=pltpu.CompilerParams(
            collective_id=collective,
            has_side_effects=True,
            vmem_limit_bytes=60 * 1024 * 1024,
        ),
        cost_estimate=pl.CostEstimate(flops=flops, bytes_accessed=200_000_000, transcendentals=0),
    )(*operands)


def local(
    inputs,
    cotangent,
    master_qkv,
    qkv_moment1,
    qkv_moment2,
    master_out,
    out_moment1,
    out_moment2,
    master_up,
    up_moment1,
    up_moment2,
    master_down,
    down_moment1,
    down_moment2,
    norm_gains,
    gain_moment1,
    gain_moment2,
    shared_biases,
    shared_moment1,
    shared_moment2,
    split_biases,
    split_moment1,
    split_moment2,
):
    seq_count, block_len, model_width = inputs.shape
    row_count = seq_count * block_len
    width_part = master_qkv.shape[2]
    hidden_rows = master_up.shape[1]
    local_heads = width_part // HD
    tp_count = lax.axis_size("tp")
    chunks = 2 * seq_count
    own_rows = row_count // chunks // tp_count

    def own_part(values):
        blocks = values.reshape(chunks, tp_count * own_rows, model_width)
        taken = lax.dynamic_slice_in_dim(blocks, lax.axis_index("tp") * own_rows, own_rows, axis=1)
        return taken.reshape(-1, model_width)

    own_shape = jax.ShapeDtypeStruct((row_count // tp_count, model_width), jnp.float32)
    sums_shape = jax.ShapeDtypeStruct((8, model_width), jnp.float32)
    gains = [norm_gains[i : i + 1] for i in range(2)]
    shared = [shared_biases[i : i + 1] for i in range(4)]
    inputs_own = own_part(inputs)
    cotangent_own = own_part(cotangent)

    projected_bias = jnp.concatenate(
        [split_biases[0], jnp.zeros((width_part,), jnp.float32), split_biases[1]]
    )
    projected, act_one, qkv_flat, out_flat, up_low, down_low = project(
        inputs.reshape(row_count, model_width),
        gains[0],
        shared[0],
        projected_bias[None],
        (master_qkv, master_out, master_up, master_down),
    )
    head_ids = (lax.axis_index("tp") * local_heads + jnp.arange(local_heads)).astype(jnp.float32)
    slopes = jnp.power(2.0, -8.0 * (head_ids + 1.0) / (local_heads * lax.axis_size("tp")))
    slopes = jnp.broadcast_to(slopes[:, None, None], (local_heads, 8, block_len))
    sems = line_scratch(tp_count, chunks, row_count, model_width)
    pair_rows = row_count * lax.axis_size("ctx")
    square = vmem((block_len, block_len), jnp.float32)
    pair_sems = [pltpu.SemaphoreType.DMA((3, seq_count))] * 2
    act_two, middle, context, log_total, pairs, up_flat, down_flat = fused_call(
        functools.partial(attend_kernel, tp_count, chunks, 256),
        0,
        (
            projected,
            slopes,
            out_flat,
            inputs_own,
            shared[2],
            gains[1],
            shared[1],
            up_low,
            down_low,
        ),
        [
            jax.ShapeDtypeStruct((row_count, model_width), low),
            own_shape,
            jax.ShapeDtypeStruct((row_count, width_part), low),
            jax.ShapeDtypeStruct((row_count, width_part), jnp.float32),
            jax.ShapeDtypeStruct((pair_rows, 2 * width_part), low),
            jax.ShapeDtypeStruct((model_width, hidden_rows * width_part), low),
            jax.ShapeDtypeStruct((model_width, hidden_rows * width_part), low),
        ],
        sems
        + [square]
        + pair_sems
        + gather_sems()
        + gather_sems()
        + [pltpu.SemaphoreType.DMA((2, 2))],
        4 * row_count * model_width * width_part,
        2,
        2,
    )
    down_given, down_kept, up_given, up_kept, branch_part, back_part, bias_sum = hidden_layer(
        master_qkv.shape[0],
        act_two,
        cotangent.reshape(row_count, model_width),
        up_flat,
        down_flat,
        split_biases[2:].reshape(1, -1),
    )
    grad_attn, grad_middle, sums_two, sum_down, sum_up = tp_sum(
        tp_count,
        chunks,
        attn_epilogue,
        2,
        (back_part,),
        (middle, cotangent_own, gains[1]),
        [own_shape, sums_shape],
        [(down_given, down_kept), (up_given, up_kept)],
        ((2, 7), (4, 11)),
    )
    pair_block = (block_len, 2 * width_part)
    output, grad_projected, attn_given, attn_kept = fused_call(
        functools.partial(backward_kernel, tp_count, chunks, master_qkv.shape[0]),
        1,
        (
            branch_part,
            middle,
            shared[3],
            grad_attn,
            out_flat,
            projected,
            pairs,
            context,
            log_total,
            slopes,
            act_one,
        ),
        [
            jax.ShapeDtypeStruct((row_count, model_width), low),
            jax.ShapeDtypeStruct((row_count, 3 * width_part), low),
            jax.ShapeDtypeStruct((model_width // 2, 4 * width_part), low),
            jax.ShapeDtypeStruct((model_width // 2, 4 * width_part), low),
        ],
        sems[1:]
        + [
            square,
            vmem((row_count, width_part), low),
            vmem((pair_rows, 2 * width_part), low),
            vmem((2, seq_count, *pair_block), low),
            vmem((seq_count, *pair_block), low),
        ]
        + pair_sems,
        12 * row_count * model_width * width_part,
    )
    output = output.reshape(seq_count, block_len, model_width)
    query_low = grad_projected[:, :width_part]
    value_low = grad_projected[:, 2 * width_part :]
    split_grads = jnp.concatenate(
        [
            jnp.sum(query_low, axis=0, dtype=jnp.float32)[None],
            jnp.sum(value_low, axis=0, dtype=jnp.float32)[None],
            bias_sum[0].reshape(hidden_rows, width_part),
        ],
        axis=0,
    )
    vectors = jnp.concatenate(
        [
            jnp.zeros((2, model_width), jnp.float32),
            sums_two[0:3],
            jnp.sum(cotangent_own, axis=0, dtype=jnp.float32)[None],
            jnp.zeros((2, model_width), jnp.float32),
        ]
    )
    vectors = jnp.concatenate([vectors, jnp.pad(split_grads, ((0, 2), (0, 0)))], axis=1)
    input_low, _, vector_sum, sum_attn = tp_sum(
        tp_count,
        chunks,
        input_epilogue,
        3,
        (grad_projected, qkv_flat),
        (inputs_own, grad_middle, gains[0]),
        [sums_shape],
        [(attn_given, attn_kept)],
        ((2, 8),),
        vectors,
    )
    input_grad = input_low.astype(jnp.float32).reshape(seq_count, block_len, model_width)

    sum_attn = sum_attn.astype(jnp.float32)
    sum_qkv = sum_attn[:, : 3 * width_part].reshape(master_qkv.shape)
    sum_out = sum_attn[:, 3 * width_part :]
    sum_up = sum_up.astype(jnp.float32).reshape(master_up.shape)
    sum_down = sum_down.astype(jnp.float32).reshape(master_down.shape)
    gain_sum = jnp.concatenate([vector_sum[0:1, :model_width], vector_sum[2:3, :model_width]])
    shared_sum = jnp.concatenate([vector_sum[1:2, :model_width], vector_sum[3:6, :model_width]])
    split_sum = vector_sum[: 2 + hidden_rows, model_width:]
    q_one, q_two, q_new = adam_update(
        master_qkv, qkv_moment1, qkv_moment2, sum_qkv, matrix_rate, True
    )
    o_one, o_two, o_new = adam_update(
        master_out, out_moment1, out_moment2, sum_out, matrix_rate, True
    )
    u_one, u_two, u_new = adam_update(master_up, up_moment1, up_moment2, sum_up, matrix_rate, True)
    d_one, d_two, d_new = adam_update(
        master_down, down_moment1, down_moment2, sum_down, matrix_rate, True
    )
    g_one, g_two, g_new = adam_update(
        norm_gains, gain_moment1, gain_moment2, gain_sum, vector_rate, False
    )
    s_one, s_two, s_new = adam_update(
        shared_biases, shared_moment1, shared_moment2, shared_sum, vector_rate, False
    )
    p_one, p_two, p_new = adam_update(
        split_biases, split_moment1, split_moment2, split_sum, vector_rate, False
    )
    return (
        output,
        input_grad,
        q_one,
        q_two,
        q_new,
        q_new.astype(jnp.bfloat16),
        o_one,
        o_two,
        o_new,
        o_new.astype(jnp.bfloat16),
        u_one,
        u_two,
        u_new,
        u_new.astype(jnp.bfloat16),
        d_one,
        d_two,
        d_new,
        d_new.astype(jnp.bfloat16),
        g_one,
        g_two,
        g_new,
        s_one,
        s_two,
        s_new,
        p_one,
        p_two,
        p_new,
    )


def solution(mesh):
    return jax.shard_map(
        local,
        mesh=mesh,
        in_specs=(
            P("fsdp", "ctx", None),
            P("fsdp", "ctx", None),
            P(("fsdp", "ctx"), None, "tp"),
            P(("fsdp", "ctx"), None, "tp"),
            P(("fsdp", "ctx"), None, "tp"),
            P(("fsdp", "ctx"), "tp"),
            P(("fsdp", "ctx"), "tp"),
            P(("fsdp", "ctx"), "tp"),
            P(("fsdp", "ctx"), None, "tp"),
            P(("fsdp", "ctx"), None, "tp"),
            P(("fsdp", "ctx"), None, "tp"),
            P(("fsdp", "ctx"), None, "tp"),
            P(("fsdp", "ctx"), None, "tp"),
            P(("fsdp", "ctx"), None, "tp"),
            P(),
            P(),
            P(),
            P(),
            P(),
            P(),
            P(None, "tp"),
            P(None, "tp"),
            P(None, "tp"),
        ),
        out_specs=(
            P("fsdp", "ctx", None),
            P("fsdp", "ctx", None),
            P(("fsdp", "ctx"), None, "tp"),
            P(("fsdp", "ctx"), None, "tp"),
            P(("fsdp", "ctx"), None, "tp"),
            P(("fsdp", "ctx"), None, "tp"),
            P(("fsdp", "ctx"), "tp"),
            P(("fsdp", "ctx"), "tp"),
            P(("fsdp", "ctx"), "tp"),
            P(("fsdp", "ctx"), "tp"),
            P(("fsdp", "ctx"), None, "tp"),
            P(("fsdp", "ctx"), None, "tp"),
            P(("fsdp", "ctx"), None, "tp"),
            P(("fsdp", "ctx"), None, "tp"),
            P(("fsdp", "ctx"), None, "tp"),
            P(("fsdp", "ctx"), None, "tp"),
            P(("fsdp", "ctx"), None, "tp"),
            P(("fsdp", "ctx"), None, "tp"),
            P(),
            P(),
            P(),
            P(),
            P(),
            P(),
            P(None, "tp"),
            P(None, "tp"),
            P(None, "tp"),
        ),
        check_vma=False,
    )
```

```python
import functools

import jax
import jax.numpy as jnp
from jax import lax
from jax.experimental import pallas as pl
from jax.experimental.pallas import tpu as pltpu
from jax.sharding import PartitionSpec as P

HD = 128
STEP = 10


norm_epsilon = 1e-05
matrix_rate = 0.04
vector_rate = 0.4
decay_weight = 0.1
decay_rate = 0.5
adam_epsilon = 1e-08
low = jnp.bfloat16


def normalize(values):
    center = jnp.mean(values, axis=-1, keepdims=True)
    shifted = values - center
    variance = jnp.mean(shifted * shifted, axis=-1, keepdims=True)
    inverse = lax.rsqrt(variance + norm_epsilon)
    return (shifted * inverse, inverse)


def norm_back(incoming, normed, inverse, gain):
    scaled = incoming * gain
    return inverse * (
        scaled
        - jnp.mean(scaled, axis=-1, keepdims=True)
        - normed * jnp.mean(scaled * normed, axis=-1, keepdims=True)
    )


def gelu_tanh(values):
    return (
        0.5
        * values
        * (1.0 + jnp.tanh(0.7978845608028654 * (values + 0.044715 * values * values * values)))
    )


def adam_update(master, moment_one, moment_two, gradient, rate, decayed):
    first = decay_rate * moment_one + (1.0 - decay_rate) * gradient
    second = decay_rate * moment_two + (1.0 - decay_rate) * gradient * gradient
    correction = 1.0 - decay_rate**STEP
    update = first / correction / (jnp.sqrt(second / correction) + adam_epsilon)
    if decayed:
        update = update + decay_weight * master
    return (first, second, master - rate * update)


def adam_kernel(flat, master, one, two, one_out, two_out, new_out, copy_out, *scratch):
    if scratch:
        gradient = scratch[0]
        piece = master.shape[2]
        for r in range(master.shape[1]):
            gradient[:, r, :] = flat[:, r * piece : (r + 1) * piece].astype(jnp.float32)
        gradient = gradient[...]
    else:
        gradient = flat[...].astype(jnp.float32)[None]
    first, second, new = adam_update(master[...], one[...], two[...], gradient, matrix_rate, True)
    one_out[...] = first
    two_out[...] = second
    new_out[...] = new
    copy_out[...] = new.astype(low)


def adam_matrix(flat, master, one, two):
    full = jax.ShapeDtypeStruct(master.shape, jnp.float32)
    if master.shape[0] == flat.shape[0]:
        rows, groups, piece = master.shape
        tile, steps = 32, rows // 32
        block = pl.BlockSpec((tile, groups, piece), lambda i: (i, 0, 0))
        flat_block = pl.BlockSpec((tile, groups * piece), lambda i: (i, 0))
        scratch = [pltpu.VMEM((tile, groups, piece), jnp.float32)]
    else:
        steps, rows, piece = master.shape
        groups, scratch = steps, []
        block = pl.BlockSpec((1, rows, piece), lambda i: (i, 0, 0))
        flat_block = pl.BlockSpec((rows, piece), lambda i: (0, i))
    return pl.pallas_call(
        adam_kernel,
        grid=(steps,),
        out_shape=[full] * 3 + [jax.ShapeDtypeStruct(master.shape, low)],
        in_specs=[flat_block] + [block] * 3,
        out_specs=[block] * 4,
        scratch_shapes=scratch,
        cost_estimate=pl.CostEstimate(
            flops=20 * rows * groups * piece,
            bytes_accessed=28 * rows * groups * piece,
            transcendentals=2 * rows * groups * piece,
        ),
    )(flat, master, one, two)


def contract_rows(left, right):
    return lax.dot_general(
        left, right, (((0,), (0,)), ((), ())), preferred_element_type=jnp.float32
    )


def contract_cols(left, right):
    return lax.dot_general(
        left, right, (((1,), (1,)), ((), ())), preferred_element_type=jnp.float32
    )


MESH = pl.DeviceIdType.MESH
vmem = pltpu.VMEM


class Line:
    def __init__(self, n, chunks, part, full, landing, total, sems, finish, pace=1):
        self.n, self.chunks = n, chunks
        self.part, self.full, self.landing, self.total = part, full, landing, total
        self.sum_send, self.sum_recv, self.row_send, self.row_recv = sems
        self.finish = finish
        self.z = lax.axis_index("tp")
        self.chunk_rows = full.shape[0] // chunks
        self.own = self.chunk_rows // n
        self.pace = pace
        self.slots = self.start(chunks - 1) + 2 * n - 1

    def start(self, c):
        return c // 2 * self.pace

    def slot(self, t):
        for c in range(self.chunks):
            if 0 < t - self.start(c) < 2 * self.n:
                self.stage(c, t - self.start(c))

    def place(self, c, j):
        return pl.ds(pl.multiple_of(c * self.chunk_rows + j * self.own, self.own), self.own)

    def flow(self, d):
        return self.z if d == 0 else self.n - 1 - self.z

    def toward(self, d, away):
        return {"tp": self.z + (1 if (d == 0) != away else -1)}

    def sum_copy(self, d, c, k, source, away=False):
        return pltpu.make_async_remote_copy(
            src_ref=source,
            dst_ref=self.landing.at[d, c, k - 1],
            send_sem=self.sum_send.at[d, c, k - 1],
            recv_sem=self.sum_recv.at[d, c, k - 1],
            device_id=self.toward(d, away),
            device_id_type=MESH,
        )

    def sum_arrive(self, d, c, k):
        self.sum_copy(d, c, k, self.landing.at[d, c, k - 1], True).wait_recv()

    def row_copy(self, d, c, k, away=False):
        back = k if away else k - 1
        rows = self.place(c, self.z - back if d == 0 else self.z + back)
        return pltpu.make_async_remote_copy(
            src_ref=self.full.at[rows],
            dst_ref=self.full.at[rows],
            send_sem=self.row_send.at[d, c, k - 1],
            recv_sem=self.row_recv.at[d, c, k - 1],
            device_id=self.toward(d, away),
            device_id_type=MESH,
        )

    def stage(self, c, s):
        n, z = self.n, self.z
        if s < n:
            for d in range(2):
                q = self.flow(d)
                rows = self.place(c, z + n - s if d == 0 else z - n + s)

                @pl.when(q == 0)
                def first():
                    self.sum_copy(d, c, s, self.part.at[rows]).start()

                if s > 1:

                    @pl.when((q >= 1) & (q < s))
                    def later():
                        self.sum_arrive(d, c, s - 1)
                        held = self.landing.at[d, c, s - 2]
                        held[...] = (
                            self.part[rows].astype(jnp.float32) + held[...].astype(jnp.float32)
                        ).astype(low)
                        self.sum_copy(d, c, s, held).start()

        elif s == n:
            rows = self.place(c, z)
            self.total[...] = self.part[rows].astype(jnp.float32)
            for d in range(2):

                @pl.when(self.flow(d) >= 1)
                def ended():
                    self.sum_arrive(d, c, n - 1)
                    self.total[...] += self.landing[d, c, n - 2].astype(jnp.float32)

            self.full[rows] = self.finish(c, self.total[...]).astype(low)
            for d in range(2):

                @pl.when(self.flow(d) < n - 1)
                def spread():
                    self.row_copy(d, c, 1).start()

        else:
            k = s - n + 1
            for d in range(2):
                q = self.flow(d)

                @pl.when(q >= k - 1)
                def arrived():
                    self.row_copy(d, c, k - 1, True).wait_recv()

                if k < n:

                    @pl.when((q >= k - 1) & (q < n - 1))
                    def onward():
                        self.row_copy(d, c, k).start()

    def drain(self):
        n = self.n
        for c in range(self.chunks):
            for d in range(2):
                q = self.flow(d)
                for k in range(1, n):

                    @pl.when(q < k)
                    def sum_sent():
                        self.sum_copy(d, c, k, self.landing.at[d, c, k - 1]).wait_send()

                    @pl.when((q >= k - 1) & (q < n - 1))
                    def row_sent():
                        self.row_copy(d, c, k).wait_send()


def peers(axes):
    found = []
    for axis in axes:
        bit = 1
        while bit < lax.axis_size(axis):
            me = lax.axis_index(axis)
            found.append({axis: me + bit * (1 - 2 * ((me // bit) % 2))})
            bit *= 2
    return found


def greet(n, others):
    z = lax.axis_index("tp")
    barrier = pltpu.get_barrier_semaphore()

    @pl.when(z > 0)
    def to_lower():
        pl.semaphore_signal(barrier, inc=1, device_id={"tp": z - 1}, device_id_type=MESH)

    @pl.when(z < n - 1)
    def to_upper():
        pl.semaphore_signal(barrier, inc=1, device_id={"tp": z + 1}, device_id_type=MESH)

    for other in others:
        pl.semaphore_signal(barrier, inc=1, device_id=other, device_id_type=MESH)

    @pl.when((z > 0) & (z < n - 1))
    def from_both():
        pl.semaphore_wait(barrier, 2 + len(others))

    @pl.when((z == 0) | (z == n - 1))
    def from_one():
        pl.semaphore_wait(barrier, 1 + len(others))


def line_scratch(n, chunks, rows, width):
    own = rows // chunks // n
    return [
        vmem((rows, width), low),
        vmem((2, chunks, n - 1, own, width), low),
        vmem((own, width), jnp.float32),
    ] + [pltpu.SemaphoreType.DMA((2, chunks, n - 1))] * 4


class Exchange:
    def __init__(self, whole, start, arrived, send_sem, recv_sem):
        self.whole, self.held, self.arrived = whole, start, arrived
        self.send_sem, self.recv_sem = send_sem, recv_sem
        self.inner = len(peers(("ctx", "fsdp")))
        self.peers = peers(("ctx", "fsdp", "tp"))

    def copy(self, i):
        columns = slice(None) if i < self.inner else slice(0, self.whole)
        return pltpu.make_async_remote_copy(
            src_ref=self.held.at[i, :, columns],
            dst_ref=self.arrived.at[i, :, columns],
            send_sem=self.send_sem.at[i],
            recv_sem=self.recv_sem.at[i],
            device_id=self.peers[i],
            device_id_type=MESH,
        )

    def step(self, i):
        if i > 0:
            self.copy(i - 1).wait_recv()
            if i - 1 < self.inner:
                self.held[i] = self.held[i - 1] + self.arrived[i - 1]
            else:
                self.held[i] = self.held[i - 1]
                self.held[i, :, : self.whole] += self.arrived[i - 1, :, : self.whole]
        if i < len(self.peers):
            self.copy(i).start()

    def drain(self):
        for i in range(len(self.peers)):
            self.copy(i).wait_send()


def sum_kernel(n, chunks, epilogue, counts, with_product, with_vectors, plan, *refs):
    refs = list(refs)

    def taken(count):
        out = refs[:count]
        del refs[:count]
        return out

    operands = taken(2 if with_product else 1)
    extras, weights = taken(counts[0]), taken(2 * counts[2])
    (full,) = taken(1)
    outs, sums = taken(counts[1]), taken(counts[2])
    part = taken(1)[0] if with_product else operands[0]
    landing, total = taken(2)
    sems = taken(4)
    moves = [
        Halving(weights[2 * i], weights[2 * i + 1], sums[i], taken(8)) for i in range(counts[2])
    ]
    rows, width = full.shape
    chunk_rows = rows // chunks
    block = 2 * chunk_rows
    greet(n, peers(("ctx", "fsdp", "tp") if with_vectors else ("ctx", "fsdp")))
    finish = epilogue(chunk_rows // n, extras, outs)
    line = Line(n, chunks, part, full, landing, total, sems, finish)

    def multiply(b):
        if not with_product:
            return
        own = slice(b * block, (b + 1) * block)

        @pl.loop(0, width // 256)
        def one(i):
            columns = pl.ds(pl.multiple_of(i * 256, 256), 256)
            part[own, columns] = contract_cols(operands[0][own, :], operands[1][columns, :]).astype(
                low
            )

    for move in moves:
        move.start()
    multiply(0)
    ended = line.start(chunks - 1) + n
    vectors = None
    for t in range(1, line.slots + 1):
        line.slot(t)
        if t < rows // block:
            multiply(t)
        for i, move in enumerate(moves):
            if t == plan[i][0]:
                move.core_step()
            if t == plan[i][1]:
                move.middle_step()
        if with_vectors and t == ended:
            held, arrived, send_sem, recv_sem = refs
            vectors = Exchange(width, held, arrived, send_sem, recv_sem)
            held[0] = extras[-1][...]
            held[0, 0:2, :width] = outs[0][0:2]
        if vectors is not None and t - ended <= len(vectors.peers):
            vectors.step(t - ended)
            done = t - ended
    if vectors is not None:
        for i in range(done + 1, len(vectors.peers) + 1):
            vectors.step(i)
        outs[-1][...] = vectors.held[len(vectors.peers)]
        vectors.drain()
    for move in moves:
        move.last_step()
    for move in moves:
        move.drain()
    line.drain()


def tp_sum(
    n, chunks, epilogue, collective, operands, extras, out_shapes, weights, plan, vectors=None
):
    rows = operands[0].shape[0]
    with_product = len(operands) == 2
    width = operands[-1].shape[0] if with_product else operands[0].shape[1]
    outs = list(out_shapes)
    scratch = line_scratch(n, chunks, rows, width)
    if not with_product:
        scratch = scratch[1:]
    count = lax.axis_size("fsdp")
    sums = []
    for given, _ in weights:
        own = jax.ShapeDtypeStruct((given.shape[0] // (2 * count), given.shape[1]), low)
        sums.append(own)
        scratch += halving_scratch(count, *own.shape)
    if vectors is not None:
        extras = (*extras, vectors)
        outs.append(jax.ShapeDtypeStruct(vectors.shape, jnp.float32))
        steps = len(peers(("ctx", "fsdp", "tp")))
        scratch += [
            vmem((steps + 1, *vectors.shape), jnp.float32),
            vmem((steps, *vectors.shape), jnp.float32),
            pltpu.SemaphoreType.DMA((steps,)),
            pltpu.SemaphoreType.DMA((steps,)),
        ]
    counts = (len(extras), len(outs), len(weights))
    return fused_call(
        functools.partial(
            sum_kernel, n, chunks, epilogue, counts, with_product, vectors is not None, plan
        ),
        collective,
        (*operands, *extras, *[ref for pair in weights for ref in pair]),
        [jax.ShapeDtypeStruct((rows, width), low)] + outs + sums,
        scratch,
        12 * rows * width * 512,
        2 * len(weights),
    )


def middle_epilogue(own, extras, outs):
    stream, bias, gain, shift = extras
    (middle,) = outs

    def finish(c, total):
        rows = slice(c * own, (c + 1) * own)
        value = stream[rows].astype(jnp.float32) + total + bias[...]
        middle[rows] = value
        return normalize(value)[0] * gain[...] + shift[...]

    return finish


def output_epilogue(own, extras, outs):
    middle, bias = extras

    def finish(c, total):
        return middle[c * own : (c + 1) * own] + total + bias[...]

    return finish


def attn_epilogue(own, extras, outs):
    middle, cotangent, gain = extras[:3]
    grad_middle, sums = outs[:2]
    sums[...] = jnp.zeros_like(sums)

    def finish(c, total):
        rows = slice(c * own, (c + 1) * own)
        normed, inverse = normalize(middle[rows])
        value = cotangent[rows].astype(jnp.float32) + norm_back(total, normed, inverse, gain[...])
        grad_middle[rows] = value
        sums[0:1] += jnp.sum(total * normed, axis=0, keepdims=True)
        sums[1:2] += jnp.sum(total, axis=0, keepdims=True)
        sums[2:3] += jnp.sum(value.astype(low).astype(jnp.float32), axis=0, keepdims=True)
        return value

    return finish


def input_epilogue(own, extras, outs):
    stream, grad_middle, gain = extras[:3]
    sums = outs[0]
    sums[...] = jnp.zeros_like(sums)

    def finish(c, total):
        rows = slice(c * own, (c + 1) * own)
        normed, inverse = normalize(stream[rows].astype(jnp.float32))
        sums[0:1] += jnp.sum(total * normed, axis=0, keepdims=True)
        sums[1:2] += jnp.sum(total, axis=0, keepdims=True)
        return grad_middle[rows] + norm_back(total, normed, inverse, gain[...])

    return finish


def flipped(index, bits):
    out, bit = index, 1
    while bit <= bits:
        if bits & bit:
            out = out + bit * (1 - 2 * ((index // bit) % 2))
        bit *= 2
    return out


class Halving:
    def __init__(self, given, kept, out, refs):
        self.given, self.kept, self.out = given, kept, out
        self.mine, self.held, self.landing = refs[:3]
        self.own_sem, self.core_send, self.core_recv, self.half_send, self.half_recv = refs[3:]
        self.count = lax.axis_size("fsdp")
        self.rows = out.shape[0]
        self.half = out.shape[1] // 2
        _, self.place, _, self.beside, self.across = ctx_place()
        self.turn = lax.axis_index("fsdp")

    def shards(self):
        return [(far, over) for far in range(self.count - 1, -1, -1) for over in (1, 0)]

    def shard(self, far, over):
        p = flipped(self.turn, far) * 2 + flipped(self.place, over)
        return pl.ds(pl.multiple_of(p * self.rows, self.rows), self.rows)

    def core_copy(self, far, over):
        i = 2 * far + over
        return ctx_copy(
            self.given.at[self.shard(far, over)],
            self.held.at[i],
            self.core_send.at[i],
            self.core_recv.at[i],
            self.beside,
        )

    def own_copy(self, far, over):
        i = 2 * far + over
        return pltpu.make_async_copy(
            self.kept.at[self.shard(far, over)], self.mine.at[i], self.own_sem.at[i]
        )

    def half_copy(self, way, bit, far, over):
        n = self.count
        if way == 0:
            i = n + far - 1 if bit else far
        else:
            i = 2 * n - 1 + 2 * (far - 1) + over if bit else 4 * n - 3
        device = {"fsdp": flipped(self.turn, bit)} if bit else self.across
        columns = slice(way * self.half, (way + 1) * self.half)
        copy = ctx_copy(
            self.held.at[2 * far + over, :, columns],
            self.landing.at[i],
            self.half_send.at[i],
            self.half_recv.at[i],
            device,
        )
        return copy, i, columns

    def start(self):
        for far, over in self.shards():
            self.core_copy(far, over).start()
        for far, over in self.shards():
            self.own_copy(far, over).start()

    def send(self, way, bit, far, over):
        self.half_copy(way, bit, far, over)[0].start()

    def take(self, way, bit, far, over):
        copy, i, columns = self.half_copy(way, bit, far, over)
        copy.wait_recv()
        far, over = (far - bit, over) if bit else (far, 0)
        k = 2 * far + over
        self.held[k, :, columns] = add_low(self.held[k, :, columns], self.landing[i])
        return far

    def core_step(self):
        top = self.count // 2
        for far, over in self.shards():
            k = 2 * far + over
            self.own_copy(far, over).wait()
            self.core_copy(far, over).wait_recv()
            self.held[k] = add_low(self.held[k], self.mine[k])
            if over:
                self.send(0, 0, far, over)
            if far >= top:
                self.send(1, top, far, over)

    def middle_step(self):
        top = self.count // 2
        for far in range(self.count - 1, -1, -1):
            self.take(0, 0, far, 1)
            if far >= top:
                self.send(0, top, far, 0)
        bit = top
        while bit > 1:
            for far in range(2 * bit - 1, bit - 1, -1):
                left = self.take(0, bit, far, 0)
                if left >= bit // 2:
                    self.send(0, bit // 2, left, 0)
            bit //= 2
        bit = top
        while bit:
            for far in range(2 * bit - 1, bit - 1, -1):
                for over in (1, 0):
                    left = self.take(1, bit, far, over)
                    if bit > 1 and left >= bit // 2:
                        self.send(1, bit // 2, left, over)
                    if bit == 1 and over:
                        self.send(1, 0, 0, 1)
            bit //= 2

    def last_step(self):
        self.take(0, 1, 1, 0)
        self.take(1, 0, 0, 1)
        self.out[...] = self.held[0]

    def drain(self):
        for far in range(self.count):
            for over in range(2):
                self.core_copy(far, over).wait_send()
            self.half_copy(0, 0, far, 1)[0].wait_send()
            if far:
                bit = 1
                while 2 * bit <= far:
                    bit *= 2
                self.half_copy(0, bit, far, 0)[0].wait_send()
                for over in range(2):
                    self.half_copy(1, bit, far, over)[0].wait_send()
        self.half_copy(1, 0, 0, 1)[0].wait_send()


def add_low(left, right):
    return (left.astype(jnp.float32) + right.astype(jnp.float32)).astype(low)


def halving_scratch(count, rows, width):
    sem = pltpu.SemaphoreType.DMA
    return (
        [vmem((2 * count, rows, width), low)] * 2
        + [vmem((4 * count - 2, rows, width // 2), low)]
        + [sem((2 * count,))] * 3
        + [sem((4 * count - 2,))] * 2
    )


def split_store(value, tile, rows, given, kept, columns):
    side = lax.axis_index("ctx") % 2
    height = value.shape[0]
    step = min(rows, height)
    for k in range(height // step):
        start = tile * height + k * step
        shard = start // rows
        place = shard // 2 * rows + start % rows
        place = pl.ds(place if isinstance(place, int) else pl.multiple_of(place, step), step)
        piece = value[k * step : (k + 1) * step].astype(low)

        @pl.when((shard + side) % 2 == 0)
        def keep():
            kept[place, columns] = piece

        @pl.when((shard + side) % 2 == 1)
        def give():
            given[place, columns] = piece


def hidden_kernel(shard_rows, tiles, *refs):
    (
        act,
        grad_branch,
        grad_turned,
        up,
        down,
        bias,
        up_rows,
        down_rows,
        down_given,
        down_kept,
        up_given,
        up_kept,
        branch_part,
        back_part,
        bias_sum,
        act_turned,
        gelu_all,
        grad_all,
    ) = refs
    i = pl.program_id(0)
    width = act.shape[1]
    tile = up.shape[1]

    @pl.when(i == 0)
    def begin():
        @pl.loop(0, width // 256)
        def turn(k):
            place = pl.ds(pl.multiple_of(k * 256, 256), 256)
            act_turned[place, :] = act[:, place].T

    @pl.when(i < tiles)
    def units():
        columns = pl.ds(pl.multiple_of(i * tile, tile), tile)
        hidden = jnp.dot(act[...], up[...], preferred_element_type=jnp.float32) + bias[...]
        squared = hidden * hidden
        bend = jnp.tanh(0.7978845608028654 * (hidden + 0.044715 * squared * hidden))
        gelu_low = (0.5 * hidden * (1.0 + bend)).astype(low)
        slope = 0.5 * (1.0 + bend) + 0.5 * hidden * (1.0 - bend * bend) * 0.7978845608028654 * (
            1.0 + 3.0 * 0.044715 * squared
        )
        incoming = jnp.dot(grad_branch[...], down[...], preferred_element_type=jnp.float32)
        grad_up_proj = (incoming * slope).astype(low)
        gelu_all[:, columns] = gelu_low
        grad_all[:, columns] = grad_up_proj
        bias_sum[...] = jnp.broadcast_to(
            jnp.sum(grad_up_proj.astype(jnp.float32), axis=0, keepdims=True), bias_sum.shape
        )
        for k in range(width // 512):
            place = slice(k * 512, (k + 1) * 512)
            split_store(
                jnp.dot(grad_turned[place, :], gelu_low, preferred_element_type=jnp.float32),
                k,
                shard_rows,
                down_given,
                down_kept,
                slice(None),
            )
            split_store(
                jnp.dot(act_turned[place, :], grad_up_proj, preferred_element_type=jnp.float32),
                k,
                shard_rows,
                up_given,
                up_kept,
                slice(None),
            )

    @pl.when(i >= tiles)
    def products():
        branch_part[...] = contract_cols(gelu_all[...], down_rows[...]).astype(low)
        back_part[...] = contract_cols(grad_all[...], up_rows[...]).astype(low)


def hidden_layer(shard_rows, act, grad_branch, up, down, bias):
    rows, width = act.shape
    hidden = up.shape[1]
    tile = 512
    tiles = hidden // tile

    def whole(shape):
        return pl.BlockSpec(shape, lambda i: (0, 0), pipeline_mode=pl.Buffered(1))

    def columns(height):
        return pl.BlockSpec((height, tile), lambda i: (0, jnp.minimum(i, tiles - 1)))

    later = pl.BlockSpec((tile, hidden), lambda i: (jnp.maximum(i - tiles, 0), 0))
    parts = pl.BlockSpec((rows, tile), lambda i: (0, jnp.maximum(i - tiles, 0)))
    return pl.pallas_call(
        functools.partial(hidden_kernel, shard_rows, tiles),
        grid=(tiles + width // tile,),
        out_shape=[jax.ShapeDtypeStruct((width // 2, hidden), low)] * 4
        + [jax.ShapeDtypeStruct((rows, width), low)] * 2
        + [jax.ShapeDtypeStruct((8, hidden), jnp.float32)],
        in_specs=[
            whole((rows, width)),
            whole((rows, width)),
            whole((width, rows)),
            columns(width),
            columns(width),
            columns(1),
            later,
            later,
        ],
        out_specs=[columns(width // 2)] * 4 + [parts] * 2 + [columns(8)],
        scratch_shapes=[
            vmem((width, rows), low),
            vmem((rows, hidden), low),
            vmem((rows, hidden), low),
        ],
        compiler_params=pltpu.CompilerParams(vmem_limit_bytes=60 * 1024 * 1024),
        cost_estimate=pl.CostEstimate(
            flops=12 * rows * width * hidden, bytes_accessed=100_000_000, transcendentals=0
        ),
    )(act, grad_branch, grad_branch.T, up, down, bias, up, down)


class Gather:
    def __init__(self, rows, whole, refs):
        self.rows, self.whole = rows, whole
        self.half_send, self.half_recv, self.core_send, self.core_recv = refs
        count = lax.axis_size("fsdp")
        self.group = 2 * count
        bits = [2 * b for b in (1, 2, 4, 8, 16, 32) if b < count]
        self.orders = [[1, *bits], [*bits, 1]]
        self.half = whole.shape[1] // 2
        _, self.place, self.side, self.beside, self.across = ctx_place()
        self.turn = lax.axis_index("fsdp")

    def piece(self, way, d, other=False):
        pair = flipped(self.turn, d // 2) * 2 + flipped(self.place, d % 2)
        shard = 2 * pair + (1 - self.side if other else self.side)
        return self.whole.at[
            pl.ds(pl.multiple_of(shard * self.rows, self.rows), self.rows),
            way * self.half : (way + 1) * self.half,
        ]

    def bit_copy(self, way, d, bit):
        device = self.across if bit == 1 else {"fsdp": flipped(self.turn, bit // 2)}
        piece = self.piece(way, d - bit)
        return ctx_copy(
            piece, piece, self.half_send.at[way, d], self.half_recv.at[way, d], device
        )

    def core_copy(self, way, d, other=False):
        piece = self.piece(way, d, other)
        return ctx_copy(
            piece, piece, self.core_send.at[way, d], self.core_recv.at[way, d], self.beside
        )

    def pass_on(self, way, d, after):
        for bit in self.orders[way][after:]:
            self.bit_copy(way, d + bit, bit).start()
        self.core_copy(way, d).start()

    def begin(self):
        for way in range(2):
            self.pass_on(way, 0, 0)

    def take(self, step):
        for i in range(2**step):
            for way in range(2):
                order = self.orders[way]
                d = order[step] + sum(order[k] for k in range(step) if i & 2**k)
                device = {"fsdp": flipped(self.turn, order[step] // 2)}
                piece = self.piece(way, d)
                ctx_copy(
                    piece,
                    piece,
                    self.half_send.at[way, d],
                    self.half_recv.at[way, d],
                    self.across if order[step] == 1 else device,
                ).wait_recv()
                self.pass_on(way, d, step + 1)

    def finish(self):
        for d in range(self.group):
            for way in range(2):
                self.core_copy(way, d, True).wait_recv()

    def drain(self):
        for way in range(2):
            have = [0]
            for bit in self.orders[way]:
                for d in have:
                    self.bit_copy(way, d + bit, bit).wait_send()
                have += [d + bit for d in have]
            for d in range(self.group):
                self.core_copy(way, d).wait_send()


def meet(others):
    barrier = pltpu.get_barrier_semaphore()
    for other in others:
        pl.semaphore_signal(barrier, inc=1, device_id=other, device_id_type=MESH)
    pl.semaphore_wait(barrier, len(others))


def gather_sems():
    return [pltpu.SemaphoreType.DMA((2, 2 * lax.axis_size("fsdp")))] * 4


def project_kernel(*refs):
    stream, gain, shift, bias, master_qkv, master_out, master_up, master_down = refs[:8]
    projected, act, qkv_out, out_out, up_low, down_low, whole, own, *rest = refs[8:]
    sems, out_sem = rest[:4], rest[4]
    meet(peers(("ctx", "fsdp")))
    groups, shard_rows, piece = master_qkv.shape
    rows, width = stream.shape
    gather = Gather(shard_rows, whole, sems)
    for r in range(groups):
        own[:, r * piece : (r + 1) * piece] = master_qkv[r].astype(low)
    own[:, groups * piece :] = master_out[...].astype(low)
    for way in range(2):
        gather.piece(way, 0)[...] = own[:, way * gather.half : (way + 1) * gather.half]
    gather.begin()
    for master, flat in ((master_up, up_low), (master_down, down_low)):
        for r in range(master.shape[1]):
            flat[:, r * piece : (r + 1) * piece] = master[:, r, :].astype(low)

    @pl.loop(0, rows // 64)
    def norm(i):
        place = pl.ds(pl.multiple_of(i * 64, 64), 64)
        act[place, :] = (
            normalize(stream[place, :].astype(jnp.float32))[0] * gain[...] + shift[...]
        ).astype(low)

    for step in range(len(gather.orders[0])):
        gather.take(step)
    gather.finish()
    wide = projected.shape[1]
    copies = [
        pltpu.make_async_copy(whole.at[:, :wide], qkv_out, out_sem.at[0]),
        pltpu.make_async_copy(whole.at[:, wide:], out_out, out_sem.at[1]),
    ]
    for copy in copies:
        copy.start()

    @pl.loop(0, wide // 512)
    def product(i):
        columns = pl.ds(pl.multiple_of(i * 512, 512), 512)
        projected[:, columns] = (
            jnp.dot(act[...], whole[:, columns], preferred_element_type=jnp.float32)
            + bias[:, columns]
        ).astype(low)

    for copy in copies:
        copy.wait()
    gather.drain()


def project(stream, gain, shift, bias, masters):
    rows, width = stream.shape
    wide = bias.shape[1]
    _, shard_rows, piece = masters[0].shape
    hidden = masters[2].shape[1] * piece
    in_vmem, loose = pl.BlockSpec(memory_space=vmem), pl.BlockSpec(memory_space=pl.ANY)
    depth = shard_rows * lax.axis_size("ctx") * lax.axis_size("fsdp")
    return pl.pallas_call(
        project_kernel,
        out_shape=[
            jax.ShapeDtypeStruct((rows, wide), low),
            jax.ShapeDtypeStruct((rows, width), low),
            jax.ShapeDtypeStruct((depth, wide), low),
            jax.ShapeDtypeStruct((depth, piece), low),
            jax.ShapeDtypeStruct((shard_rows, hidden), low),
            jax.ShapeDtypeStruct((shard_rows, hidden), low),
        ],
        in_specs=[in_vmem] * 8,
        out_specs=[in_vmem] * 2 + [loose] * 2 + [in_vmem] * 2,
        scratch_shapes=[vmem((depth, wide + piece), low), vmem((shard_rows, wide + piece), low)]
        + gather_sems()
        + [pltpu.SemaphoreType.DMA((2,))],
        compiler_params=pltpu.CompilerParams(
            collective_id=4, has_side_effects=True, vmem_limit_bytes=56 * 1024 * 1024
        ),
        cost_estimate=pl.CostEstimate(
            flops=2 * rows * width * wide, bytes_accessed=150_000_000, transcendentals=0
        ),
    )(stream, gain, shift, bias, *masters)


def ctx_place():
    me = lax.axis_index("ctx")
    half, side = me // 2, me % 2
    return me, half, side, {"ctx": me + 1 - 2 * side}, {"ctx": me + 2 - 4 * half}


def ctx_copy(source, target, send, recv, device):
    return pltpu.make_async_remote_copy(
        src_ref=source,
        dst_ref=target,
        send_sem=send,
        recv_sem=recv,
        device_id=device,
        device_id_type=MESH,
    )


class Spread:
    def __init__(self, block, own, pairs, send, recv):
        self.block, self.own, self.pairs, self.send, self.recv = block, own, pairs, send, recv
        self.me, self.half, self.side, self.beside, self.across = ctx_place()

    def rows(self, s, b):
        start = (s * lax.axis_size("ctx") + b) * self.block
        return pl.ds(pl.multiple_of(start, self.block), self.block)

    def copy(self, kind, s, b, own, device):
        target = self.pairs.at[self.rows(s, b)]
        wide = self.pairs.shape[1]
        source = self.own.at[s * self.block : (s + 1) * self.block, wide // 2 :] if own else target
        return ctx_copy(source, target, self.send.at[kind, s], self.recv.at[kind, s], device)

    def start(self, s):
        rows = slice(s * self.block, (s + 1) * self.block)

        @pl.when(self.half == 0)
        def over():
            self.copy(0, s, self.me, True, self.across).start()

        @pl.when(self.side == 0)
        def aside():
            self.copy(1, s, self.me, True, self.beside).start()

        self.pairs[self.rows(s, self.me)] = self.own[rows, self.pairs.shape[1] // 2 :]

    def forward(self, s):
        @pl.when(self.half == 1)
        def onward():
            self.copy(0, s, self.me - 2, False, self.across).wait_recv()
            self.copy(2, s, self.me - 2, False, self.beside).start()

    def arrive(self, s):
        @pl.when(self.half == 1)
        def second():
            self.copy(2, s, 1 - self.side, False, self.beside).wait_recv()

        @pl.when(self.side == 1)
        def first():
            self.copy(1, s, self.me - 1, False, self.beside).wait_recv()

    def drain_own(self, s):
        @pl.when(self.half == 0)
        def over():
            self.copy(0, s, self.me, True, self.across).wait_send()

        @pl.when(self.side == 0)
        def aside():
            self.copy(1, s, self.me, True, self.beside).wait_send()

    def drain(self, s):
        @pl.when(self.half == 1)
        def onward():
            self.copy(2, s, self.me - 2, False, self.beside).wait_send()


class Collect:
    def __init__(self, block, parts, beside_in, across_in, send, recv):
        self.block, self.parts = block, parts
        self.beside_in, self.across_in, self.send, self.recv = beside_in, across_in, send, recv
        self.me, self.half, self.side, self.beside, self.across = ctx_place()

    def rows(self, s, b):
        start = (s * lax.axis_size("ctx") + b) * self.block
        return pl.ds(pl.multiple_of(start, self.block), self.block)

    def aside(self, s, k, away=False):
        b = 2 * k + (self.side if away else 1 - self.side)
        return ctx_copy(
            self.parts.at[self.rows(s, b)],
            self.beside_in.at[k, s],
            self.send.at[k, s],
            self.recv.at[k, s],
            self.beside,
        )

    def over(self, s):
        return ctx_copy(
            self.parts.at[self.rows(s, self.side)],
            self.across_in.at[s],
            self.send.at[2, s],
            self.recv.at[2, s],
            self.across,
        )

    def start(self, s):
        for k in range(2):

            @pl.when(2 * k + 1 - self.side < self.me)
            def give():
                self.aside(s, k).start()

    def forward(self, s):
        for k in range(2):

            @pl.when(2 * k + self.side < self.me + 1 - 2 * self.side)
            def take():
                self.aside(s, k, True).wait_recv()

        @pl.when(self.half == 1)
        def onward():
            held = self.parts.at[self.rows(s, self.side)]
            held[...] = (
                held[...].astype(jnp.float32) + self.beside_in[0, s].astype(jnp.float32)
            ).astype(low)
            self.over(s).start()

    def finish(self, s, target):
        target[...] = self.parts[self.rows(s, self.me)]
        for k in range(2):

            @pl.when((self.side == 0) & (self.half == k))
            def near():
                target[...] = (
                    target[...].astype(jnp.float32) + self.beside_in[k, s].astype(jnp.float32)
                ).astype(low)

        @pl.when(self.half == 0)
        def far():
            self.over(s).wait_recv()
            target[...] = (
                target[...].astype(jnp.float32) + self.across_in[s].astype(jnp.float32)
            ).astype(low)

    def drain(self, s):
        for k in range(2):

            @pl.when(2 * k + 1 - self.side < self.me)
            def gave():
                self.aside(s, k).wait_send()

        @pl.when(self.half == 1)
        def sent():
            self.over(s).wait_send()


def offsets(base):
    shape = base.shape
    base[...] = (
        lax.broadcasted_iota(jnp.int32, shape, 0) - lax.broadcasted_iota(jnp.int32, shape, 1)
    ).astype(jnp.float32)


def head_scores(query, key, slope, base, j):
    far = base[...] + (j * base.shape[0]).astype(jnp.float32)
    return contract_cols(query, key) * HD ** (-0.5) - slope * jnp.abs(far)


def head_columns(h, shift=0):
    return slice(shift + h * HD, shift + (h + 1) * HD)


def forward_heads(s, heads, block, projected, pairs, slopes, base, context, log_total):
    me = lax.axis_index("ctx")
    count = lax.axis_size("ctx")
    own = slice(s * block, (s + 1) * block)
    wide = pairs.shape[1] // 2
    queries = [projected[own, head_columns(h)] for h in heads]

    def step(j, carry):
        rows = pl.ds(pl.multiple_of((s * count + me - j) * block, block), block)
        scores = [
            head_scores(query, pairs[rows, head_columns(h)], slopes[h, 0:1], base, j)
            for h, query in zip(heads, queries)
        ]
        higher = [
            jnp.maximum(peak, jnp.max(score, axis=-1, keepdims=True))
            for score, (peak, _, _) in zip(scores, carry)
        ]
        exponents = [jnp.exp(score - peak) for score, peak in zip(scores, higher)]
        out = []
        for h, exponent, peak, (before, weight, total) in zip(heads, exponents, higher, carry):
            shrink = jnp.exp(before - peak)
            value = pairs[rows, head_columns(h, wide)]
            out.append(
                (
                    peak,
                    weight * shrink + jnp.sum(exponent, axis=-1, keepdims=True),
                    total * shrink
                    + jnp.dot(exponent.astype(low), value, preferred_element_type=jnp.float32),
                )
            )
        return tuple(out)

    start = (
        jnp.full((block, 1), -1e30, jnp.float32),
        jnp.zeros((block, 1), jnp.float32),
        jnp.zeros((block, HD), jnp.float32),
    )
    ends = lax.fori_loop(0, me + 1, step, tuple(start for _ in heads))
    for h, (peak, weight, total) in zip(heads, ends):
        context[own, head_columns(h)] = (total / weight).astype(low)
        log_total[own, head_columns(h)] = jnp.broadcast_to(peak + jnp.log(weight), (block, HD))


def backward_heads(
    s, heads, block, projected, pairs, slopes, base, context, log_total, grad, parts, out
):
    me = lax.axis_index("ctx")
    count = lax.axis_size("ctx")
    own = slice(s * block, (s + 1) * block)
    wide = pairs.shape[1] // 2
    queries = [projected[own, head_columns(h)] for h in heads]
    incomings = [grad[own, head_columns(h)] for h in heads]
    levels = [log_total[own, head_columns(h)][:, 0:1] for h in heads]
    means = [
        jnp.sum(
            incoming.astype(jnp.float32) * context[own, head_columns(h)].astype(jnp.float32),
            axis=-1,
            keepdims=True,
        )
        for h, incoming in zip(heads, incomings)
    ]

    def step(j, totals):
        rows = pl.ds(pl.multiple_of((s * count + me - j) * block, block), block)
        keys = [pairs[rows, head_columns(h)] for h in heads]
        probs = [
            jnp.exp(head_scores(query, key, slopes[h, 0:1], base, j) - level)
            for h, query, key, level in zip(heads, queries, keys, levels)
        ]
        grad_probs = [
            contract_cols(incoming, pairs[rows, head_columns(h, wide)])
            for h, incoming in zip(heads, incomings)
        ]
        grad_scores = [
            (prob * (grad_prob - mean)).astype(low)
            for prob, grad_prob, mean in zip(probs, grad_probs, means)
        ]
        for h, prob, grad_score, query, incoming in zip(
            heads, probs, grad_scores, queries, incomings
        ):
            parts[rows, head_columns(h)] = (
                contract_rows(grad_score, query) * HD ** (-0.5)
            ).astype(low)
            parts[rows, head_columns(h, wide)] = contract_rows(prob.astype(low), incoming).astype(
                low
            )
        return tuple(
            total + jnp.dot(grad_score, key, preferred_element_type=jnp.float32)
            for total, grad_score, key in zip(totals, grad_scores, keys)
        )

    totals = lax.fori_loop(
        0, me + 1, step, tuple(jnp.zeros((block, HD), jnp.float32) for _ in heads)
    )
    for h, total in zip(heads, totals):
        out[own, head_columns(h)] = (total * HD ** (-0.5)).astype(low)


def attend_kernel(n, chunks, tile, *refs):
    (
        projected,
        slopes,
        out_weight,
        stream,
        bias,
        gain,
        shift,
        full,
        middle,
        context,
        log_total,
        pairs,
        part,
        landing,
        total,
        *rest,
    ) = refs
    sems, (base, send, recv) = rest[:4], rest[4:]
    rows, width = full.shape
    seqs = chunks // 2
    block = rows // seqs
    heads = context.shape[1] // HD
    pace = heads // 2
    _, _, _, beside, across = ctx_place()
    greet(n, [beside, across])
    finish = middle_epilogue(rows // chunks // n, (stream, bias, gain, shift), (middle,))
    line = Line(n, chunks, part, full, landing, total, sems, finish, 2)
    spread = Spread(block, projected, pairs, send, recv)
    spread.start(0)
    offsets(base)

    def attend(s, first, last):
        if first == 0:
            spread.forward(s)
            if s + 1 < seqs:
                spread.drain_own(s)
                spread.start(s + 1)
            spread.arrive(s)
        for h in range(first, last, 2):
            forward_heads(
                s,
                range(h, min(h + 2, last)),
                block,
                projected,
                pairs,
                slopes,
                base,
                context,
                log_total,
            )

    def multiply(s):
        own = slice(s * block, (s + 1) * block)

        @pl.loop(0, width // tile)
        def one(i):
            columns = pl.ds(pl.multiple_of(i * tile, tile), tile)
            part[own, columns] = contract_cols(context[own, :], out_weight[columns, :]).astype(low)

    attend(0, 0, heads)
    multiply(0)
    for t in range(1, line.slots + 1):
        line.slot(t)
        s = (t + 1) // 2
        if s < seqs:
            attend(s, 0 if t % 2 else pace, pace if t % 2 else heads)
            if t % 2 == 0:
                multiply(s)
    spread.drain_own(seqs - 1)
    for s in range(seqs):
        spread.drain(s)
    line.drain()


def backward_kernel(n, chunks, shard_rows, *refs):
    (
        part,
        middle,
        bias,
        grad_attn,
        out_weight,
        projected,
        pairs,
        context,
        log_total,
        slopes,
        act,
        full,
        grad_projected,
        given,
        kept,
        landing,
        total,
        *rest,
    ) = refs
    sems, (base, grad_context, parts, beside_in, across_in, send, recv) = rest[:4], rest[4:]
    rows, width = full.shape
    seqs = chunks // 2
    block = rows // seqs
    heads = context.shape[1] // HD
    wide = context.shape[1]
    pace = heads // 2
    _, _, _, beside, across = ctx_place()
    greet(n, [beside, across])
    finish = output_epilogue(rows // chunks // n, (middle, bias), ())
    line = Line(n, chunks, part, full, landing, total, sems, finish)
    collect = Collect(block, parts, beside_in, across_in, send, recv)
    offsets(base)

    def backward(s, first, last):
        own = slice(s * block, (s + 1) * block)
        if first == 0:
            grad_context[own, :] = jnp.dot(
                grad_attn[own, :], out_weight[...], preferred_element_type=jnp.float32
            ).astype(low)
        backward_heads(
            s,
            range(first, last),
            block,
            projected,
            pairs,
            slopes,
            base,
            context,
            log_total,
            grad_context,
            parts,
            grad_projected,
        )
        if last == heads:
            collect.start(s)

    def finished(s):
        collect.finish(s, grad_projected.at[s * block : (s + 1) * block, wide:])

    def features(source, right, columns, first, last):
        @pl.loop(first, last)
        def one(i):
            place = pl.ds(pl.multiple_of(i * 256, 256), 256)
            value = contract_rows(source[:, place], right[...])
            split_store(value, i, shard_rows, given, kept, columns)

    attn_columns = slice(0, 3 * wide)
    out_columns = slice(3 * wide, 4 * wide)

    tiles = width // 256
    tasks = []
    for s in range(seqs):
        tasks.append([functools.partial(backward, s, 0, pace)])
        tasks.append([functools.partial(backward, s, pace, heads)])
    tasks += [[] for _ in range(max(3, line.slots - len(tasks)))]
    for s in range(seqs):
        tasks[2 * s + 2].append(functools.partial(collect.forward, s))
    after = 2 * seqs
    tasks[after].append(functools.partial(features, grad_attn, context, out_columns, 0, tiles))
    for s in range(seqs):
        tasks[after + 1].append(functools.partial(finished, s))
    tasks[after + 2].append(
        functools.partial(features, act, grad_projected, attn_columns, 0, tiles)
    )
    for t in range(1, max(line.slots, len(tasks)) + 1):
        line.slot(t)
        for task in tasks[t - 1] if t <= len(tasks) else []:
            task()
    for s in range(seqs):
        collect.drain(s)
    line.drain()


def fused_call(body, collective, operands, outs, scratch, flops, loose=0):
    whole = pl.BlockSpec(memory_space=vmem)
    away = pl.BlockSpec(memory_space=pl.ANY)
    specs = [whole] * (len(operands) - loose) + [away] * loose
    return pl.pallas_call(
        body,
        out_shape=outs,
        in_specs=specs,
        out_specs=[whole] * len(outs),
        scratch_shapes=scratch,
        compiler_params=pltpu.CompilerParams(
            collective_id=collective,
            has_side_effects=True,
            vmem_limit_bytes=60 * 1024 * 1024,
        ),
        cost_estimate=pl.CostEstimate(flops=flops, bytes_accessed=200_000_000, transcendentals=0),
    )(*operands)


def local(
    inputs,
    cotangent,
    master_qkv,
    qkv_moment1,
    qkv_moment2,
    master_out,
    out_moment1,
    out_moment2,
    master_up,
    up_moment1,
    up_moment2,
    master_down,
    down_moment1,
    down_moment2,
    norm_gains,
    gain_moment1,
    gain_moment2,
    shared_biases,
    shared_moment1,
    shared_moment2,
    split_biases,
    split_moment1,
    split_moment2,
):
    seq_count, block_len, model_width = inputs.shape
    row_count = seq_count * block_len
    width_part = master_qkv.shape[2]
    hidden_rows = master_up.shape[1]
    local_heads = width_part // HD
    tp_count = lax.axis_size("tp")
    chunks = 2 * seq_count
    own_rows = row_count // chunks // tp_count

    def own_part(values):
        blocks = values.reshape(chunks, tp_count * own_rows, model_width)
        taken = lax.dynamic_slice_in_dim(blocks, lax.axis_index("tp") * own_rows, own_rows, axis=1)
        return taken.reshape(-1, model_width)

    own_shape = jax.ShapeDtypeStruct((row_count // tp_count, model_width), jnp.float32)
    sums_shape = jax.ShapeDtypeStruct((8, model_width), jnp.float32)
    gains = [norm_gains[i : i + 1] for i in range(2)]
    shared = [shared_biases[i : i + 1] for i in range(4)]
    inputs_own = own_part(inputs)
    cotangent_own = own_part(cotangent)

    projected_bias = jnp.concatenate(
        [split_biases[0], jnp.zeros((width_part,), jnp.float32), split_biases[1]]
    )
    projected, act_one, qkv_flat, out_flat, up_low, down_low = project(
        inputs.reshape(row_count, model_width),
        gains[0],
        shared[0],
        projected_bias[None],
        (jnp.swapaxes(master_qkv, 0, 1), master_out, master_up, master_down),
    )
    head_ids = (lax.axis_index("tp") * local_heads + jnp.arange(local_heads)).astype(jnp.float32)
    slopes = jnp.power(2.0, -8.0 * (head_ids + 1.0) / (local_heads * lax.axis_size("tp")))
    slopes = jnp.broadcast_to(slopes[:, None, None], (local_heads, 8, block_len))
    sems = line_scratch(tp_count, chunks, row_count, model_width)
    pair_rows = row_count * lax.axis_size("ctx")
    square = vmem((block_len, block_len), jnp.float32)
    pair_sems = [pltpu.SemaphoreType.DMA((3, seq_count))] * 2
    up_flat, down_flat = (
        lax.all_gather(rows, ("fsdp", "ctx"), axis=0, tiled=True) for rows in (up_low, down_low)
    )
    act_two, middle, context, log_total, pairs = fused_call(
        functools.partial(attend_kernel, tp_count, chunks, 256),
        0,
        (
            projected,
            slopes,
            out_flat,
            inputs_own,
            shared[2],
            gains[1],
            shared[1],
        ),
        [
            jax.ShapeDtypeStruct((row_count, model_width), low),
            own_shape,
            jax.ShapeDtypeStruct((row_count, width_part), low),
            jax.ShapeDtypeStruct((row_count, width_part), jnp.float32),
            jax.ShapeDtypeStruct((pair_rows, 2 * width_part), low),
        ],
        sems + [square] + pair_sems,
        4 * row_count * model_width * width_part,
    )
    down_given, down_kept, up_given, up_kept, branch_part, back_part, bias_sum = hidden_layer(
        master_qkv.shape[0],
        act_two,
        cotangent.reshape(row_count, model_width),
        up_flat,
        down_flat,
        split_biases[2:].reshape(1, -1),
    )
    grad_attn, grad_middle, sums_two, sum_down, sum_up = tp_sum(
        tp_count,
        chunks,
        attn_epilogue,
        2,
        (back_part,),
        (middle, cotangent_own, gains[1]),
        [own_shape, sums_shape],
        [(down_given, down_kept), (up_given, up_kept)],
        ((2, 5), (3, 8)),
    )
    pair_block = (block_len, 2 * width_part)
    output, grad_projected, attn_given, attn_kept = fused_call(
        functools.partial(backward_kernel, tp_count, chunks, master_qkv.shape[0]),
        1,
        (
            branch_part,
            middle,
            shared[3],
            grad_attn,
            out_flat,
            projected,
            pairs,
            context,
            log_total,
            slopes,
            act_one,
        ),
        [
            jax.ShapeDtypeStruct((row_count, model_width), low),
            jax.ShapeDtypeStruct((row_count, 3 * width_part), low),
            jax.ShapeDtypeStruct((model_width // 2, 4 * width_part), low),
            jax.ShapeDtypeStruct((model_width // 2, 4 * width_part), low),
        ],
        sems[1:]
        + [
            square,
            vmem((row_count, width_part), low),
            vmem((pair_rows, 2 * width_part), low),
            vmem((2, seq_count, *pair_block), low),
            vmem((seq_count, *pair_block), low),
        ]
        + pair_sems,
        12 * row_count * model_width * width_part,
    )
    output = output.reshape(seq_count, block_len, model_width)
    query_low = grad_projected[:, :width_part]
    value_low = grad_projected[:, 2 * width_part :]
    split_grads = jnp.concatenate(
        [
            jnp.sum(query_low, axis=0, dtype=jnp.float32)[None],
            jnp.sum(value_low, axis=0, dtype=jnp.float32)[None],
            bias_sum[0].reshape(hidden_rows, width_part),
        ],
        axis=0,
    )
    vectors = jnp.concatenate(
        [
            jnp.zeros((2, model_width), jnp.float32),
            sums_two[0:3],
            jnp.sum(cotangent_own, axis=0, dtype=jnp.float32)[None],
            jnp.zeros((2, model_width), jnp.float32),
        ]
    )
    vectors = jnp.concatenate([vectors, jnp.pad(split_grads, ((0, 2), (0, 0)))], axis=1)
    input_low, _, vector_sum, sum_attn = tp_sum(
        tp_count,
        chunks,
        input_epilogue,
        3,
        (grad_projected, qkv_flat),
        (inputs_own, grad_middle, gains[0]),
        [sums_shape],
        [(attn_given, attn_kept)],
        ((2, 6),),
        vectors,
    )
    input_grad = input_low.astype(jnp.float32).reshape(seq_count, block_len, model_width)

    gain_sum = jnp.concatenate([vector_sum[0:1, :model_width], vector_sum[2:3, :model_width]])
    shared_sum = jnp.concatenate([vector_sum[1:2, :model_width], vector_sum[3:6, :model_width]])
    split_sum = vector_sum[: 2 + hidden_rows, model_width:]
    q_one, q_two, q_new, q_copy = (
        jnp.swapaxes(out, 0, 1)
        for out in adam_matrix(
            sum_attn,
            *(jnp.swapaxes(values, 0, 1) for values in (master_qkv, qkv_moment1, qkv_moment2)),
        )
    )
    sum_out = sum_attn[:, 3 * width_part :].astype(jnp.float32)
    o_one, o_two, o_new = adam_update(
        master_out, out_moment1, out_moment2, sum_out, matrix_rate, True
    )
    u_one, u_two, u_new, u_copy = adam_matrix(sum_up, master_up, up_moment1, up_moment2)
    d_one, d_two, d_new, d_copy = adam_matrix(sum_down, master_down, down_moment1, down_moment2)
    g_one, g_two, g_new = adam_update(
        norm_gains, gain_moment1, gain_moment2, gain_sum, vector_rate, False
    )
    s_one, s_two, s_new = adam_update(
        shared_biases, shared_moment1, shared_moment2, shared_sum, vector_rate, False
    )
    p_one, p_two, p_new = adam_update(
        split_biases, split_moment1, split_moment2, split_sum, vector_rate, False
    )
    return (
        output,
        input_grad,
        q_one,
        q_two,
        q_new,
        q_copy,
        o_one,
        o_two,
        o_new,
        o_new.astype(jnp.bfloat16),
        u_one,
        u_two,
        u_new,
        u_copy,
        d_one,
        d_two,
        d_new,
        d_copy,
        g_one,
        g_two,
        g_new,
        s_one,
        s_two,
        s_new,
        p_one,
        p_two,
        p_new,
    )


def solution(mesh):
    return jax.shard_map(
        local,
        mesh=mesh,
        in_specs=(
            P("fsdp", "ctx", None),
            P("fsdp", "ctx", None),
            P(("fsdp", "ctx"), None, "tp"),
            P(("fsdp", "ctx"), None, "tp"),
            P(("fsdp", "ctx"), None, "tp"),
            P(("fsdp", "ctx"), "tp"),
            P(("fsdp", "ctx"), "tp"),
            P(("fsdp", "ctx"), "tp"),
            P(("fsdp", "ctx"), None, "tp"),
            P(("fsdp", "ctx"), None, "tp"),
            P(("fsdp", "ctx"), None, "tp"),
            P(("fsdp", "ctx"), None, "tp"),
            P(("fsdp", "ctx"), None, "tp"),
            P(("fsdp", "ctx"), None, "tp"),
            P(),
            P(),
            P(),
            P(),
            P(),
            P(),
            P(None, "tp"),
            P(None, "tp"),
            P(None, "tp"),
        ),
        out_specs=(
            P("fsdp", "ctx", None),
            P("fsdp", "ctx", None),
            P(("fsdp", "ctx"), None, "tp"),
            P(("fsdp", "ctx"), None, "tp"),
            P(("fsdp", "ctx"), None, "tp"),
            P(("fsdp", "ctx"), None, "tp"),
            P(("fsdp", "ctx"), "tp"),
            P(("fsdp", "ctx"), "tp"),
            P(("fsdp", "ctx"), "tp"),
            P(("fsdp", "ctx"), "tp"),
            P(("fsdp", "ctx"), None, "tp"),
            P(("fsdp", "ctx"), None, "tp"),
            P(("fsdp", "ctx"), None, "tp"),
            P(("fsdp", "ctx"), None, "tp"),
            P(("fsdp", "ctx"), None, "tp"),
            P(("fsdp", "ctx"), None, "tp"),
            P(("fsdp", "ctx"), None, "tp"),
            P(("fsdp", "ctx"), None, "tp"),
            P(),
            P(),
            P(),
            P(),
            P(),
            P(),
            P(None, "tp"),
            P(None, "tp"),
            P(None, "tp"),
        ),
        check_vma=False,
    )
```

```python
import functools

import jax
import jax.numpy as jnp
from jax import lax
from jax.experimental import pallas as pl
from jax.experimental.pallas import tpu as pltpu
from jax.sharding import PartitionSpec as P

HD = 128
STEP = 10


norm_epsilon = 1e-05
matrix_rate = 0.04
vector_rate = 0.4
decay_weight = 0.1
decay_rate = 0.5
adam_epsilon = 1e-08
low = jnp.bfloat16


def normalize(values):
    center = jnp.mean(values, axis=-1, keepdims=True)
    shifted = values - center
    variance = jnp.mean(shifted * shifted, axis=-1, keepdims=True)
    inverse = lax.rsqrt(variance + norm_epsilon)
    return (shifted * inverse, inverse)


def norm_back(incoming, normed, inverse, gain):
    scaled = incoming * gain
    return inverse * (
        scaled
        - jnp.mean(scaled, axis=-1, keepdims=True)
        - normed * jnp.mean(scaled * normed, axis=-1, keepdims=True)
    )


def gelu_tanh(values):
    return (
        0.5
        * values
        * (1.0 + jnp.tanh(0.7978845608028654 * (values + 0.044715 * values * values * values)))
    )


def adam_update(master, moment_one, moment_two, gradient, rate, decayed):
    first = decay_rate * moment_one + (1.0 - decay_rate) * gradient
    second = decay_rate * moment_two + (1.0 - decay_rate) * gradient * gradient
    correction = 1.0 - decay_rate**STEP
    update = first / correction / (jnp.sqrt(second / correction) + adam_epsilon)
    if decayed:
        update = update + decay_weight * master
    return (first, second, master - rate * update)


def adam_kernel(flat, master, one, two, one_out, two_out, new_out, copy_out, *scratch):
    if scratch:
        gradient = scratch[0]
        piece = master.shape[2]
        for r in range(master.shape[1]):
            gradient[:, r, :] = flat[:, r * piece : (r + 1) * piece].astype(jnp.float32)
        gradient = gradient[...]
    else:
        gradient = flat[...].astype(jnp.float32)[None]
    first, second, new = adam_update(master[...], one[...], two[...], gradient, matrix_rate, True)
    one_out[...] = first
    two_out[...] = second
    new_out[...] = new
    copy_out[...] = new.astype(low)


def adam_matrix(flat, master, one, two):
    full = jax.ShapeDtypeStruct(master.shape, jnp.float32)
    if master.shape[0] == flat.shape[0]:
        rows, groups, piece = master.shape
        tile, steps = 64, rows // 64
        block = pl.BlockSpec((tile, groups, piece), lambda i: (i, 0, 0))
        flat_block = pl.BlockSpec((tile, groups * piece), lambda i: (i, 0))
        scratch = [pltpu.VMEM((tile, groups, piece), jnp.float32)]
    else:
        steps, rows, piece = master.shape
        groups, scratch = steps, []
        block = pl.BlockSpec((1, rows, piece), lambda i: (i, 0, 0))
        flat_block = pl.BlockSpec((rows, piece), lambda i: (0, i))
    return pl.pallas_call(
        adam_kernel,
        grid=(steps,),
        out_shape=[full] * 3 + [jax.ShapeDtypeStruct(master.shape, low)],
        in_specs=[flat_block] + [block] * 3,
        out_specs=[block] * 4,
        scratch_shapes=scratch,
        cost_estimate=pl.CostEstimate(
            flops=20 * rows * groups * piece,
            bytes_accessed=28 * rows * groups * piece,
            transcendentals=2 * rows * groups * piece,
        ),
    )(flat, master, one, two)


def contract_rows(left, right):
    return lax.dot_general(
        left, right, (((0,), (0,)), ((), ())), preferred_element_type=jnp.float32
    )


def contract_cols(left, right):
    return lax.dot_general(
        left, right, (((1,), (1,)), ((), ())), preferred_element_type=jnp.float32
    )


MESH = pl.DeviceIdType.MESH
vmem = pltpu.VMEM


class Line:
    def __init__(self, n, chunks, part, full, landing, total, sems, finish, pace=0):
        self.n, self.chunks = n, chunks
        self.part, self.full, self.landing, self.total = part, full, landing, total
        self.sum_send, self.sum_recv, self.row_send, self.row_recv = sems
        self.finish = finish
        self.z = lax.axis_index("tp")
        self.chunk_rows = full.shape[0] // chunks
        self.own = self.chunk_rows // n
        self.pace = pace
        self.slots = self.start(chunks - 1) + 2 * n - 1

    def start(self, c):
        return c // 2 * self.pace if self.pace else c

    def slot(self, t):
        for c in range(self.chunks):
            if 0 < t - self.start(c) < 2 * self.n:
                self.stage(c, t - self.start(c))

    def place(self, c, j):
        return pl.ds(pl.multiple_of(c * self.chunk_rows + j * self.own, self.own), self.own)

    def flow(self, d):
        return self.z if d == 0 else self.n - 1 - self.z

    def toward(self, d, away):
        return {"tp": self.z + (1 if (d == 0) != away else -1)}

    def sum_copy(self, d, c, k, source, away=False):
        return pltpu.make_async_remote_copy(
            src_ref=source,
            dst_ref=self.landing.at[d, c, k - 1],
            send_sem=self.sum_send.at[d, c, k - 1],
            recv_sem=self.sum_recv.at[d, c, k - 1],
            device_id=self.toward(d, away),
            device_id_type=MESH,
        )

    def sum_arrive(self, d, c, k):
        self.sum_copy(d, c, k, self.landing.at[d, c, k - 1], True).wait_recv()

    def row_copy(self, d, c, k, away=False):
        back = k if away else k - 1
        rows = self.place(c, self.z - back if d == 0 else self.z + back)
        return pltpu.make_async_remote_copy(
            src_ref=self.full.at[rows],
            dst_ref=self.full.at[rows],
            send_sem=self.row_send.at[d, c, k - 1],
            recv_sem=self.row_recv.at[d, c, k - 1],
            device_id=self.toward(d, away),
            device_id_type=MESH,
        )

    def stage(self, c, s):
        n, z = self.n, self.z
        if s < n:
            for d in range(2):
                q = self.flow(d)
                rows = self.place(c, z + n - s if d == 0 else z - n + s)

                @pl.when(q == 0)
                def first():
                    self.sum_copy(d, c, s, self.part.at[rows]).start()

                if s > 1:

                    @pl.when((q >= 1) & (q < s))
                    def later():
                        self.sum_arrive(d, c, s - 1)
                        held = self.landing.at[d, c, s - 2]
                        held[...] = (
                            self.part[rows].astype(jnp.float32) + held[...].astype(jnp.float32)
                        ).astype(low)
                        self.sum_copy(d, c, s, held).start()

        elif s == n:
            rows = self.place(c, z)
            self.total[...] = self.part[rows].astype(jnp.float32)
            for d in range(2):

                @pl.when(self.flow(d) >= 1)
                def ended():
                    self.sum_arrive(d, c, n - 1)
                    self.total[...] += self.landing[d, c, n - 2].astype(jnp.float32)

            self.full[rows] = self.finish(c, self.total[...]).astype(low)
            for d in range(2):

                @pl.when(self.flow(d) < n - 1)
                def spread():
                    self.row_copy(d, c, 1).start()

        else:
            k = s - n + 1
            for d in range(2):
                q = self.flow(d)

                @pl.when(q >= k - 1)
                def arrived():
                    self.row_copy(d, c, k - 1, True).wait_recv()

                if k < n:

                    @pl.when((q >= k - 1) & (q < n - 1))
                    def onward():
                        self.row_copy(d, c, k).start()

    def drain(self):
        n = self.n
        for c in range(self.chunks):
            for d in range(2):
                q = self.flow(d)
                for k in range(1, n):

                    @pl.when(q < k)
                    def sum_sent():
                        self.sum_copy(d, c, k, self.landing.at[d, c, k - 1]).wait_send()

                    @pl.when((q >= k - 1) & (q < n - 1))
                    def row_sent():
                        self.row_copy(d, c, k).wait_send()


def peers(axes):
    found = []
    for axis in axes:
        bit = 1
        while bit < lax.axis_size(axis):
            me = lax.axis_index(axis)
            found.append({axis: me + bit * (1 - 2 * ((me // bit) % 2))})
            bit *= 2
    return found


def greet(n, others):
    z = lax.axis_index("tp")
    barrier = pltpu.get_barrier_semaphore()

    @pl.when(z > 0)
    def to_lower():
        pl.semaphore_signal(barrier, inc=1, device_id={"tp": z - 1}, device_id_type=MESH)

    @pl.when(z < n - 1)
    def to_upper():
        pl.semaphore_signal(barrier, inc=1, device_id={"tp": z + 1}, device_id_type=MESH)

    for other in others:
        pl.semaphore_signal(barrier, inc=1, device_id=other, device_id_type=MESH)

    @pl.when((z > 0) & (z < n - 1))
    def from_both():
        pl.semaphore_wait(barrier, 2 + len(others))

    @pl.when((z == 0) | (z == n - 1))
    def from_one():
        pl.semaphore_wait(barrier, 1 + len(others))


def line_scratch(n, chunks, rows, width):
    own = rows // chunks // n
    return [
        vmem((rows, width), low),
        vmem((2, chunks, n - 1, own, width), low),
        vmem((own, width), jnp.float32),
    ] + [pltpu.SemaphoreType.DMA((2, chunks, n - 1))] * 4


class Exchange:
    def __init__(self, whole, start, arrived, send_sem, recv_sem):
        self.whole, self.held, self.arrived = whole, start, arrived
        self.send_sem, self.recv_sem = send_sem, recv_sem
        self.inner = len(peers(("ctx", "fsdp")))
        self.peers = peers(("ctx", "fsdp", "tp"))

    def copy(self, i):
        columns = slice(None) if i < self.inner else slice(0, self.whole)
        return pltpu.make_async_remote_copy(
            src_ref=self.held.at[i, :, columns],
            dst_ref=self.arrived.at[i, :, columns],
            send_sem=self.send_sem.at[i],
            recv_sem=self.recv_sem.at[i],
            device_id=self.peers[i],
            device_id_type=MESH,
        )

    def step(self, i):
        if i > 0:
            self.copy(i - 1).wait_recv()
            if i - 1 < self.inner:
                self.held[i] = self.held[i - 1] + self.arrived[i - 1]
            else:
                self.held[i] = self.held[i - 1]
                self.held[i, :, : self.whole] += self.arrived[i - 1, :, : self.whole]
        if i < len(self.peers):
            self.copy(i).start()

    def drain(self):
        for i in range(len(self.peers)):
            self.copy(i).wait_send()


def sum_kernel(n, chunks, epilogue, counts, with_product, with_vectors, plan, *refs):
    refs = list(refs)

    def taken(count):
        out = refs[:count]
        del refs[:count]
        return out

    operands = taken(2 if with_product else 1)
    extras, weights = taken(counts[0]), taken(2 * counts[2])
    (full,) = taken(1)
    outs, sums = taken(counts[1]), taken(counts[2])
    part = taken(1)[0] if with_product else operands[0]
    landing, total = taken(2)
    sems = taken(4)
    moves = [
        Halving(weights[2 * i], weights[2 * i + 1], sums[i], taken(8)) for i in range(counts[2])
    ]
    rows, width = full.shape
    chunk_rows = rows // chunks
    block = 2 * chunk_rows
    greet(n, peers(("ctx", "fsdp", "tp") if with_vectors else ("ctx", "fsdp")))
    finish = epilogue(chunk_rows // n, extras, outs)
    line = Line(n, chunks, part, full, landing, total, sems, finish)

    def multiply(b):
        if not with_product:
            return
        own = slice(b * block, (b + 1) * block)

        @pl.loop(0, width // 256)
        def one(i):
            columns = pl.ds(pl.multiple_of(i * 256, 256), 256)
            part[own, columns] = contract_cols(operands[0][own, :], operands[1][columns, :]).astype(
                low
            )

    for move in moves:
        move.start()
    multiply(0)
    ended = line.start(chunks - 1) + n
    vectors = None
    for t in range(1, line.slots + 1):
        line.slot(t)
        if t % 2 == 0 and t < chunks:
            multiply(t // 2)
        for i, move in enumerate(moves):
            if t == plan[i][0]:
                move.core_step()
            if t == plan[i][1]:
                move.middle_step()
        if with_vectors and t == ended:
            held, arrived, send_sem, recv_sem = refs
            vectors = Exchange(width, held, arrived, send_sem, recv_sem)
            held[0] = extras[-1][...]
            held[0, 0:2, :width] = outs[0][0:2]
        if vectors is not None and t - ended <= len(vectors.peers):
            vectors.step(t - ended)
            done = t - ended
    if vectors is not None:
        for i in range(done + 1, len(vectors.peers) + 1):
            vectors.step(i)
        outs[-1][...] = vectors.held[len(vectors.peers)]
        vectors.drain()
    for move in moves:
        move.last_step()
    for move in moves:
        move.drain()
    line.drain()


def tp_sum(
    n, chunks, epilogue, collective, operands, extras, out_shapes, weights, plan, vectors=None
):
    rows = operands[0].shape[0]
    with_product = len(operands) == 2
    width = operands[-1].shape[0] if with_product else operands[0].shape[1]
    outs = list(out_shapes)
    scratch = line_scratch(n, chunks, rows, width)
    if not with_product:
        scratch = scratch[1:]
    count = lax.axis_size("fsdp")
    sums = []
    for given, _ in weights:
        own = jax.ShapeDtypeStruct((given.shape[0] // (2 * count), given.shape[1]), low)
        sums.append(own)
        scratch += halving_scratch(count, *own.shape)
    if vectors is not None:
        extras = (*extras, vectors)
        outs.append(jax.ShapeDtypeStruct(vectors.shape, jnp.float32))
        steps = len(peers(("ctx", "fsdp", "tp")))
        scratch += [
            vmem((steps + 1, *vectors.shape), jnp.float32),
            vmem((steps, *vectors.shape), jnp.float32),
            pltpu.SemaphoreType.DMA((steps,)),
            pltpu.SemaphoreType.DMA((steps,)),
        ]
    counts = (len(extras), len(outs), len(weights))
    return fused_call(
        functools.partial(
            sum_kernel, n, chunks, epilogue, counts, with_product, vectors is not None, plan
        ),
        collective,
        (*operands, *extras, *[ref for pair in weights for ref in pair]),
        [jax.ShapeDtypeStruct((rows, width), low)] + outs + sums,
        scratch,
        12 * rows * width * 512,
        2 * len(weights),
    )


def middle_epilogue(own, extras, outs):
    stream, bias, gain, shift = extras
    (middle,) = outs

    def finish(c, total):
        rows = slice(c * own, (c + 1) * own)
        value = stream[rows].astype(jnp.float32) + total + bias[...]
        middle[rows] = value
        return normalize(value)[0] * gain[...] + shift[...]

    return finish


def output_epilogue(own, extras, outs):
    middle, bias = extras

    def finish(c, total):
        return middle[c * own : (c + 1) * own] + total + bias[...]

    return finish


def attn_epilogue(own, extras, outs):
    middle, cotangent, gain = extras[:3]
    grad_middle, sums = outs[:2]
    sums[...] = jnp.zeros_like(sums)

    def finish(c, total):
        rows = slice(c * own, (c + 1) * own)
        normed, inverse = normalize(middle[rows])
        value = cotangent[rows].astype(jnp.float32) + norm_back(total, normed, inverse, gain[...])
        grad_middle[rows] = value
        sums[0:1] += jnp.sum(total * normed, axis=0, keepdims=True)
        sums[1:2] += jnp.sum(total, axis=0, keepdims=True)
        sums[2:3] += jnp.sum(value.astype(low).astype(jnp.float32), axis=0, keepdims=True)
        return value

    return finish


def input_epilogue(own, extras, outs):
    stream, grad_middle, gain = extras[:3]
    sums = outs[0]
    sums[...] = jnp.zeros_like(sums)

    def finish(c, total):
        rows = slice(c * own, (c + 1) * own)
        normed, inverse = normalize(stream[rows].astype(jnp.float32))
        sums[0:1] += jnp.sum(total * normed, axis=0, keepdims=True)
        sums[1:2] += jnp.sum(total, axis=0, keepdims=True)
        return grad_middle[rows] + norm_back(total, normed, inverse, gain[...])

    return finish


def flipped(index, bits):
    out, bit = index, 1
    while bit <= bits:
        if bits & bit:
            out = out + bit * (1 - 2 * ((index // bit) % 2))
        bit *= 2
    return out


class Halving:
    def __init__(self, given, kept, out, refs):
        self.given, self.kept, self.out = given, kept, out
        self.mine, self.held, self.landing = refs[:3]
        self.own_sem, self.core_send, self.core_recv, self.half_send, self.half_recv = refs[3:]
        self.count = lax.axis_size("fsdp")
        self.rows = out.shape[0]
        self.half = out.shape[1] // 2
        _, self.place, _, self.beside, self.across = ctx_place()
        self.turn = lax.axis_index("fsdp")

    def shards(self):
        return [(far, over) for far in range(self.count - 1, -1, -1) for over in (1, 0)]

    def shard(self, far, over):
        p = flipped(self.turn, far) * 2 + flipped(self.place, over)
        return pl.ds(pl.multiple_of(p * self.rows, self.rows), self.rows)

    def core_copy(self, far, over):
        i = 2 * far + over
        return ctx_copy(
            self.given.at[self.shard(far, over)],
            self.held.at[i],
            self.core_send.at[i],
            self.core_recv.at[i],
            self.beside,
        )

    def own_copy(self, far, over):
        i = 2 * far + over
        return pltpu.make_async_copy(
            self.kept.at[self.shard(far, over)], self.mine.at[i], self.own_sem.at[i]
        )

    def half_copy(self, way, bit, far, over):
        n = self.count
        if way == 0:
            i = n + far - 1 if bit else far
        else:
            i = 2 * n - 1 + 2 * (far - 1) + over if bit else 4 * n - 3
        device = {"fsdp": flipped(self.turn, bit)} if bit else self.across
        columns = slice(way * self.half, (way + 1) * self.half)
        copy = ctx_copy(
            self.held.at[2 * far + over, :, columns],
            self.landing.at[i],
            self.half_send.at[i],
            self.half_recv.at[i],
            device,
        )
        return copy, i, columns

    def start(self):
        for far, over in self.shards():
            self.core_copy(far, over).start()
        for far, over in self.shards():
            self.own_copy(far, over).start()

    def send(self, way, bit, far, over):
        self.half_copy(way, bit, far, over)[0].start()

    def take(self, way, bit, far, over):
        copy, i, columns = self.half_copy(way, bit, far, over)
        copy.wait_recv()
        far, over = (far - bit, over) if bit else (far, 0)
        k = 2 * far + over
        self.held[k, :, columns] = add_low(self.held[k, :, columns], self.landing[i])
        return far

    def core_step(self):
        top = self.count // 2
        for far, over in self.shards():
            k = 2 * far + over
            self.own_copy(far, over).wait()
            self.core_copy(far, over).wait_recv()
            self.held[k] = add_low(self.held[k], self.mine[k])
            if over:
                self.send(0, 0, far, over)
            if far >= top:
                self.send(1, top, far, over)

    def middle_step(self):
        top = self.count // 2
        for far in range(self.count - 1, -1, -1):
            self.take(0, 0, far, 1)
            if far >= top:
                self.send(0, top, far, 0)
        bit = top
        while bit > 1:
            for far in range(2 * bit - 1, bit - 1, -1):
                left = self.take(0, bit, far, 0)
                if left >= bit // 2:
                    self.send(0, bit // 2, left, 0)
            bit //= 2
        bit = top
        while bit:
            for far in range(2 * bit - 1, bit - 1, -1):
                for over in (1, 0):
                    left = self.take(1, bit, far, over)
                    if bit > 1 and left >= bit // 2:
                        self.send(1, bit // 2, left, over)
                    if bit == 1 and over:
                        self.send(1, 0, 0, 1)
            bit //= 2

    def last_step(self):
        self.take(0, 1, 1, 0)
        self.take(1, 0, 0, 1)
        self.out[...] = self.held[0]

    def drain(self):
        for far in range(self.count):
            for over in range(2):
                self.core_copy(far, over).wait_send()
            self.half_copy(0, 0, far, 1)[0].wait_send()
            if far:
                bit = 1
                while 2 * bit <= far:
                    bit *= 2
                self.half_copy(0, bit, far, 0)[0].wait_send()
                for over in range(2):
                    self.half_copy(1, bit, far, over)[0].wait_send()
        self.half_copy(1, 0, 0, 1)[0].wait_send()


def add_low(left, right):
    return (left.astype(jnp.float32) + right.astype(jnp.float32)).astype(low)


def halving_scratch(count, rows, width):
    sem = pltpu.SemaphoreType.DMA
    return (
        [vmem((2 * count, rows, width), low)] * 2
        + [vmem((4 * count - 2, rows, width // 2), low)]
        + [sem((2 * count,))] * 3
        + [sem((4 * count - 2,))] * 2
    )


def split_store(value, tile, rows, given, kept, columns):
    side = lax.axis_index("ctx") % 2
    height = value.shape[0]
    step = min(rows, height)
    for k in range(height // step):
        start = tile * height + k * step
        shard = start // rows
        place = shard // 2 * rows + start % rows
        place = pl.ds(place if isinstance(place, int) else pl.multiple_of(place, step), step)
        piece = value[k * step : (k + 1) * step].astype(low)

        @pl.when((shard + side) % 2 == 0)
        def keep():
            kept[place, columns] = piece

        @pl.when((shard + side) % 2 == 1)
        def give():
            given[place, columns] = piece


def hidden_kernel(shard_rows, tiles, *refs):
    (
        act,
        grad_branch,
        grad_turned,
        up,
        down,
        bias,
        up_rows,
        down_rows,
        down_given,
        down_kept,
        up_given,
        up_kept,
        branch_part,
        back_part,
        bias_sum,
        act_turned,
        gelu_all,
        grad_all,
    ) = refs
    i = pl.program_id(0)
    width = act.shape[1]
    tile = up.shape[1]

    @pl.when(i == 0)
    def begin():
        @pl.loop(0, width // 256)
        def turn(k):
            place = pl.ds(pl.multiple_of(k * 256, 256), 256)
            act_turned[place, :] = act[:, place].T

    @pl.when(i < tiles)
    def units():
        columns = pl.ds(pl.multiple_of(i * tile, tile), tile)
        hidden = jnp.dot(act[...], up[...], preferred_element_type=jnp.float32) + bias[...]
        squared = hidden * hidden
        bend = jnp.tanh(0.7978845608028654 * (hidden + 0.044715 * squared * hidden))
        gelu_low = (0.5 * hidden * (1.0 + bend)).astype(low)
        slope = 0.5 * (1.0 + bend) + 0.5 * hidden * (1.0 - bend * bend) * 0.7978845608028654 * (
            1.0 + 3.0 * 0.044715 * squared
        )
        incoming = jnp.dot(grad_branch[...], down[...], preferred_element_type=jnp.float32)
        grad_up_proj = (incoming * slope).astype(low)
        gelu_all[:, columns] = gelu_low
        grad_all[:, columns] = grad_up_proj
        bias_sum[...] = jnp.broadcast_to(
            jnp.sum(grad_up_proj.astype(jnp.float32), axis=0, keepdims=True), bias_sum.shape
        )
        for k in range(width // 512):
            place = slice(k * 512, (k + 1) * 512)
            split_store(
                jnp.dot(grad_turned[place, :], gelu_low, preferred_element_type=jnp.float32),
                k,
                shard_rows,
                down_given,
                down_kept,
                slice(None),
            )
            split_store(
                jnp.dot(act_turned[place, :], grad_up_proj, preferred_element_type=jnp.float32),
                k,
                shard_rows,
                up_given,
                up_kept,
                slice(None),
            )

    @pl.when(i >= tiles)
    def products():
        branch_part[...] = contract_cols(gelu_all[...], down_rows[...]).astype(low)
        back_part[...] = contract_cols(grad_all[...], up_rows[...]).astype(low)


def hidden_layer(shard_rows, act, grad_branch, up, down, bias):
    rows, width = act.shape
    hidden = up.shape[1]
    tile = 512
    tiles = hidden // tile

    def whole(shape):
        return pl.BlockSpec(shape, lambda i: (0, 0), pipeline_mode=pl.Buffered(1))

    def columns(height):
        return pl.BlockSpec((height, tile), lambda i: (0, jnp.minimum(i, tiles - 1)))

    later = pl.BlockSpec((tile, hidden), lambda i: (jnp.maximum(i - tiles, 0), 0))
    parts = pl.BlockSpec((rows, tile), lambda i: (0, jnp.maximum(i - tiles, 0)))
    return pl.pallas_call(
        functools.partial(hidden_kernel, shard_rows, tiles),
        grid=(tiles + width // tile,),
        out_shape=[jax.ShapeDtypeStruct((width // 2, hidden), low)] * 4
        + [jax.ShapeDtypeStruct((rows, width), low)] * 2
        + [jax.ShapeDtypeStruct((8, hidden), jnp.float32)],
        in_specs=[
            whole((rows, width)),
            whole((rows, width)),
            whole((width, rows)),
            columns(width),
            columns(width),
            columns(1),
            later,
            later,
        ],
        out_specs=[columns(width // 2)] * 4 + [parts] * 2 + [columns(8)],
        scratch_shapes=[
            vmem((width, rows), low),
            vmem((rows, hidden), low),
            vmem((rows, hidden), low),
        ],
        compiler_params=pltpu.CompilerParams(vmem_limit_bytes=60 * 1024 * 1024),
        cost_estimate=pl.CostEstimate(
            flops=12 * rows * width * hidden, bytes_accessed=100_000_000, transcendentals=0
        ),
    )(act, grad_branch, grad_branch.T, up, down, bias, up, down)


class Gather:
    def __init__(self, rows, whole, refs):
        self.rows, self.whole = rows, whole
        self.half_send, self.half_recv, self.core_send, self.core_recv = refs
        count = lax.axis_size("fsdp")
        self.group = 2 * count
        bits = [2 * b for b in (1, 2, 4, 8, 16, 32) if b < count]
        self.orders = [[1, *bits], [*bits, 1]]
        self.half = whole.shape[1] // 2
        _, self.place, self.side, self.beside, self.across = ctx_place()
        self.turn = lax.axis_index("fsdp")

    def piece(self, way, d, other=False):
        pair = flipped(self.turn, d // 2) * 2 + flipped(self.place, d % 2)
        shard = 2 * pair + (1 - self.side if other else self.side)
        return self.whole.at[
            pl.ds(pl.multiple_of(shard * self.rows, self.rows), self.rows),
            way * self.half : (way + 1) * self.half,
        ]

    def bit_copy(self, way, d, bit):
        device = self.across if bit == 1 else {"fsdp": flipped(self.turn, bit // 2)}
        piece = self.piece(way, d - bit)
        return ctx_copy(
            piece, piece, self.half_send.at[way, d], self.half_recv.at[way, d], device
        )

    def core_copy(self, way, d, other=False):
        piece = self.piece(way, d, other)
        return ctx_copy(
            piece, piece, self.core_send.at[way, d], self.core_recv.at[way, d], self.beside
        )

    def pass_on(self, way, d, after):
        for bit in self.orders[way][after:]:
            self.bit_copy(way, d + bit, bit).start()
        self.core_copy(way, d).start()

    def begin(self):
        for way in range(2):
            self.pass_on(way, 0, 0)

    def take(self, step):
        for i in range(2**step):
            for way in range(2):
                order = self.orders[way]
                d = order[step] + sum(order[k] for k in range(step) if i & 2**k)
                device = {"fsdp": flipped(self.turn, order[step] // 2)}
                piece = self.piece(way, d)
                ctx_copy(
                    piece,
                    piece,
                    self.half_send.at[way, d],
                    self.half_recv.at[way, d],
                    self.across if order[step] == 1 else device,
                ).wait_recv()
                self.pass_on(way, d, step + 1)

    def finish(self):
        for d in range(self.group):
            for way in range(2):
                self.core_copy(way, d, True).wait_recv()

    def drain(self):
        for way in range(2):
            have = [0]
            for bit in self.orders[way]:
                for d in have:
                    self.bit_copy(way, d + bit, bit).wait_send()
                have += [d + bit for d in have]
            for d in range(self.group):
                self.core_copy(way, d).wait_send()


def meet(others):
    barrier = pltpu.get_barrier_semaphore()
    for other in others:
        pl.semaphore_signal(barrier, inc=1, device_id=other, device_id_type=MESH)
    pl.semaphore_wait(barrier, len(others))


def gather_sems():
    return [pltpu.SemaphoreType.DMA((2, 2 * lax.axis_size("fsdp")))] * 4


def project_kernel(*refs):
    stream, gain, shift, bias, master_qkv, master_out, master_up, master_down = refs[:8]
    projected, act, qkv_out, out_out, up_low, down_low, whole, own, *rest = refs[8:]
    sems, out_sem = rest[:4], rest[4]
    meet(peers(("ctx", "fsdp")))
    groups, shard_rows, piece = master_qkv.shape
    rows, width = stream.shape
    gather = Gather(shard_rows, whole, sems)
    for r in range(groups):
        own[:, r * piece : (r + 1) * piece] = master_qkv[r].astype(low)
    own[:, groups * piece :] = master_out[...].astype(low)
    for way in range(2):
        gather.piece(way, 0)[...] = own[:, way * gather.half : (way + 1) * gather.half]
    gather.begin()
    for master, flat in ((master_up, up_low), (master_down, down_low)):
        for r in range(master.shape[1]):
            flat[:, r * piece : (r + 1) * piece] = master[:, r, :].astype(low)

    @pl.loop(0, rows // 64)
    def norm(i):
        place = pl.ds(pl.multiple_of(i * 64, 64), 64)
        act[place, :] = (
            normalize(stream[place, :].astype(jnp.float32))[0] * gain[...] + shift[...]
        ).astype(low)

    for step in range(len(gather.orders[0])):
        gather.take(step)
    gather.finish()
    wide = projected.shape[1]
    copies = [
        pltpu.make_async_copy(whole.at[:, :wide], qkv_out, out_sem.at[0]),
        pltpu.make_async_copy(whole.at[:, wide:], out_out, out_sem.at[1]),
    ]
    for copy in copies:
        copy.start()

    @pl.loop(0, wide // 512)
    def product(i):
        columns = pl.ds(pl.multiple_of(i * 512, 512), 512)
        projected[:, columns] = (
            jnp.dot(act[...], whole[:, columns], preferred_element_type=jnp.float32)
            + bias[:, columns]
        ).astype(low)

    for copy in copies:
        copy.wait()
    gather.drain()


def project(stream, gain, shift, bias, masters):
    rows, width = stream.shape
    wide = bias.shape[1]
    _, shard_rows, piece = masters[0].shape
    hidden = masters[2].shape[1] * piece
    in_vmem, loose = pl.BlockSpec(memory_space=vmem), pl.BlockSpec(memory_space=pl.ANY)
    depth = shard_rows * lax.axis_size("ctx") * lax.axis_size("fsdp")
    return pl.pallas_call(
        project_kernel,
        out_shape=[
            jax.ShapeDtypeStruct((rows, wide), low),
            jax.ShapeDtypeStruct((rows, width), low),
            jax.ShapeDtypeStruct((depth, wide), low),
            jax.ShapeDtypeStruct((depth, piece), low),
            jax.ShapeDtypeStruct((shard_rows, hidden), low),
            jax.ShapeDtypeStruct((shard_rows, hidden), low),
        ],
        in_specs=[in_vmem] * 8,
        out_specs=[in_vmem] * 2 + [loose] * 2 + [in_vmem] * 2,
        scratch_shapes=[vmem((depth, wide + piece), low), vmem((shard_rows, wide + piece), low)]
        + gather_sems()
        + [pltpu.SemaphoreType.DMA((2,))],
        compiler_params=pltpu.CompilerParams(
            collective_id=4, has_side_effects=True, vmem_limit_bytes=56 * 1024 * 1024
        ),
        cost_estimate=pl.CostEstimate(
            flops=2 * rows * width * wide, bytes_accessed=150_000_000, transcendentals=0
        ),
    )(stream, gain, shift, bias, *masters)


def ctx_place():
    me = lax.axis_index("ctx")
    half, side = me // 2, me % 2
    return me, half, side, {"ctx": me + 1 - 2 * side}, {"ctx": me + 2 - 4 * half}


def ctx_copy(source, target, send, recv, device):
    return pltpu.make_async_remote_copy(
        src_ref=source,
        dst_ref=target,
        send_sem=send,
        recv_sem=recv,
        device_id=device,
        device_id_type=MESH,
    )


class Spread:
    def __init__(self, block, own, pairs, send, recv):
        self.block, self.own, self.pairs, self.send, self.recv = block, own, pairs, send, recv
        self.me, self.half, self.side, self.beside, self.across = ctx_place()

    def rows(self, s, b):
        start = (s * lax.axis_size("ctx") + b) * self.block
        return pl.ds(pl.multiple_of(start, self.block), self.block)

    def copy(self, kind, s, b, own, device):
        target = self.pairs.at[self.rows(s, b)]
        wide = self.pairs.shape[1]
        source = self.own.at[s * self.block : (s + 1) * self.block, wide // 2 :] if own else target
        return ctx_copy(source, target, self.send.at[kind, s], self.recv.at[kind, s], device)

    def start(self, s):
        rows = slice(s * self.block, (s + 1) * self.block)

        @pl.when(self.half == 0)
        def over():
            self.copy(0, s, self.me, True, self.across).start()

        @pl.when(self.side == 0)
        def aside():
            self.copy(1, s, self.me, True, self.beside).start()

        self.pairs[self.rows(s, self.me)] = self.own[rows, self.pairs.shape[1] // 2 :]

    def forward(self, s):
        @pl.when(self.half == 1)
        def onward():
            self.copy(0, s, self.me - 2, False, self.across).wait_recv()
            self.copy(2, s, self.me - 2, False, self.beside).start()

    def arrive(self, s):
        @pl.when(self.half == 1)
        def second():
            self.copy(2, s, 1 - self.side, False, self.beside).wait_recv()

        @pl.when(self.side == 1)
        def first():
            self.copy(1, s, self.me - 1, False, self.beside).wait_recv()

    def drain_own(self, s):
        @pl.when(self.half == 0)
        def over():
            self.copy(0, s, self.me, True, self.across).wait_send()

        @pl.when(self.side == 0)
        def aside():
            self.copy(1, s, self.me, True, self.beside).wait_send()

    def drain(self, s):
        @pl.when(self.half == 1)
        def onward():
            self.copy(2, s, self.me - 2, False, self.beside).wait_send()


class Collect:
    def __init__(self, block, parts, beside_in, across_in, send, recv):
        self.block, self.parts = block, parts
        self.beside_in, self.across_in, self.send, self.recv = beside_in, across_in, send, recv
        self.me, self.half, self.side, self.beside, self.across = ctx_place()

    def rows(self, s, b):
        start = (s * lax.axis_size("ctx") + b) * self.block
        return pl.ds(pl.multiple_of(start, self.block), self.block)

    def aside(self, s, k, away=False):
        b = 2 * k + (self.side if away else 1 - self.side)
        return ctx_copy(
            self.parts.at[self.rows(s, b)],
            self.beside_in.at[k, s],
            self.send.at[k, s],
            self.recv.at[k, s],
            self.beside,
        )

    def over(self, s):
        return ctx_copy(
            self.parts.at[self.rows(s, self.side)],
            self.across_in.at[s],
            self.send.at[2, s],
            self.recv.at[2, s],
            self.across,
        )

    def start(self, s):
        for k in range(2):

            @pl.when(2 * k + 1 - self.side < self.me)
            def give():
                self.aside(s, k).start()

    def forward(self, s):
        for k in range(2):

            @pl.when(2 * k + self.side < self.me + 1 - 2 * self.side)
            def take():
                self.aside(s, k, True).wait_recv()

        @pl.when(self.half == 1)
        def onward():
            held = self.parts.at[self.rows(s, self.side)]
            held[...] = (
                held[...].astype(jnp.float32) + self.beside_in[0, s].astype(jnp.float32)
            ).astype(low)
            self.over(s).start()

    def finish(self, s, target):
        target[...] = self.parts[self.rows(s, self.me)]
        for k in range(2):

            @pl.when((self.side == 0) & (self.half == k))
            def near():
                target[...] = (
                    target[...].astype(jnp.float32) + self.beside_in[k, s].astype(jnp.float32)
                ).astype(low)

        @pl.when(self.half == 0)
        def far():
            self.over(s).wait_recv()
            target[...] = (
                target[...].astype(jnp.float32) + self.across_in[s].astype(jnp.float32)
            ).astype(low)

    def drain(self, s):
        for k in range(2):

            @pl.when(2 * k + 1 - self.side < self.me)
            def gave():
                self.aside(s, k).wait_send()

        @pl.when(self.half == 1)
        def sent():
            self.over(s).wait_send()


def offsets(base):
    shape = base.shape
    base[...] = (
        lax.broadcasted_iota(jnp.int32, shape, 0) - lax.broadcasted_iota(jnp.int32, shape, 1)
    ).astype(jnp.float32)


def head_scores(query, key, slope, base, j):
    far = base[...] + (j * base.shape[0]).astype(jnp.float32)
    return contract_cols(query, key) * HD ** (-0.5) - slope * jnp.abs(far)


def head_columns(h, shift=0):
    return slice(shift + h * HD, shift + (h + 1) * HD)


def distances(far):
    me = lax.axis_index("ctx")
    shape = far.shape
    column = lax.broadcasted_iota(jnp.int32, shape, 1)
    row = lax.broadcasted_iota(jnp.int32, shape, 0) + me * shape[0]
    apart = jnp.abs((row - column).astype(jnp.float32))
    far[...] = jnp.where(column < (me + 1) * shape[0], apart, 1e30)


def forward_heads(s, heads, block, projected, pairs, slopes, far, context, log_total):
    own = slice(s * block, (s + 1) * block)
    count = far.shape[1]
    keys = slice(s * count, (s + 1) * count)
    wide = pairs.shape[1] // 2
    for h in heads:
        scores = (
            contract_cols(projected[own, head_columns(h)], pairs[keys, head_columns(h)])
            * HD ** (-0.5)
            - slopes[h, 0:1, 0:1] * far[...]
        )
        peak = jnp.max(scores, axis=-1, keepdims=True)
        exponent = jnp.exp(scores - peak)
        weight = jnp.sum(exponent, axis=-1, keepdims=True)
        total = jnp.dot(
            exponent.astype(low),
            pairs[keys, head_columns(h, wide)],
            preferred_element_type=jnp.float32,
        )
        context[own, head_columns(h)] = (total / weight).astype(low)
        log_total[own, head_columns(h)] = jnp.broadcast_to(peak + jnp.log(weight), (block, HD))


def backward_heads(
    s, heads, block, projected, pairs, slopes, base, context, log_total, grad, parts, out
):
    me = lax.axis_index("ctx")
    count = lax.axis_size("ctx")
    own = slice(s * block, (s + 1) * block)
    wide = pairs.shape[1] // 2
    queries = [projected[own, head_columns(h)] for h in heads]
    incomings = [grad[own, head_columns(h)] for h in heads]
    levels = [log_total[own, head_columns(h)][:, 0:1] for h in heads]
    means = [
        jnp.sum(
            incoming.astype(jnp.float32) * context[own, head_columns(h)].astype(jnp.float32),
            axis=-1,
            keepdims=True,
        )
        for h, incoming in zip(heads, incomings)
    ]

    def step(j, totals):
        rows = pl.ds(pl.multiple_of((s * count + me - j) * block, block), block)
        keys = [pairs[rows, head_columns(h)] for h in heads]
        probs = [
            jnp.exp(head_scores(query, key, slopes[h, 0:1], base, j) - level)
            for h, query, key, level in zip(heads, queries, keys, levels)
        ]
        grad_probs = [
            contract_cols(incoming, pairs[rows, head_columns(h, wide)])
            for h, incoming in zip(heads, incomings)
        ]
        grad_scores = [
            (prob * (grad_prob - mean)).astype(low)
            for prob, grad_prob, mean in zip(probs, grad_probs, means)
        ]
        for h, prob, grad_score, query, incoming in zip(
            heads, probs, grad_scores, queries, incomings
        ):
            parts[rows, head_columns(h)] = (
                contract_rows(grad_score, query) * HD ** (-0.5)
            ).astype(low)
            parts[rows, head_columns(h, wide)] = contract_rows(prob.astype(low), incoming).astype(
                low
            )
        return tuple(
            total + jnp.dot(grad_score, key, preferred_element_type=jnp.float32)
            for total, grad_score, key in zip(totals, grad_scores, keys)
        )

    totals = lax.fori_loop(
        0, me + 1, step, tuple(jnp.zeros((block, HD), jnp.float32) for _ in heads)
    )
    for h, total in zip(heads, totals):
        out[own, head_columns(h)] = (total * HD ** (-0.5)).astype(low)


def attend_kernel(n, chunks, tile, *refs):
    (
        projected,
        slopes,
        out_weight,
        stream,
        bias,
        gain,
        shift,
        full,
        middle,
        context,
        log_total,
        pairs,
        part,
        landing,
        total,
        *rest,
    ) = refs
    sems, (base, send, recv) = rest[:4], rest[4:]
    rows, width = full.shape
    seqs = chunks // 2
    block = rows // seqs
    heads = context.shape[1] // HD
    pace = heads // 2
    _, _, _, beside, across = ctx_place()
    greet(n, [beside, across])
    finish = middle_epilogue(rows // chunks // n, (stream, bias, gain, shift), (middle,))
    line = Line(n, chunks, part, full, landing, total, sems, finish, 2)
    spread = Spread(block, projected, pairs, send, recv)
    spread.start(0)
    distances(base)
    for s in range(seqs):
        for b in range(1, pairs.shape[0] // rows):

            @pl.when(b > spread.me)
            def clear():
                pairs[spread.rows(s, b)] = jnp.zeros((block, pairs.shape[1]), low)

    def attend(s, first, last):
        if first == 0:
            spread.forward(s)
            if s + 1 < seqs:
                spread.drain_own(s)
                spread.start(s + 1)
            spread.arrive(s)
        for h in range(first, last, 2):
            forward_heads(
                s,
                range(h, min(h + 2, last)),
                block,
                projected,
                pairs,
                slopes,
                base,
                context,
                log_total,
            )

    def multiply(s):
        own = slice(s * block, (s + 1) * block)

        @pl.loop(0, width // tile)
        def one(i):
            columns = pl.ds(pl.multiple_of(i * tile, tile), tile)
            part[own, columns] = contract_cols(context[own, :], out_weight[columns, :]).astype(low)

    attend(0, 0, heads)
    multiply(0)
    for t in range(1, line.slots + 1):
        line.slot(t)
        s = (t + 1) // 2
        if s < seqs:
            attend(s, 0 if t % 2 else pace, pace if t % 2 else heads)
            if t % 2 == 0:
                multiply(s)
    spread.drain_own(seqs - 1)
    for s in range(seqs):
        spread.drain(s)
    line.drain()


def backward_kernel(n, chunks, shard_rows, *refs):
    (
        part,
        middle,
        bias,
        grad_attn,
        out_weight,
        projected,
        pairs,
        context,
        log_total,
        slopes,
        act,
        full,
        grad_projected,
        given,
        kept,
        landing,
        total,
        *rest,
    ) = refs
    sems, (base, grad_context, parts, beside_in, across_in, send, recv) = rest[:4], rest[4:]
    rows, width = full.shape
    seqs = chunks // 2
    block = rows // seqs
    heads = context.shape[1] // HD
    wide = context.shape[1]
    pace = heads // 2
    _, _, _, beside, across = ctx_place()
    greet(n, [beside, across])
    finish = output_epilogue(rows // chunks // n, (middle, bias), ())
    line = Line(n, chunks, part, full, landing, total, sems, finish)
    collect = Collect(block, parts, beside_in, across_in, send, recv)
    offsets(base)

    def backward(s, first, last):
        own = slice(s * block, (s + 1) * block)
        if first == 0:
            grad_context[own, :] = jnp.dot(
                grad_attn[own, :], out_weight[...], preferred_element_type=jnp.float32
            ).astype(low)
        backward_heads(
            s,
            range(first, last),
            block,
            projected,
            pairs,
            slopes,
            base,
            context,
            log_total,
            grad_context,
            parts,
            grad_projected,
        )
        if last == heads:
            collect.start(s)

    def finished(s):
        collect.finish(s, grad_projected.at[s * block : (s + 1) * block, wide:])

    def features(source, right, columns, first, last):
        @pl.loop(first, last)
        def one(i):
            place = pl.ds(pl.multiple_of(i * 256, 256), 256)
            value = contract_rows(source[:, place], right[...])
            split_store(value, i, shard_rows, given, kept, columns)

    attn_columns = slice(0, 3 * wide)
    out_columns = slice(3 * wide, 4 * wide)

    tiles = width // 256
    tasks = []
    for s in range(seqs):
        tasks.append([functools.partial(backward, s, 0, pace)])
        tasks.append([functools.partial(backward, s, pace, heads)])
    tasks += [[] for _ in range(max(seqs + 3, line.slots - len(tasks)))]
    for s in range(seqs):
        tasks[2 * s + 2].append(functools.partial(collect.forward, s))
    after = 2 * seqs
    tasks[after].append(functools.partial(features, grad_attn, context, out_columns, 0, tiles))
    for s in range(seqs):
        tasks[after + 1 + s].append(functools.partial(finished, s))
    for i in range(2):
        tasks[after + 1 + seqs + i].append(
            functools.partial(
                features,
                act,
                grad_projected,
                attn_columns,
                tiles * i // 2,
                tiles * (i + 1) // 2,
            )
        )
    for t in range(1, max(line.slots, len(tasks)) + 1):
        line.slot(t)
        for task in tasks[t - 1] if t <= len(tasks) else []:
            task()
    for s in range(seqs):
        collect.drain(s)
    line.drain()


def fused_call(body, collective, operands, outs, scratch, flops, loose=0):
    whole = pl.BlockSpec(memory_space=vmem)
    away = pl.BlockSpec(memory_space=pl.ANY)
    specs = [whole] * (len(operands) - loose) + [away] * loose
    return pl.pallas_call(
        body,
        out_shape=outs,
        in_specs=specs,
        out_specs=[whole] * len(outs),
        scratch_shapes=scratch,
        compiler_params=pltpu.CompilerParams(
            collective_id=collective,
            has_side_effects=True,
            vmem_limit_bytes=60 * 1024 * 1024,
        ),
        cost_estimate=pl.CostEstimate(flops=flops, bytes_accessed=200_000_000, transcendentals=0),
    )(*operands)


def local(
    inputs,
    cotangent,
    master_qkv,
    qkv_moment1,
    qkv_moment2,
    master_out,
    out_moment1,
    out_moment2,
    master_up,
    up_moment1,
    up_moment2,
    master_down,
    down_moment1,
    down_moment2,
    norm_gains,
    gain_moment1,
    gain_moment2,
    shared_biases,
    shared_moment1,
    shared_moment2,
    split_biases,
    split_moment1,
    split_moment2,
):
    seq_count, block_len, model_width = inputs.shape
    row_count = seq_count * block_len
    width_part = master_qkv.shape[2]
    hidden_rows = master_up.shape[1]
    local_heads = width_part // HD
    tp_count = lax.axis_size("tp")
    chunks = 2 * seq_count
    own_rows = row_count // chunks // tp_count

    def own_part(values):
        blocks = values.reshape(chunks, tp_count * own_rows, model_width)
        taken = lax.dynamic_slice_in_dim(blocks, lax.axis_index("tp") * own_rows, own_rows, axis=1)
        return taken.reshape(-1, model_width)

    own_shape = jax.ShapeDtypeStruct((row_count // tp_count, model_width), jnp.float32)
    sums_shape = jax.ShapeDtypeStruct((8, model_width), jnp.float32)
    gains = [norm_gains[i : i + 1] for i in range(2)]
    shared = [shared_biases[i : i + 1] for i in range(4)]
    inputs_own = own_part(inputs)
    cotangent_own = own_part(cotangent)

    projected_bias = jnp.concatenate(
        [split_biases[0], jnp.zeros((width_part,), jnp.float32), split_biases[1]]
    )
    projected, act_one, qkv_flat, out_flat, up_low, down_low = project(
        inputs.reshape(row_count, model_width),
        gains[0],
        shared[0],
        projected_bias[None],
        (jnp.swapaxes(master_qkv, 0, 1), master_out, master_up, master_down),
    )
    head_ids = (lax.axis_index("tp") * local_heads + jnp.arange(local_heads)).astype(jnp.float32)
    slopes = jnp.power(2.0, -8.0 * (head_ids + 1.0) / (local_heads * lax.axis_size("tp")))
    slopes = jnp.broadcast_to(slopes[:, None, None], (local_heads, 8, block_len))
    sems = line_scratch(tp_count, chunks, row_count, model_width)
    pair_rows = row_count * lax.axis_size("ctx")
    square = vmem((block_len, block_len), jnp.float32)
    pair_sems = [pltpu.SemaphoreType.DMA((3, seq_count))] * 2
    up_flat, down_flat = (
        lax.all_gather(rows, ("fsdp", "ctx"), axis=0, tiled=True) for rows in (up_low, down_low)
    )
    act_two, middle, context, log_total, pairs = fused_call(
        functools.partial(attend_kernel, tp_count, chunks, 256),
        0,
        (
            projected,
            slopes,
            out_flat,
            inputs_own,
            shared[2],
            gains[1],
            shared[1],
        ),
        [
            jax.ShapeDtypeStruct((row_count, model_width), low),
            own_shape,
            jax.ShapeDtypeStruct((row_count, width_part), low),
            jax.ShapeDtypeStruct((row_count, width_part), jnp.float32),
            jax.ShapeDtypeStruct((pair_rows, 2 * width_part), low),
        ],
        sems
        + [vmem((block_len, block_len * lax.axis_size("ctx")), jnp.float32)]
        + pair_sems,
        4 * row_count * model_width * width_part,
    )
    down_given, down_kept, up_given, up_kept, branch_part, back_part, bias_sum = hidden_layer(
        master_qkv.shape[0],
        act_two,
        cotangent.reshape(row_count, model_width),
        up_flat,
        down_flat,
        split_biases[2:].reshape(1, -1),
    )
    grad_attn, grad_middle, sums_two, sum_down, sum_up = tp_sum(
        tp_count,
        chunks,
        attn_epilogue,
        2,
        (back_part,),
        (middle, cotangent_own, gains[1]),
        [own_shape, sums_shape],
        [(down_given, down_kept), (up_given, up_kept)],
        ((2, 7), (4, 11)),
    )
    pair_block = (block_len, 2 * width_part)
    output, grad_projected, attn_given, attn_kept = fused_call(
        functools.partial(backward_kernel, tp_count, chunks, master_qkv.shape[0]),
        1,
        (
            branch_part,
            middle,
            shared[3],
            grad_attn,
            out_flat,
            projected,
            pairs,
            context,
            log_total,
            slopes,
            act_one,
        ),
        [
            jax.ShapeDtypeStruct((row_count, model_width), low),
            jax.ShapeDtypeStruct((row_count, 3 * width_part), low),
            jax.ShapeDtypeStruct((model_width // 2, 4 * width_part), low),
            jax.ShapeDtypeStruct((model_width // 2, 4 * width_part), low),
        ],
        sems[1:]
        + [
            square,
            vmem((row_count, width_part), low),
            vmem((pair_rows, 2 * width_part), low),
            vmem((2, seq_count, *pair_block), low),
            vmem((seq_count, *pair_block), low),
        ]
        + pair_sems,
        12 * row_count * model_width * width_part,
    )
    output = output.reshape(seq_count, block_len, model_width)
    query_low = grad_projected[:, :width_part]
    value_low = grad_projected[:, 2 * width_part :]
    split_grads = jnp.concatenate(
        [
            jnp.sum(query_low, axis=0, dtype=jnp.float32)[None],
            jnp.sum(value_low, axis=0, dtype=jnp.float32)[None],
            bias_sum[0].reshape(hidden_rows, width_part),
        ],
        axis=0,
    )
    vectors = jnp.concatenate(
        [
            jnp.zeros((2, model_width), jnp.float32),
            sums_two[0:3],
            jnp.sum(cotangent_own, axis=0, dtype=jnp.float32)[None],
            jnp.zeros((2, model_width), jnp.float32),
        ]
    )
    vectors = jnp.concatenate([vectors, jnp.pad(split_grads, ((0, 2), (0, 0)))], axis=1)
    input_low, _, vector_sum, sum_attn = tp_sum(
        tp_count,
        chunks,
        input_epilogue,
        3,
        (grad_projected, qkv_flat),
        (inputs_own, grad_middle, gains[0]),
        [sums_shape],
        [(attn_given, attn_kept)],
        ((2, 8),),
        vectors,
    )
    input_grad = input_low.astype(jnp.float32).reshape(seq_count, block_len, model_width)

    gain_sum = jnp.concatenate([vector_sum[0:1, :model_width], vector_sum[2:3, :model_width]])
    shared_sum = jnp.concatenate([vector_sum[1:2, :model_width], vector_sum[3:6, :model_width]])
    split_sum = vector_sum[: 2 + hidden_rows, model_width:]
    q_one, q_two, q_new, q_copy = (
        jnp.swapaxes(out, 0, 1)
        for out in adam_matrix(
            sum_attn,
            *(jnp.swapaxes(values, 0, 1) for values in (master_qkv, qkv_moment1, qkv_moment2)),
        )
    )
    sum_out = sum_attn[:, 3 * width_part :].astype(jnp.float32)
    o_one, o_two, o_new = adam_update(
        master_out, out_moment1, out_moment2, sum_out, matrix_rate, True
    )
    u_one, u_two, u_new, u_copy = adam_matrix(sum_up, master_up, up_moment1, up_moment2)
    d_one, d_two, d_new, d_copy = adam_matrix(sum_down, master_down, down_moment1, down_moment2)
    g_one, g_two, g_new = adam_update(
        norm_gains, gain_moment1, gain_moment2, gain_sum, vector_rate, False
    )
    s_one, s_two, s_new = adam_update(
        shared_biases, shared_moment1, shared_moment2, shared_sum, vector_rate, False
    )
    p_one, p_two, p_new = adam_update(
        split_biases, split_moment1, split_moment2, split_sum, vector_rate, False
    )
    return (
        output,
        input_grad,
        q_one,
        q_two,
        q_new,
        q_copy,
        o_one,
        o_two,
        o_new,
        o_new.astype(jnp.bfloat16),
        u_one,
        u_two,
        u_new,
        u_copy,
        d_one,
        d_two,
        d_new,
        d_copy,
        g_one,
        g_two,
        g_new,
        s_one,
        s_two,
        s_new,
        p_one,
        p_two,
        p_new,
    )


def solution(mesh):
    return jax.shard_map(
        local,
        mesh=mesh,
        in_specs=(
            P("fsdp", "ctx", None),
            P("fsdp", "ctx", None),
            P(("fsdp", "ctx"), None, "tp"),
            P(("fsdp", "ctx"), None, "tp"),
            P(("fsdp", "ctx"), None, "tp"),
            P(("fsdp", "ctx"), "tp"),
            P(("fsdp", "ctx"), "tp"),
            P(("fsdp", "ctx"), "tp"),
            P(("fsdp", "ctx"), None, "tp"),
            P(("fsdp", "ctx"), None, "tp"),
            P(("fsdp", "ctx"), None, "tp"),
            P(("fsdp", "ctx"), None, "tp"),
            P(("fsdp", "ctx"), None, "tp"),
            P(("fsdp", "ctx"), None, "tp"),
            P(),
            P(),
            P(),
            P(),
            P(),
            P(),
            P(None, "tp"),
            P(None, "tp"),
            P(None, "tp"),
        ),
        out_specs=(
            P("fsdp", "ctx", None),
            P("fsdp", "ctx", None),
            P(("fsdp", "ctx"), None, "tp"),
            P(("fsdp", "ctx"), None, "tp"),
            P(("fsdp", "ctx"), None, "tp"),
            P(("fsdp", "ctx"), None, "tp"),
            P(("fsdp", "ctx"), "tp"),
            P(("fsdp", "ctx"), "tp"),
            P(("fsdp", "ctx"), "tp"),
            P(("fsdp", "ctx"), "tp"),
            P(("fsdp", "ctx"), None, "tp"),
            P(("fsdp", "ctx"), None, "tp"),
            P(("fsdp", "ctx"), None, "tp"),
            P(("fsdp", "ctx"), None, "tp"),
            P(("fsdp", "ctx"), None, "tp"),
            P(("fsdp", "ctx"), None, "tp"),
            P(("fsdp", "ctx"), None, "tp"),
            P(("fsdp", "ctx"), None, "tp"),
            P(),
            P(),
            P(),
            P(),
            P(),
            P(),
            P(None, "tp"),
            P(None, "tp"),
            P(None, "tp"),
        ),
        check_vma=False,
    )
```
